32 devices in a mesh: dp: 4 (over y, core), seq: 8 (over z, x).
Axes of the slice: x: 2, y: 2, z: 4, core: 2. Of those that a mesh axis runs over, the one named last changes fastest.
Arguments:
- tokens: bfloat16 [8, 1024, 2048], P('dp', 'seq'), may hold values from -6 to 6
- lengths: int32 [8], P('dp'), may hold values from 256 to 1024, as said below
- cotangent: bfloat16 [8, 1024, 2048], P('dp', 'seq'), may hold values from -6 to 6
- mixer_gain: bfloat16 [2048], P(('dp', 'seq')), may hold values from 0.5 to 1.5
- feed_gain: bfloat16 [2048], P(('dp', 'seq')), may hold values from 0.5 to 1.5
- head_gain: bfloat16 [512], P(('dp', 'seq')), may hold values from 0.5 to 1.5
- w_query: bfloat16 [2048, 2048], P(('dp', 'seq')), may hold values from -0.25 to 0.25
- w_key: bfloat16 [2048, 2048], P(('dp', 'seq')), may hold values from -0.25 to 0.25
- w_value: bfloat16 [2048, 2048], P(('dp', 'seq')), may hold values from -0.125 to 0.125
- w_gate: bfloat16 [2048, 2048], P(('dp', 'seq')), may hold values from -0.125 to 0.125
- w_out: bfloat16 [2048, 2048], P(('dp', 'seq')), may hold values from -0.125 to 0.125
- rank_down: bfloat16 [2048, 16], P(('dp', 'seq')), may hold values from -0.125 to 0.125
- rank_up: bfloat16 [256, 16], P(('dp', 'seq')), may hold values from -1.5 to 1.5
- rank_bias: bfloat16 [256], P(('dp', 'seq')), may hold values from -1 to 9
- w_act: bfloat16 [5632, 2048], P(('dp', 'seq')), may hold values from -0.125 to 0.125
- w_lin: bfloat16 [5632, 2048], P(('dp', 'seq')), may hold values from -0.125 to 0.125
- w_down: bfloat16 [5632, 2048], P(('dp', 'seq')), may hold values from -0.078125 to 0.078125
Outputs:
- block_out: bfloat16 [8, 1024, 2048], P('dp', 'seq')
- tokens_grad: float32 [8, 1024, 2048], P('dp', 'seq')
- mixer_gain_grad: float32 [2048], P(('dp', 'seq'))
- feed_gain_grad: float32 [2048], P(('dp', 'seq'))
- head_gain_grad: float32 [512], P(('dp', 'seq'))
- w_query_grad: float32 [2048, 2048], P(('dp', 'seq'))
- w_key_grad: float32 [2048, 2048], P(('dp', 'seq'))
- w_value_grad: float32 [2048, 2048], P(('dp', 'seq'))
- w_gate_grad: float32 [2048, 2048], P(('dp', 'seq'))
- w_out_grad: float32 [2048, 2048], P(('dp', 'seq'))
- rank_down_grad: float32 [2048, 16], P(('dp', 'seq'))
- rank_up_grad: float32 [256, 16], P(('dp', 'seq'))
- rank_bias_grad: float32 [256], P(('dp', 'seq'))
- w_act_grad: float32 [5632, 2048], P(('dp', 'seq'))
- w_lin_grad: float32 [5632, 2048], P(('dp', 'seq'))
- w_down_grad: float32 [5632, 2048], P(('dp', 'seq'))
The draws below stay inside these ranges and needn't reach their ends.
Inputs may be any that keep to these rules, and one draw needn't show every extreme that they name: `lengths`: in each group of 2 sequences on one index of dp, one sequence, which one drawn from the seed, has all 1024 tokens live; live tokens come first in every sequence.
All inputs are finite; a program needn't handle non-finite values.
Results may differ from the reference program's by a relative error of at most 0.017.
Values may be sent and summed in bfloat16 or wider, within the bound.
A program may use at most 648 MiB of HBM per device.

```python
import jax
import jax.numpy as jnp
from jax import lax

D = 2048
HEADS = 4
SLOTS = 64
FF = 5632
RANK = 16
SEQS = 2
BLOCK = 64
LENGTH = 1024
SEQS_ALL = 8


def draw_lengths(key, part):
    key = jax.random.fold_in(key, 7)
    groups = SEQS_ALL // SEQS
    pick_key, length_key = jax.random.split(key)
    drawn = jax.random.randint(length_key, (groups, SEQS), LENGTH // 4, LENGTH + 1)
    chosen = jax.random.randint(pick_key, (groups, 1), 0, SEQS)
    drawn = jnp.where(jnp.arange(SEQS)[None, :] == chosen, LENGTH, drawn)
    return drawn.reshape(SEQS_ALL).astype(jnp.int32)


def shard_levels(own_key, shape, pieces, smallest, largest):
    def one(axis_at, shards_of):
        draws = jax.random.uniform(jax.random.fold_in(jax.random.fold_in(own_key, 6), axis_at), (shards_of,), jnp.float32, smallest / len(pieces), largest / len(pieces))
        return jnp.repeat(jnp.exp(draws), shape[axis_at] // shards_of).reshape((-1,) + (1,) * (len(shape) - axis_at - 1))

    gain = one(*pieces[0])
    for cut in pieces[1:]:
        gain = gain * one(*cut)
    return gain


def bell_draw(stream_key, extent, deviation, limit, shards=(), held_as=jnp.bfloat16):
    array = jax.random.normal(stream_key, extent, jnp.float32) * deviation
    if len(shards) > 0:
        array = shard_levels(stream_key, extent, shards, -0.22, 0.18) * array
    return jnp.clip(array, min=-limit, max=limit).astype(held_as)


def setup_inputs(seed: int = 0) -> dict:
    key_of = jax.random.split(jax.random.key(seed), 18)
    tokens = bell_draw(key_of[0], (SEQS_ALL, LENGTH, D), 1.0, 6.0, ((0, 4), (1, 8)))
    lengths = draw_lengths(jax.random.fold_in(key_of[17], 71), 0)
    cotangent = bell_draw(key_of[2], (SEQS_ALL, LENGTH, D), 1.0, 6.0, ((0, 4), (1, 8)))
    mixer_gain = jnp.clip(1.0 + 0.1 * jax.random.normal(key_of[3], (D,), jnp.float32), 0.5, 1.5).astype(jnp.bfloat16)
    feed_gain = jnp.clip(1.0 + 0.1 * jax.random.normal(key_of[4], (D,), jnp.float32), 0.5, 1.5).astype(jnp.bfloat16)
    head_gain = jnp.clip(1.0 + 0.1 * jax.random.normal(key_of[5], (D // HEADS,), jnp.float32), 0.5, 1.5).astype(jnp.bfloat16)
    w_query = bell_draw(key_of[6], (D, D), (D // 4) ** -0.5, 0.25, ((0, 32),))
    w_key = bell_draw(key_of[7], (D, D), (D // 4) ** -0.5, 0.25, ((0, 32),))
    w_value = bell_draw(key_of[8], (D, D), D ** -0.5, 0.125, ((0, 32),))
    w_gate = bell_draw(key_of[9], (D, D), D ** -0.5, 0.125, ((0, 32),))
    w_out = bell_draw(key_of[10], (D, D), D ** -0.5, 0.125, ((0, 32),))
    rank_down = bell_draw(key_of[11], (D, RANK), D ** -0.5, 0.125, ((0, 32),))
    rank_up = bell_draw(key_of[12], (HEADS * SLOTS, RANK), RANK ** -0.5, 1.5, ((0, 32),))
    rank_bias = jnp.clip(-1.0 + 10.0 * jax.random.uniform(key_of[13], (HEADS * SLOTS,), jnp.float32) ** shard_levels(key_of[13], (HEADS * SLOTS,), ((0, 32),), -0.2, 0.2), -1.0, 9.0).astype(jnp.bfloat16)
    w_act = bell_draw(key_of[14], (FF, D), D ** -0.5, 0.125, ((0, 32),))
    w_lin = bell_draw(key_of[15], (FF, D), D ** -0.5, 0.125, ((0, 32),))
    w_down = bell_draw(key_of[16], (FF, D), FF ** -0.5, 0.078125, ((0, 32),))
    return {"tokens": tokens, "lengths": lengths, "cotangent": cotangent, "mixer_gain": mixer_gain, "feed_gain": feed_gain, "head_gain": head_gain, "w_query": w_query, "w_key": w_key, "w_value": w_value, "w_gate": w_gate, "w_out": w_out, "rank_down": rank_down, "rank_up": rank_up, "rank_bias": rank_bias, "w_act": w_act, "w_lin": w_lin, "w_down": w_down}


EPS = 1e-06
GATE_NORM = 8.0
PRECISION_LEVEL = lax.Precision.HIGHEST

@jax.custom_vjp
def low(v):
    return lax.optimization_barrier(v.astype(jnp.bfloat16)).astype(jnp.float32)

@jax.custom_vjp
def low_back(v):
    return v

def low_keep(v):
    return (low(v), None)

def low_pass(kept, grad):
    return (grad,)

def back_keep(v):
    return (v, None)

def back_low(kept, grad):
    return (low(grad),)
low.defvjp(low_keep, low_pass)
low_back.defvjp(back_keep, back_low)

def matmul(former, latter):
    return jnp.dot(former, latter, precision=PRECISION_LEVEL, preferred_element_type=jnp.float32)

def rms_scale(tensor):
    return lax.rsqrt(lax.optimization_barrier(jnp.mean(tensor * tensor, axis=-1, keepdims=True)) + EPS)

def slot_block(states, inputs):
    key_memory_state, value_memory_state = states
    queries, key_features, value_features, log_decay = inputs
    block_len = queries.shape[1]
    scaling = queries.shape[2] ** (-0.5)
    running = jnp.cumsum(log_decay, axis=1)
    writes = -jnp.expm1(log_decay)
    causal = (jnp.arange(block_len)[:, None] >= jnp.arange(block_len)[None, :])[None, :, :, None]
    spread = running[:, :, None, :] - running[:, None, :, :]
    weight = jnp.where(causal, jnp.exp(jnp.where(causal, spread, 0.0)), 0.0) * writes[:, None, :, :]
    pair_dots = jnp.einsum('htd,hid->hti', queries, key_features, precision=PRECISION_LEVEL) * scaling
    carried = jnp.einsum('htd,hjd->htj', queries, key_memory_state, precision=PRECISION_LEVEL) * scaling
    growth = jnp.exp(running)
    scores = growth * carried + jnp.einsum('hti,htij->htj', pair_dots, weight, precision=PRECISION_LEVEL)
    attend = jax.nn.softmax(scores, axis=-1)
    mixing = jnp.einsum('htj,htij->hti', attend, weight, precision=PRECISION_LEVEL)
    output = jnp.einsum('htj,hjd->htd', attend * growth, value_memory_state, precision=PRECISION_LEVEL)
    output = output + jnp.einsum('hti,hid->htd', mixing, value_features, precision=PRECISION_LEVEL)
    last_total = running[:, -1, :]
    decay_factor = jnp.exp(last_total[:, None, :] - running) * writes
    retain_fraction = jnp.exp(last_total)[:, :, None]
    next_key_state = retain_fraction * key_memory_state + jnp.einsum('gov,goy->gvy', decay_factor, key_features, precision=PRECISION_LEVEL)
    next_value_state = retain_fraction * value_memory_state + jnp.einsum('gov,goy->gvy', decay_factor, value_features, precision=PRECISION_LEVEL)
    return ((next_key_state, next_value_state), output)

def slot_sequence(queries, key_features, value_features, log_decay):
    seq_len = queries.shape[0]
    block_count = seq_len // BLOCK

    def to_blocks(tensor):
        return tensor.reshape(block_count, BLOCK, HEADS, tensor.shape[-1]).transpose(0, 2, 1, 3)
    initial = jnp.zeros((HEADS, SLOTS, D // HEADS), jnp.float32)
    final_states, output = lax.scan(jax.checkpoint(slot_block), (initial, initial), (to_blocks(queries), to_blocks(key_features), to_blocks(value_features), to_blocks(log_decay)))
    return output.transpose(0, 2, 1, 3).reshape(seq_len, HEADS, D // HEADS)

def layer_sequence(params, tokens, length):
    mixer_gain, feed_gain, head_gain, w_query, w_key, w_value, w_gate, w_out, rank_down, rank_up, rank_bias, w_act, w_lin, w_down = params
    seq_len = tokens.shape[0]
    head_width = D // HEADS
    alive = (jnp.arange(seq_len) < length).astype(jnp.float32)[:, None]
    normed_in = low(tokens * rms_scale(tokens) * mixer_gain)
    queries = low(jax.nn.silu(low_back(matmul(normed_in, w_query.T))))
    key_features = low(jax.nn.silu(low_back(matmul(normed_in, w_key.T))))
    value_features = low(low_back(matmul(normed_in, w_value.T)))
    gate_pre = low_back(matmul(normed_in, w_gate.T))
    low_rank = low(low_back(matmul(normed_in, rank_down)))
    gate_logit = low_back(matmul(low_rank, rank_up.T) + rank_bias)
    log_decay = jax.nn.log_sigmoid(gate_logit) / GATE_NORM * alive
    output = slot_sequence(queries.reshape(seq_len, HEADS, head_width), key_features.reshape(seq_len, HEADS, head_width), value_features.reshape(seq_len, HEADS, head_width), log_decay.reshape(seq_len, HEADS, SLOTS))
    normed_out = output * rms_scale(output) * head_gain
    mixed = low(normed_out.reshape(seq_len, D) * jax.nn.silu(gate_pre))
    hidden = tokens + low_back(matmul(mixed, w_out.T))
    normed_mid = low(hidden * rms_scale(hidden) * feed_gain)
    gate_part = low_back(matmul(normed_mid, w_act.T))
    lin_part = low_back(matmul(normed_mid, w_lin.T))
    product = low(jax.nn.silu(gate_part) * lin_part)
    return alive * (hidden + low_back(matmul(product, w_down)))

def reference(tokens, lengths, cotangent, mixer_gain, feed_gain, head_gain, w_query, w_key, w_value, w_gate, w_out, rank_down, rank_up, rank_bias, w_act, w_lin, w_down):
    params = tuple((weight_arg.astype(jnp.float32) for weight_arg in (mixer_gain, feed_gain, head_gain, w_query, w_key, w_value, w_gate, w_out, rank_down, rank_up, rank_bias, w_act, w_lin, w_down)))
    inputs = tokens.astype(jnp.float32)

    def forward(weights, sources):

        def per_sequence(member):
            return layer_sequence(weights, member[0], member[1])
        return lax.map(jax.checkpoint(per_sequence), (sources, lengths))
    result, pullback = jax.vjp(forward, params, inputs)
    param_grads, tokens_grad = pullback(cotangent.astype(jnp.float32))
    return (result.astype(jnp.bfloat16), tokens_grad, param_grads[0], param_grads[1], param_grads[2], param_grads[3], param_grads[4], param_grads[5], param_grads[6], param_grads[7], param_grads[8], param_grads[9], param_grads[10], param_grads[11], param_grads[12], param_grads[13])
```

```python
import functools

import jax
import jax.numpy as jnp
from jax import lax
from jax.experimental import pallas as pl
from jax.experimental.pallas import tpu as pltpu
from jax.sharding import PartitionSpec as P

HEADS = 4
SLOTS = 64
EPS = 1e-06
GATE_NORM = 8.0
F32 = jnp.float32
BF16 = jnp.bfloat16
LEAF = 8
VMEM_LIMIT = 40 * 1024 * 1024


def mm(a, b, ca, cb):
    return lax.dot_general(
        a.astype(BF16), b.astype(BF16), (((ca,), (cb,)), ((), ())), preferred_element_type=F32
    )


def mm_exact(a, b, ca, cb):
    return lax.dot_general(
        a,
        b,
        (((ca,), (cb,)), ((), ())),
        precision=lax.Precision.HIGHEST,
        preferred_element_type=F32,
    )


def two_parts(x):
    high = x.astype(BF16)
    return high, (x - high.astype(F32)).astype(BF16)


def mm_left(exact, b, ca, cb):
    high, low = two_parts(b)
    return mm(exact, high, ca, cb) + mm(exact, low, ca, cb)


def mm_right(a, exact, ca, cb):
    high, low = two_parts(a)
    return mm(high, exact, ca, cb) + mm(low, exact, ca, cb)


def mm_fine(a, b, ca, cb):
    a_high, a_low = two_parts(a)
    b_high, b_low = two_parts(b)
    return mm(a_high, b_high, ca, cb) + (mm(a_high, b_low, ca, cb) + mm(a_low, b_high, ca, cb))


def contract_last(a, b):
    return mm(a, b, 1, 1)


def contract_first(a, b):
    return mm(a, b, 0, 0)


def swish_slope(v):
    sigma = jax.nn.sigmoid(v)
    return sigma * (1.0 + v * (1.0 - sigma))


def rms_scale(v):
    return lax.rsqrt(jnp.mean(v * v, axis=-1, keepdims=True) + EPS)


def grid_index(rows, cols):
    return (
        lax.broadcasted_iota(jnp.int32, (rows, cols), 0),
        lax.broadcasted_iota(jnp.int32, (rows, cols), 1),
    )


def running_sum(decay):
    length = decay.shape[0]
    row, col = grid_index(length, length)
    return mm_exact((row >= col).astype(F32), decay, 1, 0)


def levels(length):
    found = []
    half = length // 2
    while half >= LEAF:
        found.append(half)
        half //= 2
    return found


def level_factors(running, writes, half):
    length, slots = running.shape
    pairs = running.reshape(length // (2 * half), 2 * half, slots)
    anchor = jnp.broadcast_to(pairs[:, half - 1 : half, :], pairs.shape).reshape(length, slots)
    near = jnp.exp(-jnp.abs(running - anchor))
    row, _ = grid_index(length, slots)
    right = (row % (2 * half)) >= half
    return jnp.where(right, near, 0.0), jnp.where(right, 0.0, near), right


def same_block(length, size):
    row, col = grid_index(length, length)
    return (row // size) == (col // size)


def leaf_selector(length):
    row, col = grid_index(length, LEAF)
    return ((row % LEAF) == col).astype(F32)


def leaf_take(square):
    length = square.shape[0]
    kept = jnp.where(same_block(length, LEAF), square, 0.0)
    return mm_exact(kept, leaf_selector(length), 1, 0)


def leaf_spread(columns):
    length = columns.shape[0]
    wide = mm_exact(columns, leaf_selector(length), 1, 1)
    return jnp.where(same_block(length, LEAF), wide, 0.0)


def leaf_row(tensor, at):
    length, width = tensor.shape
    blocks = tensor.reshape(length // LEAF, LEAF, width)
    return jnp.broadcast_to(blocks[:, at : at + 1, :], blocks.shape).reshape(length, width)


def leaf_decay(running, at):
    length, slots = running.shape
    row, _ = grid_index(length, slots)
    reached = (row % LEAF) >= at
    spread = running - leaf_row(running, at)
    return jnp.where(reached, jnp.exp(jnp.where(reached, spread, 0.0)), 0.0)


def masked(square, half):
    length = square.shape[0]
    if 2 * half == length:
        return square
    return jnp.where(same_block(length, 2 * half), square, 0.0)


def read_in_chunk(square, running, writes):
    total = None
    for half in levels(running.shape[0]):
        right, left, _ = level_factors(running, writes, half)
        part = right * mm_fine(masked(square, half), left * writes, 1, 0)
        total = part if total is None else total + part
    columns = leaf_take(square)
    for at in range(LEAF):
        part = columns[:, at : at + 1] * (leaf_decay(running, at) * leaf_row(writes, at))
        total = part if total is None else total + part
    return total


def mix_in_chunk(attend, running, writes):
    total = None
    for half in levels(running.shape[0]):
        right, left, _ = level_factors(running, writes, half)
        part = masked(mm(attend * right, left * writes, 1, 1), half)
        total = part if total is None else total + part
    columns = [
        jnp.sum(
            attend * (leaf_decay(running, at) * leaf_row(writes, at)), axis=1, keepdims=True
        )
        for at in range(LEAF)
    ]
    part = leaf_spread(jnp.concatenate(columns, axis=1))
    return part if total is None else total + part


def summary_kernel(k_ref, v_ref, decay_ref, writes_ref, state_ref, keep_ref):
    running = running_sum(decay_ref[0])
    length = running.shape[0]
    last = running[length - 1 : length, :]
    fade = jnp.exp(last - running) * writes_ref[0]
    width = k_ref.shape[2]
    state_ref[0, :, :width] = mm(fade, k_ref[0], 0, 0)
    state_ref[0, :, width:] = mm(fade, v_ref[0], 0, 0)
    keep_ref[0] = jnp.exp(last)


def forward_kernel(
    q_ref, k_ref, v_ref, gate_ref, decay_ref, writes_ref, state_ref, gain_ref,
    mixed_ref, out_ref, attend_ref,
):
    q, k, v = q_ref[0], k_ref[0], v_ref[0]
    writes = writes_ref[0]
    width = q.shape[1]
    scale = width ** (-0.5)
    running = running_sum(decay_ref[0])
    growth = jnp.exp(running)
    state = state_ref[0]
    dots = mm(q, k, 1, 1) * scale
    scores = growth * (mm(q, state[:, :width], 1, 1) * scale)
    scores = scores + read_in_chunk(dots, running, writes)
    top = jnp.max(scores, axis=1, keepdims=True)
    raw = jnp.exp(scores - top)
    attend = raw / jnp.sum(raw, axis=1, keepdims=True)
    mixing = mix_in_chunk(attend, running, writes)
    out = mm(attend * growth, state[:, width:], 1, 0) + mm(mixing, v, 1, 0)
    out_ref[0] = out
    attend_ref[0] = attend
    gate = gate_ref[0]
    normed = out * rms_scale(out) * gain_ref[...]
    mixed_ref[0] = (normed * (gate * jax.nn.sigmoid(gate))).astype(BF16)


def back_first_kernel(
    grad_mixed_ref, gate_ref, out_ref, attend_ref, q_ref, v_ref, decay_ref, writes_ref,
    state_ref, gain_ref,
    grad_gate_ref, grad_out_ref, grad_scores_ref, adjoint_ref, gain_grad_ref,
):
    q, v = q_ref[0], v_ref[0]
    writes = writes_ref[0]
    width = q.shape[1]
    scale = width ** (-0.5)
    grad_mixed, gate, out = grad_mixed_ref[0], gate_ref[0], out_ref[0]
    gain = gain_ref[...]
    inverse = rms_scale(out)
    normed = out * inverse
    grad_gate_ref[0] = (grad_mixed * (normed * gain) * swish_slope(gate)).astype(BF16)
    e = grad_mixed * (gate * jax.nn.sigmoid(gate))
    gain_grad_ref[0] = jnp.sum(e * normed, axis=0, keepdims=True)
    eg = e * gain
    grad_out = inverse * (eg - normed * jnp.mean(eg * normed, axis=1, keepdims=True))
    grad_out_ref[0] = grad_out.astype(BF16)
    running = running_sum(decay_ref[0])
    growth = jnp.exp(running)
    attend = attend_ref[0]
    u = growth * mm_right(grad_out, state_ref[0, :, width:], 1, 1)
    u = u + read_in_chunk(mm_right(grad_out, v, 1, 1), running, writes)
    grad_scores = attend * (u - jnp.sum(attend * u, axis=1, keepdims=True))
    grad_scores_ref[0] = grad_scores
    adjoint_ref[0, :, :width] = mm(growth * grad_scores * scale, q, 0, 0)
    adjoint_ref[0, :, width:] = mm(growth * attend, grad_out.astype(BF16), 0, 0)


def back_second_kernel(
    grad_out_ref, grad_scores_ref, attend_ref, q_ref, k_ref, v_ref, decay_ref, writes_ref,
    state_ref, adjoint_ref, q_pre_ref, k_pre_ref, logit_ref, alive_ref,
    dq_ref, dk_ref, dv_ref, dlogit_ref,
):
    q, k, v, grad_out = q_ref[0], k_ref[0], v_ref[0], grad_out_ref[0]
    attend, grad_scores = attend_ref[0], grad_scores_ref[0]
    decay, writes = decay_ref[0], writes_ref[0]
    length, slots = decay.shape
    width = q.shape[1]
    scale = width ** (-0.5)
    running = running_sum(decay)
    growth = jnp.exp(running)
    keep = jnp.exp(decay)
    last = running[length - 1 : length, :]
    fade = jnp.exp(last - running)
    state, adjoint = state_ref[0], adjoint_ref[0]
    key_state, value_state = state[:, :width], state[:, width:]
    key_adjoint, value_adjoint = adjoint[:, :width], adjoint[:, width:]
    key_dots = mm(q, k, 1, 1) * scale
    value_dots = mm(grad_out, v, 1, 1)
    row, col = grid_index(length, length)

    columns_sum = jnp.zeros((length, slots), F32)
    crossing = jnp.zeros((length, slots), F32)
    mix_key = jnp.zeros((length, length), F32)
    mix_value = jnp.zeros((length, length), F32)
    for half in levels(length):
        right, left, is_right = level_factors(running, writes, half)
        key_part, value_part = masked(key_dots, half), masked(value_dots, half)
        left_w = left * writes
        gs_right, at_right = grad_scores * right, attend * right
        mix_key = mix_key + masked(mm(gs_right, left_w, 1, 1), half)
        mix_value = mix_value + masked(mm(at_right, left_w, 1, 1), half)
        rows_sum = gs_right * mm_fine(key_part, left_w, 1, 0) + at_right * mm_fine(value_part, left_w, 1, 0)
        open_sum = left * (mm_fine(key_part, gs_right, 0, 0) + mm_fine(value_part, at_right, 0, 0))
        columns_sum = columns_sum + open_sum
        sums = jnp.where(is_right, rows_sum, open_sum * writes)
        forward = jnp.where((row % (2 * half)) >= half, col - row, row - col - 1) >= 0
        wanted = ((row // half) == (col // half)) & forward
        crossing = crossing + mm_left(wanted.astype(F32), sums, 1, 0)
    key_leaf, value_leaf = leaf_take(key_dots), leaf_take(value_dots)
    leaf_at = lax.broadcasted_iota(jnp.int32, (length, slots), 0) % LEAF
    difference = jnp.zeros((length, slots), F32)
    mix_key_columns, mix_value_columns = [], []
    for at in range(LEAF):
        fall = leaf_decay(running, at)
        mass = leaf_row(writes, at)
        mix_key_columns.append(jnp.sum(grad_scores * fall * mass, axis=1, keepdims=True))
        mix_value_columns.append(jnp.sum(attend * fall * mass, axis=1, keepdims=True))
        terms = fall * (
            grad_scores * key_leaf[:, at : at + 1] + attend * value_leaf[:, at : at + 1]
        )
        blocks = terms.reshape(length // LEAF, LEAF, slots)
        whole = jnp.broadcast_to(
            jnp.sum(blocks, axis=1, keepdims=True), blocks.shape
        ).reshape(length, slots)
        columns_sum = columns_sum + jnp.where(leaf_at == at, whole, 0.0)
        later = jnp.where(leaf_at > at, terms, 0.0)
        later_blocks = later.reshape(length // LEAF, LEAF, slots)
        later_whole = jnp.broadcast_to(
            jnp.sum(later_blocks, axis=1, keepdims=True), later_blocks.shape
        ).reshape(length, slots)
        difference = difference + mass * (later - jnp.where(leaf_at == at, later_whole, 0.0))
    mix_key = mix_key + leaf_spread(jnp.concatenate(mix_key_columns, axis=1))
    mix_value = mix_value + leaf_spread(jnp.concatenate(mix_value_columns, axis=1))
    suffix_leaf = (((row // LEAF) == (col // LEAF)) & (col >= row)).astype(F32)
    crossing = crossing + mm_exact(suffix_leaf, difference, 1, 0)

    start_terms = growth * (
        grad_scores * (mm(q, key_state, 1, 1) * scale)
        + attend * mm(grad_out, value_state, 1, 1)
    )
    crossing = crossing + mm_left((col >= row).astype(F32), start_terms, 1, 0)
    end_open = fade * (mm(k, key_adjoint, 1, 1) + mm(v, value_adjoint, 1, 1))
    columns_sum = columns_sum + end_open
    crossing = crossing + mm_left((col < row).astype(F32), end_open * writes, 1, 0)
    through = mm_exact(
        jnp.ones((8, 2 * width), F32), state.astype(F32) * adjoint.astype(F32), 1, 1
    )[0:1, :]
    crossing = crossing + jnp.exp(last) * through
    grad_decay = crossing - keep * columns_sum

    grad_q = (mm(grad_scores * growth, key_state, 1, 0) + mm(mix_key, k, 1, 0)) * scale
    fade_w = fade * writes
    grad_k = mm(mix_key, q, 0, 0) * scale + mm(fade_w, key_adjoint, 1, 0)
    grad_v = mm(mix_value, grad_out, 0, 0) + mm(fade_w, value_adjoint, 1, 0)
    dq_ref[0] = (grad_q * swish_slope(q_pre_ref[0])).astype(BF16)
    dk_ref[0] = (grad_k * swish_slope(k_pre_ref[0])).astype(BF16)
    dv_ref[0] = grad_v.astype(BF16)
    dlogit_ref[0] = (
        alive_ref[0] * grad_decay * jax.nn.sigmoid(-logit_ref[0]) * (1.0 / GATE_NORM)
    ).astype(BF16)


def per_sequence(kernel, inputs, outputs, shared=()):
    count = inputs[0].shape[0]

    def spec(shape):
        return pl.BlockSpec((1,) + tuple(shape[1:]), lambda s: (s, 0, 0))

    return pl.pallas_call(
        kernel,
        grid=(count,),
        in_specs=[spec(x.shape) for x in inputs]
        + [pl.BlockSpec(x.shape, lambda s: (0, 0)) for x in shared],
        out_specs=[spec(x.shape) for x in outputs],
        out_shape=outputs,
        compiler_params=pltpu.CompilerParams(vmem_limit_bytes=VMEM_LIMIT),
    )(*inputs, *shared)


class Lanes:
    def __init__(self):
        self.seq = lax.axis_size("seq")
        self.dp = lax.axis_size("dp")
        self.outer = self.seq // 2
        self.at = lax.axis_index("seq")
        self.d = lax.axis_index("dp")
        self.inner_at = lax.rem(self.at, 2)
        self.outer_at = self.at // 2
        self.groups = [[2 * k + i for k in range(self.outer)] for i in range(2)]

    def swap_inner(self, x):
        return lax.ppermute(x, "seq", [(i, i ^ 1) for i in range(self.seq)])

    def gather_outer(self, x):
        return lax.all_gather(x, "seq", axis=0, tiled=True, axis_index_groups=self.groups)

    def scatter_outer(self, x):
        return lax.psum_scatter(
            x, "seq", scatter_dimension=0, tiled=True, axis_index_groups=self.groups
        )

    def swap_dp(self, x, bit):
        return lax.ppermute(x, "dp", [(i, i ^ bit) for i in range(self.dp)])

    def gather_dp(self, x):
        far = self.swap_dp(x, 2)
        both = jnp.concatenate([x, far], axis=0)
        return jnp.concatenate([both, self.swap_dp(both, 1)], axis=0)

    def scatter_dp(self, x):
        rows = x.shape[0] // 4
        got = self.swap_dp(x[2 * rows :].astype(BF16), 1)
        mine = x[: 2 * rows] + got.astype(F32)
        got = self.swap_dp(mine[rows:].astype(BF16), 2)
        return mine[:rows] + got.astype(F32)

    def gather_plane(self, x):
        half = x.shape[0] // 2
        a, b = x[:half], x[half:]
        a = jnp.concatenate([a, self.swap_inner(a)], axis=0)
        b = jnp.concatenate([b, self.swap_dp(b, 2)], axis=0)
        a = jnp.concatenate([a, self.swap_dp(a, 2)], axis=0)
        b = jnp.concatenate([b, self.swap_inner(b)], axis=0)
        both = jnp.concatenate([a, b], axis=0)
        return jnp.concatenate([both, self.swap_dp(both, 1)], axis=0)

    def fold(self, x, swap):
        half = x.shape[0] // 2
        return x[:half] + swap(x[half:].astype(BF16)).astype(F32)

    def scatter_plane(self, x):
        x = self.fold(x, lambda p: self.swap_dp(p, 1))
        half = x.shape[0] // 2
        a = self.fold(x[:half], lambda p: self.swap_dp(p, 2))
        b = self.fold(x[half:], self.swap_inner)
        a = self.fold(a, self.swap_inner)
        b = self.fold(b, lambda p: self.swap_dp(p, 2))
        return jnp.concatenate([a, b], axis=0)

    def scatter_grad(self, own, other):
        got = self.swap_inner(other.astype(BF16))
        return self.scatter_outer((own + got.astype(F32)).astype(BF16))

    def swap_seq(self, x, bit):
        return lax.ppermute(x, "seq", [(i, i ^ bit) for i in range(self.seq)])

    def steps(self):
        found, bit = [], 1
        while bit < self.seq:
            found.append((functools.partial(self.swap_seq, bit=bit), (self.at // bit) % 2 == 1))
            bit *= 2
        bit = 1
        while bit < self.dp:
            found.append((functools.partial(self.swap_dp, bit=bit), (self.d // bit) % 2 == 1))
            bit *= 2
        return found

    def gather_small(self, x):
        x = x[None]
        for swap, is_set in self.steps():
            got = swap(x)
            x = jnp.concatenate([jnp.where(is_set, got, x), jnp.where(is_set, x, got)], axis=0)
        return x

    def scatter_small(self, x):
        for swap, is_set in reversed(self.steps()):
            half = x.shape[0] // 2
            low, high = x[:half], x[half:]
            x = jnp.where(is_set, high, low) + swap(jnp.where(is_set, low, high))
        return x[0]

    def exchange_heads(self, blocks):
        got = [lax.dynamic_index_in_dim(blocks, self.d, 0, keepdims=False)]
        for r in range(1, self.dp):
            part = lax.dynamic_index_in_dim(
                blocks, jnp.bitwise_xor(self.d, r), 0, keepdims=False
            )
            got.append(self.swap_dp(part, r))
        bit = 1
        while bit < self.dp:
            is_set = (self.d // bit) % 2 == 1
            got = [jnp.where(is_set, got[i ^ bit], got[i]) for i in range(self.dp)]
            bit *= 2
        return jnp.stack(got)

    def pick(self, natural, axis):
        first = lax.index_in_dim(natural, 0, axis, keepdims=False)
        second = lax.index_in_dim(natural, 1, axis, keepdims=False)
        even = self.inner_at == 0
        return jnp.where(even, first, second), jnp.where(even, second, first)


def swap_halves(x, parts):
    size = x.shape[-1] // (2 * parts)
    pieces = [x[..., i * size : (i + 1) * size] for i in range(2 * parts)]
    order = [i ^ 1 for i in range(2 * parts)]
    return jnp.concatenate([pieces[i] for i in order], axis=-1)


def chain(lanes, keeps, total, backward):
    half = total.shape[0] // 2
    even = lanes.inner_at == 0
    own_t = jnp.where(even, total[:half], total[half:])
    other_t = jnp.where(even, total[half:], total[:half])
    got_t = swap_halves(lanes.swap_inner(other_t.astype(BF16)), 2).astype(F32)
    keeps = jnp.where(even, keeps[:, :half], keeps[:, half:])
    keeps = keeps.reshape(lanes.outer, 2, half, -1)
    pair = lax.dynamic_index_in_dim(keeps, lanes.outer_at, 0, keepdims=False)
    is_first = jnp.logical_not(even) if backward else even
    first_t, second_t = jnp.where(is_first, own_t, got_t), jnp.where(is_first, got_t, own_t)
    first_k, second_k = (pair[1], pair[0]) if backward else (pair[0], pair[1])
    entering = jnp.zeros(own_t.shape, F32)
    reach = jnp.ones(first_k.shape, F32)
    block_t = second_k[..., None] * first_t + second_t
    block_keeps = keeps[:, 0] * keeps[:, 1]
    bit = 1
    while bit < lanes.outer:
        at = lanes.outer_at // bit
        is_set = at % 2 == 1
        later = jnp.logical_not(is_set) if backward else is_set
        last_step = 2 * bit == lanes.outer
        moves = [
            (i, i ^ (2 * bit))
            for i in range(lanes.seq)
            if not last_step or (((i // (2 * bit)) % 2 == 1) == backward)
        ]
        got_t = lax.ppermute(block_t.astype(BF16), "seq", moves).astype(F32)
        mine_k = lax.dynamic_index_in_dim(block_keeps, at, 0, keepdims=False)
        got_k = lax.dynamic_index_in_dim(
            block_keeps, jnp.bitwise_xor(at, 1), 0, keepdims=False
        )
        entering = entering + jnp.where(later, reach, 0.0)[..., None] * got_t
        reach = jnp.where(later, reach * got_k, reach)
        ahead_t, behind_t = jnp.where(later, got_t, block_t), jnp.where(later, block_t, got_t)
        block_t = jnp.where(later, mine_k, got_k)[..., None] * ahead_t + behind_t
        block_keeps = block_keeps.reshape(-1, 2, *block_keeps.shape[1:])
        block_keeps = block_keeps[:, 0] * block_keeps[:, 1]
        bit *= 2
    after = first_k[..., None] * entering + first_t
    mine = jnp.where(is_first, entering, after)
    theirs = jnp.where(is_first, after, entering)
    got = swap_halves(lanes.swap_inner(theirs.astype(BF16)), 2)
    mine = mine.astype(BF16)
    return jnp.concatenate(
        [jnp.where(even, mine, got), jnp.where(even, got, mine)], axis=0
    )


def per_device(
    tokens, lengths, cotangent, mixer_gain, feed_gain, head_gain, w_query, w_key, w_value,
    w_gate, w_out, rank_down, rank_up, rank_bias, w_act, w_lin, w_down,
):
    lanes = Lanes()
    seq_count, piece, width = tokens.shape
    rows = seq_count * piece
    sequences = lanes.dp * seq_count
    all_rows = lanes.dp * rows
    head_width = width // HEADS
    half_width = head_width // 2
    rank = rank_down.shape[1]
    devices = lanes.dp * lanes.seq

    counts = lengths.astype(F32)
    high = jnp.floor(counts / 256.0)
    small_parts = [
        mixer_gain, feed_gain, head_gain, rank_down.reshape(-1), rank_up.reshape(-1),
        rank_bias, high.astype(BF16), (counts - 256.0 * high).astype(BF16),
    ]
    sizes = [p.shape[0] for p in small_parts]
    used = sum(sizes)
    padded = -(-used // 128) * 128
    small = jnp.concatenate(small_parts + [jnp.zeros((padded - used,), BF16)])
    smalls = lanes.gather_small(small)
    cuts, offset = [], 0
    for size in sizes:
        cuts.append(smalls[:, offset : offset + size])
        offset += size
    mixer_full = cuts[0].reshape(1, width).astype(F32)
    feed_full = cuts[1].reshape(1, width).astype(F32)
    head_natural = cuts[2].reshape(lanes.outer, 2, half_width // lanes.outer)
    head_own, head_other = lanes.pick(head_natural, 1)
    head_full = jnp.concatenate(
        [head_own.reshape(1, half_width), head_other.reshape(1, half_width)], axis=1
    ).astype(F32)
    down_full = cuts[3].reshape(width, rank)
    up_mine = lax.dynamic_index_in_dim(
        cuts[4].reshape(lanes.dp, SLOTS, rank), lanes.d, 0, keepdims=False
    )
    bias_mine = lax.dynamic_index_in_dim(
        cuts[5].reshape(lanes.dp, 1, SLOTS), lanes.d, 0, keepdims=False
    ).astype(F32)
    all_lengths = cuts[6].astype(F32) * 256.0 + cuts[7].astype(F32)
    all_lengths = all_lengths.reshape(lanes.dp, lanes.seq, seq_count)[:, 0]

    position = (lanes.at * piece + jnp.arange(piece)).astype(F32)
    alive_own = (position[None, :] < counts[:, None]).astype(F32).reshape(rows, 1)
    group_lengths = jnp.concatenate(
        [
            lax.dynamic_index_in_dim(
                all_lengths, jnp.bitwise_xor(lanes.d, r), 0, keepdims=False
            )
            for r in (0, 2, 1, 3)
        ]
    )
    alive = (position[None, :] < group_lengths[:, None]).astype(F32).reshape(all_rows, 1)

    head_rows = w_query.shape[0]

    def gather_two(first, second):
        own = lanes.gather_outer(jnp.concatenate([first, second], axis=0))
        both = [
            x.reshape(lanes.outer, 2, head_rows, width) for x in (own, lanes.swap_inner(own))
        ]
        return [[x[:, m].reshape(half_width, width) for x in both] for m in range(2)]

    (k_own, k_other), (v_own, v_other) = gather_two(w_key, w_value)
    (q_own, q_other), (g_own, g_other) = gather_two(w_query, w_gate)

    out_rows = w_out.shape[0]
    out_split = w_out.reshape(out_rows, lanes.dp, lanes.outer, 2, -1)
    out_own, out_other = lanes.pick(out_split, 3)
    out_local = jnp.concatenate(
        [
            out_own.reshape(out_rows, lanes.dp, half_width),
            out_other.reshape(out_rows, lanes.dp, half_width),
        ],
        axis=2,
    )
    out_mine = lanes.exchange_heads(out_local.transpose(1, 0, 2))
    out_own = lanes.gather_outer(out_mine[None])
    out_other = swap_halves(lanes.swap_inner(out_own), 1)
    even = lanes.inner_at == 0
    out_natural = jnp.stack(
        [jnp.where(even, out_own, out_other), jnp.where(even, out_other, out_own)], axis=2
    )
    out_full = out_natural.transpose(1, 0, 2, 3, 4).reshape(width, head_width)

    down = lanes.gather_outer(w_down)
    act = lanes.gather_outer(w_act)
    lin = lanes.gather_outer(w_lin)

    own_tokens = tokens.reshape(rows, width)
    sources = lanes.gather_dp(own_tokens).astype(F32)
    normed_in = (sources * rms_scale(sources) * mixer_full).astype(BF16)
    grad_out = cotangent.reshape(rows, width).astype(F32) * alive_own
    grad_feed = lanes.gather_plane(grad_out.astype(BF16))

    def project(own, other):
        return jnp.concatenate(
            [contract_last(normed_in, own), contract_last(normed_in, other)], axis=1
        )

    query_pre, key_pre = project(q_own, q_other), project(k_own, k_other)
    value_pre, gate_pre = project(v_own, v_other), project(g_own, g_other)
    low_rank = mm(normed_in, down_full, 1, 0).astype(BF16)
    gate_logit = contract_last(low_rank, up_mine) + bias_mine
    log_decay = jax.nn.log_sigmoid(gate_logit) / GATE_NORM * alive
    writes = -jnp.expm1(log_decay)

    def seqs(x):
        return x.reshape(sequences, piece, x.shape[1])

    def flat(x):
        return x.reshape(all_rows, x.shape[2])

    queries = seqs(jax.nn.silu(query_pre).astype(BF16))
    key_feats = seqs(jax.nn.silu(key_pre).astype(BF16))
    value_feats = seqs(value_pre.astype(BF16))
    decays, writes = seqs(log_decay), seqs(writes)
    gates = seqs(gate_pre)

    def shaped(like_rows, columns, kind):
        return jax.ShapeDtypeStruct((sequences, like_rows, columns), kind)

    summary, keep_all = per_sequence(
        summary_kernel,
        [key_feats, value_feats, decays, writes],
        [shaped(SLOTS, 2 * head_width, F32), shaped(1, SLOTS, F32)],
    )
    keep_all = keep_all.reshape(sequences, SLOTS)
    keeps = keep_all[None]
    bit = 1
    while bit < lanes.seq:
        got = lanes.swap_seq(keeps, bit)
        is_set = (lanes.at // bit) % 2 == 1
        keeps = jnp.concatenate(
            [jnp.where(is_set, got, keeps), jnp.where(is_set, keeps, got)], axis=0
        )
        bit *= 2
    state_in = chain(lanes, keeps, summary, False)
    mixed, slot_out, attend = per_sequence(
        forward_kernel,
        [queries, key_feats, value_feats, gates, decays, writes, state_in],
        [
            shaped(piece, head_width, BF16),
            shaped(piece, head_width, F32),
            shaped(piece, SLOTS, F32),
        ],
        shared=[head_full],
    )
    mixed_flat = flat(mixed)
    hidden = own_tokens.astype(F32) + lanes.scatter_dp(contract_last(mixed_flat, out_full))
    mid_scale = rms_scale(hidden)
    normed_mid = lanes.gather_plane((hidden * mid_scale * feed_full).astype(BF16))

    grad_product = contract_last(grad_feed, down)
    gate_part = contract_last(normed_mid, act)
    lin_part = contract_last(normed_mid, lin)
    sigma = jax.nn.sigmoid(gate_part)
    swish = gate_part * sigma
    product = (swish * lin_part).astype(BF16)
    grad_gate = (
        grad_product * lin_part * (sigma * (1.0 + gate_part * (1.0 - sigma)))
    ).astype(BF16)
    grad_lin = (grad_product * swish).astype(BF16)
    grad_mid = lanes.scatter_plane(mm(grad_gate, act, 1, 0) + mm(grad_lin, lin, 1, 0))
    w_down_grad = lanes.scatter_outer(contract_first(product, grad_feed).astype(BF16))
    w_act_grad = lanes.scatter_outer(contract_first(grad_gate, normed_mid).astype(BF16))
    w_lin_grad = lanes.scatter_outer(contract_first(grad_lin, normed_mid).astype(BF16))
    w_down_grad, w_act_grad, w_lin_grad = [
        x.astype(F32) for x in (w_down_grad, w_act_grad, w_lin_grad)
    ]

    mid_unit = hidden * mid_scale
    feed_gain_part = jnp.sum(grad_mid * mid_unit, axis=0)
    scaled = grad_mid * feed_full
    grad_hidden = grad_out + mid_scale * (
        scaled - mid_unit * jnp.mean(scaled * mid_unit, axis=-1, keepdims=True)
    )
    grad_attn = lanes.gather_dp(grad_hidden.astype(BF16))

    product, grad_attn = lax.optimization_barrier((product, grad_attn))
    feed_sum = lanes.scatter_plane(mm(product, down, 1, 0))
    block_out = (alive_own * (hidden + feed_sum)).astype(BF16)

    grad_mixed = mm(grad_attn, out_full, 1, 0)
    out_grad = contract_first(grad_attn, mixed_flat).astype(BF16)
    out_grad = out_grad.reshape(lanes.dp, lanes.outer, 2, out_rows, head_width)
    own_part, other_part = lanes.pick(out_grad, 2)
    got = swap_halves(lanes.swap_inner(other_part), 1)
    out_sum = (own_part.astype(F32) + got.astype(F32)).astype(BF16).transpose(1, 0, 2, 3)
    out_mine = lanes.scatter_outer(out_sum.reshape(-1, head_width))
    out_mine = out_mine.reshape(lanes.dp, out_rows, head_width)
    out_mine = lanes.exchange_heads(out_mine).transpose(1, 0, 2)
    out_mine = out_mine.reshape(out_rows, lanes.dp, 2, lanes.outer, -1)
    low_half, high_half = lanes.pick(out_mine, 2)
    w_out_grad = jnp.stack([low_half, high_half], axis=3).reshape(out_rows, width).astype(F32)

    grad_gate_pre, grad_slot, grad_scores, adjoint, head_parts = per_sequence(
        back_first_kernel,
        [seqs(grad_mixed), gates, slot_out, attend, queries, value_feats, decays, writes, state_in],
        [
            shaped(piece, head_width, BF16),
            shaped(piece, head_width, BF16),
            shaped(piece, SLOTS, F32),
            shaped(SLOTS, 2 * head_width, F32),
            shaped(1, head_width, F32),
        ],
        shared=[head_full],
    )
    adjoint_in = chain(lanes, keeps, adjoint, True)
    grad_query_pre, grad_key_pre, grad_value_pre, grad_logit = per_sequence(
        back_second_kernel,
        [
            grad_slot, grad_scores, attend, queries, key_feats, value_feats, decays, writes,
            state_in, adjoint_in, seqs(query_pre), seqs(key_pre), seqs(gate_logit), seqs(alive),
        ],
        [
            shaped(piece, head_width, BF16),
            shaped(piece, head_width, BF16),
            shaped(piece, head_width, BF16),
            shaped(piece, SLOTS, BF16),
        ],
    )
    grad_logit = flat(grad_logit)
    bias_part = jnp.sum(grad_logit.astype(F32), axis=0)
    up_part = contract_first(grad_logit, low_rank)
    grad_rank = mm(grad_logit, up_mine, 1, 0).astype(BF16)
    down_part = contract_first(normed_in, grad_rank)

    grad_in = contract_last(grad_rank, down_full)
    mixer_grads = []
    for grad_pre, (own, other) in zip(
        (grad_gate_pre, grad_query_pre, grad_key_pre, grad_value_pre),
        ((g_own, g_other), (q_own, q_other), (k_own, k_other), (v_own, v_other)),
    ):
        grad_pre = flat(grad_pre)
        low, high = grad_pre[:, :half_width], grad_pre[:, half_width:]
        grad_in = grad_in + mm(low, own, 1, 0) + mm(high, other, 1, 0)
        mixer_grads.append(
            lanes.scatter_grad(
                contract_first(low, normed_in), contract_first(high, normed_in)
            ).astype(F32)
        )
    w_gate_grad, w_query_grad, w_key_grad, w_value_grad = mixer_grads
    grad_in = lanes.scatter_dp(grad_in)
    own_sources = own_tokens.astype(F32)
    in_scale = rms_scale(own_sources)
    in_unit = own_sources * in_scale
    mixer_gain_part = jnp.sum(grad_in * in_unit, axis=0)
    scaled = grad_in * mixer_full
    tokens_grad = grad_hidden + in_scale * (
        scaled - in_unit * jnp.mean(scaled * in_unit, axis=-1, keepdims=True)
    )
    tokens_grad = tokens_grad.reshape(seq_count, piece, width)

    head_part = jnp.sum(head_parts, axis=(0, 1)).reshape(2, lanes.outer, -1)
    low_half, high_half = lanes.pick(head_part, 0)
    head_part = jnp.stack([low_half, high_half], axis=1)
    mine = (jnp.arange(lanes.dp) == lanes.d).astype(F32)
    up_all = mine[:, None] * up_part.reshape(1, -1)
    bias_all = mine[:, None] * bias_part.reshape(1, -1)
    parts = [
        mixer_gain_part.reshape(devices, -1),
        feed_gain_part.reshape(devices, -1),
        head_part.reshape(devices, -1),
        down_part.reshape(devices, -1),
        up_all.reshape(devices, -1),
        bias_all.reshape(devices, -1),
    ]
    sizes = [p.shape[1] for p in parts]
    padded = -(-sum(sizes) // 128) * 128
    parts.append(jnp.zeros((devices, padded - sum(sizes)), F32))
    reduced = lanes.scatter_small(jnp.concatenate(parts, axis=1))
    smalls, offset = [], 0
    for size in sizes:
        smalls.append(reduced[offset : offset + size])
        offset += size
    return (
        block_out.reshape(seq_count, piece, width),
        tokens_grad,
        smalls[0],
        smalls[1],
        smalls[2],
        w_query_grad,
        w_key_grad,
        w_value_grad,
        w_gate_grad,
        w_out_grad,
        smalls[3].reshape(-1, rank),
        smalls[4].reshape(-1, rank),
        smalls[5],
        w_act_grad,
        w_lin_grad,
        w_down_grad,
    )


def solution(mesh):
    vector = P(("dp", "seq"))
    matrix = P(("dp", "seq"), None)
    stream = P("dp", "seq", None)
    return jax.shard_map(
        per_device,
        mesh=mesh,
        in_specs=(
            stream, P("dp"), stream, vector, vector, vector, matrix, matrix, matrix, matrix,
            matrix, matrix, matrix, vector, matrix, matrix, matrix,
        ),
        out_specs=(
            stream, stream, vector, vector, vector, matrix, matrix, matrix, matrix, matrix,
            matrix, matrix, vector, matrix, matrix, matrix,
        ),
        check_vma=False,
    )
```

```python
import functools

import jax
import jax.numpy as jnp
from jax import lax
from jax.experimental import pallas as pl
from jax.experimental.pallas import tpu as pltpu
from jax.sharding import PartitionSpec as P

HEADS = 4
SLOTS = 64
EPS = 1e-06
GATE_NORM = 8.0
F32 = jnp.float32
BF16 = jnp.bfloat16
LEAF = 8
VMEM_LIMIT = 40 * 1024 * 1024


def mm(a, b, ca, cb):
    return lax.dot_general(
        a.astype(BF16), b.astype(BF16), (((ca,), (cb,)), ((), ())), preferred_element_type=F32
    )


def mm_exact(a, b, ca, cb):
    return lax.dot_general(
        a,
        b,
        (((ca,), (cb,)), ((), ())),
        precision=lax.Precision.HIGHEST,
        preferred_element_type=F32,
    )


def two_parts(x):
    high = x.astype(BF16)
    return high, (x - high.astype(F32)).astype(BF16)


def mm_left(exact, b, ca, cb):
    high, low = two_parts(b)
    return mm(exact, high, ca, cb) + mm(exact, low, ca, cb)


def mm_right(a, exact, ca, cb):
    high, low = two_parts(a)
    return mm(high, exact, ca, cb) + mm(low, exact, ca, cb)


def mm_fine(a, b, ca, cb):
    a_high, a_low = two_parts(a)
    b_high, b_low = two_parts(b)
    return mm(a_high, b_high, ca, cb) + (mm(a_high, b_low, ca, cb) + mm(a_low, b_high, ca, cb))


def contract_last(a, b):
    return mm(a, b, 1, 1)


def contract_first(a, b):
    return mm(a, b, 0, 0)


def swish_slope(v):
    sigma = jax.nn.sigmoid(v)
    return sigma * (1.0 + v * (1.0 - sigma))


def rms_scale(v):
    return lax.rsqrt(jnp.mean(v * v, axis=-1, keepdims=True) + EPS)


def grid_index(rows, cols):
    return (
        lax.broadcasted_iota(jnp.int32, (rows, cols), 0),
        lax.broadcasted_iota(jnp.int32, (rows, cols), 1),
    )


def running_sum(decay):
    length = decay.shape[0]
    row, col = grid_index(length, length)
    return mm_exact((row >= col).astype(F32), decay, 1, 0)


def levels(length):
    found = []
    half = length // 2
    while half >= LEAF:
        found.append(half)
        half //= 2
    return found


def level_factors(running, writes, half):
    length, slots = running.shape
    pairs = running.reshape(length // (2 * half), 2 * half, slots)
    anchor = jnp.broadcast_to(pairs[:, half - 1 : half, :], pairs.shape).reshape(length, slots)
    near = jnp.exp(-jnp.abs(running - anchor))
    row, _ = grid_index(length, slots)
    right = (row % (2 * half)) >= half
    return jnp.where(right, near, 0.0), jnp.where(right, 0.0, near), right


def same_block(length, size):
    row, col = grid_index(length, length)
    return (row // size) == (col // size)


def leaf_selector(length):
    row, col = grid_index(length, LEAF)
    return ((row % LEAF) == col).astype(F32)


def leaf_take(square):
    length = square.shape[0]
    kept = jnp.where(same_block(length, LEAF), square, 0.0)
    return mm_exact(kept, leaf_selector(length), 1, 0)


def leaf_spread(columns):
    length = columns.shape[0]
    wide = mm_exact(columns, leaf_selector(length), 1, 1)
    return jnp.where(same_block(length, LEAF), wide, 0.0)


def leaf_row(tensor, at):
    length, width = tensor.shape
    blocks = tensor.reshape(length // LEAF, LEAF, width)
    return jnp.broadcast_to(blocks[:, at : at + 1, :], blocks.shape).reshape(length, width)


def leaf_decay(running, at):
    length, slots = running.shape
    row, _ = grid_index(length, slots)
    reached = (row % LEAF) >= at
    spread = running - leaf_row(running, at)
    return jnp.where(reached, jnp.exp(jnp.where(reached, spread, 0.0)), 0.0)


def masked(square, half):
    length = square.shape[0]
    if 2 * half == length:
        return square
    return jnp.where(same_block(length, 2 * half), square, 0.0)


def read_in_chunk(square, running, writes):
    total = None
    for half in levels(running.shape[0]):
        right, left, _ = level_factors(running, writes, half)
        part = right * mm_fine(masked(square, half), left * writes, 1, 0)
        total = part if total is None else total + part
    columns = leaf_take(square)
    for at in range(LEAF):
        part = columns[:, at : at + 1] * (leaf_decay(running, at) * leaf_row(writes, at))
        total = part if total is None else total + part
    return total


def mix_in_chunk(attend, running, writes):
    total = None
    for half in levels(running.shape[0]):
        right, left, _ = level_factors(running, writes, half)
        part = masked(mm(attend * right, left * writes, 1, 1), half)
        total = part if total is None else total + part
    columns = [
        jnp.sum(
            attend * (leaf_decay(running, at) * leaf_row(writes, at)), axis=1, keepdims=True
        )
        for at in range(LEAF)
    ]
    part = leaf_spread(jnp.concatenate(columns, axis=1))
    return part if total is None else total + part


def summary(k, v, decay, writes):
    running = running_sum(decay)
    length = running.shape[0]
    last = running[length - 1 : length, :]
    fade = jnp.exp(last - running) * writes
    return jnp.concatenate([mm(fade, k, 0, 0), mm(fade, v, 0, 0)], axis=1), jnp.exp(last)


def forward_kernel(
    q_ref, k_ref, v_ref, gate_ref, decay_ref, writes_ref, state_ref, gain_ref,
    mixed_ref, out_ref, attend_ref,
):
    q, k, v = q_ref[0], k_ref[0], v_ref[0]
    writes = writes_ref[0]
    width = q.shape[1]
    scale = width ** (-0.5)
    running = running_sum(decay_ref[0])
    growth = jnp.exp(running)
    state = state_ref[0]
    dots = mm(q, k, 1, 1) * scale
    scores = growth * (mm(q, state[:, :width], 1, 1) * scale)
    scores = scores + read_in_chunk(dots, running, writes)
    top = jnp.max(scores, axis=1, keepdims=True)
    raw = jnp.exp(scores - top)
    attend = raw / jnp.sum(raw, axis=1, keepdims=True)
    mixing = mix_in_chunk(attend, running, writes)
    out = mm(attend * growth, state[:, width:], 1, 0) + mm(mixing, v, 1, 0)
    out_ref[0] = out
    attend_ref[0] = attend
    gate = gate_ref[0]
    normed = out * rms_scale(out) * gain_ref[...]
    mixed_ref[0] = (normed * (gate * jax.nn.sigmoid(gate))).astype(BF16)


def back_first_kernel(
    grad_mixed_ref, gate_ref, out_ref, attend_ref, q_ref, v_ref, decay_ref, writes_ref,
    state_ref, gain_ref,
    grad_gate_ref, grad_out_ref, grad_scores_ref, adjoint_ref, gain_grad_ref,
):
    q, v = q_ref[0], v_ref[0]
    writes = writes_ref[0]
    width = q.shape[1]
    scale = width ** (-0.5)
    grad_mixed, gate, out = grad_mixed_ref[0], gate_ref[0], out_ref[0]
    gain = gain_ref[...]
    inverse = rms_scale(out)
    normed = out * inverse
    grad_gate_ref[0] = (grad_mixed * (normed * gain) * swish_slope(gate)).astype(BF16)
    e = grad_mixed * (gate * jax.nn.sigmoid(gate))
    gain_grad_ref[0] = jnp.sum(e * normed, axis=0, keepdims=True)
    eg = e * gain
    grad_out = inverse * (eg - normed * jnp.mean(eg * normed, axis=1, keepdims=True))
    grad_out_ref[0] = grad_out.astype(BF16)
    running = running_sum(decay_ref[0])
    growth = jnp.exp(running)
    attend = attend_ref[0]
    u = growth * mm_right(grad_out, state_ref[0, :, width:], 1, 1)
    u = u + read_in_chunk(mm_right(grad_out, v, 1, 1), running, writes)
    grad_scores = attend * (u - jnp.sum(attend * u, axis=1, keepdims=True))
    grad_scores_ref[0] = grad_scores
    adjoint_ref[0, :, :width] = mm(growth * grad_scores * scale, q, 0, 0)
    adjoint_ref[0, :, width:] = mm(growth * attend, grad_out.astype(BF16), 0, 0)


def back_second_kernel(
    grad_out_ref, grad_scores_ref, attend_ref, q_ref, k_ref, v_ref, decay_ref, writes_ref,
    state_ref, adjoint_ref, q_pre_ref, k_pre_ref, logit_ref, alive_ref,
    grad_pre_ref, dlogit_ref,
):
    q, k, v, grad_out = q_ref[0], k_ref[0], v_ref[0], grad_out_ref[0]
    attend, grad_scores = attend_ref[0], grad_scores_ref[0]
    decay, writes = decay_ref[0], writes_ref[0]
    length, slots = decay.shape
    width = q.shape[1]
    scale = width ** (-0.5)
    running = running_sum(decay)
    growth = jnp.exp(running)
    keep = jnp.exp(decay)
    last = running[length - 1 : length, :]
    fade = jnp.exp(last - running)
    state, adjoint = state_ref[0], adjoint_ref[0]
    key_state, value_state = state[:, :width], state[:, width:]
    key_adjoint, value_adjoint = adjoint[:, :width], adjoint[:, width:]
    key_dots = mm(q, k, 1, 1) * scale
    value_dots = mm(grad_out, v, 1, 1)
    row, col = grid_index(length, length)

    columns_sum = jnp.zeros((length, slots), F32)
    crossing = jnp.zeros((length, slots), F32)
    mix_key = jnp.zeros((length, length), F32)
    mix_value = jnp.zeros((length, length), F32)
    for half in levels(length):
        right, left, is_right = level_factors(running, writes, half)
        key_part, value_part = masked(key_dots, half), masked(value_dots, half)
        left_w = left * writes
        gs_right, at_right = grad_scores * right, attend * right
        mix_key = mix_key + masked(mm(gs_right, left_w, 1, 1), half)
        mix_value = mix_value + masked(mm(at_right, left_w, 1, 1), half)
        rows_sum = gs_right * mm_fine(key_part, left_w, 1, 0) + at_right * mm_fine(value_part, left_w, 1, 0)
        open_sum = left * (mm_fine(key_part, gs_right, 0, 0) + mm_fine(value_part, at_right, 0, 0))
        columns_sum = columns_sum + open_sum
        sums = jnp.where(is_right, rows_sum, open_sum * writes)
        forward = jnp.where((row % (2 * half)) >= half, col - row, row - col - 1) >= 0
        wanted = ((row // half) == (col // half)) & forward
        crossing = crossing + mm_left(wanted.astype(F32), sums, 1, 0)
    key_leaf, value_leaf = leaf_take(key_dots), leaf_take(value_dots)
    leaf_at = lax.broadcasted_iota(jnp.int32, (length, slots), 0) % LEAF
    difference = jnp.zeros((length, slots), F32)
    mix_key_columns, mix_value_columns = [], []
    for at in range(LEAF):
        fall = leaf_decay(running, at)
        mass = leaf_row(writes, at)
        mix_key_columns.append(jnp.sum(grad_scores * fall * mass, axis=1, keepdims=True))
        mix_value_columns.append(jnp.sum(attend * fall * mass, axis=1, keepdims=True))
        terms = fall * (
            grad_scores * key_leaf[:, at : at + 1] + attend * value_leaf[:, at : at + 1]
        )
        blocks = terms.reshape(length // LEAF, LEAF, slots)
        whole = jnp.broadcast_to(
            jnp.sum(blocks, axis=1, keepdims=True), blocks.shape
        ).reshape(length, slots)
        columns_sum = columns_sum + jnp.where(leaf_at == at, whole, 0.0)
        later = jnp.where(leaf_at > at, terms, 0.0)
        later_blocks = later.reshape(length // LEAF, LEAF, slots)
        later_whole = jnp.broadcast_to(
            jnp.sum(later_blocks, axis=1, keepdims=True), later_blocks.shape
        ).reshape(length, slots)
        difference = difference + mass * (later - jnp.where(leaf_at == at, later_whole, 0.0))
    mix_key = mix_key + leaf_spread(jnp.concatenate(mix_key_columns, axis=1))
    mix_value = mix_value + leaf_spread(jnp.concatenate(mix_value_columns, axis=1))
    suffix_leaf = (((row // LEAF) == (col // LEAF)) & (col >= row)).astype(F32)
    crossing = crossing + mm_exact(suffix_leaf, difference, 1, 0)

    start_terms = growth * (
        grad_scores * (mm(q, key_state, 1, 1) * scale)
        + attend * mm(grad_out, value_state, 1, 1)
    )
    crossing = crossing + mm_left((col >= row).astype(F32), start_terms, 1, 0)
    end_open = fade * (mm(k, key_adjoint, 1, 1) + mm(v, value_adjoint, 1, 1))
    columns_sum = columns_sum + end_open
    crossing = crossing + mm_left((col < row).astype(F32), end_open * writes, 1, 0)
    through = mm_exact(
        jnp.ones((8, 2 * width), F32), state.astype(F32) * adjoint.astype(F32), 1, 1
    )[0:1, :]
    crossing = crossing + jnp.exp(last) * through
    grad_decay = crossing - keep * columns_sum

    grad_q = (mm(grad_scores * growth, key_state, 1, 0) + mm(mix_key, k, 1, 0)) * scale
    fade_w = fade * writes
    grad_k = mm(mix_key, q, 0, 0) * scale + mm(fade_w, key_adjoint, 1, 0)
    grad_v = mm(mix_value, grad_out, 0, 0) + mm(fade_w, value_adjoint, 1, 0)
    grad_pre_ref[0, :, :width] = (grad_k * swish_slope(k_pre_ref[0])).astype(BF16)
    grad_pre_ref[0, :, width : 2 * width] = (grad_q * swish_slope(q_pre_ref[0])).astype(BF16)
    grad_pre_ref[0, :, 2 * width :] = grad_v.astype(BF16)
    dlogit_ref[0] = (
        alive_ref[0] * grad_decay * jax.nn.sigmoid(-logit_ref[0]) * (1.0 / GATE_NORM)
    ).astype(BF16)


def per_sequence(kernel, inputs, outputs, shared=()):
    inputs = [x if isinstance(x, tuple) else (x, None) for x in inputs]
    count = inputs[0][0].shape[0]

    def spec(shape, at=None):
        if at is None:
            return pl.BlockSpec((1,) + tuple(shape[1:]), lambda s: (s, 0, 0))
        return pl.BlockSpec((1, shape[1], shape[2] // 3), lambda s: (s, 0, at))

    return pl.pallas_call(
        kernel,
        grid=(count,),
        in_specs=[spec(x.shape, at) for x, at in inputs]
        + [pl.BlockSpec(x.shape, lambda s: (0, 0)) for x in shared],
        out_specs=[spec(x.shape) for x in outputs],
        out_shape=outputs,
        compiler_params=pltpu.CompilerParams(vmem_limit_bytes=VMEM_LIMIT),
    )(*[x for x, _ in inputs], *shared)


CHUNKS = 8
STRIP = 16


def send(src, dst, send_sem, recv_sem, where):
    copy = pltpu.make_async_remote_copy(
        src_ref=src,
        dst_ref=dst,
        send_sem=send_sem,
        recv_sem=recv_sem,
        device_id=where,
        device_id_type=pl.DeviceIdType.MESH,
    )
    copy.start()
    return copy


def greet(partners):
    barrier = pltpu.get_barrier_semaphore()
    for where in partners:
        pl.semaphore_signal(
            barrier, inc=1, device_id=where, device_id_type=pl.DeviceIdType.MESH
        )
    return barrier


def near_partners():
    d, at = lax.axis_index("dp"), lax.axis_index("seq")
    x = {"seq": jnp.bitwise_xor(at, 1)}
    y = {"dp": jnp.bitwise_xor(d, 2)}
    core = {"dp": jnp.bitwise_xor(d, 1)}
    return x, y, core


def everyone(seq, dp, act):
    me = lax.axis_index("dp") * seq + lax.axis_index("seq")

    def turn(r, carry):
        other = jnp.bitwise_xor(me, r)
        act(r, {"dp": other // seq, "seq": other % seq})
        return carry

    lax.fori_loop(1, seq * dp, turn, 0)


def greet_everyone(seq, dp):
    barrier = pltpu.get_barrier_semaphore()
    everyone(
        seq,
        dp,
        lambda r, where: pl.semaphore_signal(
            barrier, inc=1, device_id=where, device_id_type=pl.DeviceIdType.MESH
        ),
    )
    pl.semaphore_wait(barrier, seq * dp - 1)


def gather_kernel(outer, dp, *refs):
    mats, refs = refs[:4], refs[4:]
    tok, small, refs = refs[0], refs[1], refs[2:]
    three, gate, out_tok, out_small, refs = refs[0], refs[1], refs[2], refs[3], refs[4:]
    (
        local_sem, up_send, up_recv, down_send, down_recv, x_send, x_recv,
        tok_send, tok_recv, small_send, small_recv,
    ) = refs
    outs = [three.at[0], three.at[1], three.at[2], gate]
    seq = 2 * outer
    at = lax.axis_index("seq")
    me = lax.axis_index("dp") * seq + at
    z = at // 2
    x, y, core = near_partners()
    above, below = {"seq": at + 2}, {"seq": at - 2}
    has_above, has_below = z < outer - 1, z > 0
    greet_everyone(seq, dp)

    def push(r, where):
        return pltpu.make_async_remote_copy(
            src_ref=small, dst_ref=out_small.at[me], send_sem=small_send.at[r],
            recv_sem=small_recv.at[r], device_id=where, device_id_type=pl.DeviceIdType.MESH,
        )

    everyone(seq, dp, lambda r, where: push(r, where).start())

    def up(m, k, src, origin):
        return pltpu.make_async_remote_copy(
            src_ref=src, dst_ref=outs[m].at[0, origin], send_sem=up_send.at[m, k],
            recv_sem=up_recv.at[m, k], device_id=above, device_id_type=pl.DeviceIdType.MESH,
        )

    def down(m, k, src, origin):
        return pltpu.make_async_remote_copy(
            src_ref=src, dst_ref=outs[m].at[0, origin], send_sem=down_send.at[m, k],
            recv_sem=down_recv.at[m, k], device_id=below, device_id_type=pl.DeviceIdType.MESH,
        )

    def across(m, src, origin):
        return pltpu.make_async_remote_copy(
            src_ref=src, dst_ref=outs[m].at[1, origin], send_sem=x_send.at[m, origin],
            recv_sem=x_recv.at[m, origin], device_id=x, device_id_type=pl.DeviceIdType.MESH,
        )

    for m in range(4):
        @pl.when(has_above)
        def _():
            up(m, 0, mats[m], z).start()

        @pl.when(has_below)
        def _():
            down(m, 0, mats[m], z).start()

        across(m, mats[m], z).start()
    tok_y = send(tok, out_tok.at[1], tok_send.at[0], tok_recv.at[0], y)
    tok_core = send(tok, out_tok.at[2], tok_send.at[1], tok_recv.at[1], core)
    own_small = pltpu.make_async_copy(small, out_small.at[me], local_sem.at[0])
    own_small.start()
    own_tok = pltpu.make_async_copy(tok, out_tok.at[0], local_sem.at[1])
    own_tok.start()
    own_mats = []
    for m in range(4):
        copy = pltpu.make_async_copy(mats[m], outs[m].at[0, z], local_sem.at[2 + m])
        copy.start()
        own_mats.append(copy)

    def pass_on(k, carry):
        for m in range(4):
            @pl.when(z - k >= 0)
            def _():
                slot = outs[m].at[0, z - k]
                up(m, k - 1, slot, z - k).wait_recv()

                @pl.when(has_above)
                def _():
                    up(m, k, slot, z - k).start()

                across(m, slot, z - k).start()

            @pl.when(z + k < outer)
            def _():
                slot = outs[m].at[0, z + k]
                down(m, k - 1, slot, z + k).wait_recv()

                @pl.when(has_below)
                def _():
                    down(m, k, slot, z + k).start()

                across(m, slot, z + k).start()

        return carry

    lax.fori_loop(1, outer, pass_on, 0)
    tok_y.wait()
    tok_last = send(out_tok.at[1], out_tok.at[3], tok_send.at[2], tok_recv.at[2], core)

    def arrived(r, where):
        push(r, where).wait_send()
        theirs = out_small.at[jnp.bitwise_xor(me, r)]
        pltpu.make_async_remote_copy(
            src_ref=theirs, dst_ref=theirs, send_sem=small_send.at[r],
            recv_sem=small_recv.at[r], device_id=where, device_id_type=pl.DeviceIdType.MESH,
        ).wait_recv()

    everyone(seq, dp, arrived)

    def complete(o, carry):
        for m in range(4):
            across(m, outs[m].at[0, o], o).wait()

            @pl.when(has_above & (o <= z))
            def _():
                up(m, o, outs[m].at[0, z], z).wait_send()

            @pl.when(has_below & (o <= outer - 1 - z))
            def _():
                down(m, o, outs[m].at[0, z], z).wait_send()

        return carry

    lax.fori_loop(0, outer, complete, 0)
    for copy in own_mats:
        copy.wait()
    own_small.wait()
    own_tok.wait()
    tok_core.wait()
    tok_last.wait()


def in_hbm():
    return pl.BlockSpec(memory_space=pl.ANY)


def in_vmem():
    return pl.BlockSpec(memory_space=pltpu.VMEM)


def gather_all(outer, dp, mats, tok, small):
    seq = 2 * outer
    rows, width = mats[0].shape
    dma = pltpu.SemaphoreType.DMA
    return pl.pallas_call(
        functools.partial(gather_kernel, outer, dp),
        in_specs=[in_hbm()] * 6,
        out_specs=[in_hbm()] * 4,
        out_shape=[
            jax.ShapeDtypeStruct((3, 2, outer, rows, width), BF16),
            jax.ShapeDtypeStruct((2, outer, rows, width), BF16),
            jax.ShapeDtypeStruct((dp,) + tok.shape, BF16),
            jax.ShapeDtypeStruct((seq * dp,) + small.shape, BF16),
        ],
        scratch_shapes=[
            dma((6,)), dma((4, outer)), dma((4, outer)), dma((4, outer)), dma((4, outer)),
            dma((4, outer)), dma((4, outer)), dma((3,)), dma((3,)), dma((seq * dp,)),
            dma((seq * dp,)),
        ],
        compiler_params=pltpu.CompilerParams(
            collective_id=1, has_side_effects=True, vmem_limit_bytes=VMEM_LIMIT
        ),
    )(*mats, tok, small)


def turned(x):
    row, col = grid_index(x.shape[1], x.shape[1])
    return mm_exact((row == col).astype(F32), x, 1, 1)


def flipped(x):
    size = x.shape[-1] // 4
    return jnp.concatenate([x[:, size * i : size * (i + 1)] for i in (1, 0, 3, 2)], axis=1)


def relay_kernel(outer, backward, *refs):
    if backward:
        totals, keeps, refs = refs[0], refs[1], refs[2:]
        states, refs = refs[0], refs[1:]
    else:
        feats, decays, writes, refs = refs[0], refs[1], refs[2], refs[3:]
        states, keeps, refs = refs[0], refs[1], refs[2:]
    (
        own, to_x, from_x, to_z, from_z, to_back, from_back, keep_mine, keep_theirs,
        x_s, x_r, z_s, z_r, b_s, b_r, k_s, k_r,
    ) = refs
    half = own.shape[0]
    at = lax.axis_index("seq")
    inner, z = at % 2, at // 2
    x, _, _ = near_partners()
    above, below = {"seq": at + 2}, {"seq": at - 2}
    has_above, has_below = z < outer - 1, z > 0
    ahead, has_ahead, has_source = (
        (below, has_below, has_above) if backward else (above, has_above, has_below)
    )
    barrier = greet([x])

    @pl.when(has_above)
    def _():
        greet([above])

    @pl.when(has_below)
    def _():
        greet([below])

    pl.semaphore_wait(
        barrier, 1 + has_above.astype(jnp.int32) + has_below.astype(jnp.int32)
    )

    def compute(s):
        if backward:
            return totals[s]
        width = feats.shape[2] // 3
        total, keep = summary(
            feats[s, :, :width], feats[s, :, 2 * width :], decays[s], writes[s]
        )
        keep_mine[s] = keep
        return total

    crossing = []
    for i in range(half):
        to_x[i] = compute((1 - inner) * half + i).astype(BF16)
        crossing.append(send(to_x.at[i], from_x.at[i], x_s.at[i], x_r.at[i], x))
    for i in range(half):
        own[i] = compute(inner * half + i)
    if backward:
        keep_a, keep_b = keeps[0], keeps[1]
    else:
        send(keep_mine, keep_theirs, k_s.at[0], k_r.at[0], x).wait()
        mine = jnp.concatenate([keep_mine[s] for s in range(2 * half)], axis=0)
        theirs = jnp.concatenate([keep_theirs[s] for s in range(2 * half)], axis=0)
        keep_a = jnp.where(inner == 0, mine, theirs)
        keep_b = jnp.where(inner == 0, theirs, mine)
        keeps[0] = keep_a
        keeps[1] = keep_b
    if backward:
        keep_a, keep_b = keep_b, keep_a
    first_k = turned(jnp.where(inner == 0, keep_a[:half], keep_a[half:]))
    second_k = turned(jnp.where(inner == 0, keep_b[:half], keep_b[half:]))
    is_first = (inner == 1) if backward else (inner == 0)

    def along(i):
        return pltpu.make_async_remote_copy(
            src_ref=to_z.at[i], dst_ref=from_z.at[i], send_sem=z_s.at[i], recv_sem=z_r.at[i],
            device_id=ahead, device_id_type=pl.DeviceIdType.MESH,
        )

    returning = []
    for i in range(half):
        crossing[i].wait()

        @pl.when(jnp.logical_not(has_source))
        def _():
            from_z[i] = jnp.zeros_like(from_z[i])

        @pl.when(has_source)
        def _():
            along(i).wait_recv()

        got = flipped(from_x[i]).astype(F32)
        mine = own[i]
        first = jnp.where(is_first, mine, got)
        second = jnp.where(is_first, got, mine)
        entering = from_z[i].astype(F32)
        after = first_k[:, i : i + 1] * entering + first
        to_z[i] = (second_k[:, i : i + 1] * after + second).astype(BF16)

        @pl.when(has_ahead)
        def _():
            along(i).start()

        states[inner * half + i] = jnp.where(is_first, entering, after).astype(BF16)
        to_back[i] = jnp.where(is_first, after, entering).astype(BF16)
        returning.append(send(to_back.at[i], from_back.at[i], b_s.at[i], b_r.at[i], x))
    for i in range(half):
        returning[i].wait()
        states[(1 - inner) * half + i] = flipped(from_back[i])

        @pl.when(has_ahead)
        def _():
            along(i).wait_send()


def relay(outer, backward, inputs, sequences, slots, width):
    half = sequences // 2
    dma = pltpu.SemaphoreType.DMA
    held = pltpu.VMEM((half, slots, width), BF16)
    states = jax.ShapeDtypeStruct((sequences, slots, width), BF16)
    keeps = jax.ShapeDtypeStruct((2, sequences, slots), F32)
    keep = pltpu.VMEM((sequences, 1, slots), F32)
    return pl.pallas_call(
        functools.partial(relay_kernel, outer, backward),
        in_specs=[in_vmem()] * len(inputs),
        out_specs=in_vmem() if backward else [in_vmem()] * 2,
        out_shape=states if backward else [states, keeps],
        scratch_shapes=[pltpu.VMEM((half, slots, width), F32)] + [held] * 6 + [keep] * 2
        + [dma((half,))] * 6 + [dma((1,))] * 2,
        compiler_params=pltpu.CompilerParams(
            collective_id=7 if backward else 6, has_side_effects=True,
            vmem_limit_bytes=VMEM_LIMIT,
        ),
    )(*inputs)


def middle_kernel(
    parts, tok, gain, extra, hidden, mid, extra_all, from_core, to_y, from_y, normed,
    core_s, core_r, y_s, y_r, local_sem, gx_s, gx_r, gy_s, gy_r, gd_s, gd_r,
    ex_s, ex_r, ey_s, ey_r, ed_s, ed_r, extra_sem, gc_s, gc_r, ec_s, ec_r,
):
    rows = tok.shape[0]
    size = rows // CHUNKS
    x, y, core = near_partners()
    pl.semaphore_wait(greet([x, y, core]), 3)
    cuts = [pl.ds(c * size, size) for c in range(CHUNKS)]
    first = [
        send(parts.at[pl.ds(2, 2), cut], from_core.at[:, cut], core_s.at[c], core_r.at[c], core)
        for c, cut in enumerate(cuts)
    ]
    second = []
    for c, cut in enumerate(cuts):
        first[c].wait()

        def add(r, carry, c=c):
            at = pl.ds(c * size + r * STRIP, STRIP)
            to_y[at] = (parts[1, at].astype(F32) + from_core[1, at].astype(F32)).astype(BF16)
            return carry

        lax.fori_loop(0, size // STRIP, add, 0)
        second.append(send(to_y.at[cut], from_y.at[cut], y_s.at[c], y_r.at[c], y))
    rest = []
    own_extra = pltpu.make_async_copy(extra, extra_all.at[0], extra_sem.at[0])
    own_extra.start()
    rest.append(own_extra)
    extra_x = [
        send(extra.at[cut], extra_all.at[1, cut], ex_s.at[c], ex_r.at[c], x)
        for c, cut in enumerate(cuts)
    ]
    rest.append(send(extra, extra_all.at[4], ec_s.at[0], ec_r.at[0], core))
    over_x, over_y, diagonal = [], [], []
    for c in range(CHUNKS + 2):
        if c < CHUNKS:
            cut = cuts[c]
            second[c].wait()

            def norm(r, carry, c=c):
                at = pl.ds(c * size + r * STRIP, STRIP)
                total = tok[at].astype(F32) + (
                    (parts[0, at].astype(F32) + from_core[0, at].astype(F32))
                    + from_y[at].astype(F32)
                )
                hidden[at] = total
                normed[at] = (total * rms_scale(total) * gain[...]).astype(BF16)
                return carry

            lax.fori_loop(0, size // STRIP, norm, 0)
            over_y.append(send(normed.at[cut], mid.at[2, cut], gy_s.at[c], gy_r.at[c], y))
            over_x.append(send(normed.at[cut], mid.at[1, cut], gx_s.at[c], gx_r.at[c], x))
            rest.append(send(normed.at[cut], mid.at[4, cut], gc_s.at[0, c], gc_r.at[0, c], core))
            own = pltpu.make_async_copy(normed.at[cut], mid.at[0, cut], local_sem.at[c])
            own.start()
            rest.append(own)
        if c >= 2:
            at, cut = c - 2, cuts[c - 2]
            over_y[at].wait()
            diagonal.append(send(mid.at[2, cut], mid.at[3, cut], gd_s.at[at], gd_r.at[at], x))
            rest.append(send(mid.at[2, cut], mid.at[6, cut], gc_s.at[2, at], gc_r.at[2, at], core))
    extra_y = [
        send(extra.at[cut], extra_all.at[2, cut], ey_s.at[c], ey_r.at[c], y)
        for c, cut in enumerate(cuts)
    ]
    extra_d = []
    for c, cut in enumerate(cuts):
        extra_x[c].wait()
        extra_d.append(
            send(extra_all.at[1, cut], extra_all.at[3, cut], ed_s.at[c], ed_r.at[c], y)
        )
        over_x[c].wait()
        rest.append(send(mid.at[1, cut], mid.at[5, cut], gc_s.at[1, c], gc_r.at[1, c], core))
    rest.append(send(extra_all.at[1], extra_all.at[5], ec_s.at[1], ec_r.at[1], core))
    for c, cut in enumerate(cuts):
        diagonal[c].wait()
        rest.append(send(mid.at[3, cut], mid.at[7, cut], gc_s.at[3, c], gc_r.at[3, c], core))
    for copy in extra_y + extra_d:
        copy.wait()
    rest.append(
        send(extra_all.at[pl.ds(2, 2)], extra_all.at[pl.ds(6, 2)], ec_s.at[2], ec_r.at[2], core)
    )
    for copy in rest:
        copy.wait()


def middle(parts, tok, gain, extra):
    rows, width = tok.shape
    dma = pltpu.SemaphoreType.DMA
    buffer = pltpu.VMEM((rows, width), BF16)
    return pl.pallas_call(
        middle_kernel,
        in_specs=[in_vmem()] * 3 + [in_hbm()],
        out_specs=[in_vmem(), in_hbm(), in_hbm()],
        out_shape=[
            jax.ShapeDtypeStruct((rows, width), F32),
            jax.ShapeDtypeStruct((8, rows, width), BF16),
            jax.ShapeDtypeStruct((8, rows, width), BF16),
        ],
        scratch_shapes=[pltpu.VMEM((2, rows, width), BF16), buffer, buffer, buffer]
        + [dma((CHUNKS,))] * 17
        + [dma((1,))]
        + [dma((4, CHUNKS))] * 2
        + [dma((3,))] * 2,
        compiler_params=pltpu.CompilerParams(
            collective_id=2, has_side_effects=True, vmem_limit_bytes=VMEM_LIMIT
        ),
    )(parts, tok, gain, extra)


def middle_back_kernel(
    parts, hidden, grad_out, gain, grad_hidden, gain_grad, attn,
    from_core, to_x, from_x, to_y, from_y, rounded,
    core_s, core_r, x_s, x_r, y_s, y_r, local_sem, gy_s, gy_r, gc_s, gc_r,
):
    rows, width = hidden.shape
    size = rows // CHUNKS
    x, y, core = near_partners()
    pl.semaphore_wait(greet([x, y, core]), 3)
    cuts = [pl.ds(c * size, size) for c in range(CHUNKS)]
    first = [
        send(parts.at[pl.ds(4, 4), cut], from_core.at[:, cut], core_s.at[c], core_r.at[c], core)
        for c, cut in enumerate(cuts)
    ]
    second, third = [], []
    for c, cut in enumerate(cuts):
        first[c].wait()

        def add_core(r, carry, c=c):
            at = pl.ds(c * size + r * STRIP, STRIP)
            for j in range(2):
                g = 2 * j + 1
                to_x[j, at] = (
                    parts[g, at].astype(F32) + from_core[g, at].astype(F32)
                ).astype(BF16)
            return carry

        lax.fori_loop(0, size // STRIP, add_core, 0)
        second.append(send(to_x.at[:, cut], from_x.at[:, cut], x_s.at[c], x_r.at[c], x))
    gain_grad[...] = jnp.zeros_like(gain_grad)
    pending, over_y = [], []
    for step in range(CHUNKS + 2):
        if step < CHUNKS:
            c, cut = step, cuts[step]
            second[c].wait()

            def add_x(r, carry, c=c):
                at = pl.ds(c * size + r * STRIP, STRIP)
                to_y[at] = (
                    parts[2, at].astype(F32) + from_core[2, at].astype(F32)
                    + from_x[1, at].astype(F32)
                ).astype(BF16)
                return carry

            lax.fori_loop(0, size // STRIP, add_x, 0)
            third.append(send(to_y.at[cut], from_y.at[cut], y_s.at[c], y_r.at[c], y))
        if 1 <= step <= CHUNKS:
            c, cut = step - 1, cuts[step - 1]
            third[c].wait()

            def back(r, carry, c=c):
                at = pl.ds(c * size + r * STRIP, STRIP)
                grad_mid = (
                    (parts[0, at].astype(F32) + from_core[0, at].astype(F32))
                    + from_x[0, at].astype(F32)
                ) + from_y[at].astype(F32)
                value = hidden[at]
                scale = rms_scale(value)
                unit = value * scale
                gain_grad[...] += jnp.sum(grad_mid * unit, axis=0, keepdims=True)
                scaled = grad_mid * gain[...]
                total = grad_out[at] + scale * (
                    scaled - unit * jnp.mean(scaled * unit, axis=1, keepdims=True)
                )
                grad_hidden[at] = total
                rounded[at] = total.astype(BF16)
                return carry

            lax.fori_loop(0, size // STRIP, back, 0)
            over_y.append(send(rounded.at[cut], attn.at[1, cut], gy_s.at[c], gy_r.at[c], y))
            pending.append(
                send(rounded.at[cut], attn.at[2, cut], gc_s.at[0, c], gc_r.at[0, c], core)
            )
            own = pltpu.make_async_copy(rounded.at[cut], attn.at[0, cut], local_sem.at[c])
            own.start()
            pending.append(own)
        if step >= 2:
            c, cut = step - 2, cuts[step - 2]
            over_y[c].wait()
            pending.append(
                send(attn.at[1, cut], attn.at[3, cut], gc_s.at[1, c], gc_r.at[1, c], core)
            )
    for copy in pending:
        copy.wait()


def middle_back(parts, hidden, grad_out, gain):
    rows, width = hidden.shape
    dma = pltpu.SemaphoreType.DMA

    def buffer(*lead):
        return pltpu.VMEM(lead + (rows, width), BF16)

    return pl.pallas_call(
        middle_back_kernel,
        in_specs=[in_vmem()] * 4,
        out_specs=[in_vmem(), in_vmem(), in_hbm()],
        out_shape=[
            jax.ShapeDtypeStruct((rows, width), F32),
            jax.ShapeDtypeStruct((1, width), F32),
            jax.ShapeDtypeStruct((4, rows, width), BF16),
        ],
        scratch_shapes=[buffer(4), buffer(2), buffer(2), buffer(), buffer(), buffer()]
        + [dma((CHUNKS,))] * 9
        + [dma((2, CHUNKS))] * 2,
        compiler_params=pltpu.CompilerParams(
            collective_id=3, has_side_effects=True, vmem_limit_bytes=VMEM_LIMIT
        ),
    )(parts, hidden, grad_out, gain)


def final_kernel(outer, dp, mats, parts, tok, base, gain, small, *refs):
    out, tokens_grad, out_small, refs = refs[0], refs[1], refs[2], refs[3:]
    (
        from_x, from_below, from_above, total, from_core, to_y, from_y, gain_grad,
        to_all, from_all,
        x_s, x_r, up_s, up_r, down_s, down_r, core_s, core_r, y_s, y_r, all_s, all_r,
    ) = refs
    rows, width = tok.shape
    size = rows // CHUNKS
    high = total.shape[2]
    seq = 2 * outer
    at = lax.axis_index("seq")
    me = lax.axis_index("dp") * seq + at
    z = at // 2
    x, y, core = near_partners()
    above, below = {"seq": at + 2}, {"seq": at - 2}
    has_above, has_below = z < outer - 1, z > 0
    greet_everyone(seq, dp)
    cuts = [pl.ds(c * size, size) for c in range(CHUNKS)]
    first = [
        send(parts.at[pl.ds(2, 2), cut], from_core.at[:, cut], core_s.at[c], core_r.at[c], core)
        for c, cut in enumerate(cuts)
    ]

    def block_of(i):
        return jnp.where(i % 2 == 0, outer - 1 - i // 2, i // 2)

    def across(m, b):
        return pltpu.make_async_remote_copy(
            src_ref=mats.at[m, 1, b], dst_ref=from_x.at[m, b], send_sem=x_s.at[m, b],
            recv_sem=x_r.at[m, b], device_id=x, device_id_type=pl.DeviceIdType.MESH,
        )

    def up(m, b):
        return pltpu.make_async_remote_copy(
            src_ref=total.at[m, b], dst_ref=from_below.at[m, b], send_sem=up_s.at[m, b],
            recv_sem=up_r.at[m, b], device_id=above, device_id_type=pl.DeviceIdType.MESH,
        )

    def down(m, b):
        return pltpu.make_async_remote_copy(
            src_ref=total.at[m, b], dst_ref=from_above.at[m, b], send_sem=down_s.at[m, b],
            recv_sem=down_r.at[m, b], device_id=below, device_id_type=pl.DeviceIdType.MESH,
        )

    def start_x(i, carry):
        for m in range(3):
            across(m, block_of(i)).start()
        return carry

    lax.fori_loop(0, outer, start_x, 0)
    second = []
    for c, cut in enumerate(cuts):
        first[c].wait()

        def add(r, carry, c=c):
            strip = pl.ds(c * size + r * STRIP, STRIP)
            to_y[strip] = (
                parts[1, strip].astype(F32) + from_core[1, strip].astype(F32)
            ).astype(BF16)
            return carry

        lax.fori_loop(0, size // STRIP, add, 0)
        second.append(send(to_y.at[cut], from_y.at[cut], y_s.at[c], y_r.at[c], y))

    def add_into(m, b, other):
        def strip_sum(r, carry):
            strip = pl.ds(r * STRIP, STRIP)
            total[m, b, strip] = (
                total[m, b, strip].astype(F32) + other[m, b, strip].astype(F32)
            ).astype(BF16)
            return carry

        lax.fori_loop(0, high // STRIP, strip_sum, 0)

    def reduce_block(i, carry):
        b = block_of(i)
        for m in range(3):
            across(m, b).wait()

            def strip_sum(r, carry, m=m):
                strip = pl.ds(r * STRIP, STRIP)
                total[m, b, strip] = (
                    mats[m, 0, b, strip].astype(F32) + from_x[m, b, strip].astype(F32)
                ).astype(BF16)
                return carry

            lax.fori_loop(0, high // STRIP, strip_sum, 0)

            @pl.when(b > z)
            def _():
                @pl.when(has_below)
                def _():
                    up(m, b).wait_recv()
                    add_into(m, b, from_below)

                up(m, b).start()

            @pl.when(b < z)
            def _():
                @pl.when(has_above)
                def _():
                    down(m, b).wait_recv()
                    add_into(m, b, from_above)

                down(m, b).start()

        return carry

    lax.fori_loop(0, outer // 2, reduce_block, 0)
    gain_grad[...] = jnp.zeros_like(gain_grad)
    for c in range(CHUNKS):
        second[c].wait()

        def back(r, carry, c=c):
            strip = pl.ds(c * size + r * STRIP, STRIP)
            grad = (
                parts[0, strip].astype(F32) + from_core[0, strip].astype(F32)
            ) + from_y[strip].astype(F32)
            value = tok[strip].astype(F32)
            scale = rms_scale(value)
            unit = value * scale
            gain_grad[...] += jnp.sum(grad * unit, axis=0, keepdims=True)
            scaled = grad * gain[...]
            tokens_grad[strip] = base[strip] + scale * (
                scaled - unit * jnp.mean(scaled * unit, axis=1, keepdims=True)
            )
            return carry

        lax.fori_loop(0, size // STRIP, back, 0)
    devices = seq * dp
    each = width // devices
    row, col = grid_index(devices, width)
    spread = jnp.where(col // each == row, gain_grad[...], 0.0)
    picked_row, picked_col = grid_index(width, 128)
    gathered = mm_exact(spread, ((picked_row % each) == picked_col).astype(F32), 1, 0)
    height = small.shape[1]
    to_all[:, :height] = small[...]
    to_all[:, height:] = jnp.broadcast_to(
        gathered.reshape(devices, 1, 128), (devices, to_all.shape[1] - height, 128)
    )

    def push(r, where):
        return pltpu.make_async_remote_copy(
            src_ref=to_all.at[jnp.bitwise_xor(me, r)], dst_ref=from_all.at[r],
            send_sem=all_s.at[r], recv_sem=all_r.at[r], device_id=where,
            device_id_type=pl.DeviceIdType.MESH,
        )

    everyone(seq, dp, lambda r, where: push(r, where).start())
    lax.fori_loop(outer // 2, outer, reduce_block, 0)
    out_small[...] = to_all[me]

    def add_small(r, where):
        push(r, where).wait()
        out_small[...] += from_all[r]

    everyone(seq, dp, add_small)
    for m in range(3):
        out[m] = total[m, z].astype(F32)

        @pl.when(has_below)
        def _():
            up(m, z).wait_recv()
            out[m] += from_below[m, z].astype(F32)

        @pl.when(has_above)
        def _():
            down(m, z).wait_recv()
            out[m] += from_above[m, z].astype(F32)

    def sent(b, carry):
        for m in range(3):
            @pl.when(b > z)
            def _():
                up(m, b).wait_send()

            @pl.when(b < z)
            def _():
                down(m, b).wait_send()

        return carry

    lax.fori_loop(0, outer, sent, 0)


def finish(outer, dp, mats, parts, tok, base, gain, small):
    rows, width = tok.shape
    high = mats.shape[3]
    devices = 2 * outer * dp
    dma = pltpu.SemaphoreType.DMA
    blocks = pltpu.VMEM((3, outer, high, width), BF16)
    buffer = pltpu.VMEM((rows, width), BF16)
    payload = (small.shape[1] + 8, 128)
    return pl.pallas_call(
        functools.partial(final_kernel, outer, dp),
        in_specs=[in_vmem()] * 6,
        out_specs=[in_vmem()] * 3,
        out_shape=[
            jax.ShapeDtypeStruct((3, high, width), F32),
            jax.ShapeDtypeStruct((rows, width), F32),
            jax.ShapeDtypeStruct(payload, F32),
        ],
        scratch_shapes=[blocks] * 4
        + [
            pltpu.VMEM((2, rows, width), BF16), buffer, buffer, pltpu.VMEM((1, width), F32),
            pltpu.VMEM((devices,) + payload, F32), pltpu.VMEM((devices,) + payload, F32),
        ]
        + [dma((3, outer))] * 6
        + [dma((CHUNKS,))] * 4
        + [dma((devices,))] * 2,
        compiler_params=pltpu.CompilerParams(
            collective_id=4, has_side_effects=True, vmem_limit_bytes=VMEM_LIMIT
        ),
    )(mats, parts, tok, base, gain, small)


class Lanes:
    def __init__(self):
        self.seq = lax.axis_size("seq")
        self.dp = lax.axis_size("dp")
        self.outer = self.seq // 2
        self.at = lax.axis_index("seq")
        self.d = lax.axis_index("dp")
        self.inner_at = lax.rem(self.at, 2)
        self.outer_at = self.at // 2
        self.groups = [[2 * k + i for k in range(self.outer)] for i in range(2)]

    def swap_inner(self, x):
        return lax.ppermute(x, "seq", [(i, i ^ 1) for i in range(self.seq)])

    def gather_outer(self, x):
        return lax.all_gather(x, "seq", axis=0, tiled=True, axis_index_groups=self.groups)

    def scatter_outer(self, x):
        return lax.psum_scatter(
            x, "seq", scatter_dimension=0, tiled=True, axis_index_groups=self.groups
        )

    def swap_dp(self, x, bit):
        return lax.ppermute(x, "dp", [(i, i ^ bit) for i in range(self.dp)])

    def fold(self, x, swap):
        half = x.shape[0] // 2
        return x[:half] + swap(x[half:].astype(BF16)).astype(F32)

    def swap_seq(self, x, bit):
        return lax.ppermute(x, "seq", [(i, i ^ bit) for i in range(self.seq)])

    def exchange_heads(self, blocks):
        got = [lax.dynamic_index_in_dim(blocks, self.d, 0, keepdims=False)]
        for r in range(1, self.dp):
            part = lax.dynamic_index_in_dim(
                blocks, jnp.bitwise_xor(self.d, r), 0, keepdims=False
            )
            got.append(self.swap_dp(part, r))
        bit = 1
        while bit < self.dp:
            is_set = (self.d // bit) % 2 == 1
            got = [jnp.where(is_set, got[i ^ bit], got[i]) for i in range(self.dp)]
            bit *= 2
        return jnp.stack(got)

    def pick(self, natural, axis):
        first = lax.index_in_dim(natural, 0, axis, keepdims=False)
        second = lax.index_in_dim(natural, 1, axis, keepdims=False)
        even = self.inner_at == 0
        return jnp.where(even, first, second), jnp.where(even, second, first)


def swap_halves(x, parts):
    size = x.shape[-1] // (2 * parts)
    pieces = [x[..., i * size : (i + 1) * size] for i in range(2 * parts)]
    order = [i ^ 1 for i in range(2 * parts)]
    return jnp.concatenate([pieces[i] for i in order], axis=-1)


def per_device(
    tokens, lengths, cotangent, mixer_gain, feed_gain, head_gain, w_query, w_key, w_value,
    w_gate, w_out, rank_down, rank_up, rank_bias, w_act, w_lin, w_down,
):
    lanes = Lanes()
    seq_count, piece, width = tokens.shape
    rows = seq_count * piece
    sequences = lanes.dp * seq_count
    all_rows = lanes.dp * rows
    head_width = width // HEADS
    half_width = head_width // 2
    rank = rank_down.shape[1]
    devices = lanes.dp * lanes.seq

    counts = lengths.astype(F32)
    high = jnp.floor(counts / 256.0)
    small_parts = [
        mixer_gain, feed_gain, head_gain, rank_down.reshape(-1), rank_up.reshape(-1),
        rank_bias, high.astype(BF16), (counts - 256.0 * high).astype(BF16),
    ]
    sizes = [p.shape[0] for p in small_parts]
    used = sum(sizes)
    padded = -(-used // 2048) * 2048
    small = jnp.concatenate(small_parts + [jnp.zeros((padded - used,), BF16)])
    own_tokens = tokens.reshape(rows, width)
    w_kqv, w_g, plane_tokens, smalls = gather_all(
        lanes.outer, lanes.dp, [w_key, w_query, w_value, w_gate], own_tokens,
        small.reshape(-1, 128),
    )
    w_kqv = w_kqv.reshape(3 * head_width, width)
    w_g = w_g.reshape(head_width, width)
    smalls = smalls.reshape(devices, padded)
    cuts, offset = [], 0
    for size in sizes:
        cuts.append(smalls[:, offset : offset + size])
        offset += size
    mixer_full = cuts[0].reshape(1, width).astype(F32)
    feed_full = cuts[1].reshape(1, width).astype(F32)
    head_natural = cuts[2].reshape(lanes.outer, 2, half_width // lanes.outer)
    head_own, head_other = lanes.pick(head_natural, 1)
    head_full = jnp.concatenate(
        [head_own.reshape(1, half_width), head_other.reshape(1, half_width)], axis=1
    ).astype(F32)
    down_full = cuts[3].reshape(width, rank)
    up_mine = lax.dynamic_index_in_dim(
        cuts[4].reshape(lanes.dp, SLOTS, rank), lanes.d, 0, keepdims=False
    )
    bias_mine = lax.dynamic_index_in_dim(
        cuts[5].reshape(lanes.dp, 1, SLOTS), lanes.d, 0, keepdims=False
    ).astype(F32)
    all_lengths = cuts[6].astype(F32) * 256.0 + cuts[7].astype(F32)
    all_lengths = all_lengths.reshape(lanes.dp, lanes.seq, seq_count)[:, 0]

    position = (lanes.at * piece + jnp.arange(piece)).astype(F32)
    alive_own = (position[None, :] < counts[:, None]).astype(F32).reshape(rows, 1)
    group_lengths = jnp.concatenate(
        [
            lax.dynamic_index_in_dim(
                all_lengths, jnp.bitwise_xor(lanes.d, r), 0, keepdims=False
            )
            for r in (0, 2, 1, 3)
        ]
    )
    alive = (position[None, :] < group_lengths[:, None]).astype(F32).reshape(all_rows, 1)

    w_out, smalls = lax.optimization_barrier((w_out, smalls))
    out_rows = w_out.shape[0]
    out_split = w_out.reshape(out_rows, lanes.dp, lanes.outer, 2, -1)
    out_own, out_other = lanes.pick(out_split, 3)
    out_local = jnp.concatenate(
        [
            out_own.reshape(out_rows, lanes.dp, half_width),
            out_other.reshape(out_rows, lanes.dp, half_width),
        ],
        axis=2,
    )
    out_mine = lanes.exchange_heads(out_local.transpose(1, 0, 2))
    sources = plane_tokens.reshape(all_rows, width).astype(F32)
    normed_in = (sources * rms_scale(sources) * mixer_full).astype(BF16)
    grad_out = cotangent.reshape(rows, width).astype(F32) * alive_own

    pre = contract_last(normed_in, w_kqv)
    low_rank = mm(normed_in, down_full, 1, 0).astype(BF16)
    gate_logit = contract_last(low_rank, up_mine) + bias_mine
    log_decay = jax.nn.log_sigmoid(gate_logit) / GATE_NORM * alive
    writes = -jnp.expm1(log_decay)

    def seqs(x):
        return x.reshape(sequences, piece, x.shape[1])

    def flat(x):
        return x.reshape(all_rows, x.shape[2])

    is_value = jnp.arange(3 * head_width) >= 2 * head_width
    feats = seqs(jnp.where(is_value, pre, pre * jax.nn.sigmoid(pre)).astype(BF16))
    pre = seqs(pre)
    decays, writes = seqs(log_decay), seqs(writes)

    def shaped(like_rows, columns, kind):
        return jax.ShapeDtypeStruct((sequences, like_rows, columns), kind)

    out_own = lanes.gather_outer(out_mine[None])
    out_own, feats = lax.optimization_barrier((out_own, feats))
    keys, queries, values = (feats, 0), (feats, 1), (feats, 2)
    state_in, keeps = relay(
        lanes.outer, False, [feats, decays, writes], sequences, SLOTS, 2 * head_width
    )
    gates = seqs(contract_last(normed_in, w_g))
    out_other = swap_halves(lanes.swap_inner(out_own), 1)
    even = lanes.inner_at == 0
    natural = jnp.stack(
        [jnp.where(even, out_own, out_other), jnp.where(even, out_other, out_own)], axis=2
    )
    out_full = natural.transpose(1, 0, 2, 3, 4).reshape(width, head_width)
    w_down, w_act, w_lin, state_in = lax.optimization_barrier((w_down, w_act, w_lin, state_in))
    feed = lax.all_gather(
        jnp.stack([w_down, w_act, w_lin]), "seq", axis=1, tiled=True,
        axis_index_groups=lanes.groups,
    )
    down, act, lin = feed[0], feed[1], feed[2]
    mixed, slot_out, attend = per_sequence(
        forward_kernel,
        [queries, keys, values, gates, decays, writes, state_in],
        [
            shaped(piece, head_width, BF16),
            shaped(piece, head_width, F32),
            shaped(piece, SLOTS, F32),
        ],
        shared=[head_full],
    )
    mixed_flat = flat(mixed)
    parts = contract_last(mixed_flat, out_full).astype(BF16)
    hidden, normed_mid, grad_feed = middle(
        parts.reshape(4, rows, width), own_tokens, feed_full, grad_out.astype(BF16)
    )
    normed_mid = normed_mid.reshape(8 * rows, width)
    grad_feed = grad_feed.reshape(8 * rows, width)

    grad_product = contract_last(grad_feed, down)
    gate_part = contract_last(normed_mid, act)
    lin_part = contract_last(normed_mid, lin)
    sigma = jax.nn.sigmoid(gate_part)
    swish = gate_part * sigma
    product = (swish * lin_part).astype(BF16)
    grad_gate = (
        grad_product * lin_part * (sigma * (1.0 + gate_part * (1.0 - sigma)))
    ).astype(BF16)
    grad_lin = (grad_product * swish).astype(BF16)
    feed_grads = jnp.stack(
        [
            contract_first(product, grad_feed).astype(BF16),
            contract_first(grad_gate, normed_mid).astype(BF16),
            contract_first(grad_lin, normed_mid).astype(BF16),
        ]
    )
    grad_gate, grad_lin, feed_grads = lax.optimization_barrier((grad_gate, grad_lin, feed_grads))
    feed_grads = lax.psum_scatter(
        feed_grads, "seq", scatter_dimension=1, tiled=True, axis_index_groups=lanes.groups
    )
    mid_parts = (mm(grad_gate, act, 1, 0) + mm(grad_lin, lin, 1, 0)).astype(BF16)
    grad_hidden, feed_gain_part, grad_attn = middle_back(
        mid_parts.reshape(8, rows, width), hidden, grad_out, feed_full
    )
    grad_attn = grad_attn.reshape(all_rows, width)

    grad_mixed = mm(grad_attn, out_full, 1, 0)
    grad_gate_pre, grad_slot, grad_scores, adjoint, head_parts = per_sequence(
        back_first_kernel,
        [seqs(grad_mixed), gates, slot_out, attend, queries, values, decays, writes, state_in],
        [
            shaped(piece, head_width, BF16),
            shaped(piece, head_width, BF16),
            shaped(piece, SLOTS, F32),
            shaped(SLOTS, 2 * head_width, F32),
            shaped(1, head_width, F32),
        ],
        shared=[head_full],
    )
    grad_gate_flat = flat(grad_gate_pre)
    out_grad = contract_first(grad_attn, mixed_flat).astype(BF16)
    out_grad = out_grad.reshape(lanes.dp, lanes.outer, 2, out_rows, head_width)
    own_part, other_part = lanes.pick(out_grad, 2)
    got = swap_halves(lanes.swap_inner(other_part), 1)
    out_sum = (own_part.astype(F32) + got.astype(F32)).astype(BF16).transpose(1, 0, 2, 3)
    gate_grad = contract_first(grad_gate_flat, normed_in).astype(BF16)
    gate_in = mm(grad_gate_flat, w_g, 1, 0)
    feed_parts = mm(product, down, 1, 0).astype(BF16)
    feed_parts = lanes.fold(feed_parts, lambda p: lanes.swap_dp(p, 1))
    adjoint, out_sum, gate_grad, gate_in, feed_parts = lax.optimization_barrier(
        (adjoint, out_sum, gate_grad, gate_in, feed_parts)
    )
    feed_got = lanes.swap_dp(feed_parts[2 * rows :].astype(BF16), 2)
    adjoint_in = relay(
        lanes.outer, True, [adjoint, keeps], sequences, SLOTS, 2 * head_width
    )
    gate_grad, out_sum, adjoint_in = lax.optimization_barrier((gate_grad, out_sum, adjoint_in))
    out_mine = lanes.scatter_outer(out_sum.reshape(-1, head_width))
    gate_got = lanes.swap_inner(gate_grad[half_width:])
    grad_pre, grad_logit = per_sequence(
        back_second_kernel,
        [
            grad_slot, grad_scores, attend, queries, keys, values, decays, writes,
            state_in, adjoint_in, (pre, 1), (pre, 0), seqs(gate_logit), seqs(alive),
        ],
        [shaped(piece, 3 * head_width, BF16), shaped(piece, SLOTS, BF16)],
    )
    grad_logit = flat(grad_logit)
    bias_part = jnp.sum(grad_logit.astype(F32), axis=0)
    up_part = contract_first(grad_logit, low_rank)
    grad_rank = mm(grad_logit, up_mine, 1, 0).astype(BF16)
    down_part = contract_first(normed_in, grad_rank)

    grad_pre, feed_got, gate_got, out_mine = lax.optimization_barrier(
        (flat(grad_pre), feed_got, gate_got, out_mine)
    )
    gate_sum = (gate_grad[:half_width].astype(F32) + gate_got.astype(F32)).astype(BF16)
    gate_sum, grad_pre = lax.optimization_barrier((gate_sum, grad_pre))
    gate_sum = lanes.scatter_outer(gate_sum)
    feed_parts = feed_parts[: 2 * rows] + feed_got.astype(F32)
    feed_got = lanes.swap_inner(feed_parts[rows:].astype(BF16))
    grad_in = mm(grad_pre, w_kqv, 1, 0) + gate_in + contract_last(grad_rank, down_full)
    mixer_grads = contract_first(grad_pre, normed_in).astype(BF16)
    mixer_grads = mixer_grads.reshape(3, 2, lanes.outer, -1, width)

    head_part = jnp.sum(head_parts, axis=(0, 1)).reshape(2, lanes.outer, -1)
    low_half, high_half = lanes.pick(head_part, 0)
    head_part = jnp.stack([low_half, high_half], axis=1)
    mine = (jnp.arange(lanes.dp) == lanes.d).astype(F32)
    up_all = mine[:, None] * up_part.reshape(1, -1)
    bias_all = mine[:, None] * bias_part.reshape(1, -1)
    parts = [
        feed_gain_part.reshape(devices, -1),
        head_part.reshape(devices, -1),
        down_part.reshape(devices, -1),
        up_all.reshape(devices, -1),
        bias_all.reshape(devices, -1),
    ]
    sizes = [p.shape[1] for p in parts]
    padded = -(-sum(sizes) // 1024) * 1024
    parts.append(jnp.zeros((devices, padded - sum(sizes)), F32))
    small_parts = jnp.concatenate(parts, axis=1).reshape(devices, -1, 128)
    grad_in, mixer_grads, feed_got, gate_sum = lax.optimization_barrier(
        (grad_in.astype(BF16), mixer_grads, feed_got, gate_sum)
    )
    w_gate_grad = gate_sum.astype(F32)
    out_mine = out_mine.reshape(lanes.dp, out_rows, head_width)
    out_mine = lanes.exchange_heads(out_mine).transpose(1, 0, 2)
    out_mine = out_mine.reshape(out_rows, lanes.dp, 2, lanes.outer, -1)
    low_half, high_half = lanes.pick(out_mine, 2)
    w_out_grad = jnp.stack([low_half, high_half], axis=3).reshape(out_rows, width).astype(F32)
    feed_sum = feed_parts[:rows] + feed_got.astype(F32)
    block_out = (alive_own * (hidden + feed_sum)).astype(BF16)
    weight_grads, tokens_grad, reduced = finish(
        lanes.outer, lanes.dp, mixer_grads, grad_in.reshape(4, rows, width), own_tokens,
        grad_hidden, mixer_full, small_parts,
    )
    w_key_grad, w_query_grad, w_value_grad = weight_grads[0], weight_grads[1], weight_grads[2]
    tokens_grad = tokens_grad.reshape(seq_count, piece, width)
    mixer_gain_grad = reduced[padded // 128, : width // devices]
    reduced = reduced.reshape(-1)
    smalls, offset = [], 0
    for size in sizes:
        smalls.append(reduced[offset : offset + size])
        offset += size
    return (
        block_out.reshape(seq_count, piece, width),
        tokens_grad,
        mixer_gain_grad,
        smalls[0],
        smalls[1],
        w_query_grad,
        w_key_grad,
        w_value_grad,
        w_gate_grad,
        w_out_grad,
        smalls[2].reshape(-1, rank),
        smalls[3].reshape(-1, rank),
        smalls[4],
        feed_grads[1].astype(F32),
        feed_grads[2].astype(F32),
        feed_grads[0].astype(F32),
    )


def solution(mesh):
    vector = P(("dp", "seq"))
    matrix = P(("dp", "seq"), None)
    stream = P("dp", "seq", None)
    return jax.shard_map(
        per_device,
        mesh=mesh,
        in_specs=(
            stream, P("dp"), stream, vector, vector, vector, matrix, matrix, matrix, matrix,
            matrix, matrix, matrix, vector, matrix, matrix, matrix,
        ),
        out_specs=(
            stream, stream, vector, vector, vector, matrix, matrix, matrix, matrix, matrix,
            matrix, matrix, vector, matrix, matrix, matrix,
        ),
        check_vma=False,
    )
```

```python
import functools

import jax
import jax.numpy as jnp
from jax import lax
from jax.experimental import pallas as pl
from jax.experimental.pallas import tpu as pltpu
from jax.sharding import PartitionSpec as P

HEADS = 4
SLOTS = 64
EPS = 1e-06
GATE_NORM = 8.0
F32 = jnp.float32
BF16 = jnp.bfloat16
LEAF = 8
VMEM_LIMIT = 48 * 1024 * 1024


def mm(a, b, ca, cb):
    return lax.dot_general(
        a.astype(BF16), b.astype(BF16), (((ca,), (cb,)), ((), ())), preferred_element_type=F32
    )


def mm_exact(a, b, ca, cb):
    return lax.dot_general(
        a,
        b,
        (((ca,), (cb,)), ((), ())),
        precision=lax.Precision.HIGHEST,
        preferred_element_type=F32,
    )


def two_parts(x):
    high = x.astype(BF16)
    return high, (x - high.astype(F32)).astype(BF16)


def mm_left(exact, b, ca, cb):
    high, low = two_parts(b)
    return mm(exact, high, ca, cb) + mm(exact, low, ca, cb)


def mm_right(a, exact, ca, cb):
    high, low = two_parts(a)
    return mm(high, exact, ca, cb) + mm(low, exact, ca, cb)


def mm_fine(a, b, ca, cb):
    a_high, a_low = two_parts(a)
    b_high, b_low = two_parts(b)
    return mm(a_high, b_high, ca, cb) + (mm(a_high, b_low, ca, cb) + mm(a_low, b_high, ca, cb))


def contract_last(a, b):
    return mm(a, b, 1, 1)


def contract_first(a, b):
    return mm(a, b, 0, 0)


def swish_slope(v):
    sigma = jax.nn.sigmoid(v)
    return sigma * (1.0 + v * (1.0 - sigma))


def rms_scale(v):
    return lax.rsqrt(jnp.mean(v * v, axis=-1, keepdims=True) + EPS)


def grid_index(rows, cols):
    return (
        lax.broadcasted_iota(jnp.int32, (rows, cols), 0),
        lax.broadcasted_iota(jnp.int32, (rows, cols), 1),
    )


def running_sum(decay):
    length = decay.shape[0]
    row, col = grid_index(length, length)
    return mm_exact((row >= col).astype(F32), decay, 1, 0)


def levels(length):
    found = []
    half = length // 2
    while half >= LEAF:
        found.append(half)
        half //= 2
    return found


def level_factors(running, writes, half):
    length, slots = running.shape
    pairs = running.reshape(length // (2 * half), 2 * half, slots)
    anchor = jnp.broadcast_to(pairs[:, half - 1 : half, :], pairs.shape).reshape(length, slots)
    near = jnp.exp(-jnp.abs(running - anchor))
    row, _ = grid_index(length, slots)
    right = (row % (2 * half)) >= half
    return jnp.where(right, near, 0.0), jnp.where(right, 0.0, near), right


def same_block(length, size):
    row, col = grid_index(length, length)
    return (row // size) == (col // size)


def leaf_selector(length):
    row, col = grid_index(length, LEAF)
    return ((row % LEAF) == col).astype(F32)


def leaf_take(square):
    length = square.shape[0]
    kept = jnp.where(same_block(length, LEAF), square, 0.0)
    return mm_exact(kept, leaf_selector(length), 1, 0)


def leaf_spread(columns):
    length = columns.shape[0]
    wide = mm_exact(columns, leaf_selector(length), 1, 1)
    return jnp.where(same_block(length, LEAF), wide, 0.0)


def leaf_row(tensor, at):
    length, width = tensor.shape
    blocks = tensor.reshape(length // LEAF, LEAF, width)
    return jnp.broadcast_to(blocks[:, at : at + 1, :], blocks.shape).reshape(length, width)


def leaf_decay(running, at):
    length, slots = running.shape
    row, _ = grid_index(length, slots)
    reached = (row % LEAF) >= at
    spread = running - leaf_row(running, at)
    return jnp.where(reached, jnp.exp(jnp.where(reached, spread, 0.0)), 0.0)


def masked(square, half):
    length = square.shape[0]
    if 2 * half == length:
        return square
    return jnp.where(same_block(length, 2 * half), square, 0.0)


def read_in_chunk(square, running, writes):
    total = None
    for half in levels(running.shape[0]):
        right, left, _ = level_factors(running, writes, half)
        part = right * mm_fine(masked(square, half), left * writes, 1, 0)
        total = part if total is None else total + part
    columns = leaf_take(square)
    for at in range(LEAF):
        part = columns[:, at : at + 1] * (leaf_decay(running, at) * leaf_row(writes, at))
        total = part if total is None else total + part
    return total


def mix_in_chunk(attend, running, writes):
    total = None
    for half in levels(running.shape[0]):
        right, left, _ = level_factors(running, writes, half)
        part = masked(mm(attend * right, left * writes, 1, 1), half)
        total = part if total is None else total + part
    columns = [
        jnp.sum(
            attend * (leaf_decay(running, at) * leaf_row(writes, at)), axis=1, keepdims=True
        )
        for at in range(LEAF)
    ]
    part = leaf_spread(jnp.concatenate(columns, axis=1))
    return part if total is None else total + part


def summary(k, v, decay, writes):
    running = running_sum(decay)
    length = running.shape[0]
    last = running[length - 1 : length, :]
    fade = jnp.exp(last - running) * writes
    return jnp.concatenate([mm(fade, k, 0, 0), mm(fade, v, 0, 0)], axis=1), jnp.exp(last)


def forward_kernel(
    q_ref, k_ref, v_ref, gate_ref, decay_ref, writes_ref, state_ref, gain_ref,
    mixed_ref, out_ref, attend_ref,
):
    q, k, v = q_ref[0], k_ref[0], v_ref[0]
    writes = writes_ref[0]
    width = q.shape[1]
    scale = width ** (-0.5)
    running = running_sum(decay_ref[0])
    growth = jnp.exp(running)
    state = state_ref[0]
    dots = mm(q, k, 1, 1) * scale
    scores = growth * (mm(q, state[:, :width], 1, 1) * scale)
    scores = scores + read_in_chunk(dots, running, writes)
    top = jnp.max(scores, axis=1, keepdims=True)
    raw = jnp.exp(scores - top)
    attend = raw / jnp.sum(raw, axis=1, keepdims=True)
    mixing = mix_in_chunk(attend, running, writes)
    out = mm(attend * growth, state[:, width:], 1, 0) + mm(mixing, v, 1, 0)
    out_ref[0] = out
    attend_ref[0] = attend
    gate = gate_ref[0]
    normed = out * rms_scale(out) * gain_ref[...]
    mixed_ref[0] = (normed * (gate * jax.nn.sigmoid(gate))).astype(BF16)


def back_first_kernel(
    grad_mixed_ref, gate_ref, out_ref, attend_ref, q_ref, v_ref, decay_ref, writes_ref,
    state_ref, gain_ref,
    grad_gate_ref, grad_out_ref, grad_scores_ref, adjoint_ref, gain_grad_ref,
):
    q, v = q_ref[0], v_ref[0]
    writes = writes_ref[0]
    width = q.shape[1]
    scale = width ** (-0.5)
    grad_mixed, gate, out = grad_mixed_ref[0], gate_ref[0], out_ref[0]
    gain = gain_ref[...]
    inverse = rms_scale(out)
    normed = out * inverse
    grad_gate_ref[0] = (grad_mixed * (normed * gain) * swish_slope(gate)).astype(BF16)
    e = grad_mixed * (gate * jax.nn.sigmoid(gate))
    gain_grad_ref[0] = jnp.sum(e * normed, axis=0, keepdims=True)
    eg = e * gain
    grad_out = inverse * (eg - normed * jnp.mean(eg * normed, axis=1, keepdims=True))
    grad_out_ref[0] = grad_out.astype(BF16)
    running = running_sum(decay_ref[0])
    growth = jnp.exp(running)
    attend = attend_ref[0]
    u = growth * mm_right(grad_out, state_ref[0, :, width:], 1, 1)
    u = u + read_in_chunk(mm_right(grad_out, v, 1, 1), running, writes)
    grad_scores = attend * (u - jnp.sum(attend * u, axis=1, keepdims=True))
    grad_scores_ref[0] = grad_scores
    adjoint_ref[0, :, :width] = mm(growth * grad_scores * scale, q, 0, 0)
    adjoint_ref[0, :, width:] = mm(growth * attend, grad_out.astype(BF16), 0, 0)


def back_second_kernel(
    grad_out_ref, grad_scores_ref, attend_ref, q_ref, k_ref, v_ref, decay_ref, writes_ref,
    state_ref, adjoint_ref, q_pre_ref, k_pre_ref, logit_ref, alive_ref,
    grad_pre_ref, dlogit_ref,
):
    q, k, v, grad_out = q_ref[0], k_ref[0], v_ref[0], grad_out_ref[0]
    attend, grad_scores = attend_ref[0], grad_scores_ref[0]
    decay, writes = decay_ref[0], writes_ref[0]
    length, slots = decay.shape
    width = q.shape[1]
    scale = width ** (-0.5)
    running = running_sum(decay)
    growth = jnp.exp(running)
    keep = jnp.exp(decay)
    last = running[length - 1 : length, :]
    fade = jnp.exp(last - running)
    state, adjoint = state_ref[0], adjoint_ref[0]
    key_state, value_state = state[:, :width], state[:, width:]
    key_adjoint, value_adjoint = adjoint[:, :width], adjoint[:, width:]
    key_dots = mm(q, k, 1, 1) * scale
    value_dots = mm(grad_out, v, 1, 1)
    row, col = grid_index(length, length)

    columns_sum = jnp.zeros((length, slots), F32)
    crossing = jnp.zeros((length, slots), F32)
    mix_key = jnp.zeros((length, length), F32)
    mix_value = jnp.zeros((length, length), F32)
    for half in levels(length):
        right, left, is_right = level_factors(running, writes, half)
        key_part, value_part = masked(key_dots, half), masked(value_dots, half)
        left_w = left * writes
        gs_right, at_right = grad_scores * right, attend * right
        mix_key = mix_key + masked(mm(gs_right, left_w, 1, 1), half)
        mix_value = mix_value + masked(mm(at_right, left_w, 1, 1), half)
        rows_sum = gs_right * mm_fine(key_part, left_w, 1, 0) + at_right * mm_fine(value_part, left_w, 1, 0)
        open_sum = left * (mm_fine(key_part, gs_right, 0, 0) + mm_fine(value_part, at_right, 0, 0))
        columns_sum = columns_sum + open_sum
        sums = jnp.where(is_right, rows_sum, open_sum * writes)
        forward = jnp.where((row % (2 * half)) >= half, col - row, row - col - 1) >= 0
        wanted = ((row // half) == (col // half)) & forward
        crossing = crossing + mm_left(wanted.astype(F32), sums, 1, 0)
    key_leaf, value_leaf = leaf_take(key_dots), leaf_take(value_dots)
    leaf_at = lax.broadcasted_iota(jnp.int32, (length, slots), 0) % LEAF
    difference = jnp.zeros((length, slots), F32)
    mix_key_columns, mix_value_columns = [], []
    for at in range(LEAF):
        fall = leaf_decay(running, at)
        mass = leaf_row(writes, at)
        mix_key_columns.append(jnp.sum(grad_scores * fall * mass, axis=1, keepdims=True))
        mix_value_columns.append(jnp.sum(attend * fall * mass, axis=1, keepdims=True))
        terms = fall * (
            grad_scores * key_leaf[:, at : at + 1] + attend * value_leaf[:, at : at + 1]
        )
        blocks = terms.reshape(length // LEAF, LEAF, slots)
        whole = jnp.broadcast_to(
            jnp.sum(blocks, axis=1, keepdims=True), blocks.shape
        ).reshape(length, slots)
        columns_sum = columns_sum + jnp.where(leaf_at == at, whole, 0.0)
        later = jnp.where(leaf_at > at, terms, 0.0)
        later_blocks = later.reshape(length // LEAF, LEAF, slots)
        later_whole = jnp.broadcast_to(
            jnp.sum(later_blocks, axis=1, keepdims=True), later_blocks.shape
        ).reshape(length, slots)
        difference = difference + mass * (later - jnp.where(leaf_at == at, later_whole, 0.0))
    mix_key = mix_key + leaf_spread(jnp.concatenate(mix_key_columns, axis=1))
    mix_value = mix_value + leaf_spread(jnp.concatenate(mix_value_columns, axis=1))
    suffix_leaf = (((row // LEAF) == (col // LEAF)) & (col >= row)).astype(F32)
    crossing = crossing + mm_exact(suffix_leaf, difference, 1, 0)

    start_terms = growth * (
        grad_scores * (mm(q, key_state, 1, 1) * scale)
        + attend * mm(grad_out, value_state, 1, 1)
    )
    crossing = crossing + mm_left((col >= row).astype(F32), start_terms, 1, 0)
    end_open = fade * (mm(k, key_adjoint, 1, 1) + mm(v, value_adjoint, 1, 1))
    columns_sum = columns_sum + end_open
    crossing = crossing + mm_left((col < row).astype(F32), end_open * writes, 1, 0)
    through = mm_exact(
        jnp.ones((8, 2 * width), F32), state.astype(F32) * adjoint.astype(F32), 1, 1
    )[0:1, :]
    crossing = crossing + jnp.exp(last) * through
    grad_decay = crossing - keep * columns_sum

    grad_q = (mm(grad_scores * growth, key_state, 1, 0) + mm(mix_key, k, 1, 0)) * scale
    fade_w = fade * writes
    grad_k = mm(mix_key, q, 0, 0) * scale + mm(fade_w, key_adjoint, 1, 0)
    grad_v = mm(mix_value, grad_out, 0, 0) + mm(fade_w, value_adjoint, 1, 0)
    grad_pre_ref[0, :, :width] = (grad_k * swish_slope(k_pre_ref[0])).astype(BF16)
    grad_pre_ref[0, :, width : 2 * width] = (grad_q * swish_slope(q_pre_ref[0])).astype(BF16)
    grad_pre_ref[0, :, 2 * width :] = grad_v.astype(BF16)
    dlogit_ref[0] = (
        alive_ref[0] * grad_decay * jax.nn.sigmoid(-logit_ref[0]) * (1.0 / GATE_NORM)
    ).astype(BF16)


def per_sequence(kernel, inputs, outputs, shared=()):
    inputs = [x if isinstance(x, tuple) else (x, None) for x in inputs]
    count = inputs[0][0].shape[0]

    def spec(shape, at=None):
        if at is None:
            return pl.BlockSpec((1,) + tuple(shape[1:]), lambda s: (s, 0, 0))
        return pl.BlockSpec((1, shape[1], shape[2] // 3), lambda s: (s, 0, at))

    return pl.pallas_call(
        kernel,
        grid=(count,),
        in_specs=[spec(x.shape, at) for x, at in inputs]
        + [pl.BlockSpec(x.shape, lambda s: (0, 0)) for x in shared],
        out_specs=[spec(x.shape) for x in outputs],
        out_shape=outputs,
        compiler_params=pltpu.CompilerParams(vmem_limit_bytes=VMEM_LIMIT),
    )(*[x for x, _ in inputs], *shared)


CHUNKS = 8
STRIP = 16


def send(src, dst, send_sem, recv_sem, where):
    copy = pltpu.make_async_remote_copy(
        src_ref=src,
        dst_ref=dst,
        send_sem=send_sem,
        recv_sem=recv_sem,
        device_id=where,
        device_id_type=pl.DeviceIdType.MESH,
    )
    copy.start()
    return copy


def greet(partners):
    barrier = pltpu.get_barrier_semaphore()
    for where in partners:
        pl.semaphore_signal(
            barrier, inc=1, device_id=where, device_id_type=pl.DeviceIdType.MESH
        )
    return barrier


def near_partners():
    d, at = lax.axis_index("dp"), lax.axis_index("seq")
    x = {"seq": jnp.bitwise_xor(at, 1)}
    y = {"dp": jnp.bitwise_xor(d, 2)}
    core = {"dp": jnp.bitwise_xor(d, 1)}
    return x, y, core


def everyone(seq, dp, act):
    me = lax.axis_index("dp") * seq + lax.axis_index("seq")

    def turn(r, carry):
        other = jnp.bitwise_xor(me, r)
        act(r, {"dp": other // seq, "seq": other % seq})
        return carry

    lax.fori_loop(1, seq * dp, turn, 0)


def greet_everyone(seq, dp):
    barrier = pltpu.get_barrier_semaphore()
    everyone(
        seq,
        dp,
        lambda r, where: pl.semaphore_signal(
            barrier, inc=1, device_id=where, device_id_type=pl.DeviceIdType.MESH
        ),
    )
    pl.semaphore_wait(barrier, seq * dp - 1)


def gather_kernel(outer, dp, *refs):
    mats, refs = refs[:3], refs[3:]
    toks, small, w_out, refs = refs[:2], refs[2], refs[3], refs[4:]
    three, heads, refs = refs[0], refs[1], refs[2:]
    out_toks, out_small, refs = refs[:2], refs[2], refs[3:]
    (
        local_sem, up_send, up_recv, down_send, down_recv, x_send, x_recv,
        tok_send, tok_recv, small_send, small_recv, head_send, head_recv,
    ) = refs
    outs = [three.at[0], three.at[1], three.at[2]]
    seq = 2 * outer
    at = lax.axis_index("seq")
    d = lax.axis_index("dp")
    me = d * seq + at
    z = at // 2
    x, y, core = near_partners()
    above, below = {"seq": at + 2}, {"seq": at - 2}
    has_above, has_below = z < outer - 1, z > 0
    greet_everyone(seq, dp)

    def push(r, where):
        return pltpu.make_async_remote_copy(
            src_ref=small, dst_ref=out_small.at[me], send_sem=small_send.at[r],
            recv_sem=small_recv.at[r], device_id=where, device_id_type=pl.DeviceIdType.MESH,
        )

    everyone(seq, dp, lambda r, where: push(r, where).start())
    head = heads.shape[2]

    def columns(owner):
        return w_out.at[:, pl.ds(pl.multiple_of(owner * head, head), head)]

    own_head = pltpu.make_async_copy(columns(d), heads.at[d], local_sem.at[5])
    own_head.start()
    other_heads = [
        send(
            columns(jnp.bitwise_xor(d, r)), heads.at[d], head_send.at[r], head_recv.at[r],
            {"dp": jnp.bitwise_xor(d, r)},
        )
        for r in range(1, dp)
    ]

    def up(m, k, src, origin):
        return pltpu.make_async_remote_copy(
            src_ref=src, dst_ref=outs[m].at[0, origin], send_sem=up_send.at[m, k],
            recv_sem=up_recv.at[m, k], device_id=above, device_id_type=pl.DeviceIdType.MESH,
        )

    def down(m, k, src, origin):
        return pltpu.make_async_remote_copy(
            src_ref=src, dst_ref=outs[m].at[0, origin], send_sem=down_send.at[m, k],
            recv_sem=down_recv.at[m, k], device_id=below, device_id_type=pl.DeviceIdType.MESH,
        )

    def across(m, src, origin):
        return pltpu.make_async_remote_copy(
            src_ref=src, dst_ref=outs[m].at[1, origin], send_sem=x_send.at[m, origin],
            recv_sem=x_recv.at[m, origin], device_id=x, device_id_type=pl.DeviceIdType.MESH,
        )

    for m in range(3):
        @pl.when(has_above)
        def _():
            up(m, 0, mats[m], z).start()

        @pl.when(has_below)
        def _():
            down(m, 0, mats[m], z).start()

        across(m, mats[m], z).start()
    tok_y, tok_rest = [], []
    for n, (tok, out_tok) in enumerate(zip(toks, out_toks)):
        tok_y.append(send(tok, out_tok.at[1], tok_send.at[3 * n], tok_recv.at[3 * n], y))
        tok_rest.append(
            send(tok, out_tok.at[2], tok_send.at[3 * n + 1], tok_recv.at[3 * n + 1], core)
        )
        copy = pltpu.make_async_copy(tok, out_tok.at[0], local_sem.at[1 + 5 * n])
        copy.start()
        tok_rest.append(copy)
    own_small = pltpu.make_async_copy(small, out_small.at[me], local_sem.at[0])
    own_small.start()
    own_mats = []
    for m in range(3):
        copy = pltpu.make_async_copy(mats[m], outs[m].at[0, z], local_sem.at[2 + m])
        copy.start()
        own_mats.append(copy)

    def pass_on(k, carry):
        for m in range(3):
            @pl.when(z - k >= 0)
            def _():
                slot = outs[m].at[0, z - k]
                up(m, k - 1, slot, z - k).wait_recv()

                @pl.when(has_above)
                def _():
                    up(m, k, slot, z - k).start()

                across(m, slot, z - k).start()

            @pl.when(z + k < outer)
            def _():
                slot = outs[m].at[0, z + k]
                down(m, k - 1, slot, z + k).wait_recv()

                @pl.when(has_below)
                def _():
                    down(m, k, slot, z + k).start()

                across(m, slot, z + k).start()

        return carry

    lax.fori_loop(1, outer, pass_on, 0)
    for n, out_tok in enumerate(out_toks):
        tok_y[n].wait()
        tok_rest.append(
            send(out_tok.at[1], out_tok.at[3], tok_send.at[3 * n + 2], tok_recv.at[3 * n + 2], core)
        )

    def arrived(r, where):
        push(r, where).wait_send()
        theirs = out_small.at[jnp.bitwise_xor(me, r)]
        pltpu.make_async_remote_copy(
            src_ref=theirs, dst_ref=theirs, send_sem=small_send.at[r],
            recv_sem=small_recv.at[r], device_id=where, device_id_type=pl.DeviceIdType.MESH,
        ).wait_recv()

    everyone(seq, dp, arrived)

    def complete(o, carry):
        for m in range(3):
            across(m, outs[m].at[0, o], o).wait()

            @pl.when(has_above & (o <= z))
            def _():
                up(m, o, outs[m].at[0, z], z).wait_send()

            @pl.when(has_below & (o <= outer - 1 - z))
            def _():
                down(m, o, outs[m].at[0, z], z).wait_send()

        return carry

    lax.fori_loop(0, outer, complete, 0)
    for copy in own_mats:
        copy.wait()
    own_head.wait()
    for r, copy in enumerate(other_heads, 1):
        copy.wait_send()
        theirs = heads.at[jnp.bitwise_xor(d, r)]
        pltpu.make_async_remote_copy(
            src_ref=theirs, dst_ref=theirs, send_sem=head_send.at[r],
            recv_sem=head_recv.at[r], device_id={"dp": jnp.bitwise_xor(d, r)},
            device_id_type=pl.DeviceIdType.MESH,
        ).wait_recv()
    own_small.wait()
    for copy in tok_rest:
        copy.wait()


def in_hbm():
    return pl.BlockSpec(memory_space=pl.ANY)


def in_vmem():
    return pl.BlockSpec(memory_space=pltpu.VMEM)


def gather_all(outer, dp, mats, toks, small, w_out):
    seq = 2 * outer
    rows, width = mats[0].shape
    dma = pltpu.SemaphoreType.DMA
    return pl.pallas_call(
        functools.partial(gather_kernel, outer, dp),
        in_specs=[in_vmem()] * 5 + [in_hbm()] * 2,
        out_specs=[in_hbm()] * 5,
        out_shape=[
            jax.ShapeDtypeStruct((3, 2, outer, rows, width), BF16),
            jax.ShapeDtypeStruct((dp, w_out.shape[0], w_out.shape[1] // dp), BF16),
            jax.ShapeDtypeStruct((dp,) + toks[0].shape, BF16),
            jax.ShapeDtypeStruct((dp,) + toks[1].shape, BF16),
            jax.ShapeDtypeStruct((seq * dp,) + small.shape, BF16),
        ],
        scratch_shapes=[dma((7,))] + [dma((3, outer))] * 6
        + [dma((6,))] * 2 + [dma((seq * dp,))] * 2 + [dma((dp,))] * 2,
        compiler_params=pltpu.CompilerParams(
            collective_id=1, has_side_effects=True, vmem_limit_bytes=VMEM_LIMIT
        ),
    )(*mats, *toks, small, w_out)


def feed_kernel(mid, grad_feed, w_down, w_act, w_lin, product, grad_gate, grad_lin):
    gate = mm(mid[...], w_act[0], 1, 1)
    lin = mm(mid[...], w_lin[0], 1, 1)
    grad_product = mm(grad_feed[...], w_down[0], 1, 1)
    sigma = jax.nn.sigmoid(gate)
    swish = gate * sigma
    product[...] = (swish * lin).astype(BF16)
    grad_gate[...] = (grad_product * lin * (sigma * (1.0 + gate * (1.0 - sigma)))).astype(BF16)
    grad_lin[...] = (grad_product * swish).astype(BF16)


def feed_back_kernel(
    product, grad_gate, grad_lin, w_down, w_act, w_lin, feed, grad_mid
):
    grad_mid[...] = (
        mm(grad_gate[...], w_act[0], 1, 0) + mm(grad_lin[...], w_lin[0], 1, 0)
    ).astype(BF16)
    feed[...] = mm(product[...], w_down[0], 1, 0).astype(BF16)


def grad_in_kernel(grad_pre, grad_gate, grad_logit, w_kqv, w_g, up, down, grad_in, grad_rank):
    rank = mm(grad_logit[...], up[...], 1, 0).astype(BF16)
    grad_rank[...] = rank
    grad_in[...] = (
        mm(grad_pre[...], w_kqv[...], 1, 0)
        + (mm(grad_gate[...], w_g[...], 1, 0) + mm(rank, down[...], 1, 1))
    ).astype(BF16)


def grad_in_tiles(tiles, shared, widths):
    rows = tiles[0].shape[0]
    step = min(256, rows)
    return pl.pallas_call(
        grad_in_kernel,
        grid=(rows // step,),
        in_specs=[pl.BlockSpec((step, x.shape[1]), lambda t: (t, 0)) for x in tiles]
        + [
            pl.BlockSpec(x.shape, lambda t: (0, 0), pipeline_mode=pl.Buffered(1))
            for x in shared
        ],
        out_specs=[pl.BlockSpec((step, columns), lambda t: (t, 0)) for columns in widths],
        out_shape=[jax.ShapeDtypeStruct((rows, columns), BF16) for columns in widths],
        compiler_params=pltpu.CompilerParams(vmem_limit_bytes=VMEM_LIMIT),
    )(*tiles, *shared)


def feed_tiles(kernel, tiles, weights, widths):
    rows = tiles[0].shape[0]
    step = min(256, rows)
    _, units, width = weights.shape
    each = 2 * step * units * width

    def spec(columns):
        return pl.BlockSpec((step, columns), lambda t: (t, 0))

    def weight(at):
        return pl.BlockSpec(
            (1, units, width), lambda t: (at, 0, 0), pipeline_mode=pl.Buffered(1)
        )

    return pl.pallas_call(
        kernel,
        grid=(rows // step,),
        in_specs=[spec(x.shape[1]) for x in tiles] + [weight(m) for m in range(3)],
        out_specs=[spec(columns) for columns in widths],
        out_shape=[jax.ShapeDtypeStruct((rows, columns), BF16) for columns in widths],
        cost_estimate=pl.CostEstimate(
            flops=3 * each * (rows // step), bytes_accessed=6 * units * width + 8 * rows * width,
            transcendentals=rows * units,
        ),
        compiler_params=pltpu.CompilerParams(vmem_limit_bytes=VMEM_LIMIT),
    )(*tiles, weights, weights, weights)


def turned(x):
    row, col = grid_index(x.shape[1], x.shape[1])
    return mm_exact((row == col).astype(F32), x, 1, 1)


def flipped(x):
    size = x.shape[-1] // 4
    return jnp.concatenate([x[:, size * i : size * (i + 1)] for i in (1, 0, 3, 2)], axis=1)


def relay_kernel(outer, backward, *refs):
    if backward:
        totals, keeps, parts, refs = refs[0], refs[1], refs[2], refs[3:]
        states, sums, refs = refs[0], refs[1], refs[2:]
        side, refs = refs[-7:], refs[:-7]
    else:
        feats, decays, writes, refs = refs[0], refs[1], refs[2], refs[3:]
        states, keeps, refs = refs[0], refs[1], refs[2:]
    (
        own, to_x, from_x, to_z, from_z, to_back, from_back, keep_mine, keep_theirs,
        x_s, x_r, z_s, z_r, b_s, b_r, k_s, k_r,
    ) = refs
    half = own.shape[0]
    at = lax.axis_index("seq")
    inner, z = at % 2, at // 2
    x, y, core = near_partners()
    above, below = {"seq": at + 2}, {"seq": at - 2}
    has_above, has_below = z < outer - 1, z > 0
    ahead, has_ahead, has_source = (
        (below, has_below, has_above) if backward else (above, has_above, has_below)
    )
    barrier = greet([x, y, core] if backward else [x])

    @pl.when(has_above)
    def _():
        greet([above])

    @pl.when(has_below)
    def _():
        greet([below])

    pl.semaphore_wait(
        barrier,
        (3 if backward else 1) + has_above.astype(jnp.int32) + has_below.astype(jnp.int32),
    )

    def compute(s):
        if backward:
            return totals[s]
        width = feats.shape[2] // 3
        total, keep = summary(
            feats[s, :, :width], feats[s, :, 2 * width :], decays[s], writes[s]
        )
        keep_mine[s] = keep
        return total

    crossing = []
    for i in range(half):
        to_x[i] = compute((1 - inner) * half + i).astype(BF16)
        crossing.append(send(to_x.at[i], from_x.at[i], x_s.at[i], x_r.at[i], x))
    if backward:
        side = plane_sum_start(parts, side, y, core)
    for i in range(half):
        own[i] = compute(inner * half + i)
    if backward:
        keep_a, keep_b = keeps[0], keeps[1]
    else:
        send(keep_mine, keep_theirs, k_s.at[0], k_r.at[0], x).wait()
        mine = jnp.concatenate([keep_mine[s] for s in range(2 * half)], axis=0)
        theirs = jnp.concatenate([keep_theirs[s] for s in range(2 * half)], axis=0)
        keep_a = jnp.where(inner == 0, mine, theirs)
        keep_b = jnp.where(inner == 0, theirs, mine)
        keeps[0] = keep_a
        keeps[1] = keep_b
    if backward:
        keep_a, keep_b = keep_b, keep_a
    first_k = turned(jnp.where(inner == 0, keep_a[:half], keep_a[half:]))
    second_k = turned(jnp.where(inner == 0, keep_b[:half], keep_b[half:]))
    is_first = (inner == 1) if backward else (inner == 0)

    def along(i):
        return pltpu.make_async_remote_copy(
            src_ref=to_z.at[i], dst_ref=from_z.at[i], send_sem=z_s.at[i], recv_sem=z_r.at[i],
            device_id=ahead, device_id_type=pl.DeviceIdType.MESH,
        )

    returning = []
    for i in range(half):
        crossing[i].wait()

        @pl.when(jnp.logical_not(has_source))
        def _():
            from_z[i] = jnp.zeros_like(from_z[i])

        @pl.when(has_source)
        def _():
            along(i).wait_recv()

        got = flipped(from_x[i]).astype(F32)
        mine = own[i]
        first = jnp.where(is_first, mine, got)
        second = jnp.where(is_first, got, mine)
        entering = from_z[i].astype(F32)
        after = first_k[:, i : i + 1] * entering + first
        to_z[i] = (second_k[:, i : i + 1] * after + second).astype(BF16)

        @pl.when(has_ahead)
        def _():
            along(i).start()

        states[inner * half + i] = jnp.where(is_first, entering, after).astype(BF16)
        to_back[i] = jnp.where(is_first, after, entering).astype(BF16)
        returning.append(send(to_back.at[i], from_back.at[i], b_s.at[i], b_r.at[i], x))
    for i in range(half):
        returning[i].wait()
        states[(1 - inner) * half + i] = flipped(from_back[i])

        @pl.when(has_ahead)
        def _():
            along(i).wait_send()

    if backward:
        plane_sum_end(parts, sums, side)


def plane_sum_start(parts, side, y, core):
    from_core, to_y, from_y, core_s, core_r, y_s, y_r = side
    rows = parts.shape[1]
    size = rows // CHUNKS
    cuts = [pl.ds(c * size, size) for c in range(CHUNKS)]
    first = [
        send(parts.at[pl.ds(4, 4), cut], from_core.at[:, cut], core_s.at[c], core_r.at[c], core)
        for c, cut in enumerate(cuts)
    ]
    second = []
    for c, cut in enumerate(cuts):
        first[c].wait()

        def add(r, carry, c=c):
            at = pl.ds(c * size + r * STRIP, STRIP)
            for j in range(2):
                to_y[j, at] = (
                    parts[2 + j, at].astype(F32) + from_core[2 + j, at].astype(F32)
                ).astype(BF16)
            return carry

        lax.fori_loop(0, size // STRIP, add, 0)
        second.append(send(to_y.at[:, cut], from_y.at[:, cut], y_s.at[c], y_r.at[c], y))
    return from_core, from_y, second


def plane_sum_end(parts, sums, side):
    from_core, from_y, second = side
    size = parts.shape[1] // CHUNKS
    for c in range(CHUNKS):
        second[c].wait()

        def add(r, carry, c=c):
            at = pl.ds(c * size + r * STRIP, STRIP)
            for j in range(2):
                sums[j, at] = (
                    parts[j, at].astype(F32) + from_core[j, at].astype(F32)
                    + from_y[j, at].astype(F32)
                ).astype(BF16)
            return carry

        lax.fori_loop(0, size // STRIP, add, 0)


def relay(outer, backward, inputs, sequences, slots, width):
    half = sequences // 2
    dma = pltpu.SemaphoreType.DMA
    held = pltpu.VMEM((half, slots, width), BF16)
    states = jax.ShapeDtypeStruct((sequences, slots, width), BF16)
    keeps = jax.ShapeDtypeStruct((2, sequences, slots), F32)
    keep = pltpu.VMEM((sequences, 1, slots), F32)
    second, side = keeps, []
    if backward:
        rows, columns = inputs[2].shape[1:]
        second = jax.ShapeDtypeStruct((2, rows, columns), BF16)
        side = [
            pltpu.VMEM((4, rows, columns), BF16), pltpu.VMEM((2, rows, columns), BF16),
            pltpu.VMEM((2, rows, columns), BF16),
        ] + [dma((CHUNKS,))] * 4
    return pl.pallas_call(
        functools.partial(relay_kernel, outer, backward),
        in_specs=[in_vmem()] * len(inputs),
        out_specs=[in_vmem()] * 2,
        out_shape=[states, second],
        scratch_shapes=[pltpu.VMEM((half, slots, width), F32)] + [held] * 6 + [keep] * 2
        + [dma((half,))] * 6 + [dma((1,))] * 2 + side,
        compiler_params=pltpu.CompilerParams(
            collective_id=7 if backward else 6, has_side_effects=True,
            vmem_limit_bytes=VMEM_LIMIT,
        ),
    )(*inputs)


def middle_kernel(
    parts, tok, gain, extra, hidden, mid, extra_all, from_core, to_y, from_y, normed,
    core_s, core_r, y_s, y_r, local_sem, gx_s, gx_r, gy_s, gy_r, gd_s, gd_r,
    ex_s, ex_r, ed_s, ed_r, extra_sem, gc_s, gc_r, ec_s, ec_r,
):
    rows = tok.shape[0]
    size = rows // CHUNKS
    x, y, core = near_partners()
    pl.semaphore_wait(greet([x, y, core]), 3)
    cuts = [pl.ds(c * size, size) for c in range(CHUNKS)]
    first = [
        send(parts.at[pl.ds(2, 2), cut], from_core.at[:, cut], core_s.at[c], core_r.at[c], core)
        for c, cut in enumerate(cuts)
    ]
    second = []
    for c, cut in enumerate(cuts):
        first[c].wait()

        def add(r, carry, c=c):
            at = pl.ds(c * size + r * STRIP, STRIP)
            to_y[at] = (parts[1, at].astype(F32) + from_core[1, at].astype(F32)).astype(BF16)
            return carry

        lax.fori_loop(0, size // STRIP, add, 0)
        second.append(send(to_y.at[cut], from_y.at[cut], y_s.at[c], y_r.at[c], y))
    rest = []
    for j in range(4):
        copy = pltpu.make_async_copy(extra.at[j], extra_all.at[2 * j], extra_sem.at[j])
        copy.start()
        rest.append(copy)
    extra_x = [
        send(extra.at[0, cut], extra_all.at[1, cut], ex_s.at[c], ex_r.at[c], x)
        for c, cut in enumerate(cuts)
    ]
    over_x, over_y, diagonal = [], [], []
    for c in range(CHUNKS + 2):
        if c < CHUNKS:
            cut = cuts[c]
            second[c].wait()

            def norm(r, carry, c=c):
                at = pl.ds(c * size + r * STRIP, STRIP)
                total = tok[at].astype(F32) + (
                    (parts[0, at].astype(F32) + from_core[0, at].astype(F32))
                    + from_y[at].astype(F32)
                )
                hidden[at] = total
                normed[at] = (total * rms_scale(total) * gain[...]).astype(BF16)
                return carry

            lax.fori_loop(0, size // STRIP, norm, 0)
            over_y.append(send(normed.at[cut], mid.at[2, cut], gy_s.at[c], gy_r.at[c], y))
            over_x.append(send(normed.at[cut], mid.at[1, cut], gx_s.at[c], gx_r.at[c], x))
            rest.append(send(normed.at[cut], mid.at[4, cut], gc_s.at[0, c], gc_r.at[0, c], core))
            own = pltpu.make_async_copy(normed.at[cut], mid.at[0, cut], local_sem.at[c])
            own.start()
            rest.append(own)
        if c >= 2:
            at, cut = c - 2, cuts[c - 2]
            over_y[at].wait()
            diagonal.append(send(mid.at[2, cut], mid.at[3, cut], gd_s.at[at], gd_r.at[at], x))
            rest.append(send(mid.at[2, cut], mid.at[6, cut], gc_s.at[2, at], gc_r.at[2, at], core))
    extra_d = []
    for c, cut in enumerate(cuts):
        extra_x[c].wait()
        extra_d.append(
            send(extra_all.at[1, cut], extra_all.at[3, cut], ed_s.at[c], ed_r.at[c], y)
        )
        over_x[c].wait()
        rest.append(send(mid.at[1, cut], mid.at[5, cut], gc_s.at[1, c], gc_r.at[1, c], core))
    rest.append(send(extra_all.at[1], extra_all.at[5], ec_s.at[0], ec_r.at[0], core))
    for c, cut in enumerate(cuts):
        diagonal[c].wait()
        rest.append(send(mid.at[3, cut], mid.at[7, cut], gc_s.at[3, c], gc_r.at[3, c], core))
    for copy in extra_d:
        copy.wait()
    rest.append(send(extra_all.at[3], extra_all.at[7], ec_s.at[1], ec_r.at[1], core))
    for copy in rest:
        copy.wait()


def middle(parts, tok, gain, extra):
    rows, width = tok.shape
    dma = pltpu.SemaphoreType.DMA
    buffer = pltpu.VMEM((rows, width), BF16)
    return pl.pallas_call(
        middle_kernel,
        in_specs=[in_vmem()] * 4,
        out_specs=[in_vmem(), in_hbm(), in_hbm()],
        out_shape=[
            jax.ShapeDtypeStruct((rows, width), F32),
            jax.ShapeDtypeStruct((8, rows, width), BF16),
            jax.ShapeDtypeStruct((8, rows, width), BF16),
        ],
        scratch_shapes=[pltpu.VMEM((2, rows, width), BF16), buffer, buffer, buffer]
        + [dma((CHUNKS,))] * 15
        + [dma((4,))]
        + [dma((4, CHUNKS))] * 2
        + [dma((2,))] * 2,
        compiler_params=pltpu.CompilerParams(
            collective_id=2, has_side_effects=True, vmem_limit_bytes=VMEM_LIMIT
        ),
    )(parts, tok, gain, extra)


def middle_back_kernel(
    parts, hidden, grad_out, gain, grad_hidden, gain_grad, attn,
    from_core, to_x, from_x, to_y, from_y, rounded,
    core_s, core_r, x_s, x_r, y_s, y_r, local_sem, gy_s, gy_r, gc_s, gc_r,
):
    rows, width = hidden.shape
    size = rows // CHUNKS
    x, y, core = near_partners()
    pl.semaphore_wait(greet([x, y, core]), 3)
    cuts = [pl.ds(c * size, size) for c in range(CHUNKS)]
    first = [
        send(parts.at[pl.ds(4, 4), cut], from_core.at[:, cut], core_s.at[c], core_r.at[c], core)
        for c, cut in enumerate(cuts)
    ]
    second, third = [], []
    for c, cut in enumerate(cuts):
        first[c].wait()

        def add_core(r, carry, c=c):
            at = pl.ds(c * size + r * STRIP, STRIP)
            for j in range(2):
                g = 2 * j + 1
                to_x[j, at] = (
                    parts[g, at].astype(F32) + from_core[g, at].astype(F32)
                ).astype(BF16)
            return carry

        lax.fori_loop(0, size // STRIP, add_core, 0)
        second.append(send(to_x.at[:, cut], from_x.at[:, cut], x_s.at[c], x_r.at[c], x))
    gain_grad[...] = jnp.zeros_like(gain_grad)
    pending, over_y = [], []
    for step in range(CHUNKS + 2):
        if step < CHUNKS:
            c, cut = step, cuts[step]
            second[c].wait()

            def add_x(r, carry, c=c):
                at = pl.ds(c * size + r * STRIP, STRIP)
                to_y[at] = (
                    parts[2, at].astype(F32) + from_core[2, at].astype(F32)
                    + from_x[1, at].astype(F32)
                ).astype(BF16)
                return carry

            lax.fori_loop(0, size // STRIP, add_x, 0)
            third.append(send(to_y.at[cut], from_y.at[cut], y_s.at[c], y_r.at[c], y))
        if 1 <= step <= CHUNKS:
            c, cut = step - 1, cuts[step - 1]
            third[c].wait()

            def back(r, carry, c=c):
                at = pl.ds(c * size + r * STRIP, STRIP)
                grad_mid = (
                    (parts[0, at].astype(F32) + from_core[0, at].astype(F32))
                    + from_x[0, at].astype(F32)
                ) + from_y[at].astype(F32)
                value = hidden[at]
                scale = rms_scale(value)
                unit = value * scale
                gain_grad[...] += jnp.sum(grad_mid * unit, axis=0, keepdims=True)
                scaled = grad_mid * gain[...]
                total = grad_out[at] + scale * (
                    scaled - unit * jnp.mean(scaled * unit, axis=1, keepdims=True)
                )
                grad_hidden[at] = total
                rounded[at] = total.astype(BF16)
                return carry

            lax.fori_loop(0, size // STRIP, back, 0)
            over_y.append(send(rounded.at[cut], attn.at[1, cut], gy_s.at[c], gy_r.at[c], y))
            pending.append(
                send(rounded.at[cut], attn.at[2, cut], gc_s.at[0, c], gc_r.at[0, c], core)
            )
            own = pltpu.make_async_copy(rounded.at[cut], attn.at[0, cut], local_sem.at[c])
            own.start()
            pending.append(own)
        if step >= 2:
            c, cut = step - 2, cuts[step - 2]
            over_y[c].wait()
            pending.append(
                send(attn.at[1, cut], attn.at[3, cut], gc_s.at[1, c], gc_r.at[1, c], core)
            )
    for copy in pending:
        copy.wait()


def middle_back(parts, hidden, grad_out, gain):
    rows, width = hidden.shape
    dma = pltpu.SemaphoreType.DMA

    def buffer(*lead):
        return pltpu.VMEM(lead + (rows, width), BF16)

    return pl.pallas_call(
        middle_back_kernel,
        in_specs=[in_vmem()] * 4,
        out_specs=[in_vmem(), in_vmem(), in_hbm()],
        out_shape=[
            jax.ShapeDtypeStruct((rows, width), F32),
            jax.ShapeDtypeStruct((1, width), F32),
            jax.ShapeDtypeStruct((4, rows, width), BF16),
        ],
        scratch_shapes=[buffer(4), buffer(2), buffer(2), buffer(), buffer(), buffer()]
        + [dma((CHUNKS,))] * 9
        + [dma((2, CHUNKS))] * 2,
        compiler_params=pltpu.CompilerParams(
            collective_id=3, has_side_effects=True, vmem_limit_bytes=VMEM_LIMIT
        ),
    )(parts, hidden, grad_out, gain)


def final_kernel(outer, dp, mats, gates, parts, tok, base, gain, small, *refs):
    out, tokens_grad, out_small, refs = refs[0], refs[1], refs[2], refs[3:]
    (
        from_x, from_below, from_above, total, from_core, to_y, from_y, gain_grad,
        to_all, from_all,
        x_s, x_r, up_s, up_r, down_s, down_r, core_s, core_r, y_s, y_r, all_s, all_r,
    ) = refs
    rows, width = tok.shape
    size = rows // CHUNKS
    high = total.shape[2]
    seq = 2 * outer
    at = lax.axis_index("seq")
    me = lax.axis_index("dp") * seq + at
    z = at // 2
    x, y, core = near_partners()
    above, below = {"seq": at + 2}, {"seq": at - 2}
    has_above, has_below = z < outer - 1, z > 0
    greet_everyone(seq, dp)
    cuts = [pl.ds(c * size, size) for c in range(CHUNKS)]
    first = [
        send(parts.at[pl.ds(2, 2), cut], from_core.at[:, cut], core_s.at[c], core_r.at[c], core)
        for c, cut in enumerate(cuts)
    ]

    def block_of(i):
        return jnp.where(i % 2 == 0, outer - 1 - i // 2, i // 2)

    def across(m, b):
        return pltpu.make_async_remote_copy(
            src_ref=mats.at[m, 1, b], dst_ref=from_x.at[m, b], send_sem=x_s.at[m, b],
            recv_sem=x_r.at[m, b], device_id=x, device_id_type=pl.DeviceIdType.MESH,
        )

    def up(m, b):
        return pltpu.make_async_remote_copy(
            src_ref=total.at[m, b], dst_ref=from_below.at[m, b], send_sem=up_s.at[m, b],
            recv_sem=up_r.at[m, b], device_id=above, device_id_type=pl.DeviceIdType.MESH,
        )

    def down(m, b):
        return pltpu.make_async_remote_copy(
            src_ref=total.at[m, b], dst_ref=from_above.at[m, b], send_sem=down_s.at[m, b],
            recv_sem=down_r.at[m, b], device_id=below, device_id_type=pl.DeviceIdType.MESH,
        )

    def start_x(i, carry):
        for m in range(3):
            across(m, block_of(i)).start()
        return carry

    lax.fori_loop(0, outer, start_x, 0)
    second = []
    for c, cut in enumerate(cuts):
        first[c].wait()

        def add(r, carry, c=c):
            strip = pl.ds(c * size + r * STRIP, STRIP)
            to_y[strip] = (
                parts[1, strip].astype(F32) + from_core[1, strip].astype(F32)
            ).astype(BF16)
            return carry

        lax.fori_loop(0, size // STRIP, add, 0)
        second.append(send(to_y.at[cut], from_y.at[cut], y_s.at[c], y_r.at[c], y))

    def add_into(m, b, other):
        def strip_sum(r, carry):
            strip = pl.ds(r * STRIP, STRIP)
            total[m, b, strip] = (
                total[m, b, strip].astype(F32) + other[m, b, strip].astype(F32)
            ).astype(BF16)
            return carry

        lax.fori_loop(0, high // STRIP, strip_sum, 0)

    def reduce_block(i, carry):
        b = block_of(i)
        for m in (3, 0, 1, 2):
            if m == 3:
                total[m, b] = gates[b]
            else:
                across(m, b).wait()

                def strip_sum(r, carry, m=m):
                    strip = pl.ds(r * STRIP, STRIP)
                    total[m, b, strip] = (
                        mats[m, 0, b, strip].astype(F32) + from_x[m, b, strip].astype(F32)
                    ).astype(BF16)
                    return carry

                lax.fori_loop(0, high // STRIP, strip_sum, 0)

            @pl.when(b > z)
            def _():
                @pl.when(has_below)
                def _():
                    up(m, b).wait_recv()
                    add_into(m, b, from_below)

                up(m, b).start()

            @pl.when(b < z)
            def _():
                @pl.when(has_above)
                def _():
                    down(m, b).wait_recv()
                    add_into(m, b, from_above)

                down(m, b).start()

        return carry

    lax.fori_loop(0, outer // 2, reduce_block, 0)
    gain_grad[...] = jnp.zeros_like(gain_grad)
    for c in range(CHUNKS):
        second[c].wait()

        def back(r, carry, c=c):
            strip = pl.ds(c * size + r * STRIP, STRIP)
            grad = (
                parts[0, strip].astype(F32) + from_core[0, strip].astype(F32)
            ) + from_y[strip].astype(F32)
            value = tok[strip].astype(F32)
            scale = rms_scale(value)
            unit = value * scale
            gain_grad[...] += jnp.sum(grad * unit, axis=0, keepdims=True)
            scaled = grad * gain[...]
            tokens_grad[strip] = base[strip] + scale * (
                scaled - unit * jnp.mean(scaled * unit, axis=1, keepdims=True)
            )
            return carry

        lax.fori_loop(0, size // STRIP, back, 0)
    devices = seq * dp
    each = width // devices
    row, col = grid_index(devices, width)
    spread = jnp.where(col // each == row, gain_grad[...], 0.0)
    picked_row, picked_col = grid_index(width, 128)
    gathered = mm_exact(spread, ((picked_row % each) == picked_col).astype(F32), 1, 0)
    height = small.shape[1]
    to_all[:, :height] = small[...]
    to_all[:, height:] = jnp.broadcast_to(
        gathered.reshape(devices, 1, 128), (devices, to_all.shape[1] - height, 128)
    )

    def push(r, where):
        return pltpu.make_async_remote_copy(
            src_ref=to_all.at[jnp.bitwise_xor(me, r)], dst_ref=from_all.at[r],
            send_sem=all_s.at[r], recv_sem=all_r.at[r], device_id=where,
            device_id_type=pl.DeviceIdType.MESH,
        )

    everyone(seq, dp, lambda r, where: push(r, where).start())
    lax.fori_loop(outer // 2, outer, reduce_block, 0)
    out_small[...] = to_all[me]

    def add_small(r, where):
        push(r, where).wait()
        out_small[...] += from_all[r]

    everyone(seq, dp, add_small)
    for m in range(4):
        out[m] = total[m, z].astype(F32)

        @pl.when(has_below)
        def _():
            up(m, z).wait_recv()
            out[m] += from_below[m, z].astype(F32)

        @pl.when(has_above)
        def _():
            down(m, z).wait_recv()
            out[m] += from_above[m, z].astype(F32)

    def sent(b, carry):
        for m in range(4):
            @pl.when(b > z)
            def _():
                up(m, b).wait_send()

            @pl.when(b < z)
            def _():
                down(m, b).wait_send()

        return carry

    lax.fori_loop(0, outer, sent, 0)


def finish(outer, dp, mats, gates, parts, tok, base, gain, small):
    rows, width = tok.shape
    high = mats.shape[3]
    devices = 2 * outer * dp
    dma = pltpu.SemaphoreType.DMA
    blocks = pltpu.VMEM((4, outer, high, width), BF16)
    buffer = pltpu.VMEM((rows, width), BF16)
    payload = (small.shape[1] + 8, 128)
    return pl.pallas_call(
        functools.partial(final_kernel, outer, dp),
        in_specs=[in_vmem()] * 7,
        out_specs=[in_vmem()] * 3,
        out_shape=[
            jax.ShapeDtypeStruct((4, high, width), F32),
            jax.ShapeDtypeStruct((rows, width), F32),
            jax.ShapeDtypeStruct(payload, F32),
        ],
        scratch_shapes=[blocks] * 4
        + [
            pltpu.VMEM((2, rows, width), BF16), buffer, buffer, pltpu.VMEM((1, width), F32),
            pltpu.VMEM((devices,) + payload, F32), pltpu.VMEM((devices,) + payload, F32),
        ]
        + [dma((4, outer))] * 6
        + [dma((CHUNKS,))] * 4
        + [dma((devices,))] * 2,
        compiler_params=pltpu.CompilerParams(
            collective_id=4, has_side_effects=True, vmem_limit_bytes=VMEM_LIMIT
        ),
    )(mats, gates, parts, tok, base, gain, small)


class Lanes:
    def __init__(self):
        self.seq = lax.axis_size("seq")
        self.dp = lax.axis_size("dp")
        self.outer = self.seq // 2
        self.at = lax.axis_index("seq")
        self.d = lax.axis_index("dp")
        self.inner_at = lax.rem(self.at, 2)
        self.outer_at = self.at // 2
        self.groups = [[2 * k + i for k in range(self.outer)] for i in range(2)]

    def swap_inner(self, x):
        return lax.ppermute(x, "seq", [(i, i ^ 1) for i in range(self.seq)])

    def gather_outer(self, x):
        return lax.all_gather(x, "seq", axis=0, tiled=True, axis_index_groups=self.groups)

    def scatter_outer(self, x):
        return lax.psum_scatter(
            x, "seq", scatter_dimension=0, tiled=True, axis_index_groups=self.groups
        )

    def swap_dp(self, x, bit):
        return lax.ppermute(x, "dp", [(i, i ^ bit) for i in range(self.dp)])

    def swap_seq(self, x, bit):
        return lax.ppermute(x, "seq", [(i, i ^ bit) for i in range(self.seq)])

    def exchange_heads(self, blocks):
        got = [lax.dynamic_index_in_dim(blocks, self.d, 0, keepdims=False)]
        for r in range(1, self.dp):
            part = lax.dynamic_index_in_dim(
                blocks, jnp.bitwise_xor(self.d, r), 0, keepdims=False
            )
            got.append(self.swap_dp(part, r))
        bit = 1
        while bit < self.dp:
            is_set = (self.d // bit) % 2 == 1
            got = [jnp.where(is_set, got[i ^ bit], got[i]) for i in range(self.dp)]
            bit *= 2
        return jnp.stack(got)

    def pick(self, natural, axis):
        first = lax.index_in_dim(natural, 0, axis, keepdims=False)
        second = lax.index_in_dim(natural, 1, axis, keepdims=False)
        even = self.inner_at == 0
        return jnp.where(even, first, second), jnp.where(even, second, first)


def swap_halves(x, parts):
    size = x.shape[-1] // (2 * parts)
    pieces = [x[..., i * size : (i + 1) * size] for i in range(2 * parts)]
    order = [i ^ 1 for i in range(2 * parts)]
    return jnp.concatenate([pieces[i] for i in order], axis=-1)


def per_device(
    tokens, lengths, cotangent, mixer_gain, feed_gain, head_gain, w_query, w_key, w_value,
    w_gate, w_out, rank_down, rank_up, rank_bias, w_act, w_lin, w_down,
):
    lanes = Lanes()
    seq_count, piece, width = tokens.shape
    rows = seq_count * piece
    sequences = lanes.dp * seq_count
    all_rows = lanes.dp * rows
    head_width = width // HEADS
    half_width = head_width // 2
    rank = rank_down.shape[1]
    devices = lanes.dp * lanes.seq

    counts = lengths.astype(F32)
    high = jnp.floor(counts / 256.0)
    small_parts = [
        mixer_gain, feed_gain, head_gain, rank_down.reshape(-1), rank_up.reshape(-1),
        rank_bias, high.astype(BF16), (counts - 256.0 * high).astype(BF16),
    ]
    sizes = [p.shape[0] for p in small_parts]
    used = sum(sizes)
    padded = -(-used // 2048) * 2048
    small = jnp.concatenate(small_parts + [jnp.zeros((padded - used,), BF16)])
    own_tokens = tokens.reshape(rows, width)
    position = (lanes.at * piece + jnp.arange(piece)).astype(F32)
    alive_own = (position[None, :] < counts[:, None]).astype(F32).reshape(rows, 1)
    grad_out = cotangent.reshape(rows, width).astype(F32) * alive_own
    w_kqv, out_mine, plane_tokens, grad_feed, smalls = gather_all(
        lanes.outer, lanes.dp, [w_key, w_query, w_value], [own_tokens, grad_out.astype(BF16)],
        small.reshape(-1, 128), w_out,
    )
    w_kqv = w_kqv.reshape(3 * head_width, width)
    out_rows = w_out.shape[0]
    out_own, out_other = lanes.pick(
        out_mine.reshape(lanes.dp, out_rows, lanes.outer, 2, -1), 3
    )
    out_mine = jnp.concatenate(
        [
            out_own.reshape(lanes.dp, out_rows, half_width),
            out_other.reshape(lanes.dp, out_rows, half_width),
        ],
        axis=2,
    )
    gate_and_out = lanes.gather_outer(
        jnp.concatenate([w_gate, out_mine.reshape(out_rows, width)], axis=0)
    )
    smalls = smalls.reshape(devices, padded)
    cuts, offset = [], 0
    for size in sizes:
        cuts.append(smalls[:, offset : offset + size])
        offset += size
    mixer_full = cuts[0].reshape(1, width).astype(F32)
    feed_full = cuts[1].reshape(1, width).astype(F32)
    head_natural = cuts[2].reshape(lanes.outer, 2, half_width // lanes.outer)
    head_own, head_other = lanes.pick(head_natural, 1)
    head_full = jnp.concatenate(
        [head_own.reshape(1, half_width), head_other.reshape(1, half_width)], axis=1
    ).astype(F32)
    down_full = cuts[3].reshape(width, rank)
    up_mine = lax.dynamic_index_in_dim(
        cuts[4].reshape(lanes.dp, SLOTS, rank), lanes.d, 0, keepdims=False
    )
    bias_mine = lax.dynamic_index_in_dim(
        cuts[5].reshape(lanes.dp, 1, SLOTS), lanes.d, 0, keepdims=False
    ).astype(F32)
    all_lengths = cuts[6].astype(F32) * 256.0 + cuts[7].astype(F32)
    all_lengths = all_lengths.reshape(lanes.dp, lanes.seq, seq_count)[:, 0]

    group_lengths = jnp.concatenate(
        [
            lax.dynamic_index_in_dim(
                all_lengths, jnp.bitwise_xor(lanes.d, r), 0, keepdims=False
            )
            for r in (0, 2, 1, 3)
        ]
    )
    alive = (position[None, :] < group_lengths[:, None]).astype(F32).reshape(all_rows, 1)

    sources = plane_tokens.reshape(all_rows, width).astype(F32)
    normed_in = (sources * rms_scale(sources) * mixer_full).astype(BF16)

    pre = contract_last(normed_in, w_kqv)
    low_rank = mm(normed_in, down_full, 1, 0).astype(BF16)
    gate_logit = contract_last(low_rank, up_mine) + bias_mine
    log_decay = jax.nn.log_sigmoid(gate_logit) / GATE_NORM * alive
    writes = -jnp.expm1(log_decay)

    def seqs(x):
        return x.reshape(sequences, piece, x.shape[1])

    def flat(x):
        return x.reshape(all_rows, x.shape[2])

    is_value = jnp.arange(3 * head_width) >= 2 * head_width
    feats = seqs(jnp.where(is_value, pre, pre * jax.nn.sigmoid(pre)).astype(BF16))
    pre = seqs(pre)
    decays, writes = seqs(log_decay), seqs(writes)

    def shaped(like_rows, columns, kind):
        return jax.ShapeDtypeStruct((sequences, like_rows, columns), kind)

    gate_and_out, feats = lax.optimization_barrier((gate_and_out, feats))
    keys, queries, values = (feats, 0), (feats, 1), (feats, 2)
    state_in, keeps = relay(
        lanes.outer, False, [feats, decays, writes], sequences, SLOTS, 2 * head_width
    )
    feed = jnp.stack([w_down, w_act, w_lin])
    feed, state_in, gate_and_out = lax.optimization_barrier((feed, state_in, gate_and_out))
    feed = lax.all_gather(
        feed, "seq", axis=1, tiled=True, axis_index_groups=lanes.groups
    )
    gate_and_out = gate_and_out.reshape(lanes.outer, 2, out_rows, width)
    gate_own, out_own = gate_and_out[:, 0], gate_and_out[:, 1]
    gate_other = lanes.swap_inner(gate_own)
    w_g = jnp.concatenate([gate_own, gate_other], axis=0).reshape(head_width, width)
    gates = seqs(contract_last(normed_in, w_g))
    out_own = out_own.reshape(lanes.outer, lanes.dp, out_rows, head_width)
    out_other = swap_halves(lanes.swap_inner(out_own), 1)
    even = lanes.inner_at == 0
    natural = jnp.stack(
        [jnp.where(even, out_own, out_other), jnp.where(even, out_other, out_own)], axis=2
    )
    out_full = natural.transpose(1, 0, 2, 3, 4).reshape(width, head_width)
    mixed, slot_out, attend = per_sequence(
        forward_kernel,
        [queries, keys, values, gates, decays, writes, state_in],
        [
            shaped(piece, head_width, BF16),
            shaped(piece, head_width, F32),
            shaped(piece, SLOTS, F32),
        ],
        shared=[head_full],
    )
    mixed_flat = flat(mixed)
    parts = contract_last(mixed_flat, out_full).astype(BF16)
    hidden, normed_mid, grad_feed = middle(
        parts.reshape(4, rows, width), own_tokens, feed_full, grad_feed
    )
    normed_mid = normed_mid.reshape(8 * rows, width)
    grad_feed = grad_feed.reshape(8 * rows, width)

    units = feed.shape[1]
    product, grad_gate, grad_lin = feed_tiles(
        feed_kernel, [normed_mid, grad_feed], feed, [units] * 3
    )
    feed_grads = jnp.stack(
        [
            contract_first(product, grad_feed).astype(BF16),
            contract_first(grad_gate, normed_mid).astype(BF16),
            contract_first(grad_lin, normed_mid).astype(BF16),
        ]
    )
    product, grad_gate, grad_lin, feed_grads = lax.optimization_barrier(
        (product, grad_gate, grad_lin, feed_grads)
    )
    feed_grads = lax.psum_scatter(
        feed_grads, "seq", scatter_dimension=1, tiled=True, axis_index_groups=lanes.groups
    )
    feed_parts, mid_parts = feed_tiles(
        feed_back_kernel, [product, grad_gate, grad_lin], feed, [width] * 2
    )
    grad_hidden, feed_gain_part, grad_attn = middle_back(
        mid_parts.reshape(8, rows, width), hidden, grad_out, feed_full
    )
    grad_attn = grad_attn.reshape(all_rows, width)
    feed_parts, grad_attn = lax.optimization_barrier((feed_parts, grad_attn))

    grad_mixed = mm(grad_attn, out_full, 1, 0)
    grad_gate_pre, grad_slot, grad_scores, adjoint, head_parts = per_sequence(
        back_first_kernel,
        [seqs(grad_mixed), gates, slot_out, attend, queries, values, decays, writes, state_in],
        [
            shaped(piece, head_width, BF16),
            shaped(piece, head_width, BF16),
            shaped(piece, SLOTS, F32),
            shaped(SLOTS, 2 * head_width, F32),
            shaped(1, head_width, F32),
        ],
        shared=[head_full],
    )
    grad_gate_flat = flat(grad_gate_pre)
    out_grad = contract_first(grad_attn, mixed_flat).astype(BF16)
    out_grad = out_grad.reshape(lanes.dp, lanes.outer, 2, out_rows, head_width)
    own_part, other_part = lanes.pick(out_grad, 2)
    got = swap_halves(lanes.swap_inner(other_part), 1)
    out_sum = (own_part.astype(F32) + got.astype(F32)).astype(BF16).transpose(1, 0, 2, 3)
    gate_grad = contract_first(grad_gate_flat, normed_in).astype(BF16)
    adjoint, out_sum, gate_grad, feed_parts = lax.optimization_barrier(
        (adjoint, out_sum, gate_grad, feed_parts)
    )
    adjoint_in, feed_sums = relay(
        lanes.outer, True, [adjoint, keeps, feed_parts.reshape(8, rows, width)], sequences,
        SLOTS, 2 * head_width,
    )
    feed_got = lanes.swap_inner(feed_sums[1])
    gate_grad, out_sum, adjoint_in, feed_grads = lax.optimization_barrier(
        (gate_grad, out_sum, adjoint_in, feed_grads)
    )
    out_mine = lanes.scatter_outer(out_sum.reshape(-1, head_width))
    gate_got = lanes.swap_inner(gate_grad[half_width:])
    grad_pre, grad_logit = per_sequence(
        back_second_kernel,
        [
            grad_slot, grad_scores, attend, queries, keys, values, decays, writes,
            state_in, adjoint_in, (pre, 1), (pre, 0), seqs(gate_logit), seqs(alive),
        ],
        [shaped(piece, 3 * head_width, BF16), shaped(piece, SLOTS, BF16)],
    )
    grad_pre, gate_got, out_mine = lax.optimization_barrier(
        (flat(grad_pre), gate_got, out_mine)
    )
    gate_sum = (gate_grad[:half_width].astype(F32) + gate_got.astype(F32)).astype(BF16)
    grad_logit = flat(grad_logit)
    bias_part = jnp.sum(grad_logit.astype(F32), axis=0)
    up_part = contract_first(grad_logit, low_rank)
    grad_in, grad_rank = grad_in_tiles(
        [grad_pre, grad_gate_flat, grad_logit], [w_kqv, w_g, up_mine, down_full], [width, rank]
    )
    down_part = contract_first(normed_in, grad_rank)

    mixer_grads = contract_first(grad_pre, normed_in).astype(BF16)
    mixer_grads = mixer_grads.reshape(3, 2, lanes.outer, -1, width)

    head_part = jnp.sum(head_parts, axis=(0, 1)).reshape(2, lanes.outer, -1)
    low_half, high_half = lanes.pick(head_part, 0)
    head_part = jnp.stack([low_half, high_half], axis=1)
    mine = (jnp.arange(lanes.dp) == lanes.d).astype(F32)
    up_all = mine[:, None] * up_part.reshape(1, -1)
    bias_all = mine[:, None] * bias_part.reshape(1, -1)
    parts = [
        feed_gain_part.reshape(devices, -1),
        head_part.reshape(devices, -1),
        down_part.reshape(devices, -1),
        up_all.reshape(devices, -1),
        bias_all.reshape(devices, -1),
    ]
    sizes = [p.shape[1] for p in parts]
    padded = -(-sum(sizes) // 1024) * 1024
    parts.append(jnp.zeros((devices, padded - sum(sizes)), F32))
    small_parts = jnp.concatenate(parts, axis=1).reshape(devices, -1, 128)
    grad_in, mixer_grads, feed_got = lax.optimization_barrier((grad_in, mixer_grads, feed_got))
    out_mine = out_mine.reshape(lanes.dp, out_rows, head_width)
    out_mine = lanes.exchange_heads(out_mine).transpose(1, 0, 2)
    out_mine = out_mine.reshape(out_rows, lanes.dp, 2, lanes.outer, -1)
    low_half, high_half = lanes.pick(out_mine, 2)
    w_out_grad = jnp.stack([low_half, high_half], axis=3).reshape(out_rows, width).astype(F32)
    feed_sum = feed_sums[0].astype(F32) + feed_got.astype(F32)
    block_out = (alive_own * (hidden + feed_sum)).astype(BF16)
    weight_grads, tokens_grad, reduced = finish(
        lanes.outer, lanes.dp, mixer_grads,
        gate_sum.reshape(lanes.outer, -1, width), grad_in.reshape(4, rows, width), own_tokens,
        grad_hidden, mixer_full, small_parts,
    )
    w_key_grad, w_query_grad, w_value_grad, w_gate_grad = [weight_grads[m] for m in range(4)]
    tokens_grad = tokens_grad.reshape(seq_count, piece, width)
    mixer_gain_grad = reduced[padded // 128, : width // devices]
    reduced = reduced.reshape(-1)
    smalls, offset = [], 0
    for size in sizes:
        smalls.append(reduced[offset : offset + size])
        offset += size
    return (
        block_out.reshape(seq_count, piece, width),
        tokens_grad,
        mixer_gain_grad,
        smalls[0],
        smalls[1],
        w_query_grad,
        w_key_grad,
        w_value_grad,
        w_gate_grad,
        w_out_grad,
        smalls[2].reshape(-1, rank),
        smalls[3].reshape(-1, rank),
        smalls[4],
        feed_grads[1].astype(F32),
        feed_grads[2].astype(F32),
        feed_grads[0].astype(F32),
    )


def solution(mesh):
    vector = P(("dp", "seq"))
    matrix = P(("dp", "seq"), None)
    stream = P("dp", "seq", None)
    return jax.shard_map(
        per_device,
        mesh=mesh,
        in_specs=(
            stream, P("dp"), stream, vector, vector, vector, matrix, matrix, matrix, matrix,
            matrix, matrix, matrix, vector, matrix, matrix, matrix,
        ),
        out_specs=(
            stream, stream, vector, vector, vector, matrix, matrix, matrix, matrix, matrix,
            matrix, matrix, vector, matrix, matrix, matrix,
        ),
        check_vma=False,
    )
```

```python
import functools

import jax
import jax.numpy as jnp
from jax import lax
from jax.experimental import pallas as pl
from jax.experimental.pallas import tpu as pltpu
from jax.sharding import PartitionSpec as P

HEADS = 4
SLOTS = 64
EPS = 1e-06
GATE_NORM = 8.0
F32 = jnp.float32
BF16 = jnp.bfloat16
LEAF = 8
VMEM_LIMIT = 48 * 1024 * 1024


def mm(a, b, ca, cb):
    return lax.dot_general(
        a.astype(BF16), b.astype(BF16), (((ca,), (cb,)), ((), ())), preferred_element_type=F32
    )


def mm_exact(a, b, ca, cb):
    return lax.dot_general(
        a,
        b,
        (((ca,), (cb,)), ((), ())),
        precision=lax.Precision.HIGHEST,
        preferred_element_type=F32,
    )


def two_parts(x):
    high = x.astype(BF16)
    return high, (x - high.astype(F32)).astype(BF16)


def mm_left(exact, b, ca, cb):
    high, low = two_parts(b)
    return mm(exact, high, ca, cb) + mm(exact, low, ca, cb)


def mm_right(a, exact, ca, cb):
    high, low = two_parts(a)
    return mm(high, exact, ca, cb) + mm(low, exact, ca, cb)


def mm_fine(a, b, ca, cb):
    a_high, a_low = two_parts(a)
    b_high, b_low = two_parts(b)
    return mm(a_high, b_high, ca, cb) + (mm(a_high, b_low, ca, cb) + mm(a_low, b_high, ca, cb))


def contract_last(a, b):
    return mm(a, b, 1, 1)


def contract_first(a, b):
    return mm(a, b, 0, 0)


def swish_slope(v):
    sigma = jax.nn.sigmoid(v)
    return sigma * (1.0 + v * (1.0 - sigma))


def rms_scale(v):
    return lax.rsqrt(jnp.mean(v * v, axis=-1, keepdims=True) + EPS)


def grid_index(rows, cols):
    return (
        lax.broadcasted_iota(jnp.int32, (rows, cols), 0),
        lax.broadcasted_iota(jnp.int32, (rows, cols), 1),
    )


def running_sum(decay):
    length = decay.shape[0]
    row, col = grid_index(length, length)
    return mm_exact((row >= col).astype(F32), decay, 1, 0)


def levels(length):
    found = []
    half = length // 2
    while half >= LEAF:
        found.append(half)
        half //= 2
    return found


def level_factors(running, writes, half):
    length, slots = running.shape
    pairs = running.reshape(length // (2 * half), 2 * half, slots)
    anchor = jnp.broadcast_to(pairs[:, half - 1 : half, :], pairs.shape).reshape(length, slots)
    near = jnp.exp(-jnp.abs(running - anchor))
    row, _ = grid_index(length, slots)
    right = (row % (2 * half)) >= half
    return jnp.where(right, near, 0.0), jnp.where(right, 0.0, near), right


def same_block(length, size):
    row, col = grid_index(length, length)
    return (row // size) == (col // size)


def leaf_selector(length):
    row, col = grid_index(length, LEAF)
    return ((row % LEAF) == col).astype(F32)


def leaf_take(square):
    length = square.shape[0]
    kept = jnp.where(same_block(length, LEAF), square, 0.0)
    return mm_exact(kept, leaf_selector(length), 1, 0)


def leaf_spread(columns):
    length = columns.shape[0]
    wide = mm_exact(columns, leaf_selector(length), 1, 1)
    return jnp.where(same_block(length, LEAF), wide, 0.0)


def leaf_row(tensor, at):
    length, width = tensor.shape
    blocks = tensor.reshape(length // LEAF, LEAF, width)
    return jnp.broadcast_to(blocks[:, at : at + 1, :], blocks.shape).reshape(length, width)


def leaf_decay(running, at):
    length, slots = running.shape
    row, _ = grid_index(length, slots)
    reached = (row % LEAF) >= at
    spread = running - leaf_row(running, at)
    return jnp.where(reached, jnp.exp(jnp.where(reached, spread, 0.0)), 0.0)


def masked(square, half):
    length = square.shape[0]
    if 2 * half == length:
        return square
    return jnp.where(same_block(length, 2 * half), square, 0.0)


def read_in_chunk(square, running, writes):
    total = None
    for half in levels(running.shape[0]):
        right, left, _ = level_factors(running, writes, half)
        part = right * mm_fine(masked(square, half), left * writes, 1, 0)
        total = part if total is None else total + part
    columns = leaf_take(square)
    for at in range(LEAF):
        part = columns[:, at : at + 1] * (leaf_decay(running, at) * leaf_row(writes, at))
        total = part if total is None else total + part
    return total


def mix_in_chunk(attend, running, writes):
    total = None
    for half in levels(running.shape[0]):
        right, left, _ = level_factors(running, writes, half)
        part = masked(mm(attend * right, left * writes, 1, 1), half)
        total = part if total is None else total + part
    columns = [
        jnp.sum(
            attend * (leaf_decay(running, at) * leaf_row(writes, at)), axis=1, keepdims=True
        )
        for at in range(LEAF)
    ]
    part = leaf_spread(jnp.concatenate(columns, axis=1))
    return part if total is None else total + part


def summary(k, v, decay, writes):
    running = running_sum(decay)
    length = running.shape[0]
    last = running[length - 1 : length, :]
    fade = jnp.exp(last - running) * writes
    return jnp.concatenate([mm(fade, k, 0, 0), mm(fade, v, 0, 0)], axis=1), jnp.exp(last)


def forward_kernel(
    q_ref, k_ref, v_ref, gate_ref, decay_ref, writes_ref, state_ref, gain_ref,
    mixed_ref, out_ref, attend_ref,
):
    q, k, v = q_ref[0], k_ref[0], v_ref[0]
    writes = writes_ref[0]
    width = q.shape[1]
    scale = width ** (-0.5)
    running = running_sum(decay_ref[0])
    growth = jnp.exp(running)
    state = state_ref[0]
    dots = mm(q, k, 1, 1) * scale
    scores = growth * (mm(q, state[:, :width], 1, 1) * scale)
    scores = scores + read_in_chunk(dots, running, writes)
    top = jnp.max(scores, axis=1, keepdims=True)
    raw = jnp.exp(scores - top)
    attend = raw / jnp.sum(raw, axis=1, keepdims=True)
    mixing = mix_in_chunk(attend, running, writes)
    out = mm(attend * growth, state[:, width:], 1, 0) + mm(mixing, v, 1, 0)
    out_ref[0] = out
    attend_ref[0] = attend
    gate = gate_ref[0]
    normed = out * rms_scale(out) * gain_ref[...]
    mixed_ref[0] = (normed * (gate * jax.nn.sigmoid(gate))).astype(BF16)


def back_first_kernel(
    grad_mixed_ref, gate_ref, out_ref, attend_ref, q_ref, v_ref, decay_ref, writes_ref,
    state_ref, gain_ref,
    grad_gate_ref, grad_out_ref, grad_scores_ref, adjoint_ref, gain_grad_ref,
):
    q, v = q_ref[0], v_ref[0]
    writes = writes_ref[0]
    width = q.shape[1]
    scale = width ** (-0.5)
    grad_mixed, gate, out = grad_mixed_ref[0], gate_ref[0], out_ref[0]
    gain = gain_ref[...]
    inverse = rms_scale(out)
    normed = out * inverse
    grad_gate_ref[0] = (grad_mixed * (normed * gain) * swish_slope(gate)).astype(BF16)
    e = grad_mixed * (gate * jax.nn.sigmoid(gate))
    gain_grad_ref[0] = jnp.sum(e * normed, axis=0, keepdims=True)
    eg = e * gain
    grad_out = inverse * (eg - normed * jnp.mean(eg * normed, axis=1, keepdims=True))
    grad_out_ref[0] = grad_out.astype(BF16)
    running = running_sum(decay_ref[0])
    growth = jnp.exp(running)
    attend = attend_ref[0]
    u = growth * mm_right(grad_out, state_ref[0, :, width:], 1, 1)
    u = u + read_in_chunk(mm_right(grad_out, v, 1, 1), running, writes)
    grad_scores = attend * (u - jnp.sum(attend * u, axis=1, keepdims=True))
    grad_scores_ref[0] = grad_scores
    adjoint_ref[0, :, :width] = mm(growth * grad_scores * scale, q, 0, 0)
    adjoint_ref[0, :, width:] = mm(growth * attend, grad_out.astype(BF16), 0, 0)


def back_second_kernel(
    grad_out_ref, grad_scores_ref, attend_ref, q_ref, k_ref, v_ref, decay_ref, writes_ref,
    state_ref, adjoint_ref, q_pre_ref, k_pre_ref, logit_ref, alive_ref,
    grad_pre_ref, dlogit_ref,
):
    q, k, v, grad_out = q_ref[0], k_ref[0], v_ref[0], grad_out_ref[0]
    attend, grad_scores = attend_ref[0], grad_scores_ref[0]
    decay, writes = decay_ref[0], writes_ref[0]
    length, slots = decay.shape
    width = q.shape[1]
    scale = width ** (-0.5)
    running = running_sum(decay)
    growth = jnp.exp(running)
    keep = jnp.exp(decay)
    last = running[length - 1 : length, :]
    fade = jnp.exp(last - running)
    state, adjoint = state_ref[0], adjoint_ref[0]
    key_state, value_state = state[:, :width], state[:, width:]
    key_adjoint, value_adjoint = adjoint[:, :width], adjoint[:, width:]
    key_dots = mm(q, k, 1, 1) * scale
    value_dots = mm(grad_out, v, 1, 1)
    row, col = grid_index(length, length)

    columns_sum = jnp.zeros((length, slots), F32)
    crossing = jnp.zeros((length, slots), F32)
    mix_key = jnp.zeros((length, length), F32)
    mix_value = jnp.zeros((length, length), F32)
    for half in levels(length):
        right, left, is_right = level_factors(running, writes, half)
        key_part, value_part = masked(key_dots, half), masked(value_dots, half)
        left_w = left * writes
        gs_right, at_right = grad_scores * right, attend * right
        mix_key = mix_key + masked(mm(gs_right, left_w, 1, 1), half)
        mix_value = mix_value + masked(mm(at_right, left_w, 1, 1), half)
        rows_sum = gs_right * mm_fine(key_part, left_w, 1, 0) + at_right * mm_fine(value_part, left_w, 1, 0)
        open_sum = left * (mm_fine(key_part, gs_right, 0, 0) + mm_fine(value_part, at_right, 0, 0))
        columns_sum = columns_sum + open_sum
        sums = jnp.where(is_right, rows_sum, open_sum * writes)
        forward = jnp.where((row % (2 * half)) >= half, col - row, row - col - 1) >= 0
        wanted = ((row // half) == (col // half)) & forward
        crossing = crossing + mm_left(wanted.astype(F32), sums, 1, 0)
    key_leaf, value_leaf = leaf_take(key_dots), leaf_take(value_dots)
    leaf_at = lax.broadcasted_iota(jnp.int32, (length, slots), 0) % LEAF
    difference = jnp.zeros((length, slots), F32)
    mix_key_columns, mix_value_columns = [], []
    for at in range(LEAF):
        fall = leaf_decay(running, at)
        mass = leaf_row(writes, at)
        mix_key_columns.append(jnp.sum(grad_scores * fall * mass, axis=1, keepdims=True))
        mix_value_columns.append(jnp.sum(attend * fall * mass, axis=1, keepdims=True))
        terms = fall * (
            grad_scores * key_leaf[:, at : at + 1] + attend * value_leaf[:, at : at + 1]
        )
        blocks = terms.reshape(length // LEAF, LEAF, slots)
        whole = jnp.broadcast_to(
            jnp.sum(blocks, axis=1, keepdims=True), blocks.shape
        ).reshape(length, slots)
        columns_sum = columns_sum + jnp.where(leaf_at == at, whole, 0.0)
        later = jnp.where(leaf_at > at, terms, 0.0)
        later_blocks = later.reshape(length // LEAF, LEAF, slots)
        later_whole = jnp.broadcast_to(
            jnp.sum(later_blocks, axis=1, keepdims=True), later_blocks.shape
        ).reshape(length, slots)
        difference = difference + mass * (later - jnp.where(leaf_at == at, later_whole, 0.0))
    mix_key = mix_key + leaf_spread(jnp.concatenate(mix_key_columns, axis=1))
    mix_value = mix_value + leaf_spread(jnp.concatenate(mix_value_columns, axis=1))
    suffix_leaf = (((row // LEAF) == (col // LEAF)) & (col >= row)).astype(F32)
    crossing = crossing + mm_exact(suffix_leaf, difference, 1, 0)

    start_terms = growth * (
        grad_scores * (mm(q, key_state, 1, 1) * scale)
        + attend * mm(grad_out, value_state, 1, 1)
    )
    crossing = crossing + mm_left((col >= row).astype(F32), start_terms, 1, 0)
    end_open = fade * (mm(k, key_adjoint, 1, 1) + mm(v, value_adjoint, 1, 1))
    columns_sum = columns_sum + end_open
    crossing = crossing + mm_left((col < row).astype(F32), end_open * writes, 1, 0)
    through = mm_exact(
        jnp.ones((8, 2 * width), F32), state.astype(F32) * adjoint.astype(F32), 1, 1
    )[0:1, :]
    crossing = crossing + jnp.exp(last) * through
    grad_decay = crossing - keep * columns_sum

    grad_q = (mm(grad_scores * growth, key_state, 1, 0) + mm(mix_key, k, 1, 0)) * scale
    fade_w = fade * writes
    grad_k = mm(mix_key, q, 0, 0) * scale + mm(fade_w, key_adjoint, 1, 0)
    grad_v = mm(mix_value, grad_out, 0, 0) + mm(fade_w, value_adjoint, 1, 0)
    grad_pre_ref[0, :, :width] = (grad_k * swish_slope(k_pre_ref[0])).astype(BF16)
    grad_pre_ref[0, :, width : 2 * width] = (grad_q * swish_slope(q_pre_ref[0])).astype(BF16)
    grad_pre_ref[0, :, 2 * width :] = grad_v.astype(BF16)
    dlogit_ref[0] = (
        alive_ref[0] * grad_decay * jax.nn.sigmoid(-logit_ref[0]) * (1.0 / GATE_NORM)
    ).astype(BF16)


def per_sequence(kernel, inputs, outputs, shared=()):
    inputs = [x if isinstance(x, tuple) else (x, None) for x in inputs]
    count = inputs[0][0].shape[0]

    def spec(shape, at=None):
        if at is None:
            return pl.BlockSpec((1,) + tuple(shape[1:]), lambda s: (s, 0, 0))
        return pl.BlockSpec((1, shape[1], shape[2] // 3), lambda s: (s, 0, at))

    return pl.pallas_call(
        kernel,
        grid=(count,),
        in_specs=[spec(x.shape, at) for x, at in inputs]
        + [pl.BlockSpec(x.shape, lambda s: (0, 0)) for x in shared],
        out_specs=[spec(x.shape) for x in outputs],
        out_shape=outputs,
        compiler_params=pltpu.CompilerParams(vmem_limit_bytes=VMEM_LIMIT),
    )(*[x for x, _ in inputs], *shared)


CHUNKS = 8
STRIP = 16


def send(src, dst, send_sem, recv_sem, where):
    copy = pltpu.make_async_remote_copy(
        src_ref=src,
        dst_ref=dst,
        send_sem=send_sem,
        recv_sem=recv_sem,
        device_id=where,
        device_id_type=pl.DeviceIdType.MESH,
    )
    copy.start()
    return copy


def greet(partners):
    barrier = pltpu.get_barrier_semaphore()
    for where in partners:
        pl.semaphore_signal(
            barrier, inc=1, device_id=where, device_id_type=pl.DeviceIdType.MESH
        )
    return barrier


def near_partners():
    d, at = lax.axis_index("dp"), lax.axis_index("seq")
    x = {"seq": jnp.bitwise_xor(at, 1)}
    y = {"dp": jnp.bitwise_xor(d, 2)}
    core = {"dp": jnp.bitwise_xor(d, 1)}
    return x, y, core


def everyone(seq, dp, act):
    me = lax.axis_index("dp") * seq + lax.axis_index("seq")

    def turn(r, carry):
        other = jnp.bitwise_xor(me, r)
        act(r, {"dp": other // seq, "seq": other % seq})
        return carry

    lax.fori_loop(1, seq * dp, turn, 0)


def greet_everyone(seq, dp):
    barrier = pltpu.get_barrier_semaphore()
    everyone(
        seq,
        dp,
        lambda r, where: pl.semaphore_signal(
            barrier, inc=1, device_id=where, device_id_type=pl.DeviceIdType.MESH
        ),
    )
    pl.semaphore_wait(barrier, seq * dp - 1)


def gather_kernel(outer, dp, *refs):
    mats, refs = refs[:3], refs[3:]
    toks, small, w_out, refs = refs[:2], refs[2], refs[3], refs[4:]
    three, heads, refs = refs[0], refs[1], refs[2:]
    out_toks, out_small, refs = refs[:2], refs[2], refs[3:]
    (
        local_sem, up_send, up_recv, down_send, down_recv, x_send, x_recv,
        tok_send, tok_recv, small_send, small_recv, head_send, head_recv,
    ) = refs
    outs = [three.at[0], three.at[1], three.at[2]]
    seq = 2 * outer
    at = lax.axis_index("seq")
    d = lax.axis_index("dp")
    me = d * seq + at
    z = at // 2
    x, y, core = near_partners()
    above, below = {"seq": at + 2}, {"seq": at - 2}
    has_above, has_below = z < outer - 1, z > 0
    greet_everyone(seq, dp)

    def push(r, where):
        return pltpu.make_async_remote_copy(
            src_ref=small, dst_ref=out_small.at[me], send_sem=small_send.at[r],
            recv_sem=small_recv.at[r], device_id=where, device_id_type=pl.DeviceIdType.MESH,
        )

    everyone(seq, dp, lambda r, where: push(r, where).start())
    head = heads.shape[2]

    def columns(owner):
        return w_out.at[:, pl.ds(pl.multiple_of(owner * head, head), head)]

    own_head = pltpu.make_async_copy(columns(d), heads.at[d], local_sem.at[5])
    own_head.start()
    other_heads = [
        send(
            columns(jnp.bitwise_xor(d, r)), heads.at[d], head_send.at[r], head_recv.at[r],
            {"dp": jnp.bitwise_xor(d, r)},
        )
        for r in range(1, dp)
    ]

    def up(m, k, src, origin):
        return pltpu.make_async_remote_copy(
            src_ref=src, dst_ref=outs[m].at[0, origin], send_sem=up_send.at[m, k],
            recv_sem=up_recv.at[m, k], device_id=above, device_id_type=pl.DeviceIdType.MESH,
        )

    def down(m, k, src, origin):
        return pltpu.make_async_remote_copy(
            src_ref=src, dst_ref=outs[m].at[0, origin], send_sem=down_send.at[m, k],
            recv_sem=down_recv.at[m, k], device_id=below, device_id_type=pl.DeviceIdType.MESH,
        )

    def across(m, src, origin):
        return pltpu.make_async_remote_copy(
            src_ref=src, dst_ref=outs[m].at[1, origin], send_sem=x_send.at[m, origin],
            recv_sem=x_recv.at[m, origin], device_id=x, device_id_type=pl.DeviceIdType.MESH,
        )

    for m in range(3):
        @pl.when(has_above)
        def _():
            up(m, 0, mats[m], z).start()

        @pl.when(has_below)
        def _():
            down(m, 0, mats[m], z).start()

        across(m, mats[m], z).start()
    tok_y, tok_rest = [], []
    for n, (tok, out_tok) in enumerate(zip(toks, out_toks)):
        tok_y.append(send(tok, out_tok.at[1], tok_send.at[3 * n], tok_recv.at[3 * n], y))
        tok_rest.append(
            send(tok, out_tok.at[2], tok_send.at[3 * n + 1], tok_recv.at[3 * n + 1], core)
        )
        copy = pltpu.make_async_copy(tok, out_tok.at[0], local_sem.at[1 + 5 * n])
        copy.start()
        tok_rest.append(copy)
    own_small = pltpu.make_async_copy(small, out_small.at[me], local_sem.at[0])
    own_small.start()
    own_mats = []
    for m in range(3):
        copy = pltpu.make_async_copy(mats[m], outs[m].at[0, z], local_sem.at[2 + m])
        copy.start()
        own_mats.append(copy)

    def pass_on(k, carry):
        for m in range(3):
            @pl.when(z - k >= 0)
            def _():
                slot = outs[m].at[0, z - k]
                up(m, k - 1, slot, z - k).wait_recv()

                @pl.when(has_above)
                def _():
                    up(m, k, slot, z - k).start()

                across(m, slot, z - k).start()

            @pl.when(z + k < outer)
            def _():
                slot = outs[m].at[0, z + k]
                down(m, k - 1, slot, z + k).wait_recv()

                @pl.when(has_below)
                def _():
                    down(m, k, slot, z + k).start()

                across(m, slot, z + k).start()

        return carry

    lax.fori_loop(1, outer, pass_on, 0)
    for n, out_tok in enumerate(out_toks):
        tok_y[n].wait()
        tok_rest.append(
            send(out_tok.at[1], out_tok.at[3], tok_send.at[3 * n + 2], tok_recv.at[3 * n + 2], core)
        )

    def arrived(r, where):
        push(r, where).wait_send()
        theirs = out_small.at[jnp.bitwise_xor(me, r)]
        pltpu.make_async_remote_copy(
            src_ref=theirs, dst_ref=theirs, send_sem=small_send.at[r],
            recv_sem=small_recv.at[r], device_id=where, device_id_type=pl.DeviceIdType.MESH,
        ).wait_recv()

    everyone(seq, dp, arrived)

    def complete(o, carry):
        for m in range(3):
            across(m, outs[m].at[0, o], o).wait()

            @pl.when(has_above & (o <= z))
            def _():
                up(m, o, outs[m].at[0, z], z).wait_send()

            @pl.when(has_below & (o <= outer - 1 - z))
            def _():
                down(m, o, outs[m].at[0, z], z).wait_send()

        return carry

    lax.fori_loop(0, outer, complete, 0)
    for copy in own_mats:
        copy.wait()
    own_head.wait()
    for r, copy in enumerate(other_heads, 1):
        copy.wait_send()
        theirs = heads.at[jnp.bitwise_xor(d, r)]
        pltpu.make_async_remote_copy(
            src_ref=theirs, dst_ref=theirs, send_sem=head_send.at[r],
            recv_sem=head_recv.at[r], device_id={"dp": jnp.bitwise_xor(d, r)},
            device_id_type=pl.DeviceIdType.MESH,
        ).wait_recv()
    own_small.wait()
    for copy in tok_rest:
        copy.wait()


def in_hbm():
    return pl.BlockSpec(memory_space=pl.ANY)


def in_vmem():
    return pl.BlockSpec(memory_space=pltpu.VMEM)


def gather_all(outer, dp, mats, toks, small, w_out):
    seq = 2 * outer
    rows, width = mats[0].shape
    dma = pltpu.SemaphoreType.DMA
    return pl.pallas_call(
        functools.partial(gather_kernel, outer, dp),
        in_specs=[in_vmem()] * 5 + [in_hbm()] * 2,
        out_specs=[in_hbm()] * 5,
        out_shape=[
            jax.ShapeDtypeStruct((3, 2, outer, rows, width), BF16),
            jax.ShapeDtypeStruct((dp, w_out.shape[0], w_out.shape[1] // dp), BF16),
            jax.ShapeDtypeStruct((dp,) + toks[0].shape, BF16),
            jax.ShapeDtypeStruct((dp,) + toks[1].shape, BF16),
            jax.ShapeDtypeStruct((seq * dp,) + small.shape, BF16),
        ],
        scratch_shapes=[dma((7,))] + [dma((3, outer))] * 6
        + [dma((6,))] * 2 + [dma((seq * dp,))] * 2 + [dma((dp,))] * 2,
        compiler_params=pltpu.CompilerParams(
            collective_id=1, has_side_effects=True, vmem_limit_bytes=VMEM_LIMIT
        ),
    )(*mats, *toks, small, w_out)


def feed_kernel(mid, grad_feed, w_down, w_act, w_lin, product, grad_gate, grad_lin):
    gate = mm(mid[...], w_act[0], 1, 1)
    lin = mm(mid[...], w_lin[0], 1, 1)
    grad_product = mm(grad_feed[...], w_down[0], 1, 1)
    sigma = jax.nn.sigmoid(gate)
    swish = gate * sigma
    product[...] = (swish * lin).astype(BF16)
    grad_gate[...] = (grad_product * lin * (sigma * (1.0 + gate * (1.0 - sigma)))).astype(BF16)
    grad_lin[...] = (grad_product * swish).astype(BF16)


def feed_back_kernel(
    product, grad_gate, grad_lin, w_down, w_act, w_lin, feed, grad_mid
):
    grad_mid[...] = (
        mm(grad_gate[...], w_act[0], 1, 0) + mm(grad_lin[...], w_lin[0], 1, 0)
    ).astype(BF16)
    feed[...] = mm(product[...], w_down[0], 1, 0).astype(BF16)


def feed_tiles(kernel, tiles, weights, widths):
    rows = tiles[0].shape[0]
    step = min(256, rows)
    _, units, width = weights.shape
    each = 2 * step * units * width

    def spec(columns):
        return pl.BlockSpec((step, columns), lambda t: (t, 0))

    def weight(at):
        return pl.BlockSpec(
            (1, units, width), lambda t: (at, 0, 0), pipeline_mode=pl.Buffered(1)
        )

    return pl.pallas_call(
        kernel,
        grid=(rows // step,),
        in_specs=[spec(x.shape[1]) for x in tiles] + [weight(m) for m in range(3)],
        out_specs=[spec(columns) for columns in widths],
        out_shape=[jax.ShapeDtypeStruct((rows, columns), BF16) for columns in widths],
        cost_estimate=pl.CostEstimate(
            flops=3 * each * (rows // step), bytes_accessed=6 * units * width + 8 * rows * width,
            transcendentals=rows * units,
        ),
        compiler_params=pltpu.CompilerParams(vmem_limit_bytes=VMEM_LIMIT),
    )(*tiles, weights, weights, weights)


def turned(x):
    row, col = grid_index(x.shape[1], x.shape[1])
    return mm_exact((row == col).astype(F32), x, 1, 1)


def flipped(x):
    size = x.shape[-1] // 4
    return jnp.concatenate([x[:, size * i : size * (i + 1)] for i in (1, 0, 3, 2)], axis=1)


def relay_kernel(outer, backward, *refs):
    if backward:
        totals, keeps, parts, gate_sent, refs = refs[0], refs[1], refs[2], refs[3], refs[4:]
        states, sums, gate_got, refs = refs[0], refs[1], refs[2], refs[3:]
        gate_s, gate_r = refs[-2:]
        side, refs = refs[-9:-2], refs[:-9]
    else:
        feats, decays, writes, refs = refs[0], refs[1], refs[2], refs[3:]
        states, keeps, refs = refs[0], refs[1], refs[2:]
    (
        own, to_x, from_x, to_z, from_z, to_back, from_back, keep_mine, keep_theirs,
        x_s, x_r, z_s, z_r, b_s, b_r, k_s, k_r,
    ) = refs
    half = own.shape[0]
    at = lax.axis_index("seq")
    inner, z = at % 2, at // 2
    x, y, core = near_partners()
    above, below = {"seq": at + 2}, {"seq": at - 2}
    has_above, has_below = z < outer - 1, z > 0
    ahead, has_ahead, has_source = (
        (below, has_below, has_above) if backward else (above, has_above, has_below)
    )
    barrier = greet([x, y, core] if backward else [x])

    @pl.when(has_above)
    def _():
        greet([above])

    @pl.when(has_below)
    def _():
        greet([below])

    pl.semaphore_wait(
        barrier,
        (3 if backward else 1) + has_above.astype(jnp.int32) + has_below.astype(jnp.int32),
    )

    def compute(s):
        if backward:
            return totals[s]
        width = feats.shape[2] // 3
        total, keep = summary(
            feats[s, :, :width], feats[s, :, 2 * width :], decays[s], writes[s]
        )
        keep_mine[s] = keep
        return total

    crossing = []
    for i in range(half):
        to_x[i] = compute((1 - inner) * half + i).astype(BF16)
        crossing.append(send(to_x.at[i], from_x.at[i], x_s.at[i], x_r.at[i], x))
    if backward:
        gate_copy = send(gate_sent, gate_got, gate_s.at[0], gate_r.at[0], x)
        side = plane_sum_start(parts, side, y, core)
    for i in range(half):
        own[i] = compute(inner * half + i)
    if backward:
        keep_a, keep_b = keeps[0], keeps[1]
    else:
        send(keep_mine, keep_theirs, k_s.at[0], k_r.at[0], x).wait()
        mine = jnp.concatenate([keep_mine[s] for s in range(2 * half)], axis=0)
        theirs = jnp.concatenate([keep_theirs[s] for s in range(2 * half)], axis=0)
        keep_a = jnp.where(inner == 0, mine, theirs)
        keep_b = jnp.where(inner == 0, theirs, mine)
        keeps[0] = keep_a
        keeps[1] = keep_b
    if backward:
        keep_a, keep_b = keep_b, keep_a
    first_k = turned(jnp.where(inner == 0, keep_a[:half], keep_a[half:]))
    second_k = turned(jnp.where(inner == 0, keep_b[:half], keep_b[half:]))
    is_first = (inner == 1) if backward else (inner == 0)

    def along(i):
        return pltpu.make_async_remote_copy(
            src_ref=to_z.at[i], dst_ref=from_z.at[i], send_sem=z_s.at[i], recv_sem=z_r.at[i],
            device_id=ahead, device_id_type=pl.DeviceIdType.MESH,
        )

    returning = []
    for i in range(half):
        crossing[i].wait()

        @pl.when(jnp.logical_not(has_source))
        def _():
            from_z[i] = jnp.zeros_like(from_z[i])

        @pl.when(has_source)
        def _():
            along(i).wait_recv()

        got = flipped(from_x[i]).astype(F32)
        mine = own[i]
        first = jnp.where(is_first, mine, got)
        second = jnp.where(is_first, got, mine)
        entering = from_z[i].astype(F32)
        after = first_k[:, i : i + 1] * entering + first
        to_z[i] = (second_k[:, i : i + 1] * after + second).astype(BF16)

        @pl.when(has_ahead)
        def _():
            along(i).start()

        states[inner * half + i] = jnp.where(is_first, entering, after).astype(BF16)
        to_back[i] = jnp.where(is_first, after, entering).astype(BF16)
        returning.append(send(to_back.at[i], from_back.at[i], b_s.at[i], b_r.at[i], x))
    for i in range(half):
        returning[i].wait()
        states[(1 - inner) * half + i] = flipped(from_back[i])

        @pl.when(has_ahead)
        def _():
            along(i).wait_send()

    if backward:
        plane_sum_end(parts, sums, side)
        gate_copy.wait()


def plane_sum_start(parts, side, y, core):
    from_core, to_y, from_y, core_s, core_r, y_s, y_r = side
    rows = parts.shape[1]
    size = rows // CHUNKS
    cuts = [pl.ds(c * size, size) for c in range(CHUNKS)]
    first = [
        send(parts.at[pl.ds(4, 4), cut], from_core.at[:, cut], core_s.at[c], core_r.at[c], core)
        for c, cut in enumerate(cuts)
    ]
    second = []
    for c, cut in enumerate(cuts):
        first[c].wait()

        for j in range(2):
            to_y[j, cut] = parts[2 + j, cut] + from_core[2 + j, cut]
        second.append(send(to_y.at[:, cut], from_y.at[:, cut], y_s.at[c], y_r.at[c], y))
    return from_core, from_y, second


def plane_sum_end(parts, sums, side):
    from_core, from_y, second = side
    size = parts.shape[1] // CHUNKS
    for c in range(CHUNKS):
        second[c].wait()

        def add(r, carry, c=c):
            at = pl.ds(c * size + r * STRIP, STRIP)
            for j in range(2):
                sums[j, at] = (
                    parts[j, at].astype(F32) + from_core[j, at].astype(F32)
                    + from_y[j, at].astype(F32)
                ).astype(BF16)
            return carry

        lax.fori_loop(0, size // STRIP, add, 0)


def relay(outer, backward, inputs, sequences, slots, width):
    half = sequences // 2
    dma = pltpu.SemaphoreType.DMA
    held = pltpu.VMEM((half, slots, width), BF16)
    states = jax.ShapeDtypeStruct((sequences, slots, width), BF16)
    keeps = jax.ShapeDtypeStruct((2, sequences, slots), F32)
    keep = pltpu.VMEM((sequences, 1, slots), F32)
    outs, side = [states, keeps], []
    if backward:
        rows, columns = inputs[2].shape[1:]
        outs = [states, jax.ShapeDtypeStruct((2, rows, columns), BF16)]
        outs.append(jax.ShapeDtypeStruct(inputs[3].shape, BF16))
        side = [
            pltpu.VMEM((4, rows, columns), BF16), pltpu.VMEM((2, rows, columns), BF16),
            pltpu.VMEM((2, rows, columns), BF16),
        ] + [dma((CHUNKS,))] * 4 + [dma((1,))] * 2
    return pl.pallas_call(
        functools.partial(relay_kernel, outer, backward),
        in_specs=[in_vmem()] * 3 + [in_hbm()] * (len(inputs) - 3),
        out_specs=[in_vmem()] * 2 + [in_hbm()] * (len(outs) - 2),
        out_shape=outs,
        scratch_shapes=[pltpu.VMEM((half, slots, width), F32)] + [held] * 6 + [keep] * 2
        + [dma((half,))] * 6 + [dma((1,))] * 2 + side,
        compiler_params=pltpu.CompilerParams(
            collective_id=7 if backward else 6, has_side_effects=True,
            vmem_limit_bytes=VMEM_LIMIT,
        ),
    )(*inputs)


def middle_kernel(
    parts, tok, gain, extra, hidden, mid, extra_all, from_core, to_y, from_y, normed,
    core_s, core_r, y_s, y_r, local_sem, gx_s, gx_r, gy_s, gy_r, gd_s, gd_r,
    ex_s, ex_r, ed_s, ed_r, extra_sem, gc_s, gc_r, ec_s, ec_r,
):
    rows = tok.shape[0]
    size = rows // CHUNKS
    x, y, core = near_partners()
    pl.semaphore_wait(greet([x, y, core]), 3)
    cuts = [pl.ds(c * size, size) for c in range(CHUNKS)]
    first = [
        send(parts.at[pl.ds(2, 2), cut], from_core.at[:, cut], core_s.at[c], core_r.at[c], core)
        for c, cut in enumerate(cuts)
    ]
    second = []
    for c, cut in enumerate(cuts):
        first[c].wait()

        to_y[cut] = parts[1, cut] + from_core[1, cut]
        second.append(send(to_y.at[cut], from_y.at[cut], y_s.at[c], y_r.at[c], y))
    rest = []
    for j in range(4):
        copy = pltpu.make_async_copy(extra.at[j], extra_all.at[2 * j], extra_sem.at[j])
        copy.start()
        rest.append(copy)
    extra_x = [
        send(extra.at[0, cut], extra_all.at[1, cut], ex_s.at[c], ex_r.at[c], x)
        for c, cut in enumerate(cuts)
    ]
    over_x, over_y, diagonal = [], [], []
    for c in range(CHUNKS + 2):
        if c < CHUNKS:
            cut = cuts[c]
            second[c].wait()

            def norm(r, carry, c=c):
                at = pl.ds(c * size + r * STRIP, STRIP)
                total = tok[at].astype(F32) + (
                    (parts[0, at].astype(F32) + from_core[0, at].astype(F32))
                    + from_y[at].astype(F32)
                )
                hidden[at] = total
                normed[at] = (total * rms_scale(total) * gain[...]).astype(BF16)
                return carry

            lax.fori_loop(0, size // STRIP, norm, 0)
            over_y.append(send(normed.at[cut], mid.at[2, cut], gy_s.at[c], gy_r.at[c], y))
            over_x.append(send(normed.at[cut], mid.at[1, cut], gx_s.at[c], gx_r.at[c], x))
            rest.append(send(normed.at[cut], mid.at[4, cut], gc_s.at[0, c], gc_r.at[0, c], core))
            own = pltpu.make_async_copy(normed.at[cut], mid.at[0, cut], local_sem.at[c])
            own.start()
            rest.append(own)
        if c >= 2:
            at, cut = c - 2, cuts[c - 2]
            over_y[at].wait()
            diagonal.append(send(mid.at[2, cut], mid.at[3, cut], gd_s.at[at], gd_r.at[at], x))
            rest.append(send(mid.at[2, cut], mid.at[6, cut], gc_s.at[2, at], gc_r.at[2, at], core))
    extra_d = []
    for c, cut in enumerate(cuts):
        extra_x[c].wait()
        extra_d.append(
            send(extra_all.at[1, cut], extra_all.at[3, cut], ed_s.at[c], ed_r.at[c], y)
        )
        over_x[c].wait()
        rest.append(send(mid.at[1, cut], mid.at[5, cut], gc_s.at[1, c], gc_r.at[1, c], core))
    rest.append(send(extra_all.at[1], extra_all.at[5], ec_s.at[0], ec_r.at[0], core))
    for c, cut in enumerate(cuts):
        diagonal[c].wait()
        rest.append(send(mid.at[3, cut], mid.at[7, cut], gc_s.at[3, c], gc_r.at[3, c], core))
    for copy in extra_d:
        copy.wait()
    rest.append(send(extra_all.at[3], extra_all.at[7], ec_s.at[1], ec_r.at[1], core))
    for copy in rest:
        copy.wait()


def middle(parts, tok, gain, extra):
    rows, width = tok.shape
    dma = pltpu.SemaphoreType.DMA
    buffer = pltpu.VMEM((rows, width), BF16)
    return pl.pallas_call(
        middle_kernel,
        in_specs=[in_vmem()] * 4,
        out_specs=[in_vmem(), in_hbm(), in_hbm()],
        out_shape=[
            jax.ShapeDtypeStruct((rows, width), F32),
            jax.ShapeDtypeStruct((8, rows, width), BF16),
            jax.ShapeDtypeStruct((8, rows, width), BF16),
        ],
        scratch_shapes=[pltpu.VMEM((2, rows, width), BF16), buffer, buffer, buffer]
        + [dma((CHUNKS,))] * 15
        + [dma((4,))]
        + [dma((4, CHUNKS))] * 2
        + [dma((2,))] * 2,
        compiler_params=pltpu.CompilerParams(
            collective_id=2, has_side_effects=True, vmem_limit_bytes=VMEM_LIMIT
        ),
    )(parts, tok, gain, extra)


def middle_back_kernel(
    parts, hidden, grad_out, gain, grad_hidden, gain_grad, attn,
    from_core, to_x, from_x, to_y, from_y, rounded,
    core_s, core_r, x_s, x_r, y_s, y_r, local_sem, gy_s, gy_r, gc_s, gc_r,
):
    rows, width = hidden.shape
    size = rows // CHUNKS
    x, y, core = near_partners()
    pl.semaphore_wait(greet([x, y, core]), 3)
    cuts = [pl.ds(c * size, size) for c in range(CHUNKS)]
    first = [
        send(parts.at[pl.ds(4, 4), cut], from_core.at[:, cut], core_s.at[c], core_r.at[c], core)
        for c, cut in enumerate(cuts)
    ]
    second, third = [], []
    for c, cut in enumerate(cuts):
        first[c].wait()

        for j in range(2):
            to_x[j, cut] = parts[2 * j + 1, cut] + from_core[2 * j + 1, cut]
        second.append(send(to_x.at[:, cut], from_x.at[:, cut], x_s.at[c], x_r.at[c], x))
    gain_grad[...] = jnp.zeros_like(gain_grad)
    pending, over_y = [], []
    for step in range(CHUNKS + 2):
        if step < CHUNKS:
            c, cut = step, cuts[step]
            second[c].wait()

            def add_x(r, carry, c=c):
                at = pl.ds(c * size + r * STRIP, STRIP)
                to_y[at] = (
                    parts[2, at].astype(F32) + from_core[2, at].astype(F32)
                    + from_x[1, at].astype(F32)
                ).astype(BF16)
                return carry

            lax.fori_loop(0, size // STRIP, add_x, 0)
            third.append(send(to_y.at[cut], from_y.at[cut], y_s.at[c], y_r.at[c], y))
        if 1 <= step <= CHUNKS:
            c, cut = step - 1, cuts[step - 1]
            third[c].wait()

            def back(r, carry, c=c):
                at = pl.ds(c * size + r * STRIP, STRIP)
                grad_mid = (
                    (parts[0, at].astype(F32) + from_core[0, at].astype(F32))
                    + from_x[0, at].astype(F32)
                ) + from_y[at].astype(F32)
                value = hidden[at]
                scale = rms_scale(value)
                unit = value * scale
                gain_grad[...] += jnp.sum(grad_mid * unit, axis=0, keepdims=True)
                scaled = grad_mid * gain[...]
                total = grad_out[at] + scale * (
                    scaled - unit * jnp.mean(scaled * unit, axis=1, keepdims=True)
                )
                grad_hidden[at] = total
                rounded[at] = total.astype(BF16)
                return carry

            lax.fori_loop(0, size // STRIP, back, 0)
            over_y.append(send(rounded.at[cut], attn.at[1, cut], gy_s.at[c], gy_r.at[c], y))
            pending.append(
                send(rounded.at[cut], attn.at[2, cut], gc_s.at[0, c], gc_r.at[0, c], core)
            )
            own = pltpu.make_async_copy(rounded.at[cut], attn.at[0, cut], local_sem.at[c])
            own.start()
            pending.append(own)
        if step >= 2:
            c, cut = step - 2, cuts[step - 2]
            over_y[c].wait()
            pending.append(
                send(attn.at[1, cut], attn.at[3, cut], gc_s.at[1, c], gc_r.at[1, c], core)
            )
    for copy in pending:
        copy.wait()


def middle_back(parts, hidden, grad_out, gain):
    rows, width = hidden.shape
    dma = pltpu.SemaphoreType.DMA

    def buffer(*lead):
        return pltpu.VMEM(lead + (rows, width), BF16)

    return pl.pallas_call(
        middle_back_kernel,
        in_specs=[in_vmem()] * 4,
        out_specs=[in_vmem(), in_vmem(), in_hbm()],
        out_shape=[
            jax.ShapeDtypeStruct((rows, width), F32),
            jax.ShapeDtypeStruct((1, width), F32),
            jax.ShapeDtypeStruct((4, rows, width), BF16),
        ],
        scratch_shapes=[buffer(4), buffer(2), buffer(2), buffer(), buffer(), buffer()]
        + [dma((CHUNKS,))] * 9
        + [dma((2, CHUNKS))] * 2,
        compiler_params=pltpu.CompilerParams(
            collective_id=3, has_side_effects=True, vmem_limit_bytes=VMEM_LIMIT
        ),
    )(parts, hidden, grad_out, gain)


def final_kernel(
    outer, dp, mats, gates, feed_sums, pre_hbm, gate_hbm, kqv_hbm, g_hbm, grad_rank, w_rank, tok,
    base, gain, small, *refs,
):
    out, tokens_grad, out_small, feed_got, refs = refs[0], refs[1], refs[2], refs[3], refs[4:]
    (
        grad_pre, grad_gate, w_kqv, w_g,
        from_x, from_below, from_above, total, parts, from_core, to_y, from_y, gain_grad,
        to_all, from_all,
        load, x_s, x_r, up_s, up_r, down_s, down_r, core_s, core_r, y_s, y_r, feed_s, feed_r,
        all_s, all_r,
    ) = refs
    rows, width = tok.shape
    size = rows // CHUNKS
    high = total.shape[2]
    seq = 2 * outer
    at = lax.axis_index("seq")
    me = lax.axis_index("dp") * seq + at
    z = at // 2
    x, y, core = near_partners()
    above, below = {"seq": at + 2}, {"seq": at - 2}
    has_above, has_below = z < outer - 1, z > 0
    greet_everyone(seq, dp)

    def block_of(i):
        ups = outer - 1 - z
        up_at = jnp.where(z < outer // 2, i, i - z)
        down_at = jnp.where(z < outer // 2, i - ups, i)
        is_up = (up_at >= 0) & (up_at < ups)
        block = jnp.where(is_up, outer - 1 - up_at, down_at)
        return jnp.where(i == outer - 1, z, block)

    def across(m, b):
        return pltpu.make_async_remote_copy(
            src_ref=mats.at[m, 1, b], dst_ref=from_x.at[m, b], send_sem=x_s.at[m, b],
            recv_sem=x_r.at[m, b], device_id=x, device_id_type=pl.DeviceIdType.MESH,
        )

    def up(m, b):
        return pltpu.make_async_remote_copy(
            src_ref=total.at[m, b], dst_ref=from_below.at[m, b], send_sem=up_s.at[m, b],
            recv_sem=up_r.at[m, b], device_id=above, device_id_type=pl.DeviceIdType.MESH,
        )

    def down(m, b):
        return pltpu.make_async_remote_copy(
            src_ref=total.at[m, b], dst_ref=from_above.at[m, b], send_sem=down_s.at[m, b],
            recv_sem=down_r.at[m, b], device_id=below, device_id_type=pl.DeviceIdType.MESH,
        )

    def start_x(i, carry):
        for m in range(3):
            across(m, block_of(i)).start()
        return carry

    lax.fori_loop(0, outer, start_x, 0)
    last_x = send(feed_sums.at[1], feed_got, feed_s.at[0], feed_r.at[0], x)
    operands = [
        pltpu.make_async_copy(src, dst, load.at[4 + n])
        for n, (src, dst) in enumerate(
            [(pre_hbm, grad_pre), (gate_hbm, grad_gate), (kqv_hbm, w_kqv), (g_hbm, w_g)]
        )
    ]
    loads = [
        pltpu.make_async_copy(mats.at[m, 0] if m < 3 else gates, total.at[m], load.at[m])
        for m in range(4)
    ]
    for copy in operands + loads:
        copy.start()
    for copy in operands:
        copy.wait()

    def grad_in(g):
        some = pl.ds(g * rows, rows)
        parts[g] = (
            mm(grad_pre[some], w_kqv[...], 1, 0)
            + (mm(grad_gate[some], w_g[...], 1, 0) + mm(grad_rank[some], w_rank[...], 1, 1))
        ).astype(BF16)

    grad_in(3)
    first = send(parts.at[3], from_core.at[1], core_s.at[1], core_r.at[1], core)
    grad_in(1)
    first.wait()

    to_y[...] = parts[1] + from_core[1]

    def over_y():
        return pltpu.make_async_remote_copy(
            src_ref=to_y, dst_ref=from_y, send_sem=y_s.at[0], recv_sem=y_r.at[0], device_id=y,
            device_id_type=pl.DeviceIdType.MESH,
        )

    over_y().start()
    grad_in(2)
    first = send(parts.at[2], from_core.at[0], core_s.at[0], core_r.at[0], core)
    grad_in(0)
    first.wait()
    gain_grad[...] = jnp.zeros_like(gain_grad)
    for copy in loads:
        copy.wait()

    def back(c):
        def strip_back(r, carry):
            strip = pl.ds(pl.multiple_of(c * size + r * STRIP, STRIP), STRIP)
            grad = (
                parts[0, strip].astype(F32) + from_core[0, strip].astype(F32)
            ) + from_y[strip].astype(F32)
            value = tok[strip].astype(F32)
            scale = rms_scale(value)
            unit = value * scale
            gain_grad[...] += jnp.sum(grad * unit, axis=0, keepdims=True)
            scaled = grad * gain[...]
            tokens_grad[strip] = base[strip] + scale * (
                scaled - unit * jnp.mean(scaled * unit, axis=1, keepdims=True)
            )
            return carry

        lax.fori_loop(0, size // STRIP, strip_back, 0)

    def add_into(m, b, other):
        total[m, b] = total[m, b] + other[m, b]

    def reduce_block(i, carry):
        b = block_of(i)
        for m in (3, 0, 1, 2):
            if m < 3:
                across(m, b).wait()
                add_into(m, b, from_x)

            @pl.when(b > z)
            def _():
                @pl.when(has_below)
                def _():
                    up(m, b).wait_recv()
                    add_into(m, b, from_below)

                up(m, b).start()

            @pl.when(b < z)
            def _():
                @pl.when(has_above)
                def _():
                    down(m, b).wait_recv()
                    add_into(m, b, from_above)

                down(m, b).start()

            if m < 3:
                turn = 2 * (3 * (i - 1) + m)
                if m == 0:
                    @pl.when(i == 1)
                    def _():
                        over_y().wait()

                @pl.when((turn >= 0) & (turn < CHUNKS))
                def _():
                    back(turn)
                    back(turn + 1)

        return carry

    lax.fori_loop(0, outer - 1, reduce_block, 0)
    devices = seq * dp
    each = width // devices
    row, col = grid_index(devices, width)
    spread = jnp.where(col // each == row, gain_grad[...], 0.0)
    picked_row, picked_col = grid_index(width, 128)
    gathered = mm_exact(spread, ((picked_row % each) == picked_col).astype(F32), 1, 0)
    height = small.shape[1]
    to_all[:, :height] = small[...]
    to_all[:, height:] = jnp.broadcast_to(
        gathered.reshape(devices, 1, 128), (devices, to_all.shape[1] - height, 128)
    )

    def push(r, where):
        return pltpu.make_async_remote_copy(
            src_ref=to_all.at[jnp.bitwise_xor(me, r)], dst_ref=from_all.at[r],
            send_sem=all_s.at[r], recv_sem=all_r.at[r], device_id=where,
            device_id_type=pl.DeviceIdType.MESH,
        )

    everyone(seq, dp, lambda r, where: push(r, where).start())
    out_small[...] = to_all[me]

    def add_small(r, where):
        push(r, where).wait()
        out_small[...] += from_all[r]

    everyone(seq, dp, add_small)
    lax.fori_loop(outer - 1, outer, reduce_block, 0)
    for m in range(4):
        out[m] = total[m, z].astype(F32)

        @pl.when(has_below)
        def _():
            up(m, z).wait_recv()
            out[m] += from_below[m, z].astype(F32)

        @pl.when(has_above)
        def _():
            down(m, z).wait_recv()
            out[m] += from_above[m, z].astype(F32)

    def sent(b, carry):
        for m in range(4):
            @pl.when(b > z)
            def _():
                up(m, b).wait_send()

            @pl.when(b < z)
            def _():
                down(m, b).wait_send()

        return carry

    lax.fori_loop(0, outer, sent, 0)
    last_x.wait()


def finish(outer, dp, mats, gates, feed_sums, operands, rest, small):
    rows, width = rest[-3].shape
    high = mats.shape[3]
    devices = 2 * outer * dp
    dma = pltpu.SemaphoreType.DMA
    blocks = pltpu.VMEM((4, outer, high, width), BF16)
    buffer = pltpu.VMEM((rows, width), BF16)
    payload = (small.shape[1] + 8, 128)
    return pl.pallas_call(
        functools.partial(final_kernel, outer, dp),
        in_specs=[in_hbm()] * (3 + len(operands)) + [in_vmem()] * (len(rest) + 1),
        out_specs=[in_vmem()] * 3 + [in_hbm()],
        out_shape=[
            jax.ShapeDtypeStruct((4, high, width), F32),
            jax.ShapeDtypeStruct((rows, width), F32),
            jax.ShapeDtypeStruct(payload, F32),
            jax.ShapeDtypeStruct((rows, width), BF16),
        ],
        scratch_shapes=[pltpu.VMEM(x.shape, BF16) for x in operands]
        + [pltpu.VMEM((3, outer, high, width), BF16)]
        + [blocks] * 3
        + [
            pltpu.VMEM((4, rows, width), BF16), pltpu.VMEM((2, rows, width), BF16), buffer,
            buffer, pltpu.VMEM((1, width), F32),
            pltpu.VMEM((devices,) + payload, F32), pltpu.VMEM((devices,) + payload, F32),
            dma((8,)),
        ]
        + [dma((4, outer))] * 6
        + [dma((2,))] * 2
        + [dma((1,))] * 4
        + [dma((devices,))] * 2,
        compiler_params=pltpu.CompilerParams(
            collective_id=4, has_side_effects=True, vmem_limit_bytes=60 * 1024 * 1024
        ),
    )(mats, gates, feed_sums, *operands, *rest, small)


class Lanes:
    def __init__(self):
        self.seq = lax.axis_size("seq")
        self.dp = lax.axis_size("dp")
        self.outer = self.seq // 2
        self.at = lax.axis_index("seq")
        self.d = lax.axis_index("dp")
        self.inner_at = lax.rem(self.at, 2)
        self.outer_at = self.at // 2
        self.groups = [[2 * k + i for k in range(self.outer)] for i in range(2)]

    def swap_inner(self, x):
        return lax.ppermute(x, "seq", [(i, i ^ 1) for i in range(self.seq)])

    def gather_outer(self, x):
        return lax.all_gather(x, "seq", axis=0, tiled=True, axis_index_groups=self.groups)

    def scatter_outer(self, x):
        return lax.psum_scatter(
            x, "seq", scatter_dimension=0, tiled=True, axis_index_groups=self.groups
        )

    def swap_dp(self, x, bit):
        return lax.ppermute(x, "dp", [(i, i ^ bit) for i in range(self.dp)])

    def swap_seq(self, x, bit):
        return lax.ppermute(x, "seq", [(i, i ^ bit) for i in range(self.seq)])

    def exchange_heads(self, blocks):
        got = [lax.dynamic_index_in_dim(blocks, self.d, 0, keepdims=False)]
        for r in range(1, self.dp):
            part = lax.dynamic_index_in_dim(
                blocks, jnp.bitwise_xor(self.d, r), 0, keepdims=False
            )
            got.append(self.swap_dp(part, r))
        bit = 1
        while bit < self.dp:
            is_set = (self.d // bit) % 2 == 1
            got = [jnp.where(is_set, got[i ^ bit], got[i]) for i in range(self.dp)]
            bit *= 2
        return jnp.stack(got)

    def pick(self, natural, axis):
        first = lax.index_in_dim(natural, 0, axis, keepdims=False)
        second = lax.index_in_dim(natural, 1, axis, keepdims=False)
        even = self.inner_at == 0
        return jnp.where(even, first, second), jnp.where(even, second, first)


def swap_halves(x, parts):
    size = x.shape[-1] // (2 * parts)
    pieces = [x[..., i * size : (i + 1) * size] for i in range(2 * parts)]
    order = [i ^ 1 for i in range(2 * parts)]
    return jnp.concatenate([pieces[i] for i in order], axis=-1)


def per_device(
    tokens, lengths, cotangent, mixer_gain, feed_gain, head_gain, w_query, w_key, w_value,
    w_gate, w_out, rank_down, rank_up, rank_bias, w_act, w_lin, w_down,
):
    lanes = Lanes()
    seq_count, piece, width = tokens.shape
    rows = seq_count * piece
    sequences = lanes.dp * seq_count
    all_rows = lanes.dp * rows
    head_width = width // HEADS
    half_width = head_width // 2
    rank = rank_down.shape[1]
    devices = lanes.dp * lanes.seq

    counts = lengths.astype(F32)
    high = jnp.floor(counts / 256.0)
    small_parts = [
        mixer_gain, feed_gain, head_gain, rank_down.reshape(-1), rank_up.reshape(-1),
        rank_bias, high.astype(BF16), (counts - 256.0 * high).astype(BF16),
    ]
    sizes = [p.shape[0] for p in small_parts]
    used = sum(sizes)
    padded = -(-used // 2048) * 2048
    small = jnp.concatenate(small_parts + [jnp.zeros((padded - used,), BF16)])
    own_tokens = tokens.reshape(rows, width)
    position = (lanes.at * piece + jnp.arange(piece)).astype(F32)
    alive_own = (position[None, :] < counts[:, None]).astype(F32).reshape(rows, 1)
    grad_out = cotangent.reshape(rows, width).astype(F32) * alive_own
    w_kqv, out_mine, plane_tokens, grad_feed, smalls = gather_all(
        lanes.outer, lanes.dp, [w_key, w_query, w_value], [own_tokens, grad_out.astype(BF16)],
        small.reshape(-1, 128), w_out,
    )
    w_kqv = w_kqv.reshape(3 * head_width, width)
    out_rows = w_out.shape[0]
    out_own, out_other = lanes.pick(
        out_mine.reshape(lanes.dp, out_rows, lanes.outer, 2, -1), 3
    )
    out_mine = jnp.concatenate(
        [
            out_own.reshape(lanes.dp, out_rows, half_width),
            out_other.reshape(lanes.dp, out_rows, half_width),
        ],
        axis=2,
    )
    gate_and_out = lanes.gather_outer(
        jnp.concatenate([w_gate, out_mine.reshape(out_rows, width)], axis=0)
    )
    smalls = smalls.reshape(devices, padded)
    cuts, offset = [], 0
    for size in sizes:
        cuts.append(smalls[:, offset : offset + size])
        offset += size
    mixer_full = cuts[0].reshape(1, width).astype(F32)
    feed_full = cuts[1].reshape(1, width).astype(F32)
    head_natural = cuts[2].reshape(lanes.outer, 2, half_width // lanes.outer)
    head_own, head_other = lanes.pick(head_natural, 1)
    head_full = jnp.concatenate(
        [head_own.reshape(1, half_width), head_other.reshape(1, half_width)], axis=1
    ).astype(F32)
    down_full = cuts[3].reshape(width, rank)
    up_mine = lax.dynamic_index_in_dim(
        cuts[4].reshape(lanes.dp, SLOTS, rank), lanes.d, 0, keepdims=False
    )
    bias_mine = lax.dynamic_index_in_dim(
        cuts[5].reshape(lanes.dp, 1, SLOTS), lanes.d, 0, keepdims=False
    ).astype(F32)
    all_lengths = cuts[6].astype(F32) * 256.0 + cuts[7].astype(F32)
    all_lengths = all_lengths.reshape(lanes.dp, lanes.seq, seq_count)[:, 0]

    group_lengths = jnp.concatenate(
        [
            lax.dynamic_index_in_dim(
                all_lengths, jnp.bitwise_xor(lanes.d, r), 0, keepdims=False
            )
            for r in (0, 2, 1, 3)
        ]
    )
    alive = (position[None, :] < group_lengths[:, None]).astype(F32).reshape(all_rows, 1)

    sources = plane_tokens.reshape(all_rows, width).astype(F32)
    normed_in = (sources * rms_scale(sources) * mixer_full).astype(BF16)

    pre = contract_last(normed_in, w_kqv)
    low_rank = mm(normed_in, down_full, 1, 0).astype(BF16)
    gate_logit = contract_last(low_rank, up_mine) + bias_mine
    log_decay = jax.nn.log_sigmoid(gate_logit) / GATE_NORM * alive
    writes = -jnp.expm1(log_decay)

    def seqs(x):
        return x.reshape(sequences, piece, x.shape[1])

    def flat(x):
        return x.reshape(all_rows, x.shape[2])

    is_value = jnp.arange(3 * head_width) >= 2 * head_width
    feats = seqs(jnp.where(is_value, pre, pre * jax.nn.sigmoid(pre)).astype(BF16))
    pre = seqs(pre)
    decays, writes = seqs(log_decay), seqs(writes)

    def shaped(like_rows, columns, kind):
        return jax.ShapeDtypeStruct((sequences, like_rows, columns), kind)

    gate_and_out, feats = lax.optimization_barrier((gate_and_out, feats))
    keys, queries, values = (feats, 0), (feats, 1), (feats, 2)
    state_in, keeps = relay(
        lanes.outer, False, [feats, decays, writes], sequences, SLOTS, 2 * head_width
    )
    feed = jnp.stack([w_down, w_act, w_lin])
    feed, state_in, gate_and_out = lax.optimization_barrier((feed, state_in, gate_and_out))
    feed = lax.all_gather(
        feed, "seq", axis=1, tiled=True, axis_index_groups=lanes.groups
    )
    gate_and_out = gate_and_out.reshape(lanes.outer, 2, out_rows, width)
    gate_own, out_own = gate_and_out[:, 0], gate_and_out[:, 1]
    gate_other = lanes.swap_inner(gate_own)
    w_g = jnp.concatenate([gate_own, gate_other], axis=0).reshape(head_width, width)
    gates = seqs(contract_last(normed_in, w_g))
    out_own = out_own.reshape(lanes.outer, lanes.dp, out_rows, head_width)
    out_other = swap_halves(lanes.swap_inner(out_own), 1)
    even = lanes.inner_at == 0
    natural = jnp.stack(
        [jnp.where(even, out_own, out_other), jnp.where(even, out_other, out_own)], axis=2
    )
    out_full = natural.transpose(1, 0, 2, 3, 4).reshape(width, head_width)
    mixed, slot_out, attend = per_sequence(
        forward_kernel,
        [queries, keys, values, gates, decays, writes, state_in],
        [
            shaped(piece, head_width, BF16),
            shaped(piece, head_width, F32),
            shaped(piece, SLOTS, F32),
        ],
        shared=[head_full],
    )
    mixed_flat = flat(mixed)
    parts = contract_last(mixed_flat, out_full).astype(BF16)
    hidden, normed_mid, grad_feed = middle(
        parts.reshape(4, rows, width), own_tokens, feed_full, grad_feed
    )
    normed_mid = normed_mid.reshape(8 * rows, width)
    grad_feed = grad_feed.reshape(8 * rows, width)

    units = feed.shape[1]
    product, grad_gate, grad_lin = feed_tiles(
        feed_kernel, [normed_mid, grad_feed], feed, [units] * 3
    )
    feed_grads = jnp.stack(
        [
            contract_first(product, grad_feed).astype(BF16),
            contract_first(grad_gate, normed_mid).astype(BF16),
            contract_first(grad_lin, normed_mid).astype(BF16),
        ]
    )
    product, grad_gate, grad_lin, feed_grads = lax.optimization_barrier(
        (product, grad_gate, grad_lin, feed_grads)
    )
    feed_grads = lax.psum_scatter(
        feed_grads, "seq", scatter_dimension=1, tiled=True, axis_index_groups=lanes.groups
    )
    feed_parts, mid_parts = feed_tiles(
        feed_back_kernel, [product, grad_gate, grad_lin], feed, [width] * 2
    )
    grad_hidden, feed_gain_part, grad_attn = middle_back(
        mid_parts.reshape(8, rows, width), hidden, grad_out, feed_full
    )
    grad_attn = grad_attn.reshape(all_rows, width)
    feed_parts, grad_attn = lax.optimization_barrier((feed_parts, grad_attn))

    grad_mixed = mm(grad_attn, out_full, 1, 0)
    grad_gate_pre, grad_slot, grad_scores, adjoint, head_parts = per_sequence(
        back_first_kernel,
        [seqs(grad_mixed), gates, slot_out, attend, queries, values, decays, writes, state_in],
        [
            shaped(piece, head_width, BF16),
            shaped(piece, head_width, BF16),
            shaped(piece, SLOTS, F32),
            shaped(SLOTS, 2 * head_width, F32),
            shaped(1, head_width, F32),
        ],
        shared=[head_full],
    )
    grad_gate_flat = flat(grad_gate_pre)
    out_grad = contract_first(grad_attn, mixed_flat).astype(BF16)
    out_grad = out_grad.reshape(lanes.dp, lanes.outer, 2, out_rows, head_width)
    own_part, other_part = lanes.pick(out_grad, 2)
    got = swap_halves(lanes.swap_inner(other_part), 1)
    out_sum = (own_part.astype(F32) + got.astype(F32)).astype(BF16).transpose(1, 0, 2, 3)
    gate_grad = contract_first(grad_gate_flat, normed_in).astype(BF16)
    adjoint, out_sum, gate_grad, feed_parts = lax.optimization_barrier(
        (adjoint, out_sum, gate_grad, feed_parts)
    )
    adjoint_in, feed_sums, gate_got = relay(
        lanes.outer, True,
        [adjoint, keeps, feed_parts.reshape(8, rows, width), gate_grad[half_width:]], sequences,
        SLOTS, 2 * head_width,
    )
    gate_grad, out_sum, adjoint_in, feed_grads = lax.optimization_barrier(
        (gate_grad, out_sum, adjoint_in, feed_grads)
    )
    out_mine = lanes.scatter_outer(out_sum.reshape(-1, head_width))
    grad_pre, grad_logit = per_sequence(
        back_second_kernel,
        [
            grad_slot, grad_scores, attend, queries, keys, values, decays, writes,
            state_in, adjoint_in, (pre, 1), (pre, 0), seqs(gate_logit), seqs(alive),
        ],
        [shaped(piece, 3 * head_width, BF16), shaped(piece, SLOTS, BF16)],
    )
    grad_pre, out_mine = lax.optimization_barrier((flat(grad_pre), out_mine))
    grad_logit = flat(grad_logit)
    bias_part = jnp.sum(grad_logit.astype(F32), axis=0)
    up_part = contract_first(grad_logit, low_rank)
    grad_rank = mm(grad_logit, up_mine, 1, 0).astype(BF16)
    down_part = contract_first(normed_in, grad_rank)

    mixer_grads = contract_first(grad_pre, normed_in).astype(BF16)
    mixer_grads = mixer_grads.reshape(3, 2, lanes.outer, -1, width)

    head_part = jnp.sum(head_parts, axis=(0, 1)).reshape(2, lanes.outer, -1)
    low_half, high_half = lanes.pick(head_part, 0)
    head_part = jnp.stack([low_half, high_half], axis=1)
    mine = (jnp.arange(lanes.dp) == lanes.d).astype(F32)
    up_all = mine[:, None] * up_part.reshape(1, -1)
    bias_all = mine[:, None] * bias_part.reshape(1, -1)
    parts = [
        feed_gain_part.reshape(devices, -1),
        head_part.reshape(devices, -1),
        down_part.reshape(devices, -1),
        up_all.reshape(devices, -1),
        bias_all.reshape(devices, -1),
    ]
    sizes = [p.shape[1] for p in parts]
    padded = -(-sum(sizes) // 1024) * 1024
    parts.append(jnp.zeros((devices, padded - sum(sizes)), F32))
    small_parts = jnp.concatenate(parts, axis=1).reshape(devices, -1, 128)
    gate_sum = (gate_grad[:half_width].astype(F32) + gate_got.astype(F32)).astype(BF16)
    out_mine = out_mine.reshape(lanes.dp, out_rows, head_width)
    out_mine = lanes.exchange_heads(out_mine).transpose(1, 0, 2)
    out_mine = out_mine.reshape(out_rows, lanes.dp, 2, lanes.outer, -1)
    low_half, high_half = lanes.pick(out_mine, 2)
    w_out_grad = jnp.stack([low_half, high_half], axis=3).reshape(out_rows, width).astype(F32)
    weight_grads, tokens_grad, reduced, feed_got = finish(
        lanes.outer, lanes.dp, mixer_grads,
        gate_sum.reshape(lanes.outer, -1, width), feed_sums,
        [grad_pre, grad_gate_flat, w_kqv, w_g],
        [grad_rank, down_full, own_tokens, grad_hidden, mixer_full],
        small_parts,
    )
    w_key_grad, w_query_grad, w_value_grad, w_gate_grad = [weight_grads[m] for m in range(4)]
    tokens_grad = tokens_grad.reshape(seq_count, piece, width)
    feed_sum = feed_sums[0].astype(F32) + feed_got.astype(F32)
    block_out = (alive_own * (hidden + feed_sum)).astype(BF16)
    mixer_gain_grad = reduced[padded // 128, : width // devices]
    reduced = reduced.reshape(-1)
    smalls, offset = [], 0
    for size in sizes:
        smalls.append(reduced[offset : offset + size])
        offset += size
    return (
        block_out.reshape(seq_count, piece, width),
        tokens_grad,
        mixer_gain_grad,
        smalls[0],
        smalls[1],
        w_query_grad,
        w_key_grad,
        w_value_grad,
        w_gate_grad,
        w_out_grad,
        smalls[2].reshape(-1, rank),
        smalls[3].reshape(-1, rank),
        smalls[4],
        feed_grads[1].astype(F32),
        feed_grads[2].astype(F32),
        feed_grads[0].astype(F32),
    )


def solution(mesh):
    vector = P(("dp", "seq"))
    matrix = P(("dp", "seq"), None)
    stream = P("dp", "seq", None)
    return jax.shard_map(
        per_device,
        mesh=mesh,
        in_specs=(
            stream, P("dp"), stream, vector, vector, vector, matrix, matrix, matrix, matrix,
            matrix, matrix, matrix, vector, matrix, matrix, matrix,
        ),
        out_specs=(
            stream, stream, vector, vector, vector, matrix, matrix, matrix, matrix, matrix,
            matrix, matrix, vector, matrix, matrix, matrix,
        ),
        check_vma=False,
    )
```

```python
import functools

import jax
import jax.numpy as jnp
from jax import lax
from jax.experimental import pallas as pl
from jax.experimental.pallas import tpu as pltpu
from jax.sharding import PartitionSpec as P

HEADS = 4
SLOTS = 64
EPS = 1e-06
GATE_NORM = 8.0
F32 = jnp.float32
BF16 = jnp.bfloat16
LEAF = 8
VMEM_LIMIT = 48 * 1024 * 1024


def mm(a, b, ca, cb):
    return lax.dot_general(
        a.astype(BF16), b.astype(BF16), (((ca,), (cb,)), ((), ())), preferred_element_type=F32
    )


def mm_exact(a, b, ca, cb):
    return lax.dot_general(
        a,
        b,
        (((ca,), (cb,)), ((), ())),
        precision=lax.Precision.HIGHEST,
        preferred_element_type=F32,
    )


def two_parts(x):
    high = x.astype(BF16)
    return high, (x - high.astype(F32)).astype(BF16)


def mm_left(exact, b, ca, cb):
    high, low = two_parts(b)
    return mm(exact, high, ca, cb) + mm(exact, low, ca, cb)


def mm_right(a, exact, ca, cb):
    high, low = two_parts(a)
    return mm(high, exact, ca, cb) + mm(low, exact, ca, cb)


def mm_fine(a, b, ca, cb):
    a_high, a_low = two_parts(a)
    b_high, b_low = two_parts(b)
    return mm(a_high, b_high, ca, cb) + (mm(a_high, b_low, ca, cb) + mm(a_low, b_high, ca, cb))


def contract_last(a, b):
    return mm(a, b, 1, 1)


def contract_first(a, b):
    return mm(a, b, 0, 0)


def swish_slope(v):
    sigma = jax.nn.sigmoid(v)
    return sigma * (1.0 + v * (1.0 - sigma))


def rms_scale(v):
    return lax.rsqrt(jnp.mean(v * v, axis=-1, keepdims=True) + EPS)


def grid_index(rows, cols):
    return (
        lax.broadcasted_iota(jnp.int32, (rows, cols), 0),
        lax.broadcasted_iota(jnp.int32, (rows, cols), 1),
    )


def running_sum(decay):
    length = decay.shape[0]
    row, col = grid_index(length, length)
    return mm_exact((row >= col).astype(F32), decay, 1, 0)


def levels(length):
    found = []
    half = length // 2
    while half >= LEAF:
        found.append(half)
        half //= 2
    return found


def level_factors(running, writes, half):
    length, slots = running.shape
    pairs = running.reshape(length // (2 * half), 2 * half, slots)
    anchor = jnp.broadcast_to(pairs[:, half - 1 : half, :], pairs.shape).reshape(length, slots)
    near = jnp.exp(-jnp.abs(running - anchor))
    row, _ = grid_index(length, slots)
    right = (row % (2 * half)) >= half
    return jnp.where(right, near, 0.0), jnp.where(right, 0.0, near), right


def same_block(length, size):
    row, col = grid_index(length, length)
    return (row // size) == (col // size)


def leaf_selector(length):
    row, col = grid_index(length, LEAF)
    return ((row % LEAF) == col).astype(F32)


def leaf_take(square):
    length = square.shape[0]
    kept = jnp.where(same_block(length, LEAF), square, 0.0)
    return mm_exact(kept, leaf_selector(length), 1, 0)


def leaf_spread(columns):
    length = columns.shape[0]
    wide = mm_exact(columns, leaf_selector(length), 1, 1)
    return jnp.where(same_block(length, LEAF), wide, 0.0)


def leaf_row(tensor, at):
    length, width = tensor.shape
    blocks = tensor.reshape(length // LEAF, LEAF, width)
    return jnp.broadcast_to(blocks[:, at : at + 1, :], blocks.shape).reshape(length, width)


def leaf_decay(running, at):
    length, slots = running.shape
    row, _ = grid_index(length, slots)
    reached = (row % LEAF) >= at
    spread = running - leaf_row(running, at)
    return jnp.where(reached, jnp.exp(jnp.where(reached, spread, 0.0)), 0.0)


def masked(square, half):
    length = square.shape[0]
    if 2 * half == length:
        return square
    return jnp.where(same_block(length, 2 * half), square, 0.0)


def read_in_chunk(square, running, writes):
    total = None
    for half in levels(running.shape[0]):
        right, left, _ = level_factors(running, writes, half)
        part = right * mm_fine(masked(square, half), left * writes, 1, 0)
        total = part if total is None else total + part
    columns = leaf_take(square)
    for at in range(LEAF):
        part = columns[:, at : at + 1] * (leaf_decay(running, at) * leaf_row(writes, at))
        total = part if total is None else total + part
    return total


def mix_in_chunk(attend, running, writes):
    total = None
    for half in levels(running.shape[0]):
        right, left, _ = level_factors(running, writes, half)
        part = masked(mm(attend * right, left * writes, 1, 1), half)
        total = part if total is None else total + part
    columns = [
        jnp.sum(
            attend * (leaf_decay(running, at) * leaf_row(writes, at)), axis=1, keepdims=True
        )
        for at in range(LEAF)
    ]
    part = leaf_spread(jnp.concatenate(columns, axis=1))
    return part if total is None else total + part


def summary(k, v, decay, writes):
    running = running_sum(decay)
    length = running.shape[0]
    last = running[length - 1 : length, :]
    fade = jnp.exp(last - running) * writes
    return jnp.concatenate([mm(fade, k, 0, 0), mm(fade, v, 0, 0)], axis=1), jnp.exp(last)


def forward_kernel(
    q_ref, k_ref, v_ref, gate_ref, decay_ref, writes_ref, state_ref, gain_ref,
    mixed_ref, out_ref, attend_ref,
):
    q, k, v = q_ref[0], k_ref[0], v_ref[0]
    writes = writes_ref[0]
    width = q.shape[1]
    scale = width ** (-0.5)
    running = running_sum(decay_ref[0])
    growth = jnp.exp(running)
    state = state_ref[0]
    dots = mm(q, k, 1, 1) * scale
    scores = growth * (mm(q, state[:, :width], 1, 1) * scale)
    scores = scores + read_in_chunk(dots, running, writes)
    top = jnp.max(scores, axis=1, keepdims=True)
    raw = jnp.exp(scores - top)
    attend = raw / jnp.sum(raw, axis=1, keepdims=True)
    mixing = mix_in_chunk(attend, running, writes)
    out = mm(attend * growth, state[:, width:], 1, 0) + mm(mixing, v, 1, 0)
    out_ref[0] = out
    attend_ref[0] = attend
    gate = gate_ref[0]
    normed = out * rms_scale(out) * gain_ref[...]
    mixed_ref[0] = (normed * (gate * jax.nn.sigmoid(gate))).astype(BF16)


def back_first_kernel(
    grad_mixed_ref, gate_ref, out_ref, attend_ref, q_ref, v_ref, decay_ref, writes_ref,
    state_ref, gain_ref,
    grad_gate_ref, grad_out_ref, grad_scores_ref, adjoint_ref, gain_grad_ref,
):
    q, v = q_ref[0], v_ref[0]
    writes = writes_ref[0]
    width = q.shape[1]
    scale = width ** (-0.5)
    grad_mixed, gate, out = grad_mixed_ref[0], gate_ref[0], out_ref[0]
    gain = gain_ref[...]
    inverse = rms_scale(out)
    normed = out * inverse
    grad_gate_ref[0] = (grad_mixed * (normed * gain) * swish_slope(gate)).astype(BF16)
    e = grad_mixed * (gate * jax.nn.sigmoid(gate))
    gain_grad_ref[0] = jnp.sum(e * normed, axis=0, keepdims=True)
    eg = e * gain
    grad_out = inverse * (eg - normed * jnp.mean(eg * normed, axis=1, keepdims=True))
    grad_out_ref[0] = grad_out.astype(BF16)
    running = running_sum(decay_ref[0])
    growth = jnp.exp(running)
    attend = attend_ref[0]
    u = growth * mm_right(grad_out, state_ref[0, :, width:], 1, 1)
    u = u + read_in_chunk(mm_right(grad_out, v, 1, 1), running, writes)
    grad_scores = attend * (u - jnp.sum(attend * u, axis=1, keepdims=True))
    grad_scores_ref[0] = grad_scores
    adjoint_ref[0, :, :width] = mm(growth * grad_scores * scale, q, 0, 0)
    adjoint_ref[0, :, width:] = mm(growth * attend, grad_out.astype(BF16), 0, 0)


def back_second_kernel(
    grad_out_ref, grad_scores_ref, attend_ref, q_ref, k_ref, v_ref, decay_ref, writes_ref,
    state_ref, adjoint_ref, q_pre_ref, k_pre_ref, logit_ref, alive_ref,
    grad_pre_ref, dlogit_ref,
):
    q, k, v, grad_out = q_ref[0], k_ref[0], v_ref[0], grad_out_ref[0]
    attend, grad_scores = attend_ref[0], grad_scores_ref[0]
    decay, writes = decay_ref[0], writes_ref[0]
    length, slots = decay.shape
    width = q.shape[1]
    scale = width ** (-0.5)
    running = running_sum(decay)
    growth = jnp.exp(running)
    keep = jnp.exp(decay)
    last = running[length - 1 : length, :]
    fade = jnp.exp(last - running)
    state, adjoint = state_ref[0], adjoint_ref[0]
    key_state, value_state = state[:, :width], state[:, width:]
    key_adjoint, value_adjoint = adjoint[:, :width], adjoint[:, width:]
    key_dots = mm(q, k, 1, 1) * scale
    value_dots = mm(grad_out, v, 1, 1)
    row, col = grid_index(length, length)

    columns_sum = jnp.zeros((length, slots), F32)
    crossing = jnp.zeros((length, slots), F32)
    mix_key = jnp.zeros((length, length), F32)
    mix_value = jnp.zeros((length, length), F32)
    for half in levels(length):
        right, left, is_right = level_factors(running, writes, half)
        key_part, value_part = masked(key_dots, half), masked(value_dots, half)
        left_w = left * writes
        gs_right, at_right = grad_scores * right, attend * right
        mix_key = mix_key + masked(mm(gs_right, left_w, 1, 1), half)
        mix_value = mix_value + masked(mm(at_right, left_w, 1, 1), half)
        rows_sum = gs_right * mm_fine(key_part, left_w, 1, 0) + at_right * mm_fine(value_part, left_w, 1, 0)
        open_sum = left * (mm_fine(key_part, gs_right, 0, 0) + mm_fine(value_part, at_right, 0, 0))
        columns_sum = columns_sum + open_sum
        sums = jnp.where(is_right, rows_sum, open_sum * writes)
        forward = jnp.where((row % (2 * half)) >= half, col - row, row - col - 1) >= 0
        wanted = ((row // half) == (col // half)) & forward
        crossing = crossing + mm_left(wanted.astype(F32), sums, 1, 0)
    key_leaf, value_leaf = leaf_take(key_dots), leaf_take(value_dots)
    leaf_at = lax.broadcasted_iota(jnp.int32, (length, slots), 0) % LEAF
    difference = jnp.zeros((length, slots), F32)
    mix_key_columns, mix_value_columns = [], []
    for at in range(LEAF):
        fall = leaf_decay(running, at)
        mass = leaf_row(writes, at)
        mix_key_columns.append(jnp.sum(grad_scores * fall * mass, axis=1, keepdims=True))
        mix_value_columns.append(jnp.sum(attend * fall * mass, axis=1, keepdims=True))
        terms = fall * (
            grad_scores * key_leaf[:, at : at + 1] + attend * value_leaf[:, at : at + 1]
        )
        blocks = terms.reshape(length // LEAF, LEAF, slots)
        whole = jnp.broadcast_to(
            jnp.sum(blocks, axis=1, keepdims=True), blocks.shape
        ).reshape(length, slots)
        columns_sum = columns_sum + jnp.where(leaf_at == at, whole, 0.0)
        later = jnp.where(leaf_at > at, terms, 0.0)
        later_blocks = later.reshape(length // LEAF, LEAF, slots)
        later_whole = jnp.broadcast_to(
            jnp.sum(later_blocks, axis=1, keepdims=True), later_blocks.shape
        ).reshape(length, slots)
        difference = difference + mass * (later - jnp.where(leaf_at == at, later_whole, 0.0))
    mix_key = mix_key + leaf_spread(jnp.concatenate(mix_key_columns, axis=1))
    mix_value = mix_value + leaf_spread(jnp.concatenate(mix_value_columns, axis=1))
    suffix_leaf = (((row // LEAF) == (col // LEAF)) & (col >= row)).astype(F32)
    crossing = crossing + mm_exact(suffix_leaf, difference, 1, 0)

    start_terms = growth * (
        grad_scores * (mm(q, key_state, 1, 1) * scale)
        + attend * mm(grad_out, value_state, 1, 1)
    )
    crossing = crossing + mm_left((col >= row).astype(F32), start_terms, 1, 0)
    end_open = fade * (mm(k, key_adjoint, 1, 1) + mm(v, value_adjoint, 1, 1))
    columns_sum = columns_sum + end_open
    crossing = crossing + mm_left((col < row).astype(F32), end_open * writes, 1, 0)
    through = mm_exact(
        jnp.ones((8, 2 * width), F32), state.astype(F32) * adjoint.astype(F32), 1, 1
    )[0:1, :]
    crossing = crossing + jnp.exp(last) * through
    grad_decay = crossing - keep * columns_sum

    grad_q = (mm(grad_scores * growth, key_state, 1, 0) + mm(mix_key, k, 1, 0)) * scale
    fade_w = fade * writes
    grad_k = mm(mix_key, q, 0, 0) * scale + mm(fade_w, key_adjoint, 1, 0)
    grad_v = mm(mix_value, grad_out, 0, 0) + mm(fade_w, value_adjoint, 1, 0)
    grad_pre_ref[0, :, :width] = (grad_k * swish_slope(k_pre_ref[0])).astype(BF16)
    grad_pre_ref[0, :, width : 2 * width] = (grad_q * swish_slope(q_pre_ref[0])).astype(BF16)
    grad_pre_ref[0, :, 2 * width :] = grad_v.astype(BF16)
    dlogit_ref[0] = (
        alive_ref[0] * grad_decay * jax.nn.sigmoid(-logit_ref[0]) * (1.0 / GATE_NORM)
    ).astype(BF16)


def per_sequence(kernel, inputs, outputs, shared=()):
    inputs = [x if isinstance(x, tuple) else (x, None) for x in inputs]
    count = inputs[0][0].shape[0]

    def spec(shape, at=None):
        if at is None:
            return pl.BlockSpec((1,) + tuple(shape[1:]), lambda s: (s, 0, 0))
        return pl.BlockSpec((1, shape[1], shape[2] // 3), lambda s: (s, 0, at))

    return pl.pallas_call(
        kernel,
        grid=(count,),
        in_specs=[spec(x.shape, at) for x, at in inputs]
        + [pl.BlockSpec(x.shape, lambda s: (0, 0)) for x in shared],
        out_specs=[spec(x.shape) for x in outputs],
        out_shape=outputs,
        compiler_params=pltpu.CompilerParams(vmem_limit_bytes=VMEM_LIMIT),
    )(*[x for x, _ in inputs], *shared)


CHUNKS = 8
STRIP = 16


def send(src, dst, send_sem, recv_sem, where):
    copy = pltpu.make_async_remote_copy(
        src_ref=src,
        dst_ref=dst,
        send_sem=send_sem,
        recv_sem=recv_sem,
        device_id=where,
        device_id_type=pl.DeviceIdType.MESH,
    )
    copy.start()
    return copy


def greet(partners):
    barrier = pltpu.get_barrier_semaphore()
    for where in partners:
        pl.semaphore_signal(
            barrier, inc=1, device_id=where, device_id_type=pl.DeviceIdType.MESH
        )
    return barrier


def near_partners():
    d, at = lax.axis_index("dp"), lax.axis_index("seq")
    x = {"seq": jnp.bitwise_xor(at, 1)}
    y = {"dp": jnp.bitwise_xor(d, 2)}
    core = {"dp": jnp.bitwise_xor(d, 1)}
    return x, y, core


def everyone(seq, dp, act):
    me = lax.axis_index("dp") * seq + lax.axis_index("seq")

    def turn(r, carry):
        other = jnp.bitwise_xor(me, r)
        act(r, {"dp": other // seq, "seq": other % seq})
        return carry

    lax.fori_loop(1, seq * dp, turn, 0)


def greet_everyone(seq, dp):
    barrier = pltpu.get_barrier_semaphore()
    everyone(
        seq,
        dp,
        lambda r, where: pl.semaphore_signal(
            barrier, inc=1, device_id=where, device_id_type=pl.DeviceIdType.MESH
        ),
    )
    pl.semaphore_wait(barrier, seq * dp - 1)


def gather_kernel(outer, dp, *refs):
    mats, refs = refs[:3], refs[3:]
    toks, small, w_out, refs = refs[:2], refs[2], refs[3], refs[4:]
    three, heads, refs = refs[0], refs[1], refs[2:]
    out_toks, out_small, refs = refs[:2], refs[2], refs[3:]
    (
        local_sem, up_send, up_recv, down_send, down_recv, x_send, x_recv,
        tok_send, tok_recv, small_send, small_recv, head_send, head_recv,
    ) = refs
    outs = [three.at[0], three.at[1], three.at[2]]
    seq = 2 * outer
    at = lax.axis_index("seq")
    d = lax.axis_index("dp")
    me = d * seq + at
    z = at // 2
    x, y, core = near_partners()
    above, below = {"seq": at + 2}, {"seq": at - 2}
    has_above, has_below = z < outer - 1, z > 0
    greet_everyone(seq, dp)

    def push(r, where):
        return pltpu.make_async_remote_copy(
            src_ref=small, dst_ref=out_small.at[me], send_sem=small_send.at[r],
            recv_sem=small_recv.at[r], device_id=where, device_id_type=pl.DeviceIdType.MESH,
        )

    everyone(seq, dp, lambda r, where: push(r, where).start())
    head = heads.shape[2]

    def columns(owner):
        return w_out.at[:, pl.ds(pl.multiple_of(owner * head, head), head)]

    own_head = pltpu.make_async_copy(columns(d), heads.at[d], local_sem.at[5])
    own_head.start()
    other_heads = [
        send(
            columns(jnp.bitwise_xor(d, r)), heads.at[d], head_send.at[r], head_recv.at[r],
            {"dp": jnp.bitwise_xor(d, r)},
        )
        for r in range(1, dp)
    ]

    def up(m, k, src, origin):
        return pltpu.make_async_remote_copy(
            src_ref=src, dst_ref=outs[m].at[0, origin], send_sem=up_send.at[m, k],
            recv_sem=up_recv.at[m, k], device_id=above, device_id_type=pl.DeviceIdType.MESH,
        )

    def down(m, k, src, origin):
        return pltpu.make_async_remote_copy(
            src_ref=src, dst_ref=outs[m].at[0, origin], send_sem=down_send.at[m, k],
            recv_sem=down_recv.at[m, k], device_id=below, device_id_type=pl.DeviceIdType.MESH,
        )

    def across(m, src, origin):
        return pltpu.make_async_remote_copy(
            src_ref=src, dst_ref=outs[m].at[1, origin], send_sem=x_send.at[m, origin],
            recv_sem=x_recv.at[m, origin], device_id=x, device_id_type=pl.DeviceIdType.MESH,
        )

    for m in range(3):
        @pl.when(has_above)
        def _():
            up(m, 0, mats[m], z).start()

        @pl.when(has_below)
        def _():
            down(m, 0, mats[m], z).start()

        across(m, mats[m], z).start()
    tok_y, tok_rest = [], []
    for n, (tok, out_tok) in enumerate(zip(toks, out_toks)):
        tok_y.append(send(tok, out_tok.at[1], tok_send.at[3 * n], tok_recv.at[3 * n], y))
        tok_rest.append(
            send(tok, out_tok.at[2], tok_send.at[3 * n + 1], tok_recv.at[3 * n + 1], core)
        )
        copy = pltpu.make_async_copy(tok, out_tok.at[0], local_sem.at[1 + 5 * n])
        copy.start()
        tok_rest.append(copy)
    own_small = pltpu.make_async_copy(small, out_small.at[me], local_sem.at[0])
    own_small.start()
    own_mats = []
    for m in range(3):
        copy = pltpu.make_async_copy(mats[m], outs[m].at[0, z], local_sem.at[2 + m])
        copy.start()
        own_mats.append(copy)

    def pass_on(k, carry):
        for m in range(3):
            @pl.when(z - k >= 0)
            def _():
                slot = outs[m].at[0, z - k]
                up(m, k - 1, slot, z - k).wait_recv()

                @pl.when(has_above)
                def _():
                    up(m, k, slot, z - k).start()

                across(m, slot, z - k).start()

            @pl.when(z + k < outer)
            def _():
                slot = outs[m].at[0, z + k]
                down(m, k - 1, slot, z + k).wait_recv()

                @pl.when(has_below)
                def _():
                    down(m, k, slot, z + k).start()

                across(m, slot, z + k).start()

        return carry

    lax.fori_loop(1, outer, pass_on, 0)
    for n, out_tok in enumerate(out_toks):
        tok_y[n].wait()
        tok_rest.append(
            send(out_tok.at[1], out_tok.at[3], tok_send.at[3 * n + 2], tok_recv.at[3 * n + 2], core)
        )

    def arrived(r, where):
        push(r, where).wait_send()
        theirs = out_small.at[jnp.bitwise_xor(me, r)]
        pltpu.make_async_remote_copy(
            src_ref=theirs, dst_ref=theirs, send_sem=small_send.at[r],
            recv_sem=small_recv.at[r], device_id=where, device_id_type=pl.DeviceIdType.MESH,
        ).wait_recv()

    everyone(seq, dp, arrived)

    def complete(o, carry):
        for m in range(3):
            across(m, outs[m].at[0, o], o).wait()

            @pl.when(has_above & (o <= z))
            def _():
                up(m, o, outs[m].at[0, z], z).wait_send()

            @pl.when(has_below & (o <= outer - 1 - z))
            def _():
                down(m, o, outs[m].at[0, z], z).wait_send()

        return carry

    lax.fori_loop(0, outer, complete, 0)
    for copy in own_mats:
        copy.wait()
    own_head.wait()
    for r, copy in enumerate(other_heads, 1):
        copy.wait_send()
        theirs = heads.at[jnp.bitwise_xor(d, r)]
        pltpu.make_async_remote_copy(
            src_ref=theirs, dst_ref=theirs, send_sem=head_send.at[r],
            recv_sem=head_recv.at[r], device_id={"dp": jnp.bitwise_xor(d, r)},
            device_id_type=pl.DeviceIdType.MESH,
        ).wait_recv()
    own_small.wait()
    for copy in tok_rest:
        copy.wait()


def in_hbm():
    return pl.BlockSpec(memory_space=pl.ANY)


def in_vmem():
    return pl.BlockSpec(memory_space=pltpu.VMEM)


def gather_all(outer, dp, mats, toks, small, w_out):
    seq = 2 * outer
    rows, width = mats[0].shape
    dma = pltpu.SemaphoreType.DMA
    return pl.pallas_call(
        functools.partial(gather_kernel, outer, dp),
        in_specs=[in_vmem()] * 5 + [in_hbm()] * 2,
        out_specs=[in_hbm()] * 5,
        out_shape=[
            jax.ShapeDtypeStruct((3, 2, outer, rows, width), BF16),
            jax.ShapeDtypeStruct((dp, w_out.shape[0], w_out.shape[1] // dp), BF16),
            jax.ShapeDtypeStruct((dp,) + toks[0].shape, BF16),
            jax.ShapeDtypeStruct((dp,) + toks[1].shape, BF16),
            jax.ShapeDtypeStruct((seq * dp,) + small.shape, BF16),
        ],
        scratch_shapes=[dma((7,))] + [dma((3, outer))] * 6
        + [dma((6,))] * 2 + [dma((seq * dp,))] * 2 + [dma((dp,))] * 2,
        compiler_params=pltpu.CompilerParams(
            collective_id=1, has_side_effects=True, vmem_limit_bytes=VMEM_LIMIT
        ),
    )(*mats, *toks, small, w_out)


def feed_kernel(mid, grad_feed, w_down, w_act, w_lin, product, grad_gate, grad_lin):
    gate = mm(mid[...], w_act[0], 1, 1)
    lin = mm(mid[...], w_lin[0], 1, 1)
    grad_product = mm(grad_feed[...], w_down[0], 1, 1)
    sigma = jax.nn.sigmoid(gate)
    swish = gate * sigma
    product[...] = (swish * lin).astype(BF16)
    grad_gate[...] = (grad_product * lin * (sigma * (1.0 + gate * (1.0 - sigma)))).astype(BF16)
    grad_lin[...] = (grad_product * swish).astype(BF16)


def feed_back_kernel(
    product, grad_gate, grad_lin, w_down, w_act, w_lin, feed, grad_mid
):
    grad_mid[...] = (
        mm(grad_gate[...], w_act[0], 1, 0) + mm(grad_lin[...], w_lin[0], 1, 0)
    ).astype(BF16)
    feed[...] = mm(product[...], w_down[0], 1, 0).astype(BF16)


def feed_tiles(kernel, tiles, weights, widths):
    rows = tiles[0].shape[0]
    step = min(256, rows)
    _, units, width = weights.shape
    each = 2 * step * units * width

    def spec(columns):
        return pl.BlockSpec((step, columns), lambda t: (t, 0))

    def weight(at):
        return pl.BlockSpec(
            (1, units, width), lambda t: (at, 0, 0), pipeline_mode=pl.Buffered(1)
        )

    return pl.pallas_call(
        kernel,
        grid=(rows // step,),
        in_specs=[spec(x.shape[1]) for x in tiles] + [weight(m) for m in range(3)],
        out_specs=[spec(columns) for columns in widths],
        out_shape=[jax.ShapeDtypeStruct((rows, columns), BF16) for columns in widths],
        cost_estimate=pl.CostEstimate(
            flops=3 * each * (rows // step), bytes_accessed=6 * units * width + 8 * rows * width,
            transcendentals=rows * units,
        ),
        compiler_params=pltpu.CompilerParams(vmem_limit_bytes=VMEM_LIMIT),
    )(*tiles, weights, weights, weights)


def turned(x):
    row, col = grid_index(x.shape[1], x.shape[1])
    return mm_exact((row == col).astype(F32), x, 1, 1)


def flipped(x):
    size = x.shape[-1] // 4
    return jnp.concatenate([x[:, size * i : size * (i + 1)] for i in (1, 0, 3, 2)], axis=1)


def relay_kernel(outer, backward, *refs):
    if backward:
        totals, keeps, parts, gate_sent, refs = refs[0], refs[1], refs[2], refs[3], refs[4:]
        states, sums, gate_got, refs = refs[0], refs[1], refs[2], refs[3:]
        gate_s, gate_r = refs[-2:]
        side, refs = refs[-9:-2], refs[:-9]
    else:
        feats, decays, writes, refs = refs[0], refs[1], refs[2], refs[3:]
        states, keeps, refs = refs[0], refs[1], refs[2:]
    (
        own, to_x, from_x, to_z, from_z, to_back, from_back, keep_mine, keep_theirs,
        x_s, x_r, z_s, z_r, b_s, b_r, k_s, k_r,
    ) = refs
    half = own.shape[0]
    at = lax.axis_index("seq")
    inner, z = at % 2, at // 2
    x, y, core = near_partners()
    above, below = {"seq": at + 2}, {"seq": at - 2}
    has_above, has_below = z < outer - 1, z > 0
    ahead, has_ahead, has_source = (
        (below, has_below, has_above) if backward else (above, has_above, has_below)
    )
    barrier = greet([x, y, core] if backward else [x])

    @pl.when(has_above)
    def _():
        greet([above])

    @pl.when(has_below)
    def _():
        greet([below])

    pl.semaphore_wait(
        barrier,
        (3 if backward else 1) + has_above.astype(jnp.int32) + has_below.astype(jnp.int32),
    )

    def compute(s):
        if backward:
            return totals[s]
        width = feats.shape[2] // 3
        total, keep = summary(
            feats[s, :, :width], feats[s, :, 2 * width :], decays[s], writes[s]
        )
        keep_mine[s] = keep
        return total

    crossing = []
    for i in range(half):
        to_x[i] = compute((1 - inner) * half + i).astype(BF16)
        crossing.append(send(to_x.at[i], from_x.at[i], x_s.at[i], x_r.at[i], x))
    if backward:
        gate_copy = send(gate_sent, gate_got, gate_s.at[0], gate_r.at[0], x)
        side = plane_sum_start(parts, side, y, core)
    for i in range(half):
        own[i] = compute(inner * half + i)
    if backward:
        keep_a, keep_b = keeps[0], keeps[1]
    else:
        send(keep_mine, keep_theirs, k_s.at[0], k_r.at[0], x).wait()
        mine = jnp.concatenate([keep_mine[s] for s in range(2 * half)], axis=0)
        theirs = jnp.concatenate([keep_theirs[s] for s in range(2 * half)], axis=0)
        keep_a = jnp.where(inner == 0, mine, theirs)
        keep_b = jnp.where(inner == 0, theirs, mine)
        keeps[0] = keep_a
        keeps[1] = keep_b
    if backward:
        keep_a, keep_b = keep_b, keep_a
    first_k = turned(jnp.where(inner == 0, keep_a[:half], keep_a[half:]))
    second_k = turned(jnp.where(inner == 0, keep_b[:half], keep_b[half:]))
    is_first = (inner == 1) if backward else (inner == 0)

    def along(i):
        return pltpu.make_async_remote_copy(
            src_ref=to_z.at[i], dst_ref=from_z.at[i], send_sem=z_s.at[i], recv_sem=z_r.at[i],
            device_id=ahead, device_id_type=pl.DeviceIdType.MESH,
        )

    returning = []
    for i in range(half):
        crossing[i].wait()

        @pl.when(jnp.logical_not(has_source))
        def _():
            from_z[i] = jnp.zeros_like(from_z[i])

        @pl.when(has_source)
        def _():
            along(i).wait_recv()

        got = flipped(from_x[i]).astype(F32)
        mine = own[i]
        first = jnp.where(is_first, mine, got)
        second = jnp.where(is_first, got, mine)
        entering = from_z[i].astype(F32)
        after = first_k[:, i : i + 1] * entering + first
        to_z[i] = (second_k[:, i : i + 1] * after + second).astype(BF16)

        @pl.when(has_ahead)
        def _():
            along(i).start()

        states[inner * half + i] = jnp.where(is_first, entering, after).astype(BF16)
        to_back[i] = jnp.where(is_first, after, entering).astype(BF16)
        returning.append(send(to_back.at[i], from_back.at[i], b_s.at[i], b_r.at[i], x))
    for i in range(half):
        returning[i].wait()
        states[(1 - inner) * half + i] = flipped(from_back[i])

        @pl.when(has_ahead)
        def _():
            along(i).wait_send()

    if backward:
        plane_sum_end(parts, sums, side)
        gate_copy.wait()


def plane_sum_start(parts, side, y, core):
    from_core, to_y, from_y, core_s, core_r, y_s, y_r = side
    rows = parts.shape[1]
    size = rows // CHUNKS
    cuts = [pl.ds(c * size, size) for c in range(CHUNKS)]
    first = [
        send(parts.at[pl.ds(4, 4), cut], from_core.at[:, cut], core_s.at[c], core_r.at[c], core)
        for c, cut in enumerate(cuts)
    ]
    second = []
    for c, cut in enumerate(cuts):
        first[c].wait()

        for j in range(2):
            to_y[j, cut] = parts[2 + j, cut] + from_core[2 + j, cut]
        second.append(send(to_y.at[:, cut], from_y.at[:, cut], y_s.at[c], y_r.at[c], y))
    return from_core, from_y, second


def plane_sum_end(parts, sums, side):
    from_core, from_y, second = side
    size = parts.shape[1] // CHUNKS
    for c in range(CHUNKS):
        second[c].wait()

        def add(r, carry, c=c):
            at = pl.ds(c * size + r * STRIP, STRIP)
            for j in range(2):
                sums[j, at] = (
                    parts[j, at].astype(F32) + from_core[j, at].astype(F32)
                    + from_y[j, at].astype(F32)
                ).astype(BF16)
            return carry

        lax.fori_loop(0, size // STRIP, add, 0)


def relay(outer, backward, inputs, sequences, slots, width):
    half = sequences // 2
    dma = pltpu.SemaphoreType.DMA
    held = pltpu.VMEM((half, slots, width), BF16)
    states = jax.ShapeDtypeStruct((sequences, slots, width), BF16)
    keeps = jax.ShapeDtypeStruct((2, sequences, slots), F32)
    keep = pltpu.VMEM((sequences, 1, slots), F32)
    outs, side = [states, keeps], []
    if backward:
        rows, columns = inputs[2].shape[1:]
        outs = [states, jax.ShapeDtypeStruct((2, rows, columns), BF16)]
        outs.append(jax.ShapeDtypeStruct(inputs[3].shape, BF16))
        side = [
            pltpu.VMEM((4, rows, columns), BF16), pltpu.VMEM((2, rows, columns), BF16),
            pltpu.VMEM((2, rows, columns), BF16),
        ] + [dma((CHUNKS,))] * 4 + [dma((1,))] * 2
    return pl.pallas_call(
        functools.partial(relay_kernel, outer, backward),
        in_specs=[in_vmem()] * 3 + [in_hbm()] * (len(inputs) - 3),
        out_specs=[in_vmem()] * 2 + [in_hbm()] * (len(outs) - 2),
        out_shape=outs,
        scratch_shapes=[pltpu.VMEM((half, slots, width), F32)] + [held] * 6 + [keep] * 2
        + [dma((half,))] * 6 + [dma((1,))] * 2 + side,
        compiler_params=pltpu.CompilerParams(
            collective_id=7 if backward else 6, has_side_effects=True,
            vmem_limit_bytes=VMEM_LIMIT,
        ),
    )(*inputs)


def middle_kernel(
    parts, tok, gain, extra, hidden, mid, extra_all, from_core, to_y, from_y, normed,
    core_s, core_r, y_s, y_r, local_sem, gx_s, gx_r, gy_s, gy_r, gd_s, gd_r,
    ex_s, ex_r, ed_s, ed_r, extra_sem, gc_s, gc_r, ec_s, ec_r,
):
    rows = tok.shape[0]
    size = rows // CHUNKS
    x, y, core = near_partners()
    pl.semaphore_wait(greet([x, y, core]), 3)
    cuts = [pl.ds(c * size, size) for c in range(CHUNKS)]
    first = [
        send(parts.at[pl.ds(2, 2), cut], from_core.at[:, cut], core_s.at[c], core_r.at[c], core)
        for c, cut in enumerate(cuts)
    ]
    second = []
    for c, cut in enumerate(cuts):
        first[c].wait()

        to_y[cut] = parts[1, cut] + from_core[1, cut]
        second.append(send(to_y.at[cut], from_y.at[cut], y_s.at[c], y_r.at[c], y))
    rest = []
    for j in range(4):
        copy = pltpu.make_async_copy(extra.at[j], extra_all.at[2 * j], extra_sem.at[j])
        copy.start()
        rest.append(copy)
    extra_x = [
        send(extra.at[0, cut], extra_all.at[1, cut], ex_s.at[c], ex_r.at[c], x)
        for c, cut in enumerate(cuts)
    ]
    over_x, over_y, diagonal = [], [], []
    for c in range(CHUNKS + 2):
        if c < CHUNKS:
            cut = cuts[c]
            second[c].wait()

            def norm(r, carry, c=c):
                at = pl.ds(c * size + r * STRIP, STRIP)
                total = tok[at].astype(F32) + (
                    (parts[0, at].astype(F32) + from_core[0, at].astype(F32))
                    + from_y[at].astype(F32)
                )
                hidden[at] = total
                normed[at] = (total * rms_scale(total) * gain[...]).astype(BF16)
                return carry

            lax.fori_loop(0, size // STRIP, norm, 0)
            over_y.append(send(normed.at[cut], mid.at[2, cut], gy_s.at[c], gy_r.at[c], y))
            over_x.append(send(normed.at[cut], mid.at[1, cut], gx_s.at[c], gx_r.at[c], x))
            rest.append(send(normed.at[cut], mid.at[4, cut], gc_s.at[0, c], gc_r.at[0, c], core))
            own = pltpu.make_async_copy(normed.at[cut], mid.at[0, cut], local_sem.at[c])
            own.start()
            rest.append(own)
        if c >= 2:
            at, cut = c - 2, cuts[c - 2]
            over_y[at].wait()
            diagonal.append(send(mid.at[2, cut], mid.at[3, cut], gd_s.at[at], gd_r.at[at], x))
            rest.append(send(mid.at[2, cut], mid.at[6, cut], gc_s.at[2, at], gc_r.at[2, at], core))
    extra_d = []
    for c, cut in enumerate(cuts):
        extra_x[c].wait()
        extra_d.append(
            send(extra_all.at[1, cut], extra_all.at[3, cut], ed_s.at[c], ed_r.at[c], y)
        )
        over_x[c].wait()
        rest.append(send(mid.at[1, cut], mid.at[5, cut], gc_s.at[1, c], gc_r.at[1, c], core))
    rest.append(send(extra_all.at[1], extra_all.at[5], ec_s.at[0], ec_r.at[0], core))
    for c, cut in enumerate(cuts):
        diagonal[c].wait()
        rest.append(send(mid.at[3, cut], mid.at[7, cut], gc_s.at[3, c], gc_r.at[3, c], core))
    for copy in extra_d:
        copy.wait()
    rest.append(send(extra_all.at[3], extra_all.at[7], ec_s.at[1], ec_r.at[1], core))
    for copy in rest:
        copy.wait()


def middle(parts, tok, gain, extra):
    rows, width = tok.shape
    dma = pltpu.SemaphoreType.DMA
    buffer = pltpu.VMEM((rows, width), BF16)
    return pl.pallas_call(
        middle_kernel,
        in_specs=[in_vmem()] * 4,
        out_specs=[in_vmem(), in_hbm(), in_hbm()],
        out_shape=[
            jax.ShapeDtypeStruct((rows, width), F32),
            jax.ShapeDtypeStruct((8, rows, width), BF16),
            jax.ShapeDtypeStruct((8, rows, width), BF16),
        ],
        scratch_shapes=[pltpu.VMEM((2, rows, width), BF16), buffer, buffer, buffer]
        + [dma((CHUNKS,))] * 15
        + [dma((4,))]
        + [dma((4, CHUNKS))] * 2
        + [dma((2,))] * 2,
        compiler_params=pltpu.CompilerParams(
            collective_id=2, has_side_effects=True, vmem_limit_bytes=VMEM_LIMIT
        ),
    )(parts, tok, gain, extra)


def middle_back_kernel(
    parts, hidden, grad_out, gain, grad_hidden, gain_grad, attn,
    from_core, to_x, from_x, to_y, from_y, rounded,
    core_s, core_r, x_s, x_r, y_s, y_r, local_sem, gy_s, gy_r, gc_s, gc_r,
):
    rows, width = hidden.shape
    size = rows // CHUNKS
    x, y, core = near_partners()
    pl.semaphore_wait(greet([x, y, core]), 3)
    cuts = [pl.ds(c * size, size) for c in range(CHUNKS)]
    first = [
        send(parts.at[pl.ds(4, 4), cut], from_core.at[:, cut], core_s.at[c], core_r.at[c], core)
        for c, cut in enumerate(cuts)
    ]
    second, third = [], []
    for c, cut in enumerate(cuts):
        first[c].wait()

        for j in range(2):
            to_x[j, cut] = parts[2 * j + 1, cut] + from_core[2 * j + 1, cut]
        second.append(send(to_x.at[:, cut], from_x.at[:, cut], x_s.at[c], x_r.at[c], x))
    gain_grad[...] = jnp.zeros_like(gain_grad)
    pending, over_y = [], []
    for step in range(CHUNKS + 2):
        if step < CHUNKS:
            c, cut = step, cuts[step]
            second[c].wait()

            def add_x(r, carry, c=c):
                at = pl.ds(c * size + r * STRIP, STRIP)
                to_y[at] = (
                    parts[2, at].astype(F32) + from_core[2, at].astype(F32)
                    + from_x[1, at].astype(F32)
                ).astype(BF16)
                return carry

            lax.fori_loop(0, size // STRIP, add_x, 0)
            third.append(send(to_y.at[cut], from_y.at[cut], y_s.at[c], y_r.at[c], y))
        if 1 <= step <= CHUNKS:
            c, cut = step - 1, cuts[step - 1]
            third[c].wait()

            def back(r, carry, c=c):
                at = pl.ds(c * size + r * STRIP, STRIP)
                grad_mid = (
                    (parts[0, at].astype(F32) + from_core[0, at].astype(F32))
                    + from_x[0, at].astype(F32)
                ) + from_y[at].astype(F32)
                value = hidden[at]
                scale = rms_scale(value)
                unit = value * scale
                gain_grad[...] += jnp.sum(grad_mid * unit, axis=0, keepdims=True)
                scaled = grad_mid * gain[...]
                total = grad_out[at] + scale * (
                    scaled - unit * jnp.mean(scaled * unit, axis=1, keepdims=True)
                )
                grad_hidden[at] = total
                rounded[at] = total.astype(BF16)
                return carry

            lax.fori_loop(0, size // STRIP, back, 0)
            over_y.append(send(rounded.at[cut], attn.at[1, cut], gy_s.at[c], gy_r.at[c], y))
            pending.append(
                send(rounded.at[cut], attn.at[2, cut], gc_s.at[0, c], gc_r.at[0, c], core)
            )
            own = pltpu.make_async_copy(rounded.at[cut], attn.at[0, cut], local_sem.at[c])
            own.start()
            pending.append(own)
        if step >= 2:
            c, cut = step - 2, cuts[step - 2]
            over_y[c].wait()
            pending.append(
                send(attn.at[1, cut], attn.at[3, cut], gc_s.at[1, c], gc_r.at[1, c], core)
            )
    for copy in pending:
        copy.wait()


def middle_back(parts, hidden, grad_out, gain):
    rows, width = hidden.shape
    dma = pltpu.SemaphoreType.DMA

    def buffer(*lead):
        return pltpu.VMEM(lead + (rows, width), BF16)

    return pl.pallas_call(
        middle_back_kernel,
        in_specs=[in_vmem()] * 4,
        out_specs=[in_vmem(), in_vmem(), in_hbm()],
        out_shape=[
            jax.ShapeDtypeStruct((rows, width), F32),
            jax.ShapeDtypeStruct((1, width), F32),
            jax.ShapeDtypeStruct((4, rows, width), BF16),
        ],
        scratch_shapes=[buffer(4), buffer(2), buffer(2), buffer(), buffer(), buffer()]
        + [dma((CHUNKS,))] * 9
        + [dma((2, CHUNKS))] * 2,
        compiler_params=pltpu.CompilerParams(
            collective_id=3, has_side_effects=True, vmem_limit_bytes=VMEM_LIMIT
        ),
    )(parts, hidden, grad_out, gain)


def final_kernel(
    outer, dp, mats, gates, pre_hbm, gate_hbm, kqv_hbm, g_hbm, grad_rank, w_rank, tok,
    base, gain, small, *refs,
):
    out, tokens_grad, out_small, refs = refs[0], refs[1], refs[2], refs[3:]
    (
        grad_pre, grad_gate, w_kqv, w_g,
        from_x, from_below, from_above, total, parts, from_core, to_y, from_y, gain_grad,
        to_all, from_all,
        load, x_s, x_r, up_s, up_r, down_s, down_r, core_s, core_r, y_s, y_r, all_s, all_r,
    ) = refs
    rows, width = tok.shape
    size = rows // CHUNKS
    high = total.shape[2]
    seq = 2 * outer
    at = lax.axis_index("seq")
    me = lax.axis_index("dp") * seq + at
    z = at // 2
    x, y, core = near_partners()
    above, below = {"seq": at + 2}, {"seq": at - 2}
    has_above, has_below = z < outer - 1, z > 0
    greet_everyone(seq, dp)

    def block_of(i):
        ups = outer - 1 - z
        up_at = jnp.where(z < outer // 2, i, i - z)
        down_at = jnp.where(z < outer // 2, i - ups, i)
        is_up = (up_at >= 0) & (up_at < ups)
        block = jnp.where(is_up, outer - 1 - up_at, down_at)
        return jnp.where(i == outer - 1, z, block)

    def across(m, b):
        return pltpu.make_async_remote_copy(
            src_ref=mats.at[m, 1, b], dst_ref=from_x.at[m, b], send_sem=x_s.at[m, b],
            recv_sem=x_r.at[m, b], device_id=x, device_id_type=pl.DeviceIdType.MESH,
        )

    def up(m, b):
        return pltpu.make_async_remote_copy(
            src_ref=total.at[m, b], dst_ref=from_below.at[m, b], send_sem=up_s.at[m, b],
            recv_sem=up_r.at[m, b], device_id=above, device_id_type=pl.DeviceIdType.MESH,
        )

    def down(m, b):
        return pltpu.make_async_remote_copy(
            src_ref=total.at[m, b], dst_ref=from_above.at[m, b], send_sem=down_s.at[m, b],
            recv_sem=down_r.at[m, b], device_id=below, device_id_type=pl.DeviceIdType.MESH,
        )

    def start_x(i, carry):
        for m in range(3):
            across(m, block_of(i)).start()
        return carry

    lax.fori_loop(0, outer, start_x, 0)
    operands = [
        pltpu.make_async_copy(src, dst, load.at[4 + n])
        for n, (src, dst) in enumerate(
            [(pre_hbm, grad_pre), (gate_hbm, grad_gate), (kqv_hbm, w_kqv), (g_hbm, w_g)]
        )
    ]
    loads = [
        pltpu.make_async_copy(mats.at[m, 0] if m < 3 else gates, total.at[m], load.at[m])
        for m in range(4)
    ]
    for copy in operands + loads:
        copy.start()
    for copy in operands:
        copy.wait()

    def grad_in(g):
        some = pl.ds(g * rows, rows)
        parts[g] = (
            mm(grad_pre[some], w_kqv[...], 1, 0)
            + (mm(grad_gate[some], w_g[...], 1, 0) + mm(grad_rank[some], w_rank[...], 1, 1))
        ).astype(BF16)

    grad_in(3)
    first = send(parts.at[3], from_core.at[1], core_s.at[1], core_r.at[1], core)
    grad_in(1)
    first.wait()

    to_y[...] = parts[1] + from_core[1]

    def over_y():
        return pltpu.make_async_remote_copy(
            src_ref=to_y, dst_ref=from_y, send_sem=y_s.at[0], recv_sem=y_r.at[0], device_id=y,
            device_id_type=pl.DeviceIdType.MESH,
        )

    over_y().start()
    grad_in(2)
    first = send(parts.at[2], from_core.at[0], core_s.at[0], core_r.at[0], core)
    grad_in(0)
    first.wait()
    gain_grad[...] = jnp.zeros_like(gain_grad)
    for copy in loads:
        copy.wait()

    def back(c):
        def strip_back(r, carry):
            strip = pl.ds(pl.multiple_of(c * size + r * STRIP, STRIP), STRIP)
            grad = (
                parts[0, strip].astype(F32) + from_core[0, strip].astype(F32)
            ) + from_y[strip].astype(F32)
            value = tok[strip].astype(F32)
            scale = rms_scale(value)
            unit = value * scale
            gain_grad[...] += jnp.sum(grad * unit, axis=0, keepdims=True)
            scaled = grad * gain[...]
            tokens_grad[strip] = base[strip] + scale * (
                scaled - unit * jnp.mean(scaled * unit, axis=1, keepdims=True)
            )
            return carry

        lax.fori_loop(0, size // STRIP, strip_back, 0)

    def add_into(m, b, other):
        total[m, b] = total[m, b] + other[m, b]

    def reduce_block(i, carry):
        b = block_of(i)
        for m in (3, 0, 1, 2):
            if m < 3:
                across(m, b).wait()
                add_into(m, b, from_x)

            @pl.when(b > z)
            def _():
                @pl.when(has_below)
                def _():
                    up(m, b).wait_recv()
                    add_into(m, b, from_below)

                up(m, b).start()

            @pl.when(b < z)
            def _():
                @pl.when(has_above)
                def _():
                    down(m, b).wait_recv()
                    add_into(m, b, from_above)

                down(m, b).start()

            if m < 3:
                turn = 2 * (3 * (i - 1) + m)
                if m == 0:
                    @pl.when(i == 1)
                    def _():
                        over_y().wait()

                @pl.when((turn >= 0) & (turn < CHUNKS))
                def _():
                    back(turn)
                    back(turn + 1)

        return carry

    lax.fori_loop(0, outer - 1, reduce_block, 0)
    devices = seq * dp
    each = width // devices
    row, col = grid_index(devices, width)
    spread = jnp.where(col // each == row, gain_grad[...], 0.0)
    picked_row, picked_col = grid_index(width, 128)
    gathered = mm_exact(spread, ((picked_row % each) == picked_col).astype(F32), 1, 0)
    height = small.shape[1]
    to_all[:, :height] = small[...]
    to_all[:, height:] = jnp.broadcast_to(
        gathered.reshape(devices, 1, 128), (devices, to_all.shape[1] - height, 128)
    )

    def push(r, where):
        return pltpu.make_async_remote_copy(
            src_ref=to_all.at[jnp.bitwise_xor(me, r)], dst_ref=from_all.at[r],
            send_sem=all_s.at[r], recv_sem=all_r.at[r], device_id=where,
            device_id_type=pl.DeviceIdType.MESH,
        )

    everyone(seq, dp, lambda r, where: push(r, where).start())
    out_small[...] = to_all[me]

    def add_small(r, where):
        push(r, where).wait()
        out_small[...] += from_all[r]

    everyone(seq, dp, add_small)
    lax.fori_loop(outer - 1, outer, reduce_block, 0)
    for m in range(4):
        out[m] = total[m, z].astype(F32)

        @pl.when(has_below)
        def _():
            up(m, z).wait_recv()
            out[m] += from_below[m, z].astype(F32)

        @pl.when(has_above)
        def _():
            down(m, z).wait_recv()
            out[m] += from_above[m, z].astype(F32)

    def sent(b, carry):
        for m in range(4):
            @pl.when(b > z)
            def _():
                up(m, b).wait_send()

            @pl.when(b < z)
            def _():
                down(m, b).wait_send()

        return carry

    lax.fori_loop(0, outer, sent, 0)


def finish(outer, dp, mats, gates, operands, rest, small):
    rows, width = rest[-3].shape
    high = mats.shape[3]
    devices = 2 * outer * dp
    dma = pltpu.SemaphoreType.DMA
    blocks = pltpu.VMEM((4, outer, high, width), BF16)
    buffer = pltpu.VMEM((rows, width), BF16)
    payload = (small.shape[1] + 8, 128)
    return pl.pallas_call(
        functools.partial(final_kernel, outer, dp),
        in_specs=[in_hbm()] * (2 + len(operands)) + [in_vmem()] * (len(rest) + 1),
        out_specs=[in_vmem()] * 3,
        out_shape=[
            jax.ShapeDtypeStruct((4, high, width), F32),
            jax.ShapeDtypeStruct((rows, width), F32),
            jax.ShapeDtypeStruct(payload, F32),
        ],
        scratch_shapes=[pltpu.VMEM(x.shape, BF16) for x in operands]
        + [pltpu.VMEM((3, outer, high, width), BF16)]
        + [blocks] * 3
        + [
            pltpu.VMEM((4, rows, width), BF16), pltpu.VMEM((2, rows, width), BF16), buffer,
            buffer, pltpu.VMEM((1, width), F32),
            pltpu.VMEM((devices,) + payload, F32), pltpu.VMEM((devices,) + payload, F32),
            dma((8,)),
        ]
        + [dma((4, outer))] * 6
        + [dma((2,))] * 2
        + [dma((1,))] * 2
        + [dma((devices,))] * 2,
        compiler_params=pltpu.CompilerParams(
            collective_id=4, has_side_effects=True, vmem_limit_bytes=60 * 1024 * 1024
        ),
    )(mats, gates, *operands, *rest, small)


class Lanes:
    def __init__(self):
        self.seq = lax.axis_size("seq")
        self.dp = lax.axis_size("dp")
        self.outer = self.seq // 2
        self.at = lax.axis_index("seq")
        self.d = lax.axis_index("dp")
        self.inner_at = lax.rem(self.at, 2)
        self.outer_at = self.at // 2
        self.groups = [[2 * k + i for k in range(self.outer)] for i in range(2)]

    def swap_inner(self, x):
        return lax.ppermute(x, "seq", [(i, i ^ 1) for i in range(self.seq)])

    def gather_outer(self, x):
        return lax.all_gather(x, "seq", axis=0, tiled=True, axis_index_groups=self.groups)

    def scatter_outer(self, x):
        return lax.psum_scatter(
            x, "seq", scatter_dimension=0, tiled=True, axis_index_groups=self.groups
        )

    def swap_dp(self, x, bit):
        return lax.ppermute(x, "dp", [(i, i ^ bit) for i in range(self.dp)])

    def swap_seq(self, x, bit):
        return lax.ppermute(x, "seq", [(i, i ^ bit) for i in range(self.seq)])

    def exchange_heads(self, blocks):
        got = [lax.dynamic_index_in_dim(blocks, self.d, 0, keepdims=False)]
        for r in range(1, self.dp):
            part = lax.dynamic_index_in_dim(
                blocks, jnp.bitwise_xor(self.d, r), 0, keepdims=False
            )
            got.append(self.swap_dp(part, r))
        bit = 1
        while bit < self.dp:
            is_set = (self.d // bit) % 2 == 1
            got = [jnp.where(is_set, got[i ^ bit], got[i]) for i in range(self.dp)]
            bit *= 2
        return jnp.stack(got)

    def pick(self, natural, axis):
        first = lax.index_in_dim(natural, 0, axis, keepdims=False)
        second = lax.index_in_dim(natural, 1, axis, keepdims=False)
        even = self.inner_at == 0
        return jnp.where(even, first, second), jnp.where(even, second, first)


def swap_halves(x, parts):
    size = x.shape[-1] // (2 * parts)
    pieces = [x[..., i * size : (i + 1) * size] for i in range(2 * parts)]
    order = [i ^ 1 for i in range(2 * parts)]
    return jnp.concatenate([pieces[i] for i in order], axis=-1)


def per_device(
    tokens, lengths, cotangent, mixer_gain, feed_gain, head_gain, w_query, w_key, w_value,
    w_gate, w_out, rank_down, rank_up, rank_bias, w_act, w_lin, w_down,
):
    lanes = Lanes()
    seq_count, piece, width = tokens.shape
    rows = seq_count * piece
    sequences = lanes.dp * seq_count
    all_rows = lanes.dp * rows
    head_width = width // HEADS
    half_width = head_width // 2
    rank = rank_down.shape[1]
    devices = lanes.dp * lanes.seq

    counts = lengths.astype(F32)
    high = jnp.floor(counts / 256.0)
    small_parts = [
        mixer_gain, feed_gain, head_gain, rank_down.reshape(-1), rank_up.reshape(-1),
        rank_bias, high.astype(BF16), (counts - 256.0 * high).astype(BF16),
    ]
    sizes = [p.shape[0] for p in small_parts]
    used = sum(sizes)
    padded = -(-used // 2048) * 2048
    small = jnp.concatenate(small_parts + [jnp.zeros((padded - used,), BF16)])
    own_tokens = tokens.reshape(rows, width)
    position = (lanes.at * piece + jnp.arange(piece)).astype(F32)
    alive_own = (position[None, :] < counts[:, None]).astype(F32).reshape(rows, 1)
    grad_out = cotangent.reshape(rows, width).astype(F32) * alive_own
    w_kqv, out_mine, plane_tokens, grad_feed, smalls = gather_all(
        lanes.outer, lanes.dp, [w_key, w_query, w_value], [own_tokens, grad_out.astype(BF16)],
        small.reshape(-1, 128), w_out,
    )
    w_kqv = w_kqv.reshape(3 * head_width, width)
    out_rows = w_out.shape[0]
    out_own, out_other = lanes.pick(
        out_mine.reshape(lanes.dp, out_rows, lanes.outer, 2, -1), 3
    )
    out_mine = jnp.concatenate(
        [
            out_own.reshape(lanes.dp, out_rows, half_width),
            out_other.reshape(lanes.dp, out_rows, half_width),
        ],
        axis=2,
    )
    gate_and_out = lanes.gather_outer(
        jnp.concatenate([w_gate, out_mine.reshape(out_rows, width)], axis=0)
    )
    smalls = smalls.reshape(devices, padded)
    cuts, offset = [], 0
    for size in sizes:
        cuts.append(smalls[:, offset : offset + size])
        offset += size
    mixer_full = cuts[0].reshape(1, width).astype(F32)
    feed_full = cuts[1].reshape(1, width).astype(F32)
    head_natural = cuts[2].reshape(lanes.outer, 2, half_width // lanes.outer)
    head_own, head_other = lanes.pick(head_natural, 1)
    head_full = jnp.concatenate(
        [head_own.reshape(1, half_width), head_other.reshape(1, half_width)], axis=1
    ).astype(F32)
    down_full = cuts[3].reshape(width, rank)
    up_mine = lax.dynamic_index_in_dim(
        cuts[4].reshape(lanes.dp, SLOTS, rank), lanes.d, 0, keepdims=False
    )
    bias_mine = lax.dynamic_index_in_dim(
        cuts[5].reshape(lanes.dp, 1, SLOTS), lanes.d, 0, keepdims=False
    ).astype(F32)
    all_lengths = cuts[6].astype(F32) * 256.0 + cuts[7].astype(F32)
    all_lengths = all_lengths.reshape(lanes.dp, lanes.seq, seq_count)[:, 0]

    group_lengths = jnp.concatenate(
        [
            lax.dynamic_index_in_dim(
                all_lengths, jnp.bitwise_xor(lanes.d, r), 0, keepdims=False
            )
            for r in (0, 2, 1, 3)
        ]
    )
    alive = (position[None, :] < group_lengths[:, None]).astype(F32).reshape(all_rows, 1)

    sources = plane_tokens.reshape(all_rows, width).astype(F32)
    normed_in = lax.optimization_barrier(
        (sources * rms_scale(sources) * mixer_full).astype(BF16)
    )

    pre = contract_last(normed_in, w_kqv)
    low_rank = mm(normed_in, down_full, 1, 0).astype(BF16)
    gate_logit = contract_last(low_rank, up_mine) + bias_mine
    log_decay = jax.nn.log_sigmoid(gate_logit) / GATE_NORM * alive
    writes = -jnp.expm1(log_decay)

    def seqs(x):
        return x.reshape(sequences, piece, x.shape[1])

    def flat(x):
        return x.reshape(all_rows, x.shape[2])

    is_value = jnp.arange(3 * head_width) >= 2 * head_width
    feats = seqs(jnp.where(is_value, pre, pre * jax.nn.sigmoid(pre)).astype(BF16))
    pre = seqs(pre)
    decays, writes = seqs(log_decay), seqs(writes)

    def shaped(like_rows, columns, kind):
        return jax.ShapeDtypeStruct((sequences, like_rows, columns), kind)

    gate_and_out, feats = lax.optimization_barrier((gate_and_out, feats))
    keys, queries, values = (feats, 0), (feats, 1), (feats, 2)
    state_in, keeps = relay(
        lanes.outer, False, [feats, decays, writes], sequences, SLOTS, 2 * head_width
    )
    feed = jnp.stack([w_down, w_act, w_lin])
    feed, state_in, gate_and_out = lax.optimization_barrier((feed, state_in, gate_and_out))
    feed = lax.all_gather(
        feed, "seq", axis=1, tiled=True, axis_index_groups=lanes.groups
    )
    gate_and_out = gate_and_out.reshape(lanes.outer, 2, out_rows, width)
    gate_own, out_own = gate_and_out[:, 0], gate_and_out[:, 1]
    gate_other = lanes.swap_inner(gate_own)
    w_g = jnp.concatenate([gate_own, gate_other], axis=0).reshape(head_width, width)
    gates = seqs(contract_last(normed_in, w_g))
    out_own = out_own.reshape(lanes.outer, lanes.dp, out_rows, head_width)
    out_other = swap_halves(lanes.swap_inner(out_own), 1)
    even = lanes.inner_at == 0
    natural = jnp.stack(
        [jnp.where(even, out_own, out_other), jnp.where(even, out_other, out_own)], axis=2
    )
    out_full = natural.transpose(1, 0, 2, 3, 4).reshape(width, head_width)
    mixed, slot_out, attend = per_sequence(
        forward_kernel,
        [queries, keys, values, gates, decays, writes, state_in],
        [
            shaped(piece, head_width, BF16),
            shaped(piece, head_width, F32),
            shaped(piece, SLOTS, F32),
        ],
        shared=[head_full],
    )
    mixed_flat = flat(mixed)
    parts = contract_last(mixed_flat, out_full).astype(BF16)
    hidden, normed_mid, grad_feed = middle(
        parts.reshape(4, rows, width), own_tokens, feed_full, grad_feed
    )
    normed_mid = normed_mid.reshape(8 * rows, width)
    grad_feed = grad_feed.reshape(8 * rows, width)

    units = feed.shape[1]
    product, grad_gate, grad_lin = feed_tiles(
        feed_kernel, [normed_mid, grad_feed], feed, [units] * 3
    )
    feed_grads = jnp.stack(
        [
            contract_first(product, grad_feed).astype(BF16),
            contract_first(grad_gate, normed_mid).astype(BF16),
            contract_first(grad_lin, normed_mid).astype(BF16),
        ]
    )
    product, grad_gate, grad_lin, feed_grads = lax.optimization_barrier(
        (product, grad_gate, grad_lin, feed_grads)
    )
    feed_grads = lax.psum_scatter(
        feed_grads, "seq", scatter_dimension=1, tiled=True, axis_index_groups=lanes.groups
    )
    feed_parts, mid_parts = feed_tiles(
        feed_back_kernel, [product, grad_gate, grad_lin], feed, [width] * 2
    )
    grad_hidden, feed_gain_part, grad_attn = middle_back(
        mid_parts.reshape(8, rows, width), hidden, grad_out, feed_full
    )
    grad_attn = grad_attn.reshape(all_rows, width)
    feed_parts, grad_attn = lax.optimization_barrier((feed_parts, grad_attn))

    grad_mixed = mm(grad_attn, out_full, 1, 0)
    grad_gate_pre, grad_slot, grad_scores, adjoint, head_parts = per_sequence(
        back_first_kernel,
        [seqs(grad_mixed), gates, slot_out, attend, queries, values, decays, writes, state_in],
        [
            shaped(piece, head_width, BF16),
            shaped(piece, head_width, BF16),
            shaped(piece, SLOTS, F32),
            shaped(SLOTS, 2 * head_width, F32),
            shaped(1, head_width, F32),
        ],
        shared=[head_full],
    )
    grad_gate_flat = flat(grad_gate_pre)
    out_grad = contract_first(grad_attn, mixed_flat).astype(BF16)
    out_grad = out_grad.reshape(lanes.dp, lanes.outer, 2, out_rows, head_width)
    own_part, other_part = lanes.pick(out_grad, 2)
    got = swap_halves(lanes.swap_inner(other_part), 1)
    out_sum = (own_part.astype(F32) + got.astype(F32)).astype(BF16).transpose(1, 0, 2, 3)
    gate_grad = contract_first(grad_gate_flat, normed_in).astype(BF16)
    adjoint, out_sum, gate_grad, feed_parts = lax.optimization_barrier(
        (adjoint, out_sum, gate_grad, feed_parts)
    )
    adjoint_in, feed_sums, gate_got = relay(
        lanes.outer, True,
        [adjoint, keeps, feed_parts.reshape(8, rows, width), gate_grad[half_width:]], sequences,
        SLOTS, 2 * head_width,
    )
    gate_grad, out_sum, adjoint_in, feed_grads = lax.optimization_barrier(
        (gate_grad, out_sum, adjoint_in, feed_grads)
    )
    out_mine = lanes.scatter_outer(out_sum.reshape(-1, head_width))
    grad_pre, grad_logit = per_sequence(
        back_second_kernel,
        [
            grad_slot, grad_scores, attend, queries, keys, values, decays, writes,
            state_in, adjoint_in, (pre, 1), (pre, 0), seqs(gate_logit), seqs(alive),
        ],
        [shaped(piece, 3 * head_width, BF16), shaped(piece, SLOTS, BF16)],
    )
    feed_got = lanes.swap_inner(feed_sums[1])
    grad_pre, out_mine = lax.optimization_barrier((flat(grad_pre), out_mine))
    grad_logit = flat(grad_logit)
    bias_part = jnp.sum(grad_logit.astype(F32), axis=0)
    up_part = contract_first(grad_logit, low_rank)
    grad_rank = mm(grad_logit, up_mine, 1, 0).astype(BF16)
    down_part = contract_first(normed_in, grad_rank)

    mixer_grads = contract_first(grad_pre, normed_in).astype(BF16)
    mixer_grads = mixer_grads.reshape(3, 2, lanes.outer, -1, width)

    head_part = jnp.sum(head_parts, axis=(0, 1)).reshape(2, lanes.outer, -1)
    low_half, high_half = lanes.pick(head_part, 0)
    head_part = jnp.stack([low_half, high_half], axis=1)
    mine = (jnp.arange(lanes.dp) == lanes.d).astype(F32)
    up_all = mine[:, None] * up_part.reshape(1, -1)
    bias_all = mine[:, None] * bias_part.reshape(1, -1)
    parts = [
        feed_gain_part.reshape(devices, -1),
        head_part.reshape(devices, -1),
        down_part.reshape(devices, -1),
        up_all.reshape(devices, -1),
        bias_all.reshape(devices, -1),
    ]
    sizes = [p.shape[1] for p in parts]
    padded = -(-sum(sizes) // 1024) * 1024
    parts.append(jnp.zeros((devices, padded - sum(sizes)), F32))
    small_parts = jnp.concatenate(parts, axis=1).reshape(devices, -1, 128)
    gate_sum = (gate_grad[:half_width].astype(F32) + gate_got.astype(F32)).astype(BF16)
    out_mine = out_mine.reshape(lanes.dp, out_rows, head_width)
    out_mine = lanes.exchange_heads(out_mine).transpose(1, 0, 2)
    out_mine = out_mine.reshape(out_rows, lanes.dp, 2, lanes.outer, -1)
    low_half, high_half = lanes.pick(out_mine, 2)
    w_out_grad = jnp.stack([low_half, high_half], axis=3).reshape(out_rows, width).astype(F32)
    mixer_grads, feed_got, w_out_grad = lax.optimization_barrier(
        (mixer_grads, feed_got, w_out_grad)
    )
    weight_grads, tokens_grad, reduced = finish(
        lanes.outer, lanes.dp, mixer_grads,
        gate_sum.reshape(lanes.outer, -1, width),
        [grad_pre, grad_gate_flat, w_kqv, w_g],
        [grad_rank, down_full, own_tokens, grad_hidden, mixer_full],
        small_parts,
    )
    w_key_grad, w_query_grad, w_value_grad, w_gate_grad = [weight_grads[m] for m in range(4)]
    tokens_grad = tokens_grad.reshape(seq_count, piece, width)
    feed_sum = feed_sums[0].astype(F32) + feed_got.astype(F32)
    block_out = (alive_own * (hidden + feed_sum)).astype(BF16)
    mixer_gain_grad = reduced[padded // 128, : width // devices]
    reduced = reduced.reshape(-1)
    smalls, offset = [], 0
    for size in sizes:
        smalls.append(reduced[offset : offset + size])
        offset += size
    return (
        block_out.reshape(seq_count, piece, width),
        tokens_grad,
        mixer_gain_grad,
        smalls[0],
        smalls[1],
        w_query_grad,
        w_key_grad,
        w_value_grad,
        w_gate_grad,
        w_out_grad,
        smalls[2].reshape(-1, rank),
        smalls[3].reshape(-1, rank),
        smalls[4],
        feed_grads[1].astype(F32),
        feed_grads[2].astype(F32),
        feed_grads[0].astype(F32),
    )


def solution(mesh):
    vector = P(("dp", "seq"))
    matrix = P(("dp", "seq"), None)
    stream = P("dp", "seq", None)
    return jax.shard_map(
        per_device,
        mesh=mesh,
        in_specs=(
            stream, P("dp"), stream, vector, vector, vector, matrix, matrix, matrix, matrix,
            matrix, matrix, matrix, vector, matrix, matrix, matrix,
        ),
        out_specs=(
            stream, stream, vector, vector, vector, matrix, matrix, matrix, matrix, matrix,
            matrix, matrix, vector, matrix, matrix, matrix,
        ),
        check_vma=False,
    )
```

```python
import functools

import jax
import jax.numpy as jnp
from jax import lax
from jax.experimental import pallas as pl
from jax.experimental.pallas import tpu as pltpu
from jax.sharding import PartitionSpec as P

HEADS = 4
SLOTS = 64
EPS = 1e-06
GATE_NORM = 8.0
F32 = jnp.float32
BF16 = jnp.bfloat16
LEAF = 8
VMEM_LIMIT = 48 * 1024 * 1024


def mm(a, b, ca, cb):
    return lax.dot_general(
        a.astype(BF16), b.astype(BF16), (((ca,), (cb,)), ((), ())), preferred_element_type=F32
    )


def mm_exact(a, b, ca, cb):
    return lax.dot_general(
        a,
        b,
        (((ca,), (cb,)), ((), ())),
        precision=lax.Precision.HIGHEST,
        preferred_element_type=F32,
    )


def two_parts(x):
    high = x.astype(BF16)
    return high, (x - high.astype(F32)).astype(BF16)


def mm_left(exact, b, ca, cb):
    high, low = two_parts(b)
    return mm(exact, high, ca, cb) + mm(exact, low, ca, cb)


def mm_right(a, exact, ca, cb):
    high, low = two_parts(a)
    return mm(high, exact, ca, cb) + mm(low, exact, ca, cb)


def mm_fine(a, b, ca, cb):
    a_high, a_low = two_parts(a)
    b_high, b_low = two_parts(b)
    return mm(a_high, b_high, ca, cb) + (mm(a_high, b_low, ca, cb) + mm(a_low, b_high, ca, cb))


def contract_last(a, b):
    return mm(a, b, 1, 1)


def contract_first(a, b):
    return mm(a, b, 0, 0)


def swish_slope(v):
    sigma = jax.nn.sigmoid(v)
    return sigma * (1.0 + v * (1.0 - sigma))


def rms_scale(v):
    return lax.rsqrt(jnp.mean(v * v, axis=-1, keepdims=True) + EPS)


def grid_index(rows, cols):
    return (
        lax.broadcasted_iota(jnp.int32, (rows, cols), 0),
        lax.broadcasted_iota(jnp.int32, (rows, cols), 1),
    )


def running_sum(decay):
    length = decay.shape[0]
    row, col = grid_index(length, length)
    return mm_exact((row >= col).astype(F32), decay, 1, 0)


def levels(length):
    found = []
    half = length // 2
    while half >= LEAF:
        found.append(half)
        half //= 2
    return found


def level_factors(running, writes, half):
    length, slots = running.shape
    pairs = running.reshape(length // (2 * half), 2 * half, slots)
    anchor = jnp.broadcast_to(pairs[:, half - 1 : half, :], pairs.shape).reshape(length, slots)
    near = jnp.exp(-jnp.abs(running - anchor))
    row, _ = grid_index(length, slots)
    right = (row % (2 * half)) >= half
    return jnp.where(right, near, 0.0), jnp.where(right, 0.0, near), right


def same_block(length, size):
    row, col = grid_index(length, length)
    return (row // size) == (col // size)


def leaf_selector(length):
    row, col = grid_index(length, LEAF)
    return ((row % LEAF) == col).astype(F32)


def leaf_take(square):
    length = square.shape[0]
    kept = jnp.where(same_block(length, LEAF), square, 0.0)
    return mm_exact(kept, leaf_selector(length), 1, 0)


def leaf_spread(columns):
    length = columns.shape[0]
    wide = mm_exact(columns, leaf_selector(length), 1, 1)
    return jnp.where(same_block(length, LEAF), wide, 0.0)


def leaf_row(tensor, at):
    length, width = tensor.shape
    blocks = tensor.reshape(length // LEAF, LEAF, width)
    return jnp.broadcast_to(blocks[:, at : at + 1, :], blocks.shape).reshape(length, width)


def leaf_decay(running, at):
    length, slots = running.shape
    row, _ = grid_index(length, slots)
    reached = (row % LEAF) >= at
    spread = running - leaf_row(running, at)
    return jnp.where(reached, jnp.exp(jnp.where(reached, spread, 0.0)), 0.0)


def masked(square, half):
    length = square.shape[0]
    if 2 * half == length:
        return square
    return jnp.where(same_block(length, 2 * half), square, 0.0)


def read_in_chunk(square, running, writes):
    total = None
    for half in levels(running.shape[0]):
        right, left, _ = level_factors(running, writes, half)
        part = right * mm_fine(masked(square, half), left * writes, 1, 0)
        total = part if total is None else total + part
    columns = leaf_take(square)
    for at in range(LEAF):
        part = columns[:, at : at + 1] * (leaf_decay(running, at) * leaf_row(writes, at))
        total = part if total is None else total + part
    return total


def mix_in_chunk(attend, running, writes):
    total = None
    for half in levels(running.shape[0]):
        right, left, _ = level_factors(running, writes, half)
        part = masked(mm(attend * right, left * writes, 1, 1), half)
        total = part if total is None else total + part
    columns = [
        jnp.sum(
            attend * (leaf_decay(running, at) * leaf_row(writes, at)), axis=1, keepdims=True
        )
        for at in range(LEAF)
    ]
    part = leaf_spread(jnp.concatenate(columns, axis=1))
    return part if total is None else total + part


def summary(k, v, decay, writes):
    running = running_sum(decay)
    length = running.shape[0]
    last = running[length - 1 : length, :]
    fade = jnp.exp(last - running) * writes
    return jnp.concatenate([mm(fade, k, 0, 0), mm(fade, v, 0, 0)], axis=1), jnp.exp(last)


def forward_kernel(
    q_ref, k_ref, v_ref, gate_ref, decay_ref, writes_ref, state_ref, gain_ref,
    mixed_ref, out_ref, attend_ref,
):
    q, k, v = q_ref[0], k_ref[0], v_ref[0]
    writes = writes_ref[0]
    width = q.shape[1]
    scale = width ** (-0.5)
    running = running_sum(decay_ref[0])
    growth = jnp.exp(running)
    state = state_ref[0]
    dots = mm(q, k, 1, 1) * scale
    scores = growth * (mm(q, state[:, :width], 1, 1) * scale)
    scores = scores + read_in_chunk(dots, running, writes)
    top = jnp.max(scores, axis=1, keepdims=True)
    raw = jnp.exp(scores - top)
    attend = raw / jnp.sum(raw, axis=1, keepdims=True)
    mixing = mix_in_chunk(attend, running, writes)
    out = mm(attend * growth, state[:, width:], 1, 0) + mm(mixing, v, 1, 0)
    out_ref[0] = out
    attend_ref[0] = attend
    gate = gate_ref[0]
    normed = out * rms_scale(out) * gain_ref[...]
    mixed_ref[0] = (normed * (gate * jax.nn.sigmoid(gate))).astype(BF16)


def back_first_kernel(
    grad_mixed_ref, gate_ref, out_ref, attend_ref, q_ref, v_ref, decay_ref, writes_ref,
    state_ref, gain_ref,
    grad_gate_ref, grad_out_ref, grad_scores_ref, adjoint_ref, gain_grad_ref,
):
    q, v = q_ref[0], v_ref[0]
    writes = writes_ref[0]
    width = q.shape[1]
    scale = width ** (-0.5)
    grad_mixed, gate, out = grad_mixed_ref[0], gate_ref[0], out_ref[0]
    gain = gain_ref[...]
    inverse = rms_scale(out)
    normed = out * inverse
    grad_gate_ref[0] = (grad_mixed * (normed * gain) * swish_slope(gate)).astype(BF16)
    e = grad_mixed * (gate * jax.nn.sigmoid(gate))
    gain_grad_ref[0] = jnp.sum(e * normed, axis=0, keepdims=True)
    eg = e * gain
    grad_out = inverse * (eg - normed * jnp.mean(eg * normed, axis=1, keepdims=True))
    grad_out_ref[0] = grad_out.astype(BF16)
    running = running_sum(decay_ref[0])
    growth = jnp.exp(running)
    attend = attend_ref[0]
    u = growth * mm_right(grad_out, state_ref[0, :, width:], 1, 1)
    u = u + read_in_chunk(mm_right(grad_out, v, 1, 1), running, writes)
    grad_scores = attend * (u - jnp.sum(attend * u, axis=1, keepdims=True))
    grad_scores_ref[0] = grad_scores
    adjoint_ref[0, :, :width] = mm(growth * grad_scores * scale, q, 0, 0)
    adjoint_ref[0, :, width:] = mm(growth * attend, grad_out.astype(BF16), 0, 0)


def back_second_kernel(
    grad_out_ref, grad_scores_ref, attend_ref, q_ref, k_ref, v_ref, decay_ref, writes_ref,
    state_ref, adjoint_ref, q_pre_ref, k_pre_ref, logit_ref, alive_ref,
    grad_pre_ref, dlogit_ref,
):
    q, k, v, grad_out = q_ref[0], k_ref[0], v_ref[0], grad_out_ref[0]
    attend, grad_scores = attend_ref[0], grad_scores_ref[0]
    decay, writes = decay_ref[0], writes_ref[0]
    length, slots = decay.shape
    width = q.shape[1]
    scale = width ** (-0.5)
    running = running_sum(decay)
    growth = jnp.exp(running)
    keep = jnp.exp(decay)
    last = running[length - 1 : length, :]
    fade = jnp.exp(last - running)
    state, adjoint = state_ref[0], adjoint_ref[0]
    key_state, value_state = state[:, :width], state[:, width:]
    key_adjoint, value_adjoint = adjoint[:, :width], adjoint[:, width:]
    key_dots = mm(q, k, 1, 1) * scale
    value_dots = mm(grad_out, v, 1, 1)
    row, col = grid_index(length, length)

    columns_sum = jnp.zeros((length, slots), F32)
    crossing = jnp.zeros((length, slots), F32)
    mix_key = jnp.zeros((length, length), F32)
    mix_value = jnp.zeros((length, length), F32)
    for half in levels(length):
        right, left, is_right = level_factors(running, writes, half)
        key_part, value_part = masked(key_dots, half), masked(value_dots, half)
        left_w = left * writes
        gs_right, at_right = grad_scores * right, attend * right
        mix_key = mix_key + masked(mm(gs_right, left_w, 1, 1), half)
        mix_value = mix_value + masked(mm(at_right, left_w, 1, 1), half)
        rows_sum = gs_right * mm_fine(key_part, left_w, 1, 0) + at_right * mm_fine(value_part, left_w, 1, 0)
        open_sum = left * (mm_fine(key_part, gs_right, 0, 0) + mm_fine(value_part, at_right, 0, 0))
        columns_sum = columns_sum + open_sum
        sums = jnp.where(is_right, rows_sum, open_sum * writes)
        forward = jnp.where((row % (2 * half)) >= half, col - row, row - col - 1) >= 0
        wanted = ((row // half) == (col // half)) & forward
        crossing = crossing + mm_left(wanted.astype(F32), sums, 1, 0)
    key_leaf, value_leaf = leaf_take(key_dots), leaf_take(value_dots)
    leaf_at = lax.broadcasted_iota(jnp.int32, (length, slots), 0) % LEAF
    difference = jnp.zeros((length, slots), F32)
    mix_key_columns, mix_value_columns = [], []
    for at in range(LEAF):
        fall = leaf_decay(running, at)
        mass = leaf_row(writes, at)
        mix_key_columns.append(jnp.sum(grad_scores * fall * mass, axis=1, keepdims=True))
        mix_value_columns.append(jnp.sum(attend * fall * mass, axis=1, keepdims=True))
        terms = fall * (
            grad_scores * key_leaf[:, at : at + 1] + attend * value_leaf[:, at : at + 1]
        )
        blocks = terms.reshape(length // LEAF, LEAF, slots)
        whole = jnp.broadcast_to(
            jnp.sum(blocks, axis=1, keepdims=True), blocks.shape
        ).reshape(length, slots)
        columns_sum = columns_sum + jnp.where(leaf_at == at, whole, 0.0)
        later = jnp.where(leaf_at > at, terms, 0.0)
        later_blocks = later.reshape(length // LEAF, LEAF, slots)
        later_whole = jnp.broadcast_to(
            jnp.sum(later_blocks, axis=1, keepdims=True), later_blocks.shape
        ).reshape(length, slots)
        difference = difference + mass * (later - jnp.where(leaf_at == at, later_whole, 0.0))
    mix_key = mix_key + leaf_spread(jnp.concatenate(mix_key_columns, axis=1))
    mix_value = mix_value + leaf_spread(jnp.concatenate(mix_value_columns, axis=1))
    suffix_leaf = (((row // LEAF) == (col // LEAF)) & (col >= row)).astype(F32)
    crossing = crossing + mm_exact(suffix_leaf, difference, 1, 0)

    start_terms = growth * (
        grad_scores * (mm(q, key_state, 1, 1) * scale)
        + attend * mm(grad_out, value_state, 1, 1)
    )
    crossing = crossing + mm_left((col >= row).astype(F32), start_terms, 1, 0)
    end_open = fade * (mm(k, key_adjoint, 1, 1) + mm(v, value_adjoint, 1, 1))
    columns_sum = columns_sum + end_open
    crossing = crossing + mm_left((col < row).astype(F32), end_open * writes, 1, 0)
    through = mm_exact(
        jnp.ones((8, 2 * width), F32), state.astype(F32) * adjoint.astype(F32), 1, 1
    )[0:1, :]
    crossing = crossing + jnp.exp(last) * through
    grad_decay = crossing - keep * columns_sum

    grad_q = (mm(grad_scores * growth, key_state, 1, 0) + mm(mix_key, k, 1, 0)) * scale
    fade_w = fade * writes
    grad_k = mm(mix_key, q, 0, 0) * scale + mm(fade_w, key_adjoint, 1, 0)
    grad_v = mm(mix_value, grad_out, 0, 0) + mm(fade_w, value_adjoint, 1, 0)
    grad_pre_ref[0, :, :width] = (grad_k * swish_slope(k_pre_ref[0])).astype(BF16)
    grad_pre_ref[0, :, width : 2 * width] = (grad_q * swish_slope(q_pre_ref[0])).astype(BF16)
    grad_pre_ref[0, :, 2 * width :] = grad_v.astype(BF16)
    dlogit_ref[0] = (
        alive_ref[0] * grad_decay * jax.nn.sigmoid(-logit_ref[0]) * (1.0 / GATE_NORM)
    ).astype(BF16)


def per_sequence(kernel, inputs, outputs, shared=()):
    inputs = [x if isinstance(x, tuple) else (x, None) for x in inputs]
    count = inputs[0][0].shape[0]

    def spec(shape, at=None):
        if at is None:
            return pl.BlockSpec((1,) + tuple(shape[1:]), lambda s: (s, 0, 0))
        return pl.BlockSpec((1, shape[1], shape[2] // 3), lambda s: (s, 0, at))

    return pl.pallas_call(
        kernel,
        grid=(count,),
        in_specs=[spec(x.shape, at) for x, at in inputs]
        + [pl.BlockSpec(x.shape, lambda s: (0, 0)) for x in shared],
        out_specs=[spec(x.shape) for x in outputs],
        out_shape=outputs,
        compiler_params=pltpu.CompilerParams(vmem_limit_bytes=VMEM_LIMIT),
    )(*[x for x, _ in inputs], *shared)


CHUNKS = 8
STRIP = 16


def send(src, dst, send_sem, recv_sem, where):
    copy = pltpu.make_async_remote_copy(
        src_ref=src,
        dst_ref=dst,
        send_sem=send_sem,
        recv_sem=recv_sem,
        device_id=where,
        device_id_type=pl.DeviceIdType.MESH,
    )
    copy.start()
    return copy


def greet(partners):
    barrier = pltpu.get_barrier_semaphore()
    for where in partners:
        pl.semaphore_signal(
            barrier, inc=1, device_id=where, device_id_type=pl.DeviceIdType.MESH
        )
    return barrier


def near_partners():
    d, at = lax.axis_index("dp"), lax.axis_index("seq")
    x = {"seq": jnp.bitwise_xor(at, 1)}
    y = {"dp": jnp.bitwise_xor(d, 2)}
    core = {"dp": jnp.bitwise_xor(d, 1)}
    return x, y, core


def everyone(seq, dp, act):
    me = lax.axis_index("dp") * seq + lax.axis_index("seq")

    def turn(r, carry):
        other = jnp.bitwise_xor(me, r)
        act(r, {"dp": other // seq, "seq": other % seq})
        return carry

    lax.fori_loop(1, seq * dp, turn, 0)


def greet_everyone(seq, dp):
    barrier = pltpu.get_barrier_semaphore()
    everyone(
        seq,
        dp,
        lambda r, where: pl.semaphore_signal(
            barrier, inc=1, device_id=where, device_id_type=pl.DeviceIdType.MESH
        ),
    )
    pl.semaphore_wait(barrier, seq * dp - 1)


def gather_kernel(outer, dp, *refs):
    mats, refs = refs[:3], refs[3:]
    toks, small, w_out, refs = refs[:2], refs[2], refs[3], refs[4:]
    three, heads, refs = refs[0], refs[1], refs[2:]
    out_toks, out_small, refs = refs[:2], refs[2], refs[3:]
    (
        local_sem, up_send, up_recv, down_send, down_recv, x_send, x_recv,
        tok_send, tok_recv, small_send, small_recv, head_send, head_recv,
    ) = refs
    outs = [three.at[0], three.at[1], three.at[2]]
    seq = 2 * outer
    at = lax.axis_index("seq")
    d = lax.axis_index("dp")
    me = d * seq + at
    z = at // 2
    x, y, core = near_partners()
    above, below = {"seq": at + 2}, {"seq": at - 2}
    has_above, has_below = z < outer - 1, z > 0
    greet_everyone(seq, dp)

    def push(r, where):
        return pltpu.make_async_remote_copy(
            src_ref=small, dst_ref=out_small.at[me], send_sem=small_send.at[r],
            recv_sem=small_recv.at[r], device_id=where, device_id_type=pl.DeviceIdType.MESH,
        )

    everyone(seq, dp, lambda r, where: push(r, where).start())
    head = heads.shape[2]

    def columns(owner):
        return w_out.at[:, pl.ds(pl.multiple_of(owner * head, head), head)]

    own_head = pltpu.make_async_copy(columns(d), heads.at[d], local_sem.at[5])
    own_head.start()
    other_heads = [
        send(
            columns(jnp.bitwise_xor(d, r)), heads.at[d], head_send.at[r], head_recv.at[r],
            {"dp": jnp.bitwise_xor(d, r)},
        )
        for r in range(1, dp)
    ]

    def up(m, k, src, origin):
        return pltpu.make_async_remote_copy(
            src_ref=src, dst_ref=outs[m].at[0, origin], send_sem=up_send.at[m, k],
            recv_sem=up_recv.at[m, k], device_id=above, device_id_type=pl.DeviceIdType.MESH,
        )

    def down(m, k, src, origin):
        return pltpu.make_async_remote_copy(
            src_ref=src, dst_ref=outs[m].at[0, origin], send_sem=down_send.at[m, k],
            recv_sem=down_recv.at[m, k], device_id=below, device_id_type=pl.DeviceIdType.MESH,
        )

    def across(m, src, origin):
        return pltpu.make_async_remote_copy(
            src_ref=src, dst_ref=outs[m].at[1, origin], send_sem=x_send.at[m, origin],
            recv_sem=x_recv.at[m, origin], device_id=x, device_id_type=pl.DeviceIdType.MESH,
        )

    for m in range(3):
        @pl.when(has_above)
        def _():
            up(m, 0, mats[m], z).start()

        @pl.when(has_below)
        def _():
            down(m, 0, mats[m], z).start()

        across(m, mats[m], z).start()
    tok_y, tok_rest = [], []
    for n, (tok, out_tok) in enumerate(zip(toks, out_toks)):
        tok_y.append(send(tok, out_tok.at[1], tok_send.at[3 * n], tok_recv.at[3 * n], y))
        tok_rest.append(
            send(tok, out_tok.at[2], tok_send.at[3 * n + 1], tok_recv.at[3 * n + 1], core)
        )
        copy = pltpu.make_async_copy(tok, out_tok.at[0], local_sem.at[1 + 5 * n])
        copy.start()
        tok_rest.append(copy)
    own_small = pltpu.make_async_copy(small, out_small.at[me], local_sem.at[0])
    own_small.start()
    own_mats = []
    for m in range(3):
        copy = pltpu.make_async_copy(mats[m], outs[m].at[0, z], local_sem.at[2 + m])
        copy.start()
        own_mats.append(copy)

    def pass_on(k, carry):
        for m in range(3):
            @pl.when(z - k >= 0)
            def _():
                slot = outs[m].at[0, z - k]
                up(m, k - 1, slot, z - k).wait_recv()

                @pl.when(has_above)
                def _():
                    up(m, k, slot, z - k).start()

                across(m, slot, z - k).start()

            @pl.when(z + k < outer)
            def _():
                slot = outs[m].at[0, z + k]
                down(m, k - 1, slot, z + k).wait_recv()

                @pl.when(has_below)
                def _():
                    down(m, k, slot, z + k).start()

                across(m, slot, z + k).start()

        return carry

    lax.fori_loop(1, outer, pass_on, 0)
    for n, out_tok in enumerate(out_toks):
        tok_y[n].wait()
        tok_rest.append(
            send(out_tok.at[1], out_tok.at[3], tok_send.at[3 * n + 2], tok_recv.at[3 * n + 2], core)
        )

    def arrived(r, where):
        push(r, where).wait_send()
        theirs = out_small.at[jnp.bitwise_xor(me, r)]
        pltpu.make_async_remote_copy(
            src_ref=theirs, dst_ref=theirs, send_sem=small_send.at[r],
            recv_sem=small_recv.at[r], device_id=where, device_id_type=pl.DeviceIdType.MESH,
        ).wait_recv()

    everyone(seq, dp, arrived)

    def complete(o, carry):
        for m in range(3):
            across(m, outs[m].at[0, o], o).wait()

            @pl.when(has_above & (o <= z))
            def _():
                up(m, o, outs[m].at[0, z], z).wait_send()

            @pl.when(has_below & (o <= outer - 1 - z))
            def _():
                down(m, o, outs[m].at[0, z], z).wait_send()

        return carry

    lax.fori_loop(0, outer, complete, 0)
    for copy in own_mats:
        copy.wait()
    own_head.wait()
    for r, copy in enumerate(other_heads, 1):
        copy.wait_send()
        theirs = heads.at[jnp.bitwise_xor(d, r)]
        pltpu.make_async_remote_copy(
            src_ref=theirs, dst_ref=theirs, send_sem=head_send.at[r],
            recv_sem=head_recv.at[r], device_id={"dp": jnp.bitwise_xor(d, r)},
            device_id_type=pl.DeviceIdType.MESH,
        ).wait_recv()
    own_small.wait()
    for copy in tok_rest:
        copy.wait()


def in_hbm():
    return pl.BlockSpec(memory_space=pl.ANY)


def in_vmem():
    return pl.BlockSpec(memory_space=pltpu.VMEM)


def gather_all(outer, dp, mats, toks, small, w_out):
    seq = 2 * outer
    rows, width = mats[0].shape
    dma = pltpu.SemaphoreType.DMA
    return pl.pallas_call(
        functools.partial(gather_kernel, outer, dp),
        in_specs=[in_vmem()] * 5 + [in_hbm()] * 2,
        out_specs=[in_hbm()] * 5,
        out_shape=[
            jax.ShapeDtypeStruct((3, 2, outer, rows, width), BF16),
            jax.ShapeDtypeStruct((dp, w_out.shape[0], w_out.shape[1] // dp), BF16),
            jax.ShapeDtypeStruct((dp,) + toks[0].shape, BF16),
            jax.ShapeDtypeStruct((dp,) + toks[1].shape, BF16),
            jax.ShapeDtypeStruct((seq * dp,) + small.shape, BF16),
        ],
        scratch_shapes=[dma((7,))] + [dma((3, outer))] * 6
        + [dma((6,))] * 2 + [dma((seq * dp,))] * 2 + [dma((dp,))] * 2,
        compiler_params=pltpu.CompilerParams(
            collective_id=1, has_side_effects=True, vmem_limit_bytes=VMEM_LIMIT
        ),
    )(*mats, *toks, small, w_out)


def feed_kernel(mid, grad_feed, w_down, w_act, w_lin, product, grad_gate, grad_lin):
    gate = mm(mid[...], w_act[0], 1, 1)
    lin = mm(mid[...], w_lin[0], 1, 1)
    grad_product = mm(grad_feed[...], w_down[0], 1, 1)
    sigma = jax.nn.sigmoid(gate)
    swish = gate * sigma
    product[...] = (swish * lin).astype(BF16)
    grad_gate[...] = (grad_product * lin * (sigma * (1.0 + gate * (1.0 - sigma)))).astype(BF16)
    grad_lin[...] = (grad_product * swish).astype(BF16)


def feed_back_kernel(
    product, grad_gate, grad_lin, w_down, w_act, w_lin, feed, grad_mid
):
    grad_mid[...] = (
        mm(grad_gate[...], w_act[0], 1, 0) + mm(grad_lin[...], w_lin[0], 1, 0)
    ).astype(BF16)
    feed[...] = mm(product[...], w_down[0], 1, 0).astype(BF16)


def feed_tiles(kernel, tiles, weights, widths):
    rows = tiles[0].shape[0]
    step = min(256, rows)
    _, units, width = weights.shape
    each = 2 * step * units * width

    def spec(columns):
        return pl.BlockSpec((step, columns), lambda t: (t, 0))

    def weight(at):
        return pl.BlockSpec(
            (1, units, width), lambda t: (at, 0, 0), pipeline_mode=pl.Buffered(1)
        )

    return pl.pallas_call(
        kernel,
        grid=(rows // step,),
        in_specs=[spec(x.shape[1]) for x in tiles] + [weight(m) for m in range(3)],
        out_specs=[spec(columns) for columns in widths],
        out_shape=[jax.ShapeDtypeStruct((rows, columns), BF16) for columns in widths],
        cost_estimate=pl.CostEstimate(
            flops=3 * each * (rows // step), bytes_accessed=6 * units * width + 8 * rows * width,
            transcendentals=rows * units,
        ),
        compiler_params=pltpu.CompilerParams(vmem_limit_bytes=VMEM_LIMIT),
    )(*tiles, weights, weights, weights)


def turned(x):
    row, col = grid_index(x.shape[1], x.shape[1])
    return mm_exact((row == col).astype(F32), x, 1, 1)


def flipped(x):
    size = x.shape[-1] // 4
    return jnp.concatenate([x[:, size * i : size * (i + 1)] for i in (1, 0, 3, 2)], axis=1)


def relay_kernel(outer, backward, *refs):
    if backward:
        totals, keeps, parts, gate_sent, refs = refs[0], refs[1], refs[2], refs[3], refs[4:]
        states, sums, gate_got, refs = refs[0], refs[1], refs[2], refs[3:]
        gate_s, gate_r = refs[-2:]
        side, refs = refs[-9:-2], refs[:-9]
    else:
        feats, decays, writes, refs = refs[0], refs[1], refs[2], refs[3:]
        states, keeps, refs = refs[0], refs[1], refs[2:]
    (
        own, to_x, from_x, to_z, from_z, to_back, from_back, keep_mine, keep_theirs,
        x_s, x_r, z_s, z_r, b_s, b_r, k_s, k_r,
    ) = refs
    half = own.shape[0]
    at = lax.axis_index("seq")
    inner, z = at % 2, at // 2
    x, y, core = near_partners()
    above, below = {"seq": at + 2}, {"seq": at - 2}
    has_above, has_below = z < outer - 1, z > 0
    ahead, has_ahead, has_source = (
        (below, has_below, has_above) if backward else (above, has_above, has_below)
    )
    barrier = greet([x, y, core] if backward else [x])

    @pl.when(has_above)
    def _():
        greet([above])

    @pl.when(has_below)
    def _():
        greet([below])

    pl.semaphore_wait(
        barrier,
        (3 if backward else 1) + has_above.astype(jnp.int32) + has_below.astype(jnp.int32),
    )

    def compute(s):
        if backward:
            return totals[s]
        width = feats.shape[2] // 3
        total, keep = summary(
            feats[s, :, :width], feats[s, :, 2 * width :], decays[s], writes[s]
        )
        keep_mine[s] = keep
        return total

    crossing = []
    for i in range(half):
        to_x[i] = compute((1 - inner) * half + i).astype(BF16)
        crossing.append(send(to_x.at[i], from_x.at[i], x_s.at[i], x_r.at[i], x))
    if backward:
        gate_copy = send(gate_sent, gate_got, gate_s.at[0], gate_r.at[0], x)
        side = plane_sum_start(parts, side, y, core)
    for i in range(half):
        own[i] = compute(inner * half + i)
    if backward:
        keep_a, keep_b = keeps[0], keeps[1]
    else:
        send(keep_mine, keep_theirs, k_s.at[0], k_r.at[0], x).wait()
        mine = jnp.concatenate([keep_mine[s] for s in range(2 * half)], axis=0)
        theirs = jnp.concatenate([keep_theirs[s] for s in range(2 * half)], axis=0)
        keep_a = jnp.where(inner == 0, mine, theirs)
        keep_b = jnp.where(inner == 0, theirs, mine)
        keeps[0] = keep_a
        keeps[1] = keep_b
    if backward:
        keep_a, keep_b = keep_b, keep_a
    first_k = turned(jnp.where(inner == 0, keep_a[:half], keep_a[half:]))
    second_k = turned(jnp.where(inner == 0, keep_b[:half], keep_b[half:]))
    is_first = (inner == 1) if backward else (inner == 0)

    def along(i):
        return pltpu.make_async_remote_copy(
            src_ref=to_z.at[i], dst_ref=from_z.at[i], send_sem=z_s.at[i], recv_sem=z_r.at[i],
            device_id=ahead, device_id_type=pl.DeviceIdType.MESH,
        )

    returning = []
    for i in range(half):
        crossing[i].wait()

        @pl.when(jnp.logical_not(has_source))
        def _():
            from_z[i] = jnp.zeros_like(from_z[i])

        @pl.when(has_source)
        def _():
            along(i).wait_recv()

        got = flipped(from_x[i]).astype(F32)
        mine = own[i]
        first = jnp.where(is_first, mine, got)
        second = jnp.where(is_first, got, mine)
        entering = from_z[i].astype(F32)
        after = first_k[:, i : i + 1] * entering + first
        to_z[i] = (second_k[:, i : i + 1] * after + second).astype(BF16)

        @pl.when(has_ahead)
        def _():
            along(i).start()

        states[inner * half + i] = jnp.where(is_first, entering, after).astype(BF16)
        to_back[i] = jnp.where(is_first, after, entering).astype(BF16)
        returning.append(send(to_back.at[i], from_back.at[i], b_s.at[i], b_r.at[i], x))
    for i in range(half):
        returning[i].wait()
        states[(1 - inner) * half + i] = flipped(from_back[i])

        @pl.when(has_ahead)
        def _():
            along(i).wait_send()

    if backward:
        plane_sum_end(parts, sums, side)
        gate_copy.wait()


def plane_sum_start(parts, side, y, core):
    from_core, to_y, from_y, core_s, core_r, y_s, y_r = side
    rows = parts.shape[1]
    size = rows // CHUNKS
    cuts = [pl.ds(c * size, size) for c in range(CHUNKS)]
    first = [
        send(parts.at[pl.ds(4, 4), cut], from_core.at[:, cut], core_s.at[c], core_r.at[c], core)
        for c, cut in enumerate(cuts)
    ]
    second = []
    for c, cut in enumerate(cuts):
        first[c].wait()

        for j in range(2):
            to_y[j, cut] = parts[2 + j, cut] + from_core[2 + j, cut]
        second.append(send(to_y.at[:, cut], from_y.at[:, cut], y_s.at[c], y_r.at[c], y))
    return from_core, from_y, second


def plane_sum_end(parts, sums, side):
    from_core, from_y, second = side
    size = parts.shape[1] // CHUNKS
    for c in range(CHUNKS):
        second[c].wait()

        def add(r, carry, c=c):
            at = pl.ds(c * size + r * STRIP, STRIP)
            for j in range(2):
                sums[j, at] = (
                    parts[j, at].astype(F32) + from_core[j, at].astype(F32)
                    + from_y[j, at].astype(F32)
                ).astype(BF16)
            return carry

        lax.fori_loop(0, size // STRIP, add, 0)


def relay(outer, backward, inputs, sequences, slots, width):
    half = sequences // 2
    dma = pltpu.SemaphoreType.DMA
    held = pltpu.VMEM((half, slots, width), BF16)
    states = jax.ShapeDtypeStruct((sequences, slots, width), BF16)
    keeps = jax.ShapeDtypeStruct((2, sequences, slots), F32)
    keep = pltpu.VMEM((sequences, 1, slots), F32)
    outs, side = [states, keeps], []
    if backward:
        rows, columns = inputs[2].shape[1:]
        outs = [states, jax.ShapeDtypeStruct((2, rows, columns), BF16)]
        outs.append(jax.ShapeDtypeStruct(inputs[3].shape, BF16))
        side = [
            pltpu.VMEM((4, rows, columns), BF16), pltpu.VMEM((2, rows, columns), BF16),
            pltpu.VMEM((2, rows, columns), BF16),
        ] + [dma((CHUNKS,))] * 4 + [dma((1,))] * 2
    return pl.pallas_call(
        functools.partial(relay_kernel, outer, backward),
        in_specs=[in_vmem()] * 3 + [in_hbm()] * (len(inputs) - 3),
        out_specs=[in_vmem()] * 2 + [in_hbm()] * (len(outs) - 2),
        out_shape=outs,
        scratch_shapes=[pltpu.VMEM((half, slots, width), F32)] + [held] * 6 + [keep] * 2
        + [dma((half,))] * 6 + [dma((1,))] * 2 + side,
        compiler_params=pltpu.CompilerParams(
            collective_id=7 if backward else 6, has_side_effects=True,
            vmem_limit_bytes=VMEM_LIMIT,
        ),
    )(*inputs)


def middle_kernel(
    parts, tok, gain, extra, hidden, mid, extra_all, from_core, to_y, from_y, normed,
    core_s, core_r, y_s, y_r, local_sem, gx_s, gx_r, gy_s, gy_r, gd_s, gd_r,
    ex_s, ex_r, ed_s, ed_r, extra_sem, gc_s, gc_r, ec_s, ec_r,
):
    rows = tok.shape[0]
    size = rows // CHUNKS
    x, y, core = near_partners()
    pl.semaphore_wait(greet([x, y, core]), 3)
    cuts = [pl.ds(c * size, size) for c in range(CHUNKS)]
    first = [
        send(parts.at[pl.ds(2, 2), cut], from_core.at[:, cut], core_s.at[c], core_r.at[c], core)
        for c, cut in enumerate(cuts)
    ]
    second = []
    for c, cut in enumerate(cuts):
        first[c].wait()

        to_y[cut] = parts[1, cut] + from_core[1, cut]
        second.append(send(to_y.at[cut], from_y.at[cut], y_s.at[c], y_r.at[c], y))
    rest = []
    for j in range(4):
        copy = pltpu.make_async_copy(extra.at[j], extra_all.at[2 * j], extra_sem.at[j])
        copy.start()
        rest.append(copy)
    extra_x = [
        send(extra.at[0, cut], extra_all.at[1, cut], ex_s.at[c], ex_r.at[c], x)
        for c, cut in enumerate(cuts)
    ]
    over_x, over_y, diagonal = [], [], []
    for c in range(CHUNKS + 2):
        if c < CHUNKS:
            cut = cuts[c]
            second[c].wait()

            def norm(r, carry, c=c):
                at = pl.ds(c * size + r * STRIP, STRIP)
                total = tok[at].astype(F32) + (
                    (parts[0, at].astype(F32) + from_core[0, at].astype(F32))
                    + from_y[at].astype(F32)
                )
                hidden[at] = total
                normed[at] = (total * rms_scale(total) * gain[...]).astype(BF16)
                return carry

            lax.fori_loop(0, size // STRIP, norm, 0)
            over_y.append(send(normed.at[cut], mid.at[2, cut], gy_s.at[c], gy_r.at[c], y))
            over_x.append(send(normed.at[cut], mid.at[1, cut], gx_s.at[c], gx_r.at[c], x))
            rest.append(send(normed.at[cut], mid.at[4, cut], gc_s.at[0, c], gc_r.at[0, c], core))
            own = pltpu.make_async_copy(normed.at[cut], mid.at[0, cut], local_sem.at[c])
            own.start()
            rest.append(own)
        if c >= 2:
            at, cut = c - 2, cuts[c - 2]
            over_y[at].wait()
            diagonal.append(send(mid.at[2, cut], mid.at[3, cut], gd_s.at[at], gd_r.at[at], x))
            rest.append(send(mid.at[2, cut], mid.at[6, cut], gc_s.at[2, at], gc_r.at[2, at], core))
    extra_d = []
    for c, cut in enumerate(cuts):
        extra_x[c].wait()
        extra_d.append(
            send(extra_all.at[1, cut], extra_all.at[3, cut], ed_s.at[c], ed_r.at[c], y)
        )
        over_x[c].wait()
        rest.append(send(mid.at[1, cut], mid.at[5, cut], gc_s.at[1, c], gc_r.at[1, c], core))
    rest.append(send(extra_all.at[1], extra_all.at[5], ec_s.at[0], ec_r.at[0], core))
    for c, cut in enumerate(cuts):
        diagonal[c].wait()
        rest.append(send(mid.at[3, cut], mid.at[7, cut], gc_s.at[3, c], gc_r.at[3, c], core))
    for copy in extra_d:
        copy.wait()
    rest.append(send(extra_all.at[3], extra_all.at[7], ec_s.at[1], ec_r.at[1], core))
    for copy in rest:
        copy.wait()


def middle(parts, tok, gain, extra):
    rows, width = tok.shape
    dma = pltpu.SemaphoreType.DMA
    buffer = pltpu.VMEM((rows, width), BF16)
    return pl.pallas_call(
        middle_kernel,
        in_specs=[in_vmem()] * 4,
        out_specs=[in_vmem(), in_hbm(), in_hbm()],
        out_shape=[
            jax.ShapeDtypeStruct((rows, width), F32),
            jax.ShapeDtypeStruct((8, rows, width), BF16),
            jax.ShapeDtypeStruct((8, rows, width), BF16),
        ],
        scratch_shapes=[pltpu.VMEM((2, rows, width), BF16), buffer, buffer, buffer]
        + [dma((CHUNKS,))] * 15
        + [dma((4,))]
        + [dma((4, CHUNKS))] * 2
        + [dma((2,))] * 2,
        compiler_params=pltpu.CompilerParams(
            collective_id=2, has_side_effects=True, vmem_limit_bytes=VMEM_LIMIT
        ),
    )(parts, tok, gain, extra)


def middle_back_kernel(
    parts, hidden, grad_out, gain, grad_hidden, gain_grad, attn,
    from_core, to_x, from_x, to_y, from_y, rounded,
    core_s, core_r, x_s, x_r, y_s, y_r, local_sem, gy_s, gy_r, gc_s, gc_r,
):
    rows, width = hidden.shape
    size = rows // CHUNKS
    x, y, core = near_partners()
    pl.semaphore_wait(greet([x, y, core]), 3)
    cuts = [pl.ds(c * size, size) for c in range(CHUNKS)]
    first = [
        send(parts.at[pl.ds(4, 4), cut], from_core.at[:, cut], core_s.at[c], core_r.at[c], core)
        for c, cut in enumerate(cuts)
    ]
    second, third = [], []
    for c, cut in enumerate(cuts):
        first[c].wait()

        for j in range(2):
            to_x[j, cut] = parts[2 * j + 1, cut] + from_core[2 * j + 1, cut]
        second.append(send(to_x.at[:, cut], from_x.at[:, cut], x_s.at[c], x_r.at[c], x))
    gain_grad[...] = jnp.zeros_like(gain_grad)
    pending, over_y = [], []
    for step in range(CHUNKS + 2):
        if step < CHUNKS:
            c, cut = step, cuts[step]
            second[c].wait()

            def add_x(r, carry, c=c):
                at = pl.ds(c * size + r * STRIP, STRIP)
                to_y[at] = (
                    parts[2, at].astype(F32) + from_core[2, at].astype(F32)
                    + from_x[1, at].astype(F32)
                ).astype(BF16)
                return carry

            lax.fori_loop(0, size // STRIP, add_x, 0)
            third.append(send(to_y.at[cut], from_y.at[cut], y_s.at[c], y_r.at[c], y))
        if 1 <= step <= CHUNKS:
            c, cut = step - 1, cuts[step - 1]
            third[c].wait()

            def back(r, carry, c=c):
                at = pl.ds(c * size + r * STRIP, STRIP)
                grad_mid = (
                    (parts[0, at].astype(F32) + from_core[0, at].astype(F32))
                    + from_x[0, at].astype(F32)
                ) + from_y[at].astype(F32)
                value = hidden[at]
                scale = rms_scale(value)
                unit = value * scale
                gain_grad[...] += jnp.sum(grad_mid * unit, axis=0, keepdims=True)
                scaled = grad_mid * gain[...]
                total = grad_out[at] + scale * (
                    scaled - unit * jnp.mean(scaled * unit, axis=1, keepdims=True)
                )
                grad_hidden[at] = total
                rounded[at] = total.astype(BF16)
                return carry

            lax.fori_loop(0, size // STRIP, back, 0)
            over_y.append(send(rounded.at[cut], attn.at[1, cut], gy_s.at[c], gy_r.at[c], y))
            pending.append(
                send(rounded.at[cut], attn.at[2, cut], gc_s.at[0, c], gc_r.at[0, c], core)
            )
            own = pltpu.make_async_copy(rounded.at[cut], attn.at[0, cut], local_sem.at[c])
            own.start()
            pending.append(own)
        if step >= 2:
            c, cut = step - 2, cuts[step - 2]
            over_y[c].wait()
            pending.append(
                send(attn.at[1, cut], attn.at[3, cut], gc_s.at[1, c], gc_r.at[1, c], core)
            )
    for copy in pending:
        copy.wait()


def middle_back(parts, hidden, grad_out, gain):
    rows, width = hidden.shape
    dma = pltpu.SemaphoreType.DMA

    def buffer(*lead):
        return pltpu.VMEM(lead + (rows, width), BF16)

    return pl.pallas_call(
        middle_back_kernel,
        in_specs=[in_vmem()] * 4,
        out_specs=[in_vmem(), in_vmem(), in_hbm()],
        out_shape=[
            jax.ShapeDtypeStruct((rows, width), F32),
            jax.ShapeDtypeStruct((1, width), F32),
            jax.ShapeDtypeStruct((4, rows, width), BF16),
        ],
        scratch_shapes=[buffer(4), buffer(2), buffer(2), buffer(), buffer(), buffer()]
        + [dma((CHUNKS,))] * 9
        + [dma((2, CHUNKS))] * 2,
        compiler_params=pltpu.CompilerParams(
            collective_id=3, has_side_effects=True, vmem_limit_bytes=VMEM_LIMIT
        ),
    )(parts, hidden, grad_out, gain)


def final_kernel(
    outer, dp, mats, gates, pre_hbm, gate_hbm, kqv_hbm, g_hbm, grad_rank, w_rank, tok,
    base, gain, small, *refs,
):
    out, tokens_grad, out_small, refs = refs[0], refs[1], refs[2], refs[3:]
    (
        grad_pre, grad_gate, w_kqv, w_g,
        from_x, from_below, from_above, total, parts, from_core, to_y, from_y, gain_grad,
        to_all, from_all,
        load, x_s, x_r, up_s, up_r, down_s, down_r, core_s, core_r, y_s, y_r, all_s, all_r,
    ) = refs
    rows, width = tok.shape
    size = rows // CHUNKS
    high = total.shape[2]
    seq = 2 * outer
    at = lax.axis_index("seq")
    me = lax.axis_index("dp") * seq + at
    z = at // 2
    x, y, core = near_partners()
    above, below = {"seq": at + 2}, {"seq": at - 2}
    has_above, has_below = z < outer - 1, z > 0
    greet_everyone(seq, dp)

    def block_of(i):
        ups = outer - 1 - z
        up_at = jnp.where(z < outer // 2, i, i - z)
        down_at = jnp.where(z < outer // 2, i - ups, i)
        is_up = (up_at >= 0) & (up_at < ups)
        block = jnp.where(is_up, outer - 1 - up_at, down_at)
        return jnp.where(i == outer - 1, z, block)

    def across(m, b):
        return pltpu.make_async_remote_copy(
            src_ref=mats.at[m, 1, b], dst_ref=from_x.at[m, b], send_sem=x_s.at[m, b],
            recv_sem=x_r.at[m, b], device_id=x, device_id_type=pl.DeviceIdType.MESH,
        )

    def up(m, b):
        return pltpu.make_async_remote_copy(
            src_ref=total.at[m, b], dst_ref=from_below.at[m, b], send_sem=up_s.at[m, b],
            recv_sem=up_r.at[m, b], device_id=above, device_id_type=pl.DeviceIdType.MESH,
        )

    def down(m, b):
        return pltpu.make_async_remote_copy(
            src_ref=total.at[m, b], dst_ref=from_above.at[m, b], send_sem=down_s.at[m, b],
            recv_sem=down_r.at[m, b], device_id=below, device_id_type=pl.DeviceIdType.MESH,
        )

    for m in range(3):
        across(m, block_of(0)).start()
    operands = [
        pltpu.make_async_copy(src, dst, load.at[4 + n])
        for n, (src, dst) in enumerate(
            [(pre_hbm, grad_pre), (gate_hbm, grad_gate), (kqv_hbm, w_kqv), (g_hbm, w_g)]
        )
    ]
    loads = [
        pltpu.make_async_copy(mats.at[m, 0] if m < 3 else gates, total.at[m], load.at[m])
        for m in range(4)
    ]
    for copy in operands + loads:
        copy.start()
    for copy in operands:
        copy.wait()

    def grad_in(g):
        some = pl.ds(g * rows, rows)
        parts[g] = (
            mm(grad_pre[some], w_kqv[...], 1, 0)
            + (mm(grad_gate[some], w_g[...], 1, 0) + mm(grad_rank[some], w_rank[...], 1, 1))
        ).astype(BF16)

    grad_in(3)
    first = send(parts.at[3], from_core.at[1], core_s.at[1], core_r.at[1], core)
    grad_in(1)
    first.wait()

    to_y[...] = parts[1] + from_core[1]

    def over_y():
        return pltpu.make_async_remote_copy(
            src_ref=to_y, dst_ref=from_y, send_sem=y_s.at[0], recv_sem=y_r.at[0], device_id=y,
            device_id_type=pl.DeviceIdType.MESH,
        )

    over_y().start()
    grad_in(2)
    first = send(parts.at[2], from_core.at[0], core_s.at[0], core_r.at[0], core)
    grad_in(0)
    first.wait()
    gain_grad[...] = jnp.zeros_like(gain_grad)
    for copy in loads:
        copy.wait()

    def back(c):
        def strip_back(r, carry):
            strip = pl.ds(pl.multiple_of(c * size + r * STRIP, STRIP), STRIP)
            grad = (
                parts[0, strip].astype(F32) + from_core[0, strip].astype(F32)
            ) + from_y[strip].astype(F32)
            value = tok[strip].astype(F32)
            scale = rms_scale(value)
            unit = value * scale
            gain_grad[...] += jnp.sum(grad * unit, axis=0, keepdims=True)
            scaled = grad * gain[...]
            tokens_grad[strip] = base[strip] + scale * (
                scaled - unit * jnp.mean(scaled * unit, axis=1, keepdims=True)
            )
            return carry

        lax.fori_loop(0, size // STRIP, strip_back, 0)

    def add_into(m, b, other):
        total[m, b] = total[m, b] + other[m, b]

    def reduce_block(i, carry):
        b = block_of(i)
        for m in (3, 0, 1, 2):
            if m < 3:
                across(m, b).wait()

                @pl.when(i + 1 < outer)
                def _():
                    across(m, block_of(i + 1)).start()

                add_into(m, b, from_x)

            @pl.when(b > z)
            def _():
                @pl.when(has_below)
                def _():
                    up(m, b).wait_recv()
                    add_into(m, b, from_below)

                up(m, b).start()

            @pl.when(b < z)
            def _():
                @pl.when(has_above)
                def _():
                    down(m, b).wait_recv()
                    add_into(m, b, from_above)

                down(m, b).start()

            if m < 3:
                turn = 2 * (3 * (i - 1) + m)
                if m == 0:
                    @pl.when(i == 1)
                    def _():
                        over_y().wait()

                @pl.when((turn >= 0) & (turn < CHUNKS))
                def _():
                    back(turn)
                    back(turn + 1)

        return carry

    lax.fori_loop(0, outer - 1, reduce_block, 0)
    devices = seq * dp
    each = width // devices
    row, col = grid_index(devices, width)
    spread = jnp.where(col // each == row, gain_grad[...], 0.0)
    picked_row, picked_col = grid_index(width, 128)
    gathered = mm_exact(spread, ((picked_row % each) == picked_col).astype(F32), 1, 0)
    height = small.shape[1]
    to_all[:, :height] = small[...]
    to_all[:, height:] = jnp.broadcast_to(
        gathered.reshape(devices, 1, 128), (devices, to_all.shape[1] - height, 128)
    )

    def push(r, where):
        return pltpu.make_async_remote_copy(
            src_ref=to_all.at[jnp.bitwise_xor(me, r)], dst_ref=from_all.at[r],
            send_sem=all_s.at[r], recv_sem=all_r.at[r], device_id=where,
            device_id_type=pl.DeviceIdType.MESH,
        )

    everyone(seq, dp, lambda r, where: push(r, where).start())
    lax.fori_loop(outer - 1, outer, reduce_block, 0)
    out_small[...] = to_all[me]

    def add_small(r, where):
        push(r, where).wait()
        out_small[...] += from_all[r]

    everyone(seq, dp, add_small)
    for m in range(4):
        out[m] = total[m, z].astype(F32)

        @pl.when(has_below)
        def _():
            up(m, z).wait_recv()
            out[m] += from_below[m, z].astype(F32)

        @pl.when(has_above)
        def _():
            down(m, z).wait_recv()
            out[m] += from_above[m, z].astype(F32)

    def sent(b, carry):
        for m in range(4):
            @pl.when(b > z)
            def _():
                up(m, b).wait_send()

            @pl.when(b < z)
            def _():
                down(m, b).wait_send()

        return carry

    lax.fori_loop(0, outer, sent, 0)


def finish(outer, dp, mats, gates, operands, rest, small):
    rows, width = rest[-3].shape
    high = mats.shape[3]
    devices = 2 * outer * dp
    dma = pltpu.SemaphoreType.DMA
    blocks = pltpu.VMEM((4, outer, high, width), BF16)
    buffer = pltpu.VMEM((rows, width), BF16)
    payload = (small.shape[1] + 8, 128)
    return pl.pallas_call(
        functools.partial(final_kernel, outer, dp),
        in_specs=[in_hbm()] * (2 + len(operands)) + [in_vmem()] * (len(rest) + 1),
        out_specs=[in_vmem()] * 3,
        out_shape=[
            jax.ShapeDtypeStruct((4, high, width), F32),
            jax.ShapeDtypeStruct((rows, width), F32),
            jax.ShapeDtypeStruct(payload, F32),
        ],
        scratch_shapes=[pltpu.VMEM(x.shape, BF16) for x in operands]
        + [pltpu.VMEM((3, outer, high, width), BF16)]
        + [blocks] * 3
        + [
            pltpu.VMEM((4, rows, width), BF16), pltpu.VMEM((2, rows, width), BF16), buffer,
            buffer, pltpu.VMEM((1, width), F32),
            pltpu.VMEM((devices,) + payload, F32), pltpu.VMEM((devices,) + payload, F32),
            dma((8,)),
        ]
        + [dma((4, outer))] * 6
        + [dma((2,))] * 2
        + [dma((1,))] * 2
        + [dma((devices,))] * 2,
        compiler_params=pltpu.CompilerParams(
            collective_id=4, has_side_effects=True, vmem_limit_bytes=60 * 1024 * 1024
        ),
    )(mats, gates, *operands, *rest, small)


class Lanes:
    def __init__(self):
        self.seq = lax.axis_size("seq")
        self.dp = lax.axis_size("dp")
        self.outer = self.seq // 2
        self.at = lax.axis_index("seq")
        self.d = lax.axis_index("dp")
        self.inner_at = lax.rem(self.at, 2)
        self.outer_at = self.at // 2
        self.groups = [[2 * k + i for k in range(self.outer)] for i in range(2)]

    def swap_inner(self, x):
        return lax.ppermute(x, "seq", [(i, i ^ 1) for i in range(self.seq)])

    def gather_outer(self, x):
        return lax.all_gather(x, "seq", axis=0, tiled=True, axis_index_groups=self.groups)

    def scatter_outer(self, x):
        return lax.psum_scatter(
            x, "seq", scatter_dimension=0, tiled=True, axis_index_groups=self.groups
        )

    def swap_dp(self, x, bit):
        return lax.ppermute(x, "dp", [(i, i ^ bit) for i in range(self.dp)])

    def swap_seq(self, x, bit):
        return lax.ppermute(x, "seq", [(i, i ^ bit) for i in range(self.seq)])

    def exchange_heads(self, blocks):
        got = [lax.dynamic_index_in_dim(blocks, self.d, 0, keepdims=False)]
        for r in range(1, self.dp):
            part = lax.dynamic_index_in_dim(
                blocks, jnp.bitwise_xor(self.d, r), 0, keepdims=False
            )
            got.append(self.swap_dp(part, r))
        bit = 1
        while bit < self.dp:
            is_set = (self.d // bit) % 2 == 1
            got = [jnp.where(is_set, got[i ^ bit], got[i]) for i in range(self.dp)]
            bit *= 2
        return jnp.stack(got)

    def pick(self, natural, axis):
        first = lax.index_in_dim(natural, 0, axis, keepdims=False)
        second = lax.index_in_dim(natural, 1, axis, keepdims=False)
        even = self.inner_at == 0
        return jnp.where(even, first, second), jnp.where(even, second, first)


def swap_halves(x, parts):
    size = x.shape[-1] // (2 * parts)
    pieces = [x[..., i * size : (i + 1) * size] for i in range(2 * parts)]
    order = [i ^ 1 for i in range(2 * parts)]
    return jnp.concatenate([pieces[i] for i in order], axis=-1)


def per_device(
    tokens, lengths, cotangent, mixer_gain, feed_gain, head_gain, w_query, w_key, w_value,
    w_gate, w_out, rank_down, rank_up, rank_bias, w_act, w_lin, w_down,
):
    lanes = Lanes()
    seq_count, piece, width = tokens.shape
    rows = seq_count * piece
    sequences = lanes.dp * seq_count
    all_rows = lanes.dp * rows
    head_width = width // HEADS
    half_width = head_width // 2
    rank = rank_down.shape[1]
    devices = lanes.dp * lanes.seq

    counts = lengths.astype(F32)
    high = jnp.floor(counts / 256.0)
    small_parts = [
        mixer_gain, feed_gain, head_gain, rank_down.reshape(-1), rank_up.reshape(-1),
        rank_bias, high.astype(BF16), (counts - 256.0 * high).astype(BF16),
    ]
    sizes = [p.shape[0] for p in small_parts]
    used = sum(sizes)
    padded = -(-used // 2048) * 2048
    small = jnp.concatenate(small_parts + [jnp.zeros((padded - used,), BF16)])
    own_tokens = tokens.reshape(rows, width)
    position = (lanes.at * piece + jnp.arange(piece)).astype(F32)
    alive_own = (position[None, :] < counts[:, None]).astype(F32).reshape(rows, 1)
    grad_out = cotangent.reshape(rows, width).astype(F32) * alive_own
    w_kqv, out_mine, plane_tokens, grad_feed, smalls = gather_all(
        lanes.outer, lanes.dp, [w_key, w_query, w_value], [own_tokens, grad_out.astype(BF16)],
        small.reshape(-1, 128), w_out,
    )
    w_kqv = w_kqv.reshape(3 * head_width, width)
    out_rows = w_out.shape[0]
    out_own, out_other = lanes.pick(
        out_mine.reshape(lanes.dp, out_rows, lanes.outer, 2, -1), 3
    )
    out_mine = jnp.concatenate(
        [
            out_own.reshape(lanes.dp, out_rows, half_width),
            out_other.reshape(lanes.dp, out_rows, half_width),
        ],
        axis=2,
    )
    gate_and_out = lanes.gather_outer(
        jnp.concatenate([w_gate, out_mine.reshape(out_rows, width)], axis=0)
    )
    smalls = smalls.reshape(devices, padded)
    cuts, offset = [], 0
    for size in sizes:
        cuts.append(smalls[:, offset : offset + size])
        offset += size
    mixer_full = cuts[0].reshape(1, width).astype(F32)
    feed_full = cuts[1].reshape(1, width).astype(F32)
    head_natural = cuts[2].reshape(lanes.outer, 2, half_width // lanes.outer)
    head_own, head_other = lanes.pick(head_natural, 1)
    head_full = jnp.concatenate(
        [head_own.reshape(1, half_width), head_other.reshape(1, half_width)], axis=1
    ).astype(F32)
    down_full = cuts[3].reshape(width, rank)
    up_mine = lax.dynamic_index_in_dim(
        cuts[4].reshape(lanes.dp, SLOTS, rank), lanes.d, 0, keepdims=False
    )
    bias_mine = lax.dynamic_index_in_dim(
        cuts[5].reshape(lanes.dp, 1, SLOTS), lanes.d, 0, keepdims=False
    ).astype(F32)
    all_lengths = cuts[6].astype(F32) * 256.0 + cuts[7].astype(F32)
    all_lengths = all_lengths.reshape(lanes.dp, lanes.seq, seq_count)[:, 0]

    group_lengths = jnp.concatenate(
        [
            lax.dynamic_index_in_dim(
                all_lengths, jnp.bitwise_xor(lanes.d, r), 0, keepdims=False
            )
            for r in (0, 2, 1, 3)
        ]
    )
    alive = (position[None, :] < group_lengths[:, None]).astype(F32).reshape(all_rows, 1)

    sources = plane_tokens.reshape(all_rows, width).astype(F32)
    normed_in = lax.optimization_barrier(
        (sources * rms_scale(sources) * mixer_full).astype(BF16)
    )

    pre = contract_last(normed_in, w_kqv)
    low_rank = mm(normed_in, down_full, 1, 0).astype(BF16)
    gate_logit = contract_last(low_rank, up_mine) + bias_mine
    log_decay = jax.nn.log_sigmoid(gate_logit) / GATE_NORM * alive
    writes = -jnp.expm1(log_decay)

    def seqs(x):
        return x.reshape(sequences, piece, x.shape[1])

    def flat(x):
        return x.reshape(all_rows, x.shape[2])

    is_value = jnp.arange(3 * head_width) >= 2 * head_width
    feats = seqs(jnp.where(is_value, pre, pre * jax.nn.sigmoid(pre)).astype(BF16))
    pre = seqs(pre)
    decays, writes = seqs(log_decay), seqs(writes)

    def shaped(like_rows, columns, kind):
        return jax.ShapeDtypeStruct((sequences, like_rows, columns), kind)

    gate_and_out, feats = lax.optimization_barrier((gate_and_out, feats))
    keys, queries, values = (feats, 0), (feats, 1), (feats, 2)
    state_in, keeps = relay(
        lanes.outer, False, [feats, decays, writes], sequences, SLOTS, 2 * head_width
    )
    feed = jnp.stack([w_down, w_act, w_lin])
    feed, state_in, gate_and_out = lax.optimization_barrier((feed, state_in, gate_and_out))
    feed = lax.all_gather(
        feed, "seq", axis=1, tiled=True, axis_index_groups=lanes.groups
    )
    gate_and_out = gate_and_out.reshape(lanes.outer, 2, out_rows, width)
    gate_own, out_own = gate_and_out[:, 0], gate_and_out[:, 1]
    gate_other = lanes.swap_inner(gate_own)
    w_g = jnp.concatenate([gate_own, gate_other], axis=0).reshape(head_width, width)
    gates = seqs(contract_last(normed_in, w_g))
    out_own = out_own.reshape(lanes.outer, lanes.dp, out_rows, head_width)
    out_other = swap_halves(lanes.swap_inner(out_own), 1)
    even = lanes.inner_at == 0
    natural = jnp.stack(
        [jnp.where(even, out_own, out_other), jnp.where(even, out_other, out_own)], axis=2
    )
    out_full = natural.transpose(1, 0, 2, 3, 4).reshape(width, head_width)
    mixed, slot_out, attend = per_sequence(
        forward_kernel,
        [queries, keys, values, gates, decays, writes, state_in],
        [
            shaped(piece, head_width, BF16),
            shaped(piece, head_width, F32),
            shaped(piece, SLOTS, F32),
        ],
        shared=[head_full],
    )
    mixed_flat = flat(mixed)
    parts = contract_last(mixed_flat, out_full).astype(BF16)
    hidden, normed_mid, grad_feed = middle(
        parts.reshape(4, rows, width), own_tokens, feed_full, grad_feed
    )
    normed_mid = normed_mid.reshape(8 * rows, width)
    grad_feed = grad_feed.reshape(8 * rows, width)

    units = feed.shape[1]
    product, grad_gate, grad_lin = feed_tiles(
        feed_kernel, [normed_mid, grad_feed], feed, [units] * 3
    )
    feed_grads = jnp.stack(
        [
            contract_first(product, grad_feed).astype(BF16),
            contract_first(grad_gate, normed_mid).astype(BF16),
            contract_first(grad_lin, normed_mid).astype(BF16),
        ]
    )
    product, grad_gate, grad_lin, feed_grads = lax.optimization_barrier(
        (product, grad_gate, grad_lin, feed_grads)
    )
    feed_grads = lax.psum_scatter(
        feed_grads, "seq", scatter_dimension=1, tiled=True, axis_index_groups=lanes.groups
    )
    feed_parts, mid_parts = feed_tiles(
        feed_back_kernel, [product, grad_gate, grad_lin], feed, [width] * 2
    )
    grad_hidden, feed_gain_part, grad_attn = middle_back(
        mid_parts.reshape(8, rows, width), hidden, grad_out, feed_full
    )
    grad_attn = grad_attn.reshape(all_rows, width)
    feed_parts, grad_attn = lax.optimization_barrier((feed_parts, grad_attn))

    grad_mixed = mm(grad_attn, out_full, 1, 0)
    grad_gate_pre, grad_slot, grad_scores, adjoint, head_parts = per_sequence(
        back_first_kernel,
        [seqs(grad_mixed), gates, slot_out, attend, queries, values, decays, writes, state_in],
        [
            shaped(piece, head_width, BF16),
            shaped(piece, head_width, BF16),
            shaped(piece, SLOTS, F32),
            shaped(SLOTS, 2 * head_width, F32),
            shaped(1, head_width, F32),
        ],
        shared=[head_full],
    )
    grad_gate_flat = flat(grad_gate_pre)
    out_grad = contract_first(grad_attn, mixed_flat).astype(BF16)
    out_grad = out_grad.reshape(lanes.dp, lanes.outer, 2, out_rows, head_width)
    own_part, other_part = lanes.pick(out_grad, 2)
    got = swap_halves(lanes.swap_inner(other_part), 1)
    out_sum = (own_part.astype(F32) + got.astype(F32)).astype(BF16).transpose(1, 0, 2, 3)
    gate_grad = contract_first(grad_gate_flat, normed_in).astype(BF16)
    adjoint, out_sum, gate_grad, feed_parts = lax.optimization_barrier(
        (adjoint, out_sum, gate_grad, feed_parts)
    )
    adjoint_in, feed_sums, gate_got = relay(
        lanes.outer, True,
        [adjoint, keeps, feed_parts.reshape(8, rows, width), gate_grad[half_width:]], sequences,
        SLOTS, 2 * head_width,
    )
    gate_grad, out_sum, adjoint_in, feed_grads = lax.optimization_barrier(
        (gate_grad, out_sum, adjoint_in, feed_grads)
    )
    out_mine = lanes.scatter_outer(out_sum.reshape(-1, head_width))
    grad_pre, grad_logit = per_sequence(
        back_second_kernel,
        [
            grad_slot, grad_scores, attend, queries, keys, values, decays, writes,
            state_in, adjoint_in, (pre, 1), (pre, 0), seqs(gate_logit), seqs(alive),
        ],
        [shaped(piece, 3 * head_width, BF16), shaped(piece, SLOTS, BF16)],
    )
    feed_got = lanes.swap_inner(feed_sums[1])
    grad_pre, out_mine = lax.optimization_barrier((flat(grad_pre), out_mine))
    grad_logit = flat(grad_logit)
    bias_part = jnp.sum(grad_logit.astype(F32), axis=0)
    up_part = contract_first(grad_logit, low_rank)
    grad_rank = mm(grad_logit, up_mine, 1, 0).astype(BF16)
    down_part = contract_first(normed_in, grad_rank)

    mixer_grads = contract_first(grad_pre, normed_in).astype(BF16)
    mixer_grads = mixer_grads.reshape(3, 2, lanes.outer, -1, width)

    head_part = jnp.sum(head_parts, axis=(0, 1)).reshape(2, lanes.outer, -1)
    low_half, high_half = lanes.pick(head_part, 0)
    head_part = jnp.stack([low_half, high_half], axis=1)
    mine = (jnp.arange(lanes.dp) == lanes.d).astype(F32)
    up_all = mine[:, None] * up_part.reshape(1, -1)
    bias_all = mine[:, None] * bias_part.reshape(1, -1)
    parts = [
        feed_gain_part.reshape(devices, -1),
        head_part.reshape(devices, -1),
        down_part.reshape(devices, -1),
        up_all.reshape(devices, -1),
        bias_all.reshape(devices, -1),
    ]
    sizes = [p.shape[1] for p in parts]
    padded = -(-sum(sizes) // 1024) * 1024
    parts.append(jnp.zeros((devices, padded - sum(sizes)), F32))
    small_parts = jnp.concatenate(parts, axis=1).reshape(devices, -1, 128)
    gate_sum = (gate_grad[:half_width].astype(F32) + gate_got.astype(F32)).astype(BF16)
    out_mine = out_mine.reshape(lanes.dp, out_rows, head_width)
    out_mine = lanes.exchange_heads(out_mine).transpose(1, 0, 2)
    out_mine = out_mine.reshape(out_rows, lanes.dp, 2, lanes.outer, -1)
    low_half, high_half = lanes.pick(out_mine, 2)
    w_out_grad = jnp.stack([low_half, high_half], axis=3).reshape(out_rows, width).astype(F32)
    mixer_grads, feed_got, w_out_grad = lax.optimization_barrier(
        (mixer_grads, feed_got, w_out_grad)
    )
    weight_grads, tokens_grad, reduced = finish(
        lanes.outer, lanes.dp, mixer_grads,
        gate_sum.reshape(lanes.outer, -1, width),
        [grad_pre, grad_gate_flat, w_kqv, w_g],
        [grad_rank, down_full, own_tokens, grad_hidden, mixer_full],
        small_parts,
    )
    w_key_grad, w_query_grad, w_value_grad, w_gate_grad = [weight_grads[m] for m in range(4)]
    tokens_grad = tokens_grad.reshape(seq_count, piece, width)
    feed_sum = feed_sums[0].astype(F32) + feed_got.astype(F32)
    block_out = (alive_own * (hidden + feed_sum)).astype(BF16)
    mixer_gain_grad = reduced[padded // 128, : width // devices]
    reduced = reduced.reshape(-1)
    smalls, offset = [], 0
    for size in sizes:
        smalls.append(reduced[offset : offset + size])
        offset += size
    return (
        block_out.reshape(seq_count, piece, width),
        tokens_grad,
        mixer_gain_grad,
        smalls[0],
        smalls[1],
        w_query_grad,
        w_key_grad,
        w_value_grad,
        w_gate_grad,
        w_out_grad,
        smalls[2].reshape(-1, rank),
        smalls[3].reshape(-1, rank),
        smalls[4],
        feed_grads[1].astype(F32),
        feed_grads[2].astype(F32),
        feed_grads[0].astype(F32),
    )


def solution(mesh):
    vector = P(("dp", "seq"))
    matrix = P(("dp", "seq"), None)
    stream = P("dp", "seq", None)
    return jax.shard_map(
        per_device,
        mesh=mesh,
        in_specs=(
            stream, P("dp"), stream, vector, vector, vector, matrix, matrix, matrix, matrix,
            matrix, matrix, matrix, vector, matrix, matrix, matrix,
        ),
        out_specs=(
            stream, stream, vector, vector, vector, matrix, matrix, matrix, matrix, matrix,
            matrix, matrix, vector, matrix, matrix, matrix,
        ),
        check_vma=False,
    )
```

```python
import functools

import jax
import jax.numpy as jnp
from jax import lax
from jax.experimental import pallas as pl
from jax.experimental.pallas import tpu as pltpu
from jax.sharding import PartitionSpec as P

HEADS = 4
SLOTS = 64
EPS = 1e-06
GATE_NORM = 8.0
F32 = jnp.float32
BF16 = jnp.bfloat16
LEAF = 8
VMEM_LIMIT = 48 * 1024 * 1024


def mm(a, b, ca, cb):
    return lax.dot_general(
        a.astype(BF16), b.astype(BF16), (((ca,), (cb,)), ((), ())), preferred_element_type=F32
    )


def mm_exact(a, b, ca, cb):
    return lax.dot_general(
        a,
        b,
        (((ca,), (cb,)), ((), ())),
        precision=lax.Precision.HIGHEST,
        preferred_element_type=F32,
    )


def two_parts(x):
    high = x.astype(BF16)
    return high, (x - high.astype(F32)).astype(BF16)


def mm_left(exact, b, ca, cb):
    high, low = two_parts(b)
    return mm(exact, high, ca, cb) + mm(exact, low, ca, cb)


def mm_right(a, exact, ca, cb):
    high, low = two_parts(a)
    return mm(high, exact, ca, cb) + mm(low, exact, ca, cb)


def mm_fine(a, b, ca, cb):
    a_high, a_low = two_parts(a)
    b_high, b_low = two_parts(b)
    return mm(a_high, b_high, ca, cb) + (mm(a_high, b_low, ca, cb) + mm(a_low, b_high, ca, cb))


def contract_last(a, b):
    return mm(a, b, 1, 1)


def contract_first(a, b):
    return mm(a, b, 0, 0)


def swish_slope(v):
    sigma = jax.nn.sigmoid(v)
    return sigma * (1.0 + v * (1.0 - sigma))


def rms_scale(v):
    return lax.rsqrt(jnp.mean(v * v, axis=-1, keepdims=True) + EPS)


def grid_index(rows, cols):
    return (
        lax.broadcasted_iota(jnp.int32, (rows, cols), 0),
        lax.broadcasted_iota(jnp.int32, (rows, cols), 1),
    )


def running_sum(decay):
    length = decay.shape[0]
    row, col = grid_index(length, length)
    return mm_exact((row >= col).astype(F32), decay, 1, 0)


def levels(length):
    found = []
    half = length // 2
    while half >= LEAF:
        found.append(half)
        half //= 2
    return found


def level_factors(running, writes, half):
    length, slots = running.shape
    pairs = running.reshape(length // (2 * half), 2 * half, slots)
    anchor = jnp.broadcast_to(pairs[:, half - 1 : half, :], pairs.shape).reshape(length, slots)
    near = jnp.exp(-jnp.abs(running - anchor))
    row, _ = grid_index(length, slots)
    right = (row % (2 * half)) >= half
    return jnp.where(right, near, 0.0), jnp.where(right, 0.0, near), right


def same_block(length, size):
    row, col = grid_index(length, length)
    return (row // size) == (col // size)


def leaf_selector(length):
    row, col = grid_index(length, LEAF)
    return ((row % LEAF) == col).astype(F32)


def leaf_take(square):
    length = square.shape[0]
    kept = jnp.where(same_block(length, LEAF), square, 0.0)
    return mm_exact(kept, leaf_selector(length), 1, 0)


def leaf_spread(columns):
    length = columns.shape[0]
    wide = mm_exact(columns, leaf_selector(length), 1, 1)
    return jnp.where(same_block(length, LEAF), wide, 0.0)


def leaf_row(tensor, at):
    length, width = tensor.shape
    blocks = tensor.reshape(length // LEAF, LEAF, width)
    return jnp.broadcast_to(blocks[:, at : at + 1, :], blocks.shape).reshape(length, width)


def leaf_decay(running, at):
    length, slots = running.shape
    row, _ = grid_index(length, slots)
    reached = (row % LEAF) >= at
    spread = running - leaf_row(running, at)
    return jnp.where(reached, jnp.exp(jnp.where(reached, spread, 0.0)), 0.0)


def masked(square, half):
    length = square.shape[0]
    if 2 * half == length:
        return square
    return jnp.where(same_block(length, 2 * half), square, 0.0)


def read_in_chunk(square, running, writes):
    total = None
    for half in levels(running.shape[0]):
        right, left, _ = level_factors(running, writes, half)
        part = right * mm_fine(masked(square, half), left * writes, 1, 0)
        total = part if total is None else total + part
    columns = leaf_take(square)
    for at in range(LEAF):
        part = columns[:, at : at + 1] * (leaf_decay(running, at) * leaf_row(writes, at))
        total = part if total is None else total + part
    return total


def mix_in_chunk(attend, running, writes):
    total = None
    for half in levels(running.shape[0]):
        right, left, _ = level_factors(running, writes, half)
        part = masked(mm(attend * right, left * writes, 1, 1), half)
        total = part if total is None else total + part
    columns = [
        jnp.sum(
            attend * (leaf_decay(running, at) * leaf_row(writes, at)), axis=1, keepdims=True
        )
        for at in range(LEAF)
    ]
    part = leaf_spread(jnp.concatenate(columns, axis=1))
    return part if total is None else total + part


def summary(k, v, decay, writes):
    running = running_sum(decay)
    length = running.shape[0]
    last = running[length - 1 : length, :]
    fade = jnp.exp(last - running) * writes
    return jnp.concatenate([mm(fade, k, 0, 0), mm(fade, v, 0, 0)], axis=1), jnp.exp(last)


def forward_kernel(
    q_ref, k_ref, v_ref, gate_ref, decay_ref, writes_ref, state_ref, gain_ref,
    mixed_ref, out_ref, attend_ref,
):
    q, k, v = q_ref[0], k_ref[0], v_ref[0]
    writes = writes_ref[0]
    width = q.shape[1]
    scale = width ** (-0.5)
    running = running_sum(decay_ref[0])
    growth = jnp.exp(running)
    state = state_ref[0]
    dots = mm(q, k, 1, 1) * scale
    scores = growth * (mm(q, state[:, :width], 1, 1) * scale)
    scores = scores + read_in_chunk(dots, running, writes)
    top = jnp.max(scores, axis=1, keepdims=True)
    raw = jnp.exp(scores - top)
    attend = raw / jnp.sum(raw, axis=1, keepdims=True)
    mixing = mix_in_chunk(attend, running, writes)
    out = mm(attend * growth, state[:, width:], 1, 0) + mm(mixing, v, 1, 0)
    out_ref[0] = out
    attend_ref[0] = attend
    gate = gate_ref[0]
    normed = out * rms_scale(out) * gain_ref[...]
    mixed_ref[0] = (normed * (gate * jax.nn.sigmoid(gate))).astype(BF16)


def back_first_kernel(
    grad_mixed_ref, gate_ref, out_ref, attend_ref, q_ref, v_ref, decay_ref, writes_ref,
    state_ref, gain_ref,
    grad_gate_ref, grad_out_ref, grad_scores_ref, adjoint_ref, gain_grad_ref,
):
    q, v = q_ref[0], v_ref[0]
    writes = writes_ref[0]
    width = q.shape[1]
    scale = width ** (-0.5)
    grad_mixed, gate, out = grad_mixed_ref[0], gate_ref[0], out_ref[0]
    gain = gain_ref[...]
    inverse = rms_scale(out)
    normed = out * inverse
    grad_gate_ref[0] = (grad_mixed * (normed * gain) * swish_slope(gate)).astype(BF16)
    e = grad_mixed * (gate * jax.nn.sigmoid(gate))
    gain_grad_ref[0] = jnp.sum(e * normed, axis=0, keepdims=True)
    eg = e * gain
    grad_out = inverse * (eg - normed * jnp.mean(eg * normed, axis=1, keepdims=True))
    grad_out_ref[0] = grad_out.astype(BF16)
    running = running_sum(decay_ref[0])
    growth = jnp.exp(running)
    attend = attend_ref[0]
    u = growth * mm_right(grad_out, state_ref[0, :, width:], 1, 1)
    u = u + read_in_chunk(mm_right(grad_out, v, 1, 1), running, writes)
    grad_scores = attend * (u - jnp.sum(attend * u, axis=1, keepdims=True))
    grad_scores_ref[0] = grad_scores
    adjoint_ref[0, :, :width] = mm(growth * grad_scores * scale, q, 0, 0)
    adjoint_ref[0, :, width:] = mm(growth * attend, grad_out.astype(BF16), 0, 0)


def back_second_kernel(
    grad_out_ref, grad_scores_ref, attend_ref, q_ref, k_ref, v_ref, decay_ref, writes_ref,
    state_ref, adjoint_ref, q_pre_ref, k_pre_ref, logit_ref, alive_ref,
    grad_pre_ref, dlogit_ref,
):
    q, k, v, grad_out = q_ref[0], k_ref[0], v_ref[0], grad_out_ref[0]
    attend, grad_scores = attend_ref[0], grad_scores_ref[0]
    decay, writes = decay_ref[0], writes_ref[0]
    length, slots = decay.shape
    width = q.shape[1]
    scale = width ** (-0.5)
    running = running_sum(decay)
    growth = jnp.exp(running)
    keep = jnp.exp(decay)
    last = running[length - 1 : length, :]
    fade = jnp.exp(last - running)
    state, adjoint = state_ref[0], adjoint_ref[0]
    key_state, value_state = state[:, :width], state[:, width:]
    key_adjoint, value_adjoint = adjoint[:, :width], adjoint[:, width:]
    key_dots = mm(q, k, 1, 1) * scale
    value_dots = mm(grad_out, v, 1, 1)
    row, col = grid_index(length, length)

    columns_sum = jnp.zeros((length, slots), F32)
    crossing = jnp.zeros((length, slots), F32)
    mix_key = jnp.zeros((length, length), F32)
    mix_value = jnp.zeros((length, length), F32)
    for half in levels(length):
        right, left, is_right = level_factors(running, writes, half)
        key_part, value_part = masked(key_dots, half), masked(value_dots, half)
        left_w = left * writes
        gs_right, at_right = grad_scores * right, attend * right
        mix_key = mix_key + masked(mm(gs_right, left_w, 1, 1), half)
        mix_value = mix_value + masked(mm(at_right, left_w, 1, 1), half)
        rows_sum = gs_right * mm_fine(key_part, left_w, 1, 0) + at_right * mm_fine(value_part, left_w, 1, 0)
        open_sum = left * (mm_fine(key_part, gs_right, 0, 0) + mm_fine(value_part, at_right, 0, 0))
        columns_sum = columns_sum + open_sum
        sums = jnp.where(is_right, rows_sum, open_sum * writes)
        forward = jnp.where((row % (2 * half)) >= half, col - row, row - col - 1) >= 0
        wanted = ((row // half) == (col // half)) & forward
        crossing = crossing + mm_left(wanted.astype(F32), sums, 1, 0)
    key_leaf, value_leaf = leaf_take(key_dots), leaf_take(value_dots)
    leaf_at = lax.broadcasted_iota(jnp.int32, (length, slots), 0) % LEAF
    difference = jnp.zeros((length, slots), F32)
    mix_key_columns, mix_value_columns = [], []
    for at in range(LEAF):
        fall = leaf_decay(running, at)
        mass = leaf_row(writes, at)
        mix_key_columns.append(jnp.sum(grad_scores * fall * mass, axis=1, keepdims=True))
        mix_value_columns.append(jnp.sum(attend * fall * mass, axis=1, keepdims=True))
        terms = fall * (
            grad_scores * key_leaf[:, at : at + 1] + attend * value_leaf[:, at : at + 1]
        )
        blocks = terms.reshape(length // LEAF, LEAF, slots)
        whole = jnp.broadcast_to(
            jnp.sum(blocks, axis=1, keepdims=True), blocks.shape
        ).reshape(length, slots)
        columns_sum = columns_sum + jnp.where(leaf_at == at, whole, 0.0)
        later = jnp.where(leaf_at > at, terms, 0.0)
        later_blocks = later.reshape(length // LEAF, LEAF, slots)
        later_whole = jnp.broadcast_to(
            jnp.sum(later_blocks, axis=1, keepdims=True), later_blocks.shape
        ).reshape(length, slots)
        difference = difference + mass * (later - jnp.where(leaf_at == at, later_whole, 0.0))
    mix_key = mix_key + leaf_spread(jnp.concatenate(mix_key_columns, axis=1))
    mix_value = mix_value + leaf_spread(jnp.concatenate(mix_value_columns, axis=1))
    suffix_leaf = (((row // LEAF) == (col // LEAF)) & (col >= row)).astype(F32)
    crossing = crossing + mm_exact(suffix_leaf, difference, 1, 0)

    start_terms = growth * (
        grad_scores * (mm(q, key_state, 1, 1) * scale)
        + attend * mm(grad_out, value_state, 1, 1)
    )
    crossing = crossing + mm_left((col >= row).astype(F32), start_terms, 1, 0)
    end_open = fade * (mm(k, key_adjoint, 1, 1) + mm(v, value_adjoint, 1, 1))
    columns_sum = columns_sum + end_open
    crossing = crossing + mm_left((col < row).astype(F32), end_open * writes, 1, 0)
    through = mm_exact(
        jnp.ones((8, 2 * width), F32), state.astype(F32) * adjoint.astype(F32), 1, 1
    )[0:1, :]
    crossing = crossing + jnp.exp(last) * through
    grad_decay = crossing - keep * columns_sum

    grad_q = (mm(grad_scores * growth, key_state, 1, 0) + mm(mix_key, k, 1, 0)) * scale
    fade_w = fade * writes
    grad_k = mm(mix_key, q, 0, 0) * scale + mm(fade_w, key_adjoint, 1, 0)
    grad_v = mm(mix_value, grad_out, 0, 0) + mm(fade_w, value_adjoint, 1, 0)
    grad_pre_ref[0, :, :width] = (grad_k * swish_slope(k_pre_ref[0])).astype(BF16)
    grad_pre_ref[0, :, width : 2 * width] = (grad_q * swish_slope(q_pre_ref[0])).astype(BF16)
    grad_pre_ref[0, :, 2 * width :] = grad_v.astype(BF16)
    dlogit_ref[0] = (
        alive_ref[0] * grad_decay * jax.nn.sigmoid(-logit_ref[0]) * (1.0 / GATE_NORM)
    ).astype(BF16)


def per_sequence(kernel, inputs, outputs, shared=()):
    inputs = [x if isinstance(x, tuple) else (x, None) for x in inputs]
    count = inputs[0][0].shape[0]

    def spec(shape, at=None):
        if at is None:
            return pl.BlockSpec((1,) + tuple(shape[1:]), lambda s: (s, 0, 0))
        return pl.BlockSpec((1, shape[1], shape[2] // 3), lambda s: (s, 0, at))

    return pl.pallas_call(
        kernel,
        grid=(count,),
        in_specs=[spec(x.shape, at) for x, at in inputs]
        + [pl.BlockSpec(x.shape, lambda s: (0, 0)) for x in shared],
        out_specs=[spec(x.shape) for x in outputs],
        out_shape=outputs,
        compiler_params=pltpu.CompilerParams(vmem_limit_bytes=VMEM_LIMIT),
    )(*[x for x, _ in inputs], *shared)


CHUNKS = 8
STRIP = 16


def send(src, dst, send_sem, recv_sem, where):
    copy = pltpu.make_async_remote_copy(
        src_ref=src,
        dst_ref=dst,
        send_sem=send_sem,
        recv_sem=recv_sem,
        device_id=where,
        device_id_type=pl.DeviceIdType.MESH,
    )
    copy.start()
    return copy


def greet(partners):
    barrier = pltpu.get_barrier_semaphore()
    for where in partners:
        pl.semaphore_signal(
            barrier, inc=1, device_id=where, device_id_type=pl.DeviceIdType.MESH
        )
    return barrier


def near_partners():
    d, at = lax.axis_index("dp"), lax.axis_index("seq")
    x = {"seq": jnp.bitwise_xor(at, 1)}
    y = {"dp": jnp.bitwise_xor(d, 2)}
    core = {"dp": jnp.bitwise_xor(d, 1)}
    return x, y, core


def everyone(seq, dp, act):
    me = lax.axis_index("dp") * seq + lax.axis_index("seq")

    def turn(r, carry):
        other = jnp.bitwise_xor(me, r)
        act(r, {"dp": other // seq, "seq": other % seq})
        return carry

    lax.fori_loop(1, seq * dp, turn, 0)


def greet_everyone(seq, dp):
    barrier = pltpu.get_barrier_semaphore()
    everyone(
        seq,
        dp,
        lambda r, where: pl.semaphore_signal(
            barrier, inc=1, device_id=where, device_id_type=pl.DeviceIdType.MESH
        ),
    )
    pl.semaphore_wait(barrier, seq * dp - 1)


def gather_kernel(outer, dp, *refs):
    mats, refs = refs[:3], refs[3:]
    toks, small, w_out, refs = refs[:2], refs[2], refs[3], refs[4:]
    three, heads, refs = refs[0], refs[1], refs[2:]
    out_toks, out_small, refs = refs[:2], refs[2], refs[3:]
    (
        local_sem, up_send, up_recv, down_send, down_recv, x_send, x_recv,
        tok_send, tok_recv, small_send, small_recv, head_send, head_recv,
    ) = refs
    outs = [three.at[0], three.at[1], three.at[2]]
    seq = 2 * outer
    at = lax.axis_index("seq")
    d = lax.axis_index("dp")
    me = d * seq + at
    z = at // 2
    x, y, core = near_partners()
    above, below = {"seq": at + 2}, {"seq": at - 2}
    has_above, has_below = z < outer - 1, z > 0
    greet_everyone(seq, dp)

    def push(r, where):
        return pltpu.make_async_remote_copy(
            src_ref=small, dst_ref=out_small.at[me], send_sem=small_send.at[r],
            recv_sem=small_recv.at[r], device_id=where, device_id_type=pl.DeviceIdType.MESH,
        )

    everyone(seq, dp, lambda r, where: push(r, where).start())
    head = heads.shape[2]

    def columns(owner):
        return w_out.at[:, pl.ds(pl.multiple_of(owner * head, head), head)]

    own_head = pltpu.make_async_copy(columns(d), heads.at[d], local_sem.at[5])
    own_head.start()
    other_heads = [
        send(
            columns(jnp.bitwise_xor(d, r)), heads.at[d], head_send.at[r], head_recv.at[r],
            {"dp": jnp.bitwise_xor(d, r)},
        )
        for r in range(1, dp)
    ]

    def up(m, k, src, origin):
        return pltpu.make_async_remote_copy(
            src_ref=src, dst_ref=outs[m].at[0, origin], send_sem=up_send.at[m, k],
            recv_sem=up_recv.at[m, k], device_id=above, device_id_type=pl.DeviceIdType.MESH,
        )

    def down(m, k, src, origin):
        return pltpu.make_async_remote_copy(
            src_ref=src, dst_ref=outs[m].at[0, origin], send_sem=down_send.at[m, k],
            recv_sem=down_recv.at[m, k], device_id=below, device_id_type=pl.DeviceIdType.MESH,
        )

    def across(m, src, origin):
        return pltpu.make_async_remote_copy(
            src_ref=src, dst_ref=outs[m].at[1, origin], send_sem=x_send.at[m, origin],
            recv_sem=x_recv.at[m, origin], device_id=x, device_id_type=pl.DeviceIdType.MESH,
        )

    for m in range(3):
        @pl.when(has_above)
        def _():
            up(m, 0, mats[m], z).start()

        @pl.when(has_below)
        def _():
            down(m, 0, mats[m], z).start()

        across(m, mats[m], z).start()
    tok_y, tok_rest = [], []
    for n, (tok, out_tok) in enumerate(zip(toks, out_toks)):
        tok_y.append(send(tok, out_tok.at[1], tok_send.at[3 * n], tok_recv.at[3 * n], y))
        tok_rest.append(
            send(tok, out_tok.at[2], tok_send.at[3 * n + 1], tok_recv.at[3 * n + 1], core)
        )
        copy = pltpu.make_async_copy(tok, out_tok.at[0], local_sem.at[1 + 5 * n])
        copy.start()
        tok_rest.append(copy)
    own_small = pltpu.make_async_copy(small, out_small.at[me], local_sem.at[0])
    own_small.start()
    own_mats = []
    for m in range(3):
        copy = pltpu.make_async_copy(mats[m], outs[m].at[0, z], local_sem.at[2 + m])
        copy.start()
        own_mats.append(copy)

    def pass_on(k, carry):
        for m in range(3):
            @pl.when(z - k >= 0)
            def _():
                slot = outs[m].at[0, z - k]
                up(m, k - 1, slot, z - k).wait_recv()

                @pl.when(has_above)
                def _():
                    up(m, k, slot, z - k).start()

                across(m, slot, z - k).start()

            @pl.when(z + k < outer)
            def _():
                slot = outs[m].at[0, z + k]
                down(m, k - 1, slot, z + k).wait_recv()

                @pl.when(has_below)
                def _():
                    down(m, k, slot, z + k).start()

                across(m, slot, z + k).start()

        return carry

    lax.fori_loop(1, outer, pass_on, 0)
    for n, out_tok in enumerate(out_toks):
        tok_y[n].wait()
        tok_rest.append(
            send(out_tok.at[1], out_tok.at[3], tok_send.at[3 * n + 2], tok_recv.at[3 * n + 2], core)
        )

    def arrived(r, where):
        push(r, where).wait_send()
        theirs = out_small.at[jnp.bitwise_xor(me, r)]
        pltpu.make_async_remote_copy(
            src_ref=theirs, dst_ref=theirs, send_sem=small_send.at[r],
            recv_sem=small_recv.at[r], device_id=where, device_id_type=pl.DeviceIdType.MESH,
        ).wait_recv()

    everyone(seq, dp, arrived)

    def complete(o, carry):
        for m in range(3):
            across(m, outs[m].at[0, o], o).wait()

            @pl.when(has_above & (o <= z))
            def _():
                up(m, o, outs[m].at[0, z], z).wait_send()

            @pl.when(has_below & (o <= outer - 1 - z))
            def _():
                down(m, o, outs[m].at[0, z], z).wait_send()

        return carry

    lax.fori_loop(0, outer, complete, 0)
    for copy in own_mats:
        copy.wait()
    own_head.wait()
    for r, copy in enumerate(other_heads, 1):
        copy.wait_send()
        theirs = heads.at[jnp.bitwise_xor(d, r)]
        pltpu.make_async_remote_copy(
            src_ref=theirs, dst_ref=theirs, send_sem=head_send.at[r],
            recv_sem=head_recv.at[r], device_id={"dp": jnp.bitwise_xor(d, r)},
            device_id_type=pl.DeviceIdType.MESH,
        ).wait_recv()
    own_small.wait()
    for copy in tok_rest:
        copy.wait()


def in_hbm():
    return pl.BlockSpec(memory_space=pl.ANY)


def in_vmem():
    return pl.BlockSpec(memory_space=pltpu.VMEM)


def gather_all(outer, dp, mats, toks, small, w_out):
    seq = 2 * outer
    rows, width = mats[0].shape
    dma = pltpu.SemaphoreType.DMA
    return pl.pallas_call(
        functools.partial(gather_kernel, outer, dp),
        in_specs=[in_vmem()] * 5 + [in_hbm()] * 2,
        out_specs=[in_hbm()] * 5,
        out_shape=[
            jax.ShapeDtypeStruct((3, 2, outer, rows, width), BF16),
            jax.ShapeDtypeStruct((dp, w_out.shape[0], w_out.shape[1] // dp), BF16),
            jax.ShapeDtypeStruct((dp,) + toks[0].shape, BF16),
            jax.ShapeDtypeStruct((dp,) + toks[1].shape, BF16),
            jax.ShapeDtypeStruct((seq * dp,) + small.shape, BF16),
        ],
        scratch_shapes=[dma((7,))] + [dma((3, outer))] * 6
        + [dma((6,))] * 2 + [dma((seq * dp,))] * 2 + [dma((dp,))] * 2,
        compiler_params=pltpu.CompilerParams(
            collective_id=1, has_side_effects=True, vmem_limit_bytes=VMEM_LIMIT
        ),
    )(*mats, *toks, small, w_out)


def feed_kernel(mid, grad_feed, w_down, w_act, w_lin, product, grad_gate, grad_lin):
    gate = mm(mid[...], w_act[0], 1, 1)
    lin = mm(mid[...], w_lin[0], 1, 1)
    grad_product = mm(grad_feed[...], w_down[0], 1, 1)
    sigma = jax.nn.sigmoid(gate)
    swish = gate * sigma
    product[...] = (swish * lin).astype(BF16)
    grad_gate[...] = (grad_product * lin * (sigma * (1.0 + gate * (1.0 - sigma)))).astype(BF16)
    grad_lin[...] = (grad_product * swish).astype(BF16)


def feed_back_kernel(
    product, grad_gate, grad_lin, w_down, w_act, w_lin, feed, grad_mid
):
    grad_mid[...] = (
        mm(grad_gate[...], w_act[0], 1, 0) + mm(grad_lin[...], w_lin[0], 1, 0)
    ).astype(BF16)
    feed[...] = mm(product[...], w_down[0], 1, 0).astype(BF16)


def feed_tiles(kernel, tiles, weights, widths):
    rows = tiles[0].shape[0]
    step = min(256, rows)
    _, units, width = weights.shape
    each = 2 * step * units * width

    def spec(columns):
        return pl.BlockSpec((step, columns), lambda t: (t, 0))

    def weight(at):
        return pl.BlockSpec(
            (1, units, width), lambda t: (at, 0, 0), pipeline_mode=pl.Buffered(1)
        )

    return pl.pallas_call(
        kernel,
        grid=(rows // step,),
        in_specs=[spec(x.shape[1]) for x in tiles] + [weight(m) for m in range(3)],
        out_specs=[spec(columns) for columns in widths],
        out_shape=[jax.ShapeDtypeStruct((rows, columns), BF16) for columns in widths],
        cost_estimate=pl.CostEstimate(
            flops=3 * each * (rows // step), bytes_accessed=6 * units * width + 8 * rows * width,
            transcendentals=rows * units,
        ),
        compiler_params=pltpu.CompilerParams(vmem_limit_bytes=VMEM_LIMIT),
    )(*tiles, weights, weights, weights)


def turned(x):
    row, col = grid_index(x.shape[1], x.shape[1])
    return mm_exact((row == col).astype(F32), x, 1, 1)


def flipped(x):
    size = x.shape[-1] // 4
    return jnp.concatenate([x[:, size * i : size * (i + 1)] for i in (1, 0, 3, 2)], axis=1)


def relay_kernel(outer, backward, *refs):
    if backward:
        totals, keeps, parts, gate_sent, refs = refs[0], refs[1], refs[2], refs[3], refs[4:]
        states, sums, gate_got, refs = refs[0], refs[1], refs[2], refs[3:]
        gate_s, gate_r = refs[-2:]
        side, refs = refs[-9:-2], refs[:-9]
    else:
        feats, decays, writes, refs = refs[0], refs[1], refs[2], refs[3:]
        states, keeps, refs = refs[0], refs[1], refs[2:]
    (
        own, to_x, from_x, to_z, from_z, to_back, from_back, keep_mine, keep_theirs,
        x_s, x_r, z_s, z_r, b_s, b_r, k_s, k_r,
    ) = refs
    half = own.shape[0]
    at = lax.axis_index("seq")
    inner, z = at % 2, at // 2
    x, y, core = near_partners()
    above, below = {"seq": at + 2}, {"seq": at - 2}
    has_above, has_below = z < outer - 1, z > 0
    ahead, has_ahead, has_source = (
        (below, has_below, has_above) if backward else (above, has_above, has_below)
    )
    barrier = greet([x, y, core] if backward else [x])

    @pl.when(has_above)
    def _():
        greet([above])

    @pl.when(has_below)
    def _():
        greet([below])

    pl.semaphore_wait(
        barrier,
        (3 if backward else 1) + has_above.astype(jnp.int32) + has_below.astype(jnp.int32),
    )

    def compute(s):
        if backward:
            return totals[s]
        width = feats.shape[2] // 3
        total, keep = summary(
            feats[s, :, :width], feats[s, :, 2 * width :], decays[s], writes[s]
        )
        keep_mine[s] = keep
        return total

    crossing = []
    for i in range(half):
        to_x[i] = compute((1 - inner) * half + i).astype(BF16)
        crossing.append(send(to_x.at[i], from_x.at[i], x_s.at[i], x_r.at[i], x))
    if backward:
        gate_copy = send(gate_sent, gate_got, gate_s.at[0], gate_r.at[0], x)
        side = plane_sum_start(parts, side, y, core)
    for i in range(half):
        own[i] = compute(inner * half + i)
    if backward:
        keep_a, keep_b = keeps[0], keeps[1]
    else:
        send(keep_mine, keep_theirs, k_s.at[0], k_r.at[0], x).wait()
        mine = jnp.concatenate([keep_mine[s] for s in range(2 * half)], axis=0)
        theirs = jnp.concatenate([keep_theirs[s] for s in range(2 * half)], axis=0)
        keep_a = jnp.where(inner == 0, mine, theirs)
        keep_b = jnp.where(inner == 0, theirs, mine)
        keeps[0] = keep_a
        keeps[1] = keep_b
    if backward:
        keep_a, keep_b = keep_b, keep_a
    first_k = turned(jnp.where(inner == 0, keep_a[:half], keep_a[half:]))
    second_k = turned(jnp.where(inner == 0, keep_b[:half], keep_b[half:]))
    is_first = (inner == 1) if backward else (inner == 0)

    def along(i):
        return pltpu.make_async_remote_copy(
            src_ref=to_z.at[i], dst_ref=from_z.at[i], send_sem=z_s.at[i], recv_sem=z_r.at[i],
            device_id=ahead, device_id_type=pl.DeviceIdType.MESH,
        )

    returning = []
    for i in range(half):
        crossing[i].wait()

        @pl.when(jnp.logical_not(has_source))
        def _():
            from_z[i] = jnp.zeros_like(from_z[i])

        @pl.when(has_source)
        def _():
            along(i).wait_recv()

        got = flipped(from_x[i]).astype(F32)
        mine = own[i]
        first = jnp.where(is_first, mine, got)
        second = jnp.where(is_first, got, mine)
        entering = from_z[i].astype(F32)
        after = first_k[:, i : i + 1] * entering + first
        to_z[i] = (second_k[:, i : i + 1] * after + second).astype(BF16)

        @pl.when(has_ahead)
        def _():
            along(i).start()

        states[inner * half + i] = jnp.where(is_first, entering, after).astype(BF16)
        to_back[i] = jnp.where(is_first, after, entering).astype(BF16)
        returning.append(send(to_back.at[i], from_back.at[i], b_s.at[i], b_r.at[i], x))
    for i in range(half):
        returning[i].wait()
        states[(1 - inner) * half + i] = flipped(from_back[i])

        @pl.when(has_ahead)
        def _():
            along(i).wait_send()

    if backward:
        plane_sum_end(parts, sums, side)
        gate_copy.wait()


def plane_sum_start(parts, side, y, core):
    from_core, to_y, from_y, core_s, core_r, y_s, y_r = side
    rows = parts.shape[1]
    size = rows // CHUNKS
    cuts = [pl.ds(c * size, size) for c in range(CHUNKS)]
    first = [
        send(parts.at[pl.ds(4, 4), cut], from_core.at[:, cut], core_s.at[c], core_r.at[c], core)
        for c, cut in enumerate(cuts)
    ]
    second = []
    for c, cut in enumerate(cuts):
        first[c].wait()

        for j in range(2):
            to_y[j, cut] = parts[2 + j, cut] + from_core[2 + j, cut]
        second.append(send(to_y.at[:, cut], from_y.at[:, cut], y_s.at[c], y_r.at[c], y))
    return from_core, from_y, second


def plane_sum_end(parts, sums, side):
    from_core, from_y, second = side
    size = parts.shape[1] // CHUNKS
    for c in range(CHUNKS):
        second[c].wait()

        def add(r, carry, c=c):
            at = pl.ds(c * size + r * STRIP, STRIP)
            for j in range(2):
                sums[j, at] = (
                    parts[j, at].astype(F32) + from_core[j, at].astype(F32)
                    + from_y[j, at].astype(F32)
                ).astype(BF16)
            return carry

        lax.fori_loop(0, size // STRIP, add, 0)


def relay(outer, backward, inputs, sequences, slots, width):
    half = sequences // 2
    dma = pltpu.SemaphoreType.DMA
    held = pltpu.VMEM((half, slots, width), BF16)
    states = jax.ShapeDtypeStruct((sequences, slots, width), BF16)
    keeps = jax.ShapeDtypeStruct((2, sequences, slots), F32)
    keep = pltpu.VMEM((sequences, 1, slots), F32)
    outs, side = [states, keeps], []
    if backward:
        rows, columns = inputs[2].shape[1:]
        outs = [states, jax.ShapeDtypeStruct((2, rows, columns), BF16)]
        outs.append(jax.ShapeDtypeStruct(inputs[3].shape, BF16))
        side = [
            pltpu.VMEM((4, rows, columns), BF16), pltpu.VMEM((2, rows, columns), BF16),
            pltpu.VMEM((2, rows, columns), BF16),
        ] + [dma((CHUNKS,))] * 4 + [dma((1,))] * 2
    return pl.pallas_call(
        functools.partial(relay_kernel, outer, backward),
        in_specs=[in_vmem()] * 3 + [in_hbm()] * (len(inputs) - 3),
        out_specs=[in_vmem()] * 2 + [in_hbm()] * (len(outs) - 2),
        out_shape=outs,
        scratch_shapes=[pltpu.VMEM((half, slots, width), F32)] + [held] * 6 + [keep] * 2
        + [dma((half,))] * 6 + [dma((1,))] * 2 + side,
        compiler_params=pltpu.CompilerParams(
            collective_id=7 if backward else 6, has_side_effects=True,
            vmem_limit_bytes=VMEM_LIMIT,
        ),
    )(*inputs)


def middle_kernel(
    parts, tok, gain, extra, hidden, mid, extra_all, from_core, to_y, from_y, normed,
    core_s, core_r, y_s, y_r, local_sem, gx_s, gx_r, gy_s, gy_r, gd_s, gd_r,
    ex_s, ex_r, ed_s, ed_r, extra_sem, gc_s, gc_r, ec_s, ec_r,
):
    rows = tok.shape[0]
    size = rows // CHUNKS
    x, y, core = near_partners()
    pl.semaphore_wait(greet([x, y, core]), 3)
    cuts = [pl.ds(c * size, size) for c in range(CHUNKS)]
    first = [
        send(parts.at[pl.ds(2, 2), cut], from_core.at[:, cut], core_s.at[c], core_r.at[c], core)
        for c, cut in enumerate(cuts)
    ]
    second = []
    for c, cut in enumerate(cuts):
        first[c].wait()

        to_y[cut] = parts[1, cut] + from_core[1, cut]
        second.append(send(to_y.at[cut], from_y.at[cut], y_s.at[c], y_r.at[c], y))
    rest = []
    for j in range(4):
        copy = pltpu.make_async_copy(extra.at[j], extra_all.at[2 * j], extra_sem.at[j])
        copy.start()
        rest.append(copy)
    extra_x = [
        send(extra.at[0, cut], extra_all.at[1, cut], ex_s.at[c], ex_r.at[c], x)
        for c, cut in enumerate(cuts)
    ]
    over_x, over_y, diagonal = [], [], []
    for c in range(CHUNKS + 2):
        if c < CHUNKS:
            cut = cuts[c]
            second[c].wait()

            def norm(r, carry, c=c):
                at = pl.ds(c * size + r * STRIP, STRIP)
                total = tok[at].astype(F32) + (
                    (parts[0, at].astype(F32) + from_core[0, at].astype(F32))
                    + from_y[at].astype(F32)
                )
                hidden[at] = total
                normed[at] = (total * rms_scale(total) * gain[...]).astype(BF16)
                return carry

            lax.fori_loop(0, size // STRIP, norm, 0)
            over_y.append(send(normed.at[cut], mid.at[2, cut], gy_s.at[c], gy_r.at[c], y))
            over_x.append(send(normed.at[cut], mid.at[1, cut], gx_s.at[c], gx_r.at[c], x))
            rest.append(send(normed.at[cut], mid.at[4, cut], gc_s.at[0, c], gc_r.at[0, c], core))
            own = pltpu.make_async_copy(normed.at[cut], mid.at[0, cut], local_sem.at[c])
            own.start()
            rest.append(own)
        if c >= 2:
            at, cut = c - 2, cuts[c - 2]
            over_y[at].wait()
            diagonal.append(send(mid.at[2, cut], mid.at[3, cut], gd_s.at[at], gd_r.at[at], x))
            rest.append(send(mid.at[2, cut], mid.at[6, cut], gc_s.at[2, at], gc_r.at[2, at], core))
    extra_d = []
    for c, cut in enumerate(cuts):
        extra_x[c].wait()
        extra_d.append(
            send(extra_all.at[1, cut], extra_all.at[3, cut], ed_s.at[c], ed_r.at[c], y)
        )
        over_x[c].wait()
        rest.append(send(mid.at[1, cut], mid.at[5, cut], gc_s.at[1, c], gc_r.at[1, c], core))
    rest.append(send(extra_all.at[1], extra_all.at[5], ec_s.at[0], ec_r.at[0], core))
    for c, cut in enumerate(cuts):
        diagonal[c].wait()
        rest.append(send(mid.at[3, cut], mid.at[7, cut], gc_s.at[3, c], gc_r.at[3, c], core))
    for copy in extra_d:
        copy.wait()
    rest.append(send(extra_all.at[3], extra_all.at[7], ec_s.at[1], ec_r.at[1], core))
    for copy in rest:
        copy.wait()


def middle(parts, tok, gain, extra):
    rows, width = tok.shape
    dma = pltpu.SemaphoreType.DMA
    buffer = pltpu.VMEM((rows, width), BF16)
    return pl.pallas_call(
        middle_kernel,
        in_specs=[in_vmem()] * 4,
        out_specs=[in_vmem(), in_hbm(), in_hbm()],
        out_shape=[
            jax.ShapeDtypeStruct((rows, width), F32),
            jax.ShapeDtypeStruct((8, rows, width), BF16),
            jax.ShapeDtypeStruct((8, rows, width), BF16),
        ],
        scratch_shapes=[pltpu.VMEM((2, rows, width), BF16), buffer, buffer, buffer]
        + [dma((CHUNKS,))] * 15
        + [dma((4,))]
        + [dma((4, CHUNKS))] * 2
        + [dma((2,))] * 2,
        compiler_params=pltpu.CompilerParams(
            collective_id=2, has_side_effects=True, vmem_limit_bytes=VMEM_LIMIT
        ),
    )(parts, tok, gain, extra)


def middle_back_kernel(
    parts, hidden, grad_out, gain, grad_hidden, gain_grad, attn,
    from_core, to_x, from_x, to_y, from_y, rounded,
    core_s, core_r, x_s, x_r, y_s, y_r, local_sem, gy_s, gy_r, gc_s, gc_r,
):
    rows, width = hidden.shape
    size = rows // CHUNKS
    x, y, core = near_partners()
    pl.semaphore_wait(greet([x, y, core]), 3)
    cuts = [pl.ds(c * size, size) for c in range(CHUNKS)]
    first = [
        send(parts.at[pl.ds(4, 4), cut], from_core.at[:, cut], core_s.at[c], core_r.at[c], core)
        for c, cut in enumerate(cuts)
    ]
    second, third = [], []
    for c, cut in enumerate(cuts):
        first[c].wait()

        for j in range(2):
            to_x[j, cut] = parts[2 * j + 1, cut] + from_core[2 * j + 1, cut]
        second.append(send(to_x.at[:, cut], from_x.at[:, cut], x_s.at[c], x_r.at[c], x))
    gain_grad[...] = jnp.zeros_like(gain_grad)
    pending, over_y = [], []
    for step in range(CHUNKS + 2):
        if step < CHUNKS:
            c, cut = step, cuts[step]
            second[c].wait()

            def add_x(r, carry, c=c):
                at = pl.ds(c * size + r * STRIP, STRIP)
                to_y[at] = (
                    parts[2, at].astype(F32) + from_core[2, at].astype(F32)
                    + from_x[1, at].astype(F32)
                ).astype(BF16)
                return carry

            lax.fori_loop(0, size // STRIP, add_x, 0)
            third.append(send(to_y.at[cut], from_y.at[cut], y_s.at[c], y_r.at[c], y))
        if 1 <= step <= CHUNKS:
            c, cut = step - 1, cuts[step - 1]
            third[c].wait()

            def back(r, carry, c=c):
                at = pl.ds(c * size + r * STRIP, STRIP)
                grad_mid = (
                    (parts[0, at].astype(F32) + from_core[0, at].astype(F32))
                    + from_x[0, at].astype(F32)
                ) + from_y[at].astype(F32)
                value = hidden[at]
                scale = rms_scale(value)
                unit = value * scale
                gain_grad[...] += jnp.sum(grad_mid * unit, axis=0, keepdims=True)
                scaled = grad_mid * gain[...]
                total = grad_out[at] + scale * (
                    scaled - unit * jnp.mean(scaled * unit, axis=1, keepdims=True)
                )
                grad_hidden[at] = total
                rounded[at] = total.astype(BF16)
                return carry

            lax.fori_loop(0, size // STRIP, back, 0)
            over_y.append(send(rounded.at[cut], attn.at[1, cut], gy_s.at[c], gy_r.at[c], y))
            pending.append(
                send(rounded.at[cut], attn.at[2, cut], gc_s.at[0, c], gc_r.at[0, c], core)
            )
            own = pltpu.make_async_copy(rounded.at[cut], attn.at[0, cut], local_sem.at[c])
            own.start()
            pending.append(own)
        if step >= 2:
            c, cut = step - 2, cuts[step - 2]
            over_y[c].wait()
            pending.append(
                send(attn.at[1, cut], attn.at[3, cut], gc_s.at[1, c], gc_r.at[1, c], core)
            )
    for copy in pending:
        copy.wait()


def middle_back(parts, hidden, grad_out, gain):
    rows, width = hidden.shape
    dma = pltpu.SemaphoreType.DMA

    def buffer(*lead):
        return pltpu.VMEM(lead + (rows, width), BF16)

    return pl.pallas_call(
        middle_back_kernel,
        in_specs=[in_vmem()] * 4,
        out_specs=[in_vmem(), in_vmem(), in_hbm()],
        out_shape=[
            jax.ShapeDtypeStruct((rows, width), F32),
            jax.ShapeDtypeStruct((1, width), F32),
            jax.ShapeDtypeStruct((4, rows, width), BF16),
        ],
        scratch_shapes=[buffer(4), buffer(2), buffer(2), buffer(), buffer(), buffer()]
        + [dma((CHUNKS,))] * 9
        + [dma((2, CHUNKS))] * 2,
        compiler_params=pltpu.CompilerParams(
            collective_id=3, has_side_effects=True, vmem_limit_bytes=VMEM_LIMIT
        ),
    )(parts, hidden, grad_out, gain)


def final_kernel(
    outer, dp, mats, gates, grad_pre, grad_gate, w_kqv, w_g, grad_rank, w_rank, tok,
    base, gain, small, *refs,
):
    out, tokens_grad, out_small, refs = refs[0], refs[1], refs[2], refs[3:]
    (
        from_x, from_below, from_above, total, parts, from_core, to_y, from_y, gain_grad,
        to_all, from_all,
        load, x_s, x_r, up_s, up_r, down_s, down_r, core_s, core_r, y_s, y_r, all_s, all_r,
    ) = refs
    rows, width = tok.shape
    size = rows // CHUNKS
    high = total.shape[2]
    seq = 2 * outer
    at = lax.axis_index("seq")
    me = lax.axis_index("dp") * seq + at
    z = at // 2
    x, y, core = near_partners()
    above, below = {"seq": at + 2}, {"seq": at - 2}
    has_above, has_below = z < outer - 1, z > 0
    greet_everyone(seq, dp)

    def block_of(i):
        ups = outer - 1 - z
        up_at = jnp.where(z < outer // 2, i, i - z)
        down_at = jnp.where(z < outer // 2, i - ups, i)
        is_up = (up_at >= 0) & (up_at < ups)
        block = jnp.where(is_up, outer - 1 - up_at, down_at)
        return jnp.where(i == outer - 1, z, block)

    def across(m, b):
        return pltpu.make_async_remote_copy(
            src_ref=mats.at[m, 1, b], dst_ref=from_x.at[m, b], send_sem=x_s.at[m, b],
            recv_sem=x_r.at[m, b], device_id=x, device_id_type=pl.DeviceIdType.MESH,
        )

    def up(m, b):
        return pltpu.make_async_remote_copy(
            src_ref=total.at[m, b], dst_ref=from_below.at[m, b], send_sem=up_s.at[m, b],
            recv_sem=up_r.at[m, b], device_id=above, device_id_type=pl.DeviceIdType.MESH,
        )

    def down(m, b):
        return pltpu.make_async_remote_copy(
            src_ref=total.at[m, b], dst_ref=from_above.at[m, b], send_sem=down_s.at[m, b],
            recv_sem=down_r.at[m, b], device_id=below, device_id_type=pl.DeviceIdType.MESH,
        )

    for m in range(3):
        across(m, block_of(0)).start()
    loads = [
        pltpu.make_async_copy(mats.at[m, 0] if m < 3 else gates, total.at[m], load.at[m])
        for m in range(4)
    ]
    for copy in loads:
        copy.start()

    def grad_in(g):
        some = pl.ds(g * rows, rows)
        parts[g] = (
            mm(grad_pre[some], w_kqv[...], 1, 0)
            + (mm(grad_gate[some], w_g[...], 1, 0) + mm(grad_rank[some], w_rank[...], 1, 1))
        ).astype(BF16)

    grad_in(3)
    first = send(parts.at[3], from_core.at[1], core_s.at[1], core_r.at[1], core)
    grad_in(1)
    first.wait()

    to_y[...] = parts[1] + from_core[1]

    def over_y():
        return pltpu.make_async_remote_copy(
            src_ref=to_y, dst_ref=from_y, send_sem=y_s.at[0], recv_sem=y_r.at[0], device_id=y,
            device_id_type=pl.DeviceIdType.MESH,
        )

    over_y().start()
    grad_in(2)
    first = send(parts.at[2], from_core.at[0], core_s.at[0], core_r.at[0], core)
    grad_in(0)
    first.wait()
    gain_grad[...] = jnp.zeros_like(gain_grad)
    for copy in loads:
        copy.wait()

    def back(c):
        def strip_back(r, carry):
            strip = pl.ds(pl.multiple_of(c * size + r * STRIP, STRIP), STRIP)
            grad = (
                parts[0, strip].astype(F32) + from_core[0, strip].astype(F32)
            ) + from_y[strip].astype(F32)
            value = tok[strip].astype(F32)
            scale = rms_scale(value)
            unit = value * scale
            gain_grad[...] += jnp.sum(grad * unit, axis=0, keepdims=True)
            scaled = grad * gain[...]
            tokens_grad[strip] = base[strip] + scale * (
                scaled - unit * jnp.mean(scaled * unit, axis=1, keepdims=True)
            )
            return carry

        lax.fori_loop(0, size // STRIP, strip_back, 0)

    def add_into(m, b, other):
        total[m, b] = total[m, b] + other[m, b]

    def reduce_block(i, carry):
        b = block_of(i)
        for m in (3, 0, 1, 2):
            if m < 3:
                across(m, b).wait()

                @pl.when(i + 1 < outer)
                def _():
                    across(m, block_of(i + 1)).start()

                add_into(m, b, from_x)

            @pl.when(b > z)
            def _():
                @pl.when(has_below)
                def _():
                    up(m, b).wait_recv()
                    add_into(m, b, from_below)

                up(m, b).start()

            @pl.when(b < z)
            def _():
                @pl.when(has_above)
                def _():
                    down(m, b).wait_recv()
                    add_into(m, b, from_above)

                down(m, b).start()

            if m < 3:
                turn = 2 * (3 * (i - 1) + m)
                if m == 0:
                    @pl.when(i == 1)
                    def _():
                        over_y().wait()

                @pl.when((turn >= 0) & (turn < CHUNKS))
                def _():
                    back(turn)
                    back(turn + 1)

        return carry

    lax.fori_loop(0, outer - 1, reduce_block, 0)
    devices = seq * dp
    each = width // devices
    row, col = grid_index(devices, width)
    spread = jnp.where(col // each == row, gain_grad[...], 0.0)
    picked_row, picked_col = grid_index(width, 128)
    gathered = mm_exact(spread, ((picked_row % each) == picked_col).astype(F32), 1, 0)
    height = small.shape[1]
    to_all[:, :height] = small[...]
    to_all[:, height:] = jnp.broadcast_to(
        gathered.reshape(devices, 1, 128), (devices, to_all.shape[1] - height, 128)
    )

    def push(r, where):
        return pltpu.make_async_remote_copy(
            src_ref=to_all.at[jnp.bitwise_xor(me, r)], dst_ref=from_all.at[r],
            send_sem=all_s.at[r], recv_sem=all_r.at[r], device_id=where,
            device_id_type=pl.DeviceIdType.MESH,
        )

    everyone(seq, dp, lambda r, where: push(r, where).start())
    lax.fori_loop(outer - 1, outer, reduce_block, 0)
    out_small[...] = to_all[me]

    def add_small(r, where):
        push(r, where).wait()
        out_small[...] += from_all[r]

    everyone(seq, dp, add_small)
    for m in range(4):
        out[m] = total[m, z].astype(F32)

        @pl.when(has_below)
        def _():
            up(m, z).wait_recv()
            out[m] += from_below[m, z].astype(F32)

        @pl.when(has_above)
        def _():
            down(m, z).wait_recv()
            out[m] += from_above[m, z].astype(F32)

    def sent(b, carry):
        for m in range(4):
            @pl.when(b > z)
            def _():
                up(m, b).wait_send()

            @pl.when(b < z)
            def _():
                down(m, b).wait_send()

        return carry

    lax.fori_loop(0, outer, sent, 0)


def finish(outer, dp, mats, gates, operands, rest, small):
    rows, width = rest[-3].shape
    high = mats.shape[3]
    devices = 2 * outer * dp
    dma = pltpu.SemaphoreType.DMA
    blocks = pltpu.VMEM((4, outer, high, width), BF16)
    buffer = pltpu.VMEM((rows, width), BF16)
    payload = (small.shape[1] + 8, 128)
    return pl.pallas_call(
        functools.partial(final_kernel, outer, dp),
        in_specs=[in_hbm()] * 2 + [in_vmem()] * (len(operands) + len(rest) + 1),
        out_specs=[in_vmem()] * 3,
        out_shape=[
            jax.ShapeDtypeStruct((4, high, width), F32),
            jax.ShapeDtypeStruct((rows, width), F32),
            jax.ShapeDtypeStruct(payload, F32),
        ],
        scratch_shapes=[pltpu.VMEM((3, outer, high, width), BF16)]
        + [blocks] * 3
        + [
            pltpu.VMEM((4, rows, width), BF16), pltpu.VMEM((2, rows, width), BF16), buffer,
            buffer, pltpu.VMEM((1, width), F32),
            pltpu.VMEM((devices,) + payload, F32), pltpu.VMEM((devices,) + payload, F32),
            dma((4,)),
        ]
        + [dma((4, outer))] * 6
        + [dma((2,))] * 2
        + [dma((1,))] * 2
        + [dma((devices,))] * 2,
        compiler_params=pltpu.CompilerParams(
            collective_id=4, has_side_effects=True, vmem_limit_bytes=60 * 1024 * 1024
        ),
    )(mats, gates, *operands, *rest, small)


class Lanes:
    def __init__(self):
        self.seq = lax.axis_size("seq")
        self.dp = lax.axis_size("dp")
        self.outer = self.seq // 2
        self.at = lax.axis_index("seq")
        self.d = lax.axis_index("dp")
        self.inner_at = lax.rem(self.at, 2)
        self.outer_at = self.at // 2
        self.groups = [[2 * k + i for k in range(self.outer)] for i in range(2)]

    def swap_inner(self, x):
        return lax.ppermute(x, "seq", [(i, i ^ 1) for i in range(self.seq)])

    def gather_outer(self, x):
        return lax.all_gather(x, "seq", axis=0, tiled=True, axis_index_groups=self.groups)

    def scatter_outer(self, x):
        return lax.psum_scatter(
            x, "seq", scatter_dimension=0, tiled=True, axis_index_groups=self.groups
        )

    def swap_dp(self, x, bit):
        return lax.ppermute(x, "dp", [(i, i ^ bit) for i in range(self.dp)])

    def swap_seq(self, x, bit):
        return lax.ppermute(x, "seq", [(i, i ^ bit) for i in range(self.seq)])

    def exchange_heads(self, blocks):
        got = [lax.dynamic_index_in_dim(blocks, self.d, 0, keepdims=False)]
        for r in range(1, self.dp):
            part = lax.dynamic_index_in_dim(
                blocks, jnp.bitwise_xor(self.d, r), 0, keepdims=False
            )
            got.append(self.swap_dp(part, r))
        bit = 1
        while bit < self.dp:
            is_set = (self.d // bit) % 2 == 1
            got = [jnp.where(is_set, got[i ^ bit], got[i]) for i in range(self.dp)]
            bit *= 2
        return jnp.stack(got)

    def pick(self, natural, axis):
        first = lax.index_in_dim(natural, 0, axis, keepdims=False)
        second = lax.index_in_dim(natural, 1, axis, keepdims=False)
        even = self.inner_at == 0
        return jnp.where(even, first, second), jnp.where(even, second, first)


def swap_halves(x, parts):
    size = x.shape[-1] // (2 * parts)
    pieces = [x[..., i * size : (i + 1) * size] for i in range(2 * parts)]
    order = [i ^ 1 for i in range(2 * parts)]
    return jnp.concatenate([pieces[i] for i in order], axis=-1)


def per_device(
    tokens, lengths, cotangent, mixer_gain, feed_gain, head_gain, w_query, w_key, w_value,
    w_gate, w_out, rank_down, rank_up, rank_bias, w_act, w_lin, w_down,
):
    lanes = Lanes()
    seq_count, piece, width = tokens.shape
    rows = seq_count * piece
    sequences = lanes.dp * seq_count
    all_rows = lanes.dp * rows
    head_width = width // HEADS
    half_width = head_width // 2
    rank = rank_down.shape[1]
    devices = lanes.dp * lanes.seq

    counts = lengths.astype(F32)
    high = jnp.floor(counts / 256.0)
    small_parts = [
        mixer_gain, feed_gain, head_gain, rank_down.reshape(-1), rank_up.reshape(-1),
        rank_bias, high.astype(BF16), (counts - 256.0 * high).astype(BF16),
    ]
    sizes = [p.shape[0] for p in small_parts]
    used = sum(sizes)
    padded = -(-used // 2048) * 2048
    small = jnp.concatenate(small_parts + [jnp.zeros((padded - used,), BF16)])
    own_tokens = tokens.reshape(rows, width)
    position = (lanes.at * piece + jnp.arange(piece)).astype(F32)
    alive_own = (position[None, :] < counts[:, None]).astype(F32).reshape(rows, 1)
    grad_out = cotangent.reshape(rows, width).astype(F32) * alive_own
    w_kqv, out_mine, plane_tokens, grad_feed, smalls = gather_all(
        lanes.outer, lanes.dp, [w_key, w_query, w_value], [own_tokens, grad_out.astype(BF16)],
        small.reshape(-1, 128), w_out,
    )
    w_kqv = w_kqv.reshape(3 * head_width, width)
    out_rows = w_out.shape[0]
    out_own, out_other = lanes.pick(
        out_mine.reshape(lanes.dp, out_rows, lanes.outer, 2, -1), 3
    )
    out_mine = jnp.concatenate(
        [
            out_own.reshape(lanes.dp, out_rows, half_width),
            out_other.reshape(lanes.dp, out_rows, half_width),
        ],
        axis=2,
    )
    gate_and_out = lanes.gather_outer(
        jnp.concatenate([w_gate, out_mine.reshape(out_rows, width)], axis=0)
    )
    smalls = smalls.reshape(devices, padded)
    cuts, offset = [], 0
    for size in sizes:
        cuts.append(smalls[:, offset : offset + size])
        offset += size
    mixer_full = cuts[0].reshape(1, width).astype(F32)
    feed_full = cuts[1].reshape(1, width).astype(F32)
    head_natural = cuts[2].reshape(lanes.outer, 2, half_width // lanes.outer)
    head_own, head_other = lanes.pick(head_natural, 1)
    head_full = jnp.concatenate(
        [head_own.reshape(1, half_width), head_other.reshape(1, half_width)], axis=1
    ).astype(F32)
    down_full = cuts[3].reshape(width, rank)
    up_mine = lax.dynamic_index_in_dim(
        cuts[4].reshape(lanes.dp, SLOTS, rank), lanes.d, 0, keepdims=False
    )
    bias_mine = lax.dynamic_index_in_dim(
        cuts[5].reshape(lanes.dp, 1, SLOTS), lanes.d, 0, keepdims=False
    ).astype(F32)
    all_lengths = cuts[6].astype(F32) * 256.0 + cuts[7].astype(F32)
    all_lengths = all_lengths.reshape(lanes.dp, lanes.seq, seq_count)[:, 0]

    group_lengths = jnp.concatenate(
        [
            lax.dynamic_index_in_dim(
                all_lengths, jnp.bitwise_xor(lanes.d, r), 0, keepdims=False
            )
            for r in (0, 2, 1, 3)
        ]
    )
    alive = (position[None, :] < group_lengths[:, None]).astype(F32).reshape(all_rows, 1)

    sources = plane_tokens.reshape(all_rows, width).astype(F32)
    normed_in = lax.optimization_barrier(
        (sources * rms_scale(sources) * mixer_full).astype(BF16)
    )

    pre = contract_last(normed_in, w_kqv)
    low_rank = mm(normed_in, down_full, 1, 0).astype(BF16)
    gate_logit = contract_last(low_rank, up_mine) + bias_mine
    log_decay = jax.nn.log_sigmoid(gate_logit) / GATE_NORM * alive
    writes = -jnp.expm1(log_decay)

    def seqs(x):
        return x.reshape(sequences, piece, x.shape[1])

    def flat(x):
        return x.reshape(all_rows, x.shape[2])

    is_value = jnp.arange(3 * head_width) >= 2 * head_width
    feats = seqs(jnp.where(is_value, pre, pre * jax.nn.sigmoid(pre)).astype(BF16))
    pre = seqs(pre)
    decays, writes = seqs(log_decay), seqs(writes)

    def shaped(like_rows, columns, kind):
        return jax.ShapeDtypeStruct((sequences, like_rows, columns), kind)

    gate_and_out, feats = lax.optimization_barrier((gate_and_out, feats))
    keys, queries, values = (feats, 0), (feats, 1), (feats, 2)
    state_in, keeps = relay(
        lanes.outer, False, [feats, decays, writes], sequences, SLOTS, 2 * head_width
    )
    feed = jnp.stack([w_down, w_act, w_lin])
    feed, state_in, gate_and_out = lax.optimization_barrier((feed, state_in, gate_and_out))
    feed = lax.all_gather(
        feed, "seq", axis=1, tiled=True, axis_index_groups=lanes.groups
    )
    gate_and_out = gate_and_out.reshape(lanes.outer, 2, out_rows, width)
    gate_own, out_own = gate_and_out[:, 0], gate_and_out[:, 1]
    gate_other = lanes.swap_inner(gate_own)
    w_g = jnp.concatenate([gate_own, gate_other], axis=0).reshape(head_width, width)
    gates = seqs(contract_last(normed_in, w_g))
    out_own = out_own.reshape(lanes.outer, lanes.dp, out_rows, head_width)
    out_other = swap_halves(lanes.swap_inner(out_own), 1)
    even = lanes.inner_at == 0
    natural = jnp.stack(
        [jnp.where(even, out_own, out_other), jnp.where(even, out_other, out_own)], axis=2
    )
    out_full = natural.transpose(1, 0, 2, 3, 4).reshape(width, head_width)
    mixed, slot_out, attend = per_sequence(
        forward_kernel,
        [queries, keys, values, gates, decays, writes, state_in],
        [
            shaped(piece, head_width, BF16),
            shaped(piece, head_width, F32),
            shaped(piece, SLOTS, F32),
        ],
        shared=[head_full],
    )
    mixed_flat = flat(mixed)
    parts = contract_last(mixed_flat, out_full).astype(BF16)
    hidden, normed_mid, grad_feed = middle(
        parts.reshape(4, rows, width), own_tokens, feed_full, grad_feed
    )
    normed_mid = normed_mid.reshape(8 * rows, width)
    grad_feed = grad_feed.reshape(8 * rows, width)

    units = feed.shape[1]
    product, grad_gate, grad_lin = feed_tiles(
        feed_kernel, [normed_mid, grad_feed], feed, [units] * 3
    )
    feed_grads = jnp.stack(
        [
            contract_first(product, grad_feed).astype(BF16),
            contract_first(grad_gate, normed_mid).astype(BF16),
            contract_first(grad_lin, normed_mid).astype(BF16),
        ]
    )
    product, grad_gate, grad_lin, feed_grads = lax.optimization_barrier(
        (product, grad_gate, grad_lin, feed_grads)
    )
    feed_grads = lax.psum_scatter(
        feed_grads, "seq", scatter_dimension=1, tiled=True, axis_index_groups=lanes.groups
    )
    feed_parts, mid_parts = feed_tiles(
        feed_back_kernel, [product, grad_gate, grad_lin], feed, [width] * 2
    )
    grad_hidden, feed_gain_part, grad_attn = middle_back(
        mid_parts.reshape(8, rows, width), hidden, grad_out, feed_full
    )
    grad_attn = grad_attn.reshape(all_rows, width)
    feed_parts, grad_attn = lax.optimization_barrier((feed_parts, grad_attn))

    grad_mixed = mm(grad_attn, out_full, 1, 0)
    grad_gate_pre, grad_slot, grad_scores, adjoint, head_parts = per_sequence(
        back_first_kernel,
        [seqs(grad_mixed), gates, slot_out, attend, queries, values, decays, writes, state_in],
        [
            shaped(piece, head_width, BF16),
            shaped(piece, head_width, BF16),
            shaped(piece, SLOTS, F32),
            shaped(SLOTS, 2 * head_width, F32),
            shaped(1, head_width, F32),
        ],
        shared=[head_full],
    )
    grad_gate_flat = flat(grad_gate_pre)
    out_grad = contract_first(grad_attn, mixed_flat).astype(BF16)
    out_grad = out_grad.reshape(lanes.dp, lanes.outer, 2, out_rows, head_width)
    own_part, other_part = lanes.pick(out_grad, 2)
    got = swap_halves(lanes.swap_inner(other_part), 1)
    out_sum = (own_part.astype(F32) + got.astype(F32)).astype(BF16).transpose(1, 0, 2, 3)
    gate_grad = contract_first(grad_gate_flat, normed_in).astype(BF16)
    adjoint, out_sum, gate_grad, feed_parts = lax.optimization_barrier(
        (adjoint, out_sum, gate_grad, feed_parts)
    )
    adjoint_in, feed_sums, gate_got = relay(
        lanes.outer, True,
        [adjoint, keeps, feed_parts.reshape(8, rows, width), gate_grad[half_width:]], sequences,
        SLOTS, 2 * head_width,
    )
    gate_grad, out_sum, adjoint_in, feed_grads = lax.optimization_barrier(
        (gate_grad, out_sum, adjoint_in, feed_grads)
    )
    out_mine = lanes.scatter_outer(out_sum.reshape(-1, head_width))
    grad_pre, grad_logit = per_sequence(
        back_second_kernel,
        [
            grad_slot, grad_scores, attend, queries, keys, values, decays, writes,
            state_in, adjoint_in, (pre, 1), (pre, 0), seqs(gate_logit), seqs(alive),
        ],
        [shaped(piece, 3 * head_width, BF16), shaped(piece, SLOTS, BF16)],
    )
    feed_got = lanes.swap_inner(feed_sums[1])
    grad_pre, out_mine = lax.optimization_barrier((flat(grad_pre), out_mine))
    grad_logit = flat(grad_logit)
    bias_part = jnp.sum(grad_logit.astype(F32), axis=0)
    up_part = contract_first(grad_logit, low_rank)
    grad_rank = mm(grad_logit, up_mine, 1, 0).astype(BF16)
    down_part = contract_first(normed_in, grad_rank)

    mixer_grads = contract_first(grad_pre, normed_in).astype(BF16)
    mixer_grads = mixer_grads.reshape(3, 2, lanes.outer, -1, width)

    head_part = jnp.sum(head_parts, axis=(0, 1)).reshape(2, lanes.outer, -1)
    low_half, high_half = lanes.pick(head_part, 0)
    head_part = jnp.stack([low_half, high_half], axis=1)
    mine = (jnp.arange(lanes.dp) == lanes.d).astype(F32)
    up_all = mine[:, None] * up_part.reshape(1, -1)
    bias_all = mine[:, None] * bias_part.reshape(1, -1)
    parts = [
        feed_gain_part.reshape(devices, -1),
        head_part.reshape(devices, -1),
        down_part.reshape(devices, -1),
        up_all.reshape(devices, -1),
        bias_all.reshape(devices, -1),
    ]
    sizes = [p.shape[1] for p in parts]
    padded = -(-sum(sizes) // 1024) * 1024
    parts.append(jnp.zeros((devices, padded - sum(sizes)), F32))
    small_parts = jnp.concatenate(parts, axis=1).reshape(devices, -1, 128)
    gate_sum = (gate_grad[:half_width].astype(F32) + gate_got.astype(F32)).astype(BF16)
    out_mine = out_mine.reshape(lanes.dp, out_rows, head_width)
    out_mine = lanes.exchange_heads(out_mine).transpose(1, 0, 2)
    out_mine = out_mine.reshape(out_rows, lanes.dp, 2, lanes.outer, -1)
    low_half, high_half = lanes.pick(out_mine, 2)
    w_out_grad = jnp.stack([low_half, high_half], axis=3).reshape(out_rows, width).astype(F32)
    mixer_grads, feed_got, w_out_grad = lax.optimization_barrier(
        (mixer_grads, feed_got, w_out_grad)
    )
    weight_grads, tokens_grad, reduced = finish(
        lanes.outer, lanes.dp, mixer_grads,
        gate_sum.reshape(lanes.outer, -1, width),
        [grad_pre, grad_gate_flat, w_kqv, w_g],
        [grad_rank, down_full, own_tokens, grad_hidden, mixer_full],
        small_parts,
    )
    w_key_grad, w_query_grad, w_value_grad, w_gate_grad = [weight_grads[m] for m in range(4)]
    tokens_grad = tokens_grad.reshape(seq_count, piece, width)
    feed_sum = feed_sums[0].astype(F32) + feed_got.astype(F32)
    block_out = (alive_own * (hidden + feed_sum)).astype(BF16)
    mixer_gain_grad = reduced[padded // 128, : width // devices]
    reduced = reduced.reshape(-1)
    smalls, offset = [], 0
    for size in sizes:
        smalls.append(reduced[offset : offset + size])
        offset += size
    return (
        block_out.reshape(seq_count, piece, width),
        tokens_grad,
        mixer_gain_grad,
        smalls[0],
        smalls[1],
        w_query_grad,
        w_key_grad,
        w_value_grad,
        w_gate_grad,
        w_out_grad,
        smalls[2].reshape(-1, rank),
        smalls[3].reshape(-1, rank),
        smalls[4],
        feed_grads[1].astype(F32),
        feed_grads[2].astype(F32),
        feed_grads[0].astype(F32),
    )


def solution(mesh):
    vector = P(("dp", "seq"))
    matrix = P(("dp", "seq"), None)
    stream = P("dp", "seq", None)
    return jax.shard_map(
        per_device,
        mesh=mesh,
        in_specs=(
            stream, P("dp"), stream, vector, vector, vector, matrix, matrix, matrix, matrix,
            matrix, matrix, matrix, vector, matrix, matrix, matrix,
        ),
        out_specs=(
            stream, stream, vector, vector, vector, matrix, matrix, matrix, matrix, matrix,
            matrix, matrix, vector, matrix, matrix, matrix,
        ),
        check_vma=False,
    )
```
